32 devices in a mesh: head: 4 (over z), seq: 8 (over y, x, core).
Axes of the slice: x: 2, y: 2, z: 4, core: 2. Of those that a mesh axis runs over, the one named last changes fastest.
Arguments:
- inputs: bfloat16 [2048, 2048], P('seq', 'head'), may hold values from -6 to 6
- cotangent: bfloat16 [2048, 2048], P('seq', 'head'), may hold values from -6 to 6
- owners: int32 [261], replicated, may hold values from 0 to 7, as said below
- master: float32 [352, 262144], P('seq', 'head'), may hold values from -16 to 16
- moment_one: float32 [352, 262144], P('seq', 'head')
- moment_two: float32 [352, 262144], P('seq', 'head'), as said below
Outputs:
- block_out: bfloat16 [2048, 2048], P('seq', 'head')
- input_grad: float32 [2048, 2048], P('seq', 'head')
- grad_slots: float32 [352, 262144], P('seq', 'head')
- master_new: float32 [352, 262144], P('seq', 'head')
- moment_one_new: float32 [352, 262144], P('seq', 'head')
- moment_two_new: float32 [352, 262144], P('seq', 'head')
- weights_low: bfloat16 [352, 262144], P('seq', 'head')
The draws below stay inside these ranges and needn't reach their ends.
Inputs may be any that keep to these rules, and one draw needn't show every extreme that they name: owners[p] is the index along seq of the device that keeps block p of every head shard; no index appears more than 44 times and some index exactly 44 times. `moment_two`: every entry is positive.
All inputs are finite; a program needn't handle non-finite values.
Results may differ from the reference program's by a relative error of at most 0.019.
Values may be sent and summed in bfloat16 or wider, within the bound.
No kernel may reach another device: no remote copies, remote signals or barrier semaphores. Data moves between devices by JAX's collectives and lax.ppermute only.
A program may use at most 1.1875 GiB of HBM per device.

```python
import jax
import jax.numpy as jnp
import numpy as np
from jax import lax

D = 2048
HEADS = 16
DK = 128
DV = 256
FF = 5632
KCONV = 4
GROUP = 64
STEP = 5
PIECE = 65536
TOKENS = 2048
NPIECE = 261
CAP = 44
SLOTS = 352
N_HEAD = 4
N_SEQ = 8


def draw_layout():
    local_heads = HEADS // N_HEAD
    return [('wq', D, local_heads * DK, D ** (-0.5), 0.05), ('wk', D, local_heads * DK, D ** (-0.5), 0.05), ('wv', D, local_heads * DV, D ** (-0.5), 0.1), ('wg', D, local_heads * DV, D ** (-0.5), 0.35), ('wo', local_heads * DV, D, (HEADS * DV) ** (-0.5), 0.6), ('wgate', D, FF // N_HEAD, D ** (-0.5), 0.3), ('wup', D, FF // N_HEAD, D ** (-0.5), 0.35), ('wdown', FF // N_HEAD, D, FF ** (-0.5), 0.6), ('cq', KCONV, local_heads * DK, 0.5, 0.2), ('ck', KCONV, local_heads * DK, 0.5, 0.2), ('cv', KCONV, local_heads * DV, 0.5, 0.2), ('wab', D, 2 * local_heads, D ** (-0.5), 0.05), ('alog', 1, local_heads, 1.0, 0.01), ('dtbias', 1, local_heads, 1.0, 0.01), ('gainone', 1, D // N_HEAD, 1.0, 1.0), ('gaintwo', 1, D // N_HEAD, 1.0, 1.0), ('wnorm', 1, DV // N_HEAD, 1.0, 1.0)]


def owner_list(key):
    slots_total = N_SEQ * CAP
    slot_ids = jnp.arange(slots_total, dtype=jnp.int32)
    full_device = jax.random.randint(jax.random.fold_in(key, 11), (), 0, N_SEQ)
    attention_logits = jax.random.randint(jax.random.fold_in(key, 12), (slots_total,), 0, 1 << 20) * slots_total + slot_ids
    attention_logits = jnp.where(slot_ids // CAP == full_device, slot_ids - slots_total, attention_logits)
    chosen = jnp.argsort(attention_logits, stable=True)[:NPIECE].astype(jnp.int32)
    shuffle = jax.random.permutation(jax.random.fold_in(key, 13), NPIECE)
    return jnp.zeros((NPIECE,), jnp.int32).at[shuffle].set(chosen // CAP)


def slot_table(owners):
    devices = jnp.arange(N_SEQ, dtype=jnp.int32)
    onehot = (owners[:, None] == devices[None, :]).astype(jnp.int32)
    before = jnp.cumsum(onehot, axis=0) - onehot
    rank_within = jnp.sum(before * onehot, axis=1)
    slot_of_piece = (owners * CAP + rank_within).astype(jnp.int32)
    matches = slot_of_piece[None, :] == jnp.arange(SLOTS, dtype=jnp.int32)[:, None]
    present = jnp.any(matches, axis=1)
    piece_of_slot = jnp.sum(matches.astype(jnp.int32) * jnp.arange(NPIECE, dtype=jnp.int32)[None, :], axis=1).astype(jnp.int32)
    return (piece_of_slot, present)


def to_slots(flat_values, owners, filler):
    piece_of_slot, present = slot_table(owners)
    chosen = jnp.transpose(flat_values[:, piece_of_slot, :], (1, 0, 2)).reshape(SLOTS, N_HEAD * PIECE)
    return jnp.where(present[:, None], chosen, filler)


def grad_scales():
    scale_list = []
    used_size = 0
    for seg_name, row_count, col_count, weight_scale, grad_scale in draw_layout():
        scale_list.append(jnp.full((row_count * col_count,), grad_scale, jnp.float32))
        used_size += row_count * col_count
    scale_list.append(jnp.full((NPIECE * PIECE - used_size,), 0.1, jnp.float32))
    return jnp.concatenate(scale_list) * TOKENS ** 0.5


def draw_owners(key, part):
    return owner_list(key)


def draw_master(key, part):
    owners = owner_list(key)
    key = jax.random.fold_in(key, 31)
    local_heads = HEADS // N_HEAD
    uniform_head = jax.random.uniform(jax.random.fold_in(key, 5), (N_HEAD, 1, local_heads), jnp.float32)
    noise = jnp.clip(jax.random.normal(key, (N_HEAD, NPIECE * PIECE), jnp.float32), -3.5, 3.5)
    ramp_low = 0.6
    ramp_ratio = 3.0
    mean_rates = jnp.exp(jnp.log(0.5 / TOKENS) + uniform_head * (jnp.log(1.0 / 40.0) - jnp.log(0.5 / TOKENS)))
    values_list = []
    offset_now = 0
    for seg_name, row_count, col_count, weight_scale, grad_scale in draw_layout():
        seg_size = row_count * col_count
        piecewise_random_perturbation = noise[:, offset_now:offset_now + seg_size].reshape(N_HEAD, row_count, col_count)
        if seg_name == 'alog':
            seg_values = jnp.log(mean_rates / 0.135)
        elif seg_name == 'dtbias':
            seg_values = -4.0 + 0.25 * piecewise_random_perturbation
        elif seg_name == 'gainone' or seg_name == 'gaintwo':
            feature = (jnp.arange(N_HEAD)[:, None, None] * col_count + jnp.arange(col_count)[None, None, :]).astype(jnp.float32) / (D - 1)
            seg_values = ramp_low * ramp_ratio ** feature * (1.0 + 0.1 * piecewise_random_perturbation)
        elif seg_name == 'wnorm':
            seg_values = 1.0 + 0.1 * piecewise_random_perturbation
        elif seg_name == 'wab':
            column_scale = jnp.where(jnp.arange(col_count) < local_heads, 2.0 * D ** (-0.5), D ** (-0.5))
            seg_values = column_scale[None, None, :] * piecewise_random_perturbation
        else:
            seg_values = weight_scale * piecewise_random_perturbation
        values_list.append(seg_values.reshape(N_HEAD, seg_size))
        offset_now += seg_size
    values_list.append(0.1 * noise[:, offset_now:])
    flat_values = jnp.concatenate(values_list, axis=1).reshape(N_HEAD, NPIECE, PIECE)
    filler = 0.05 * jnp.clip(jax.random.normal(jax.random.fold_in(key, 7), (SLOTS, N_HEAD * PIECE), jnp.float32), -3.5, 3.5)
    return to_slots(flat_values, owners, filler)


def draw_moment_one(key, part):
    owners = owner_list(key)
    key = jax.random.fold_in(key, 41)
    noise = jnp.clip(jax.random.normal(key, (N_HEAD, NPIECE * PIECE), jnp.float32), -3.0, 3.0)
    flat_values = (grad_scales()[None, :] * noise).reshape(N_HEAD, NPIECE, PIECE)
    filler = 0.1 * TOKENS ** 0.5 * jnp.clip(jax.random.normal(jax.random.fold_in(key, 7), (SLOTS, N_HEAD * PIECE), jnp.float32), -3.0, 3.0)
    return to_slots(flat_values, owners, filler)


def draw_moment_two(key, part):
    owners = owner_list(key)
    key = jax.random.fold_in(key, 51)
    factor = jnp.exp(jax.random.uniform(key, (N_HEAD, NPIECE * PIECE), jnp.float32, -0.6931, 0.6931))
    scales = grad_scales()
    flat_values = (2.0 * scales[None, :] * scales[None, :] * factor).reshape(N_HEAD, NPIECE, PIECE)
    filler_factor = jnp.exp(jax.random.uniform(jax.random.fold_in(key, 7), (SLOTS, N_HEAD * PIECE), jnp.float32, -0.6931, 0.6931))
    filler = 2.0 * 0.01 * TOKENS * filler_factor
    return to_slots(flat_values, owners, filler)


def levels(key, dims, cuts, least, top_value):
    gain, own = 1.0, jax.random.fold_in(key, 6)
    for dim, blocks in cuts:
        draws = jnp.exp(jax.random.uniform(jax.random.fold_in(own, dim), (blocks,), jnp.float32, least / len(cuts), top_value / len(cuts)))
        gain = gain * jnp.repeat(draws, dims[dim] // blocks).reshape([-1 if axis == dim else 1 for axis in range(len(dims))])
    return gain


def normal_values(rng, shape, scale, most, shards=(), kind=jnp.bfloat16):
    gain = levels(rng, shape, shards, -0.22, 0.18) if shards else 1.0
    values = jax.random.normal(rng, shape, jnp.float32) * scale * gain
    return jnp.minimum(jnp.maximum(values, -most), most).astype(kind)


def setup_inputs(seed: int = 0) -> dict:
    arg_keys = jax.random.split(jax.random.key(seed), 7)
    return {
        "inputs": normal_values(arg_keys[0], (TOKENS, D), 1.0, 6.0, ((0, 8), (1, 4))),
        "cotangent": normal_values(arg_keys[1], (TOKENS, D), 1.0, 6.0, ((0, 8), (1, 4))),
        "owners": draw_owners(jax.random.fold_in(arg_keys[6], 71), 0),
        "master": draw_master(jax.random.fold_in(arg_keys[6], 71), 0),
        "moment_one": draw_moment_one(jax.random.fold_in(arg_keys[6], 71), 0),
        "moment_two": draw_moment_two(jax.random.fold_in(arg_keys[6], 71), 0),
    }


@jax.custom_vjp
def low(v):
    return lax.optimization_barrier(v.astype(jnp.bfloat16)).astype(jnp.float32)

@jax.custom_vjp
def low_back(v):
    return v

def low_keep(v):
    return (low(v), None)

def low_pass(kept, grad):
    return (grad,)

def back_keep(v):
    return (v, None)

def back_low(kept, grad):
    return (low(grad),)
low.defvjp(low_keep, low_pass)
low_back.defvjp(back_keep, back_low)
EXACT_ARITHMETIC = lax.Precision.HIGHEST
NORM_EPSILON = 1e-06
UNIT_EPSILON = 1e-06
HEAD_EPSILON = 1e-05
ADAM_EPSILON = 1e-08
BETA_ONE = 0.5
BETA_TWO = 0.5
WEIGHT_DECAY = 0.1
PAD_RATE = 0.1

def shard_layout():
    local_heads = HEADS // N_HEAD
    return [('wq', D, local_heads * DK, 0.02), ('wk', D, local_heads * DK, 0.02), ('wv', D, local_heads * DV, 0.02), ('wg', D, local_heads * DV, 0.02), ('wo', local_heads * DV, D, 0.015), ('wgate', D, FF // N_HEAD, 0.02), ('wup', D, FF // N_HEAD, 0.02), ('wdown', FF // N_HEAD, D, 0.012), ('cq', KCONV, local_heads * DK, 0.4), ('ck', KCONV, local_heads * DK, 0.4), ('cv', KCONV, local_heads * DV, 0.4), ('wab', D, 2 * local_heads, 0.04), ('alog', 1, local_heads, 0.5), ('dtbias', 1, local_heads, 0.5), ('gainone', 1, D // N_HEAD, 0.1), ('gaintwo', 1, D // N_HEAD, 0.1), ('wnorm', 1, DV // N_HEAD, 0.1)]

def rate_table():
    rate_list = [np.full(row_count * col_count, seg_rate, np.float32) for seg_name, row_count, col_count, seg_rate in shard_layout()]
    flat_rates = np.concatenate(rate_list)
    flat_rates = np.concatenate([flat_rates, np.full(NPIECE * PIECE - flat_rates.size, PAD_RATE, np.float32)])
    return flat_rates.reshape(NPIECE, PIECE)

def piece_table(owners):
    devices = jnp.arange(N_SEQ, dtype=jnp.int32)
    onehot = (owners[:, None] == devices[None, :]).astype(jnp.int32)
    before = jnp.cumsum(onehot, axis=0) - onehot
    rank_within = lax.optimization_barrier(jnp.sum(before * onehot, axis=1))
    slot_of_piece = (owners * CAP + rank_within).astype(jnp.int32)
    matches = slot_of_piece[None, :] == jnp.arange(SLOTS, dtype=jnp.int32)[:, None]
    present = jnp.any(matches, axis=1)
    piece_of_slot = lax.optimization_barrier(jnp.sum(matches.astype(jnp.int32) * jnp.arange(NPIECE, dtype=jnp.int32)[None, :], axis=1)).astype(jnp.int32)
    return (slot_of_piece, piece_of_slot, present)

def matmul(left, right):
    return jnp.dot(left, right, precision=EXACT_ARITHMETIC, preferred_element_type=jnp.float32)

def stacked_columns(stacked):
    return jnp.transpose(stacked, (1, 0, 2)).reshape(stacked.shape[1], -1)

def stacked_rows(stacked):
    return stacked.reshape(-1, stacked.shape[2])

def short_conv(projected, conv_taps):
    row_count = projected.shape[0]
    padded = jnp.concatenate([jnp.zeros((KCONV - 1, projected.shape[1]), jnp.float32), projected], axis=0)
    running = conv_taps[0] * padded[0:row_count]
    for tap_number in range(1, KCONV):
        running = running + conv_taps[tap_number] * padded[tap_number:tap_number + row_count]
    return jax.nn.silu(running)

def token_step(current_state, inputs_now):
    current_query, current_key, value_now, decay_now, beta_now = inputs_now
    alpha_now = jnp.exp(decay_now)[:, None]
    key_state_product = jnp.einsum('xq,xqi->xi', current_key, current_state, precision=EXACT_ARITHMETIC)
    update = beta_now[:, None] * (value_now - alpha_now * key_state_product)
    current_state = alpha_now[:, :, None] * current_state + current_key[:, :, None] * update[:, None, :]
    return (current_state, jnp.einsum('xq,xqi->xi', current_query, current_state, precision=EXACT_ARITHMETIC))

def block_scan(current_state, block_inputs):
    return lax.scan(token_step, current_state, block_inputs)

def recurrence(queries, key_rows, values, decays, betas):
    token_count = queries.shape[0]
    blocks = token_count // GROUP

    def blocked(array_in):
        return array_in.reshape((blocks, GROUP) + array_in.shape[1:])
    start_state = jnp.zeros((HEADS, DK, DV), jnp.float32)
    unused, outputs = lax.scan(jax.checkpoint(block_scan), start_state, (blocked(queries), blocked(key_rows), blocked(values), blocked(decays), blocked(betas)))
    return outputs.reshape(token_count, HEADS, DV)

def forward(primal_in, pieces):
    by_name = dict(zip([segment[0] for segment in shard_layout()], pieces))
    local_heads = HEADS // N_HEAD
    row_count = primal_in.shape[0]
    scale_one = lax.rsqrt(lax.optimization_barrier(jnp.mean(primal_in * primal_in, axis=-1, keepdims=True)) + NORM_EPSILON)
    normed = low(primal_in * scale_one * by_name['gainone'].reshape(-1))
    query_proj = low_back(matmul(normed, stacked_columns(by_name['wq'])))
    key_proj = low_back(matmul(normed, stacked_columns(by_name['wk'])))
    value_proj = low_back(matmul(normed, stacked_columns(by_name['wv'])))
    gate_proj = low_back(matmul(normed, stacked_columns(by_name['wg'])))
    decay_in = low_back(matmul(normed, stacked_columns(by_name['wab'][:, :, :local_heads])))
    beta_in = low_back(matmul(normed, stacked_columns(by_name['wab'][:, :, local_heads:])))
    queries = short_conv(query_proj, stacked_columns(by_name['cq'])).reshape(row_count, HEADS, DK)
    queries = queries * lax.rsqrt(lax.optimization_barrier(jnp.sum(queries * queries, axis=-1, keepdims=True)) + UNIT_EPSILON) * DK ** (-0.5)
    key_rows = short_conv(key_proj, stacked_columns(by_name['ck'])).reshape(row_count, HEADS, DK)
    key_rows = key_rows * lax.rsqrt(lax.optimization_barrier(jnp.sum(key_rows * key_rows, axis=-1, keepdims=True)) + UNIT_EPSILON)
    values = short_conv(value_proj, stacked_columns(by_name['cv'])).reshape(row_count, HEADS, DV)
    betas = jax.nn.sigmoid(beta_in)
    decays = -jnp.exp(by_name['alog'].reshape(-1)) * jax.nn.softplus(decay_in + by_name['dtbias'].reshape(-1))
    recurred = recurrence(queries, key_rows, values, decays, betas)
    head_normed = recurred * lax.rsqrt(lax.optimization_barrier(jnp.mean(recurred * recurred, axis=-1, keepdims=True)) + HEAD_EPSILON) * by_name['wnorm'].reshape(-1)
    gated_out = low((head_normed * jax.nn.silu(gate_proj.reshape(row_count, HEADS, DV))).reshape(row_count, HEADS * DV))
    residual = primal_in + low_back(matmul(gated_out, stacked_rows(by_name['wo'])))
    resid_low = low(residual)
    scale_two = lax.rsqrt(lax.optimization_barrier(jnp.mean(resid_low * resid_low, axis=-1, keepdims=True)) + NORM_EPSILON)
    hidden_in = low(resid_low * scale_two * by_name['gaintwo'].reshape(-1))
    gate_mlp = low_back(matmul(hidden_in, stacked_columns(by_name['wgate'])))
    up_mlp = low_back(matmul(hidden_in, stacked_columns(by_name['wup'])))
    hidden = low(jax.nn.silu(gate_mlp) * up_mlp)
    return residual + low_back(matmul(hidden, stacked_rows(by_name['wdown'])))

def reference(inputs, cotangent, owners, master, moment_one, moment_two):
    slot_of_piece, piece_of_slot, present = piece_table(owners)
    low_master = master.astype(jnp.bfloat16).astype(jnp.float32)
    per_shard = jnp.transpose(low_master.reshape(SLOTS, N_HEAD, PIECE)[slot_of_piece], (1, 0, 2)).reshape(N_HEAD, NPIECE * PIECE)
    pieces = []
    offset_now = 0
    for seg_name, row_count, col_count, seg_rate in shard_layout():
        pieces.append(per_shard[:, offset_now:offset_now + row_count * col_count].reshape(N_HEAD, row_count, col_count))
        offset_now += row_count * col_count
    block_out, pullback = jax.vjp(forward, inputs.astype(jnp.float32), tuple(pieces))
    input_grad, piece_grads = pullback(cotangent.astype(jnp.float32))
    flat_grads = jnp.concatenate([grad_now.reshape(N_HEAD, -1) for grad_now in piece_grads], axis=1)
    flat_grads = jnp.pad(flat_grads, ((0, 0), (0, NPIECE * PIECE - offset_now)))
    slot_grads = jnp.transpose(flat_grads.reshape(N_HEAD, NPIECE, PIECE)[:, piece_of_slot, :], (1, 0, 2)).reshape(SLOTS, N_HEAD * PIECE)
    slot_grads = jnp.where(present[:, None], slot_grads, 0.0)
    slot_rates = jnp.asarray(rate_table())[piece_of_slot]
    slot_rates = jnp.where(present[:, None], slot_rates, PAD_RATE)
    slot_rates = jnp.tile(slot_rates, (1, N_HEAD))
    moment_new = BETA_ONE * moment_one + (1.0 - BETA_ONE) * slot_grads
    second_new = BETA_TWO * moment_two + (1.0 - BETA_TWO) * slot_grads * slot_grads
    first_hat = moment_new / (1.0 - BETA_ONE ** STEP)
    second_hat = second_new / (1.0 - BETA_TWO ** STEP)
    master_new = master - slot_rates * (first_hat / (jnp.sqrt(second_hat) + ADAM_EPSILON) + WEIGHT_DECAY * master)
    return (block_out.astype(jnp.bfloat16), input_grad, slot_grads, master_new, moment_new, second_new, master_new.astype(jnp.bfloat16))
```

```python
import jax
import jax.numpy as jnp
import numpy as np
from jax import lax
from jax.experimental import pallas as pl
from jax.experimental.pallas import tpu as pltpu
from jax.sharding import PartitionSpec as P

D = 2048
HEADS = 16
DK = 128
DV = 256
FF = 5632
KCONV = 4
STEP = 5


EXACT_ARITHMETIC = lax.Precision.HIGHEST
NORM_EPSILON = 1e-06
UNIT_EPSILON = 1e-06
HEAD_EPSILON = 1e-05
ADAM_EPSILON = 1e-08
BETA_ONE = 0.5
BETA_TWO = 0.5
WEIGHT_DECAY = 0.1
PAD_RATE = 0.1


def shifted(block, axis, distance):
    devices = range(lax.axis_size(axis))
    route = [(i - distance, i) for i in devices if i - distance in devices]
    return lax.ppermute(block, axis, route)


def shard_layout(local_heads, head_parts):
    return [
        ("wq", D, local_heads * DK, 0.02),
        ("wk", D, local_heads * DK, 0.02),
        ("wv", D, local_heads * DV, 0.02),
        ("wg", D, local_heads * DV, 0.02),
        ("wo", local_heads * DV, D, 0.015),
        ("wgate", D, FF // head_parts, 0.02),
        ("wup", D, FF // head_parts, 0.02),
        ("wdown", FF // head_parts, D, 0.012),
        ("cq", KCONV, local_heads * DK, 0.4),
        ("ck", KCONV, local_heads * DK, 0.4),
        ("cv", KCONV, local_heads * DV, 0.4),
        ("wab", D, 2 * local_heads, 0.04),
        ("alog", 1, local_heads, 0.5),
        ("dtbias", 1, local_heads, 0.5),
        ("gainone", 1, D // head_parts, 0.1),
        ("gaintwo", 1, D // head_parts, 0.1),
        ("wnorm", 1, DV // head_parts, 0.1),
    ]


def piece_table(owners, seq_parts, capacity):
    piece_count = owners.shape[0]
    devices = jnp.arange(seq_parts, dtype=jnp.int32)
    onehot = (owners[:, None] == devices[None, :]).astype(jnp.int32)
    before = jnp.cumsum(onehot, axis=0) - onehot
    rank_within = jnp.sum(before * onehot, axis=1)
    slot_of_piece = owners * capacity + rank_within
    matches = slot_of_piece[None, :] == jnp.arange(seq_parts * capacity, dtype=jnp.int32)[:, None]
    present = jnp.any(matches, axis=1)
    piece_of_slot = jnp.sum(
        matches.astype(jnp.int32) * jnp.arange(piece_count, dtype=jnp.int32)[None, :], axis=1
    )
    return (slot_of_piece, piece_of_slot, present)


def unpack(flat_weights, segments_list):
    by_name = {}
    offset_now = 0
    for seg_name, row_count, col_count, seg_rate in segments_list:
        by_name[seg_name] = flat_weights[offset_now : offset_now + row_count * col_count].reshape(
            row_count, col_count
        )
        offset_now += row_count * col_count
    return (by_name, offset_now)


def rate_parts(segments_list, piece_count, piece_size):
    piece_rates = np.full(piece_count, PAD_RATE, np.float32)
    small_rates = np.full(piece_size, PAD_RATE, np.float32)
    offset_now = 0
    big_total = (piece_count - 1) * piece_size
    for seg_name, row_count, col_count, seg_rate in segments_list:
        seg_size = row_count * col_count
        if offset_now < big_total:
            piece_rates[offset_now // piece_size : (offset_now + seg_size) // piece_size] = seg_rate
        else:
            small_rates[offset_now - big_total : offset_now - big_total + seg_size] = seg_rate
        offset_now += seg_size
    return (piece_rates, small_rates)


def product(left, right, left_axis, right_axis, exact=True):
    return lax.dot_general(
        left,
        right,
        (((left_axis,), (right_axis,)), ((), ())),
        precision=EXACT_ARITHMETIC if exact else None,
        preferred_element_type=jnp.float32,
    )


def take_lane(wide, lane):
    lanes = lax.broadcasted_iota(jnp.int32, wide.shape, 1)
    return jnp.sum(jnp.where(lanes == lane, wide, 0.0), axis=1, keepdims=True)


def put_lane(column, lane):
    lanes = lax.broadcasted_iota(jnp.int32, (column.shape[0], 128), 1)
    return jnp.where(lanes == lane, column, 0.0)


def to_row(column, diagonal):
    return jnp.sum(jnp.where(diagonal, column, 0.0), axis=0, keepdims=True)


def convolved(extended, block_ref, rim_ref, taps_ref):
    row_count = block_ref.shape[0]
    extended[0:8, :] = rim_ref[...]
    extended[8 : 8 + row_count, :] = block_ref[...]
    first = 8 - (KCONV - 1)
    running = taps_ref[0:1, :] * extended[first : first + row_count, :]
    for tap in range(1, KCONV):
        running = running + taps_ref[tap : tap + 1, :] * extended[
            first + tap : first + tap + row_count, :
        ]
    return running


def decay_terms(head, local_heads, decay_ref, scalars_ref):
    row_count = decay_ref.shape[0]
    shape = (row_count, row_count)
    row_ids = lax.broadcasted_iota(jnp.int32, shape, 0)
    column_ids = lax.broadcasted_iota(jnp.int32, shape, 1)
    decay_in = take_lane(decay_ref[...], head) + take_lane(scalars_ref[1:2, :], head)
    rate = -jnp.exp(take_lane(scalars_ref[0:1, :], head))
    soft = jnp.maximum(decay_in, 0.0) + jnp.log1p(jnp.exp(-jnp.abs(decay_in)))
    logs = rate * soft
    beta = jax.nn.sigmoid(take_lane(decay_ref[...], head + local_heads))
    diagonal = row_ids == column_ids
    logs_row = to_row(logs, diagonal)
    upto = row_ids >= column_ids
    sums = jnp.sum(jnp.where(upto, logs_row, 0.0), axis=1, keepdims=True)
    sums_row = to_row(sums, diagonal)
    within = jnp.exp(jnp.where(upto, sums - sums_row, -1e30))
    return decay_in, rate, logs, beta, sums, within, row_ids, column_ids


def unit_rows(rows):
    scale = lax.rsqrt(jnp.sum(rows * rows, axis=-1, keepdims=True) + UNIT_EPSILON)
    return rows * scale, scale


def mixer_specs(local_heads, row_count):
    def spec(rows, width, first):
        return pl.BlockSpec((rows, width), lambda h, first=first: (0, first + h))

    def three(rows):
        return [
            spec(rows, DK, 0),
            spec(rows, DK, local_heads),
            spec(rows, DV, 2 * local_heads * DK // DV),
        ]

    whole = pl.BlockSpec((row_count, 128), lambda h: (0, 0))
    scalars = pl.BlockSpec((8, 128), lambda h: (0, 0))
    return three, whole, scalars


def per_head(*shape):
    return pl.BlockSpec((1,) + shape, lambda h: (h,) + (0,) * len(shape))


def mixer_local(local_heads, projected, rim, taps, decay_proj, scalars):
    row_count = projected.shape[0]
    three, whole, scalar_spec = mixer_specs(local_heads, row_count)

    def kernel(
        pq, pk, pv, rq, rk, rv, tq, tk, tv, decay_ref, scalars_ref,
        solve_ref, fresh_ref, wy_ref, reach_ref, zero_ref, handoff_ref, ext_q, ext_k, ext_v,
    ):
        head = pl.program_id(0)
        queries = unit_rows(jax.nn.silu(convolved(ext_q, pq, rq, tq)))[0] * DK ** (-0.5)
        key_rows = unit_rows(jax.nn.silu(convolved(ext_k, pk, rk, tk)))[0]
        values = jax.nn.silu(convolved(ext_v, pv, rv, tv))
        decay_in, rate, logs, beta, sums, within, row_ids, column_ids = decay_terms(
            head, local_heads, decay_ref, scalars_ref
        )
        gram = product(key_rows, key_rows, 1, 1)
        system = jnp.where(row_ids > column_ids, beta * gram * within, 0.0)
        solve = jnp.where(row_ids == column_ids, 1.0, 0.0)
        size = 1
        while size < row_count:
            lower = (row_ids // (2 * size) == column_ids // (2 * size)) & (
                row_ids // size != column_ids // size
            )
            part = jnp.where(lower, system, 0.0)
            if size == 1:
                solve = solve - part
            else:
                solve = solve - product(solve, product(part, solve, 1, 0), 1, 0)
            size *= 2
        grown = jnp.exp(sums)
        fresh = product(solve, beta * values, 1, 0)
        wy_keys = product(solve, (beta * grown) * key_rows, 1, 0)
        attention = product(queries, key_rows, 1, 1) * within
        last = sums[row_count - 1 : row_count, :]
        tail_keys = jnp.exp(last - sums) * key_rows
        eye = lax.broadcasted_iota(jnp.int32, (DK, DK), 0) == lax.broadcasted_iota(
            jnp.int32, (DK, DK), 1
        )
        solve_ref[0] = solve
        fresh_ref[0] = fresh
        wy_ref[0] = wy_keys
        reach_ref[0] = grown * queries - product(attention, wy_keys, 1, 0)
        zero_ref[0] = product(attention, fresh, 1, 0)
        handoff_ref[0, :, :DK] = (
            jnp.where(eye, jnp.exp(last), 0.0) - product(tail_keys, wy_keys, 0, 0)
        ).astype(jnp.bfloat16)
        handoff_ref[0, :, DK:] = product(tail_keys, fresh, 0, 0).astype(jnp.bfloat16)

    def out(*shape, kind=jnp.float32):
        return jax.ShapeDtypeStruct((local_heads,) + shape, kind)

    return pl.pallas_call(
        kernel,
        grid=(local_heads,),
        in_specs=three(row_count) + three(8) + three(8) + [whole, scalar_spec],
        out_specs=[
            per_head(row_count, row_count),
            per_head(row_count, DV),
            per_head(row_count, DK),
            per_head(row_count, DK),
            per_head(row_count, DV),
            per_head(DK, DK + DV),
        ],
        out_shape=[
            out(row_count, row_count),
            out(row_count, DV),
            out(row_count, DK),
            out(row_count, DK),
            out(row_count, DV),
            out(DK, DK + DV, kind=jnp.bfloat16),
        ],
        scratch_shapes=[
            pltpu.VMEM((row_count + 8, DK), jnp.float32),
            pltpu.VMEM((row_count + 8, DK), jnp.float32),
            pltpu.VMEM((row_count + 8, DV), jnp.float32),
        ],
        compiler_params=params(),
    )(*([projected] * 3), *([rim] * 3), *([taps] * 3), decay_proj, scalars)


def mixer_out(local_heads, my_index, handoffs, reach, zero_out, projected, norm_gain):
    row_count = projected.shape[0]
    gate_first = local_heads * (2 * DK + DV)

    def kernel(index_ref, handoffs_ref, reach_ref, zero_ref, gate_ref, norm_ref, state_ref, out_ref, gated_ref):
        state_ref[...] = jnp.zeros_like(state_ref)

        def advance(j, carry):
            for h in range(local_heads):
                block = handoffs_ref[j, h]
                state_ref[h] = product(
                    block[:, :DK].astype(jnp.float32), state_ref[h], 1, 0
                ) + block[:, DK:].astype(jnp.float32)
            return carry

        lax.fori_loop(0, index_ref[0], advance, 0)
        for h in range(local_heads):
            columns = slice(DV * h, DV * h + DV)
            out = zero_ref[h] + product(reach_ref[h], state_ref[h], 1, 0)
            normed = out * lax.rsqrt(jnp.mean(out * out, axis=-1, keepdims=True) + HEAD_EPSILON)
            out_ref[:, columns] = out
            gated_ref[:, columns] = (
                normed * norm_ref[...] * jax.nn.silu(gate_ref[:, columns])
            ).astype(jnp.bfloat16)

    vmem = pl.BlockSpec(memory_space=pltpu.VMEM)
    width = local_heads * DV
    return pl.pallas_call(
        kernel,
        grid=(1,),
        in_specs=[
            pl.BlockSpec(memory_space=pltpu.SMEM),
            vmem,
            vmem,
            vmem,
            pl.BlockSpec((row_count, width), lambda i: (0, gate_first // width)),
            vmem,
        ],
        out_specs=[vmem, vmem, vmem],
        out_shape=[
            jax.ShapeDtypeStruct((local_heads, DK, DV), jnp.float32),
            jax.ShapeDtypeStruct((row_count, width), jnp.float32),
            jax.ShapeDtypeStruct((row_count, width), jnp.bfloat16),
        ],
        compiler_params=params(),
    )(my_index, handoffs, reach, zero_out, projected, norm_gain)


def mixer_gate_back(local_heads, d_gated, recurred, projected, norm_gain, reach):
    row_count = projected.shape[0]
    gate_first = local_heads * (2 * DK + DV) // DV

    def kernel(d_gated_ref, out_ref, gate_ref, norm_ref, reach_ref, d_out_ref, d_gate_ref, d_norm_ref, d_state_ref):
        out, gate, norm_row, d_gated_now = out_ref[...], gate_ref[...], norm_ref[...], d_gated_ref[...]
        scale = lax.rsqrt(jnp.mean(out * out, axis=-1, keepdims=True) + HEAD_EPSILON)
        normed = out * scale
        logistic = jax.nn.sigmoid(gate)
        silu = gate * logistic
        d_norm = jnp.sum(d_gated_now * normed * silu, axis=0, keepdims=True)

        @pl.when(pl.program_id(0) == 0)
        def _():
            d_norm_ref[...] = jnp.zeros_like(d_norm_ref)

        d_norm_ref[0:1, :] = d_norm_ref[0:1, :] + d_norm
        d_gate_ref[...] = (
            d_gated_now * normed * norm_row * logistic * (1.0 + gate * (1.0 - logistic))
        ).astype(jnp.bfloat16)
        d_normed = d_gated_now * norm_row * silu
        d_out = scale * d_normed - (scale * scale * scale) * out * jnp.mean(
            d_normed * out, axis=-1, keepdims=True
        )
        d_out_ref[...] = d_out
        d_state_ref[0] = product(reach_ref[0], d_out, 0, 0).astype(jnp.bfloat16)

    width = local_heads * DV
    block = pl.BlockSpec((row_count, DV), lambda h: (0, h))
    return pl.pallas_call(
        kernel,
        grid=(local_heads,),
        in_specs=[
            block,
            block,
            pl.BlockSpec((row_count, DV), lambda h: (0, gate_first + h)),
            pl.BlockSpec((1, DV), lambda h: (0, 0)),
            per_head(row_count, DK),
        ],
        out_specs=[block, block, pl.BlockSpec((8, DV), lambda h: (0, 0)), per_head(DK, DV)],
        out_shape=[
            jax.ShapeDtypeStruct((row_count, width), jnp.float32),
            jax.ShapeDtypeStruct((row_count, width), jnp.bfloat16),
            jax.ShapeDtypeStruct((8, DV), jnp.float32),
            jax.ShapeDtypeStruct((local_heads, DK, DV), jnp.bfloat16),
        ],
        compiler_params=params(),
    )(d_gated, recurred, projected, norm_gain, reach)


def relay_back(local_heads, my_index, handoffs, d_enterings):
    devices = handoffs.shape[0]

    def kernel(index_ref, handoffs_ref, d_ref, state_ref):
        state_ref[...] = jnp.zeros_like(state_ref)

        def advance(step, carry):
            j = devices - 1 - step
            for h in range(local_heads):
                state_ref[h] = product(
                    handoffs_ref[j, h, :, :DK].astype(jnp.float32), state_ref[h], 0, 0
                ) + d_ref[j, h].astype(jnp.float32)
            return carry

        lax.fori_loop(0, devices - 1 - index_ref[0], advance, 0)

    vmem = pl.BlockSpec(memory_space=pltpu.VMEM)
    return pl.pallas_call(
        kernel,
        in_specs=[pl.BlockSpec(memory_space=pltpu.SMEM), vmem, vmem],
        out_specs=vmem,
        out_shape=jax.ShapeDtypeStruct((local_heads, DK, DV), jnp.float32),
        compiler_params=params(),
    )(my_index, handoffs, d_enterings)


def conv_back(d_pre, extended, taps_ref, padded, d_block_ref, d_tail_ref, d_rim_ref, d_taps_ref):
    row_count = d_pre.shape[0]
    first = 8 - (KCONV - 1)
    padded[0:8, :] = jnp.zeros((8, d_pre.shape[1]), jnp.float32)
    padded[8 : 8 + row_count, :] = d_pre
    padded[8 + row_count : 16 + row_count, :] = jnp.zeros((8, d_pre.shape[1]), jnp.float32)
    total = None
    d_taps_ref[...] = jnp.zeros_like(d_taps_ref)
    for tap in range(KCONV):
        start = KCONV - 1 - tap
        term = taps_ref[tap : tap + 1, :] * padded[start : start + row_count + 8, :]
        total = term if total is None else total + term
        d_taps_ref[tap : tap + 1, :] = jnp.sum(
            d_pre * extended[first + tap : first + tap + row_count, :], axis=0, keepdims=True
        )
    d_rim_ref[...] = total[0:8, :]
    d_block_ref[...] = total[8:, :].astype(jnp.bfloat16)
    d_tail_ref[...] = total[row_count:, :]


def mixer_back(
    local_heads, projected, rim, taps, decay_proj, scalars,
    solve, fresh, wy_keys, entering_state, d_recurred, d_leaving,
):
    row_count = projected.shape[0]
    three, whole, scalar_spec = mixer_specs(local_heads, row_count)

    def kernel(
        pq, pk, pv, rq, rk, rv, tq, tk, tv, decay_ref, scalars_ref,
        solve_ref, fresh_ref, wy_ref, enter_ref, d_out_ref, d_leave_ref,
        dq_ref, dk_ref, dv_ref, tail_q, tail_k, tail_v, rim_q, rim_k, rim_v,
        taps_q, taps_k, taps_v, d_decay_ref, d_scalars_ref,
        ext_q, ext_k, ext_v, pad_k, pad_v,
    ):
        head = pl.program_id(0)

        @pl.when(head == 0)
        def _():
            d_decay_ref[...] = jnp.zeros_like(d_decay_ref)
            d_scalars_ref[...] = jnp.zeros_like(d_scalars_ref)

        pre_q = convolved(ext_q, pq, rq, tq)
        pre_k = convolved(ext_k, pk, rk, tk)
        pre_v = convolved(ext_v, pv, rv, tv)
        conv_q, conv_k = jax.nn.silu(pre_q), jax.nn.silu(pre_k)
        unit_q, scale_q = unit_rows(conv_q)
        queries = unit_q * DK ** (-0.5)
        key_rows, scale_k = unit_rows(conv_k)
        values = jax.nn.silu(pre_v)
        decay_in, rate, logs, beta, sums, within, row_ids, column_ids = decay_terms(
            head, local_heads, decay_ref, scalars_ref
        )
        strict = row_ids > column_ids
        grown = jnp.exp(sums)
        last = sums[row_count - 1 : row_count, :]
        tail = jnp.exp(last - sums)
        tail_keys = tail * key_rows
        gram = product(key_rows, key_rows, 1, 1)
        scores = jnp.where(strict, gram * within, 0.0)
        attention = product(queries, key_rows, 1, 1) * within
        enter, d_out, d_leave = enter_ref[0], d_out_ref[...], d_leave_ref[0]
        update = fresh_ref[0] - product(wy_ref[0], enter, 1, 0)
        d_update = product(attention, d_out, 0, 0) + product(tail_keys, d_leave, 1, 0)
        d_right = product(solve_ref[0], d_update, 0, 0)
        d_attention = product(d_out, update, 1, 1) * within
        d_system = -product(d_right, update, 1, 1)
        out_state = product(d_out, enter, 1, 1)
        right_state = product(d_right, enter, 1, 1)
        leave_update = product(update, d_leave, 1, 1)
        remainder = values - grown * product(key_rows, enter, 1, 0)
        d_values = beta * d_right
        d_beta = jnp.sum(d_right * remainder, axis=1, keepdims=True) + jnp.sum(
            d_system * scores, axis=1, keepdims=True
        )
        pair = beta * (d_system * scores)
        d_gram = jnp.where(strict, beta * d_system * within, 0.0)
        d_queries = grown * out_state + product(d_attention, key_rows, 1, 0)
        d_keys = (
            product(d_attention, queries, 0, 0)
            + product(d_gram, key_rows, 1, 0)
            + product(d_gram, key_rows, 0, 0)
            + tail * leave_update
            - (beta * grown) * right_state
        )
        both = pair + d_attention * product(queries, key_rows, 1, 1)
        tail_rows = jnp.sum(tail_keys * leave_update, axis=1, keepdims=True)
        diagonal = row_ids == column_ids
        columns = jnp.sum(both, axis=0, keepdims=True)
        d_sums = (
            jnp.sum(both, axis=1, keepdims=True)
            - jnp.sum(jnp.where(diagonal, columns, 0.0), axis=1, keepdims=True)
            + jnp.sum(out_state * (grown * queries), axis=1, keepdims=True)
            - jnp.sum(right_state * ((beta * grown) * key_rows), axis=1, keepdims=True)
            - tail_rows
        )
        d_last = jnp.exp(last) * jnp.sum(
            jnp.sum(d_leave * enter, axis=1, keepdims=True), axis=0, keepdims=True
        ) + jnp.sum(tail_rows, axis=0, keepdims=True)
        d_logs = d_last + jnp.sum(
            jnp.where(row_ids <= column_ids, to_row(d_sums, diagonal), 0.0), axis=1, keepdims=True
        )
        d_decay_in = d_logs * rate * jax.nn.sigmoid(decay_in)
        d_beta_in = d_beta * beta * (1.0 - beta)
        d_decay_ref[...] = (
            d_decay_ref[...]
            + put_lane(d_decay_in, head)
            + put_lane(d_beta_in, head + local_heads)
        )
        d_rate = jnp.sum(d_logs * logs, axis=0, keepdims=True)
        d_bias = jnp.sum(d_decay_in, axis=0, keepdims=True)
        d_scalars_ref[0:1, :] = d_scalars_ref[0:1, :] + put_lane(d_rate, head)
        d_scalars_ref[1:2, :] = d_scalars_ref[1:2, :] + put_lane(d_bias, head)

        def unit_back(d_unit, unit, scale):
            return scale * (d_unit - unit * jnp.sum(unit * d_unit, axis=1, keepdims=True))

        def silu_back(d_act, pre):
            logistic = jax.nn.sigmoid(pre)
            return d_act * logistic * (1.0 + pre * (1.0 - logistic))

        d_pre_q = silu_back(unit_back(d_queries * DK ** (-0.5), unit_q, scale_q), pre_q)
        conv_back(d_pre_q, ext_q, tq, pad_k, dq_ref, tail_q, rim_q, taps_q)
        d_pre_k = silu_back(unit_back(d_keys, key_rows, scale_k), pre_k)
        conv_back(d_pre_k, ext_k, tk, pad_k, dk_ref, tail_k, rim_k, taps_k)
        conv_back(silu_back(d_values, pre_v), ext_v, tv, pad_v, dv_ref, tail_v, rim_v, taps_v)

    def blocks(rows):
        return [
            pl.BlockSpec((rows, DK), lambda h: (0, h)),
            pl.BlockSpec((rows, DK), lambda h: (0, h)),
            pl.BlockSpec((rows, DV), lambda h: (0, h)),
        ]

    def shapes(rows, kind):
        return [
            jax.ShapeDtypeStruct((rows, local_heads * width), kind) for width in (DK, DK, DV)
        ]

    outs = pl.pallas_call(
        kernel,
        grid=(local_heads,),
        in_specs=three(row_count)
        + three(8)
        + three(8)
        + [
            whole,
            scalar_spec,
            per_head(row_count, row_count),
            per_head(row_count, DV),
            per_head(row_count, DK),
            per_head(DK, DV),
            pl.BlockSpec((row_count, DV), lambda h: (0, h)),
            per_head(DK, DV),
        ],
        out_specs=blocks(row_count) + blocks(8) * 3 + [whole, scalar_spec],
        out_shape=shapes(row_count, jnp.bfloat16)
        + shapes(8, jnp.float32) * 3
        + [
            jax.ShapeDtypeStruct((row_count, 128), jnp.float32),
            jax.ShapeDtypeStruct((8, 128), jnp.float32),
        ],
        scratch_shapes=[
            pltpu.VMEM((row_count + 8, DK), jnp.float32),
            pltpu.VMEM((row_count + 8, DK), jnp.float32),
            pltpu.VMEM((row_count + 8, DV), jnp.float32),
            pltpu.VMEM((row_count + 16, DK), jnp.float32),
            pltpu.VMEM((row_count + 16, DV), jnp.float32),
        ],
        compiler_params=params(),
    )(
        *([projected] * 3), *([rim] * 3), *([taps] * 3), decay_proj, scalars,
        solve, fresh, wy_keys, entering_state, d_recurred, d_leaving,
    )
    joined = [jnp.concatenate(outs[3 * i : 3 * i + 3], axis=1) for i in range(4)]
    return (*joined, outs[12], outs[13])


LANES = 128
CHUNK = 32768
TILE = 16
VMEM_LIMIT = 48 * 1024 * 1024


def params(**kwargs):
    return pltpu.CompilerParams(vmem_limit_bytes=VMEM_LIMIT, **kwargs)


def piece_kinds(segments_list, piece_count, piece_size):
    kinds = np.ones(piece_count, np.int32)
    offset_now = 0
    for seg_name, row_count, col_count, seg_rate in segments_list:
        if offset_now >= (piece_count - 1) * piece_size:
            break
        tiles = col_count // LANES
        if tiles in (2, 4, 8, 16):
            first = offset_now // piece_size
            kinds[first : first + row_count * col_count // piece_size] = tiles
        offset_now += row_count * col_count
    return kinds


def pack_blocks(master, slot_kinds, kinds_used):
    capacity, piece_size = master.shape
    chunks = piece_size // CHUNK
    rows = CHUNK // LANES
    slot_blocks = pl.cdiv(capacity, 8)

    def kernel(kinds_ref, master_ref, out_ref, scratch):
        first = pl.program_id(0) * 8
        for j in range(rows):
            scratch[8 * j : 8 * j + 8, :] = master_ref[:, LANES * j : LANES * j + LANES]
        for s in range(8):
            kind_now = kinds_ref[first + s]
            for kind in kinds_used:

                @pl.when(kind_now == kind)
                def _():
                    for tile in range(rows // TILE):
                        row_tile, column = divmod(tile, kind)
                        start = (row_tile * TILE * kind + column) * 8 + s
                        out_ref[s, TILE * tile : TILE * tile + TILE, :] = scratch[
                            pl.ds(start, TILE, stride=8 * kind), :
                        ].astype(jnp.bfloat16)

    return pl.pallas_call(
        kernel,
        grid_spec=pltpu.PrefetchScalarGridSpec(
            num_scalar_prefetch=1,
            grid=(slot_blocks, chunks),
            in_specs=[pl.BlockSpec((8, CHUNK), lambda i, j, kinds: (i, j))],
            out_specs=pl.BlockSpec((8, rows, LANES), lambda i, j, kinds: (i, j, 0)),
            scratch_shapes=[pltpu.VMEM((8 * rows, LANES), jnp.float32)],
        ),
        out_shape=jax.ShapeDtypeStruct((capacity, piece_size // LANES, LANES), jnp.bfloat16),
        compiler_params=params(),
    )(slot_kinds, master)


def tiled_matrix(gathered, positions, col_count, blocks_a_step):
    tiles = col_count // LANES
    piece_rows = gathered.shape[1]
    rows = piece_rows // tiles
    count = positions.shape[0]

    def kernel(positions_ref, *refs):
        out_ref = refs[blocks_a_step]
        for block in range(blocks_a_step):
            for tile in range(piece_rows // TILE):
                row_tile, column = divmod(tile, tiles)
                row = rows * block + TILE * row_tile
                out_ref[row : row + TILE, LANES * column : LANES * column + LANES] = refs[block][
                    0, TILE * tile : TILE * tile + TILE, :
                ]

    return pl.pallas_call(
        kernel,
        grid_spec=pltpu.PrefetchScalarGridSpec(
            num_scalar_prefetch=1,
            grid=(count // blocks_a_step,),
            in_specs=[
                pl.BlockSpec(
                    (1, piece_rows, LANES),
                    lambda g, positions, j=j: (positions[g * blocks_a_step + j], 0, 0),
                )
                for j in range(blocks_a_step)
            ],
            out_specs=pl.BlockSpec((rows * blocks_a_step, col_count), lambda g, positions: (g, 0)),
        ),
        out_shape=jax.ShapeDtypeStruct((count * rows, col_count), jnp.bfloat16),
        compiler_params=params(),
    )(positions, *([gathered] * blocks_a_step))


def spread_matrix(gathered, positions, col_count):
    tiles = col_count // LANES
    rows = gathered.shape[1]
    count = positions.shape[0]
    groups = count // tiles

    def kernel(positions_ref, *refs):
        ins, out_ref, scratch = refs[:tiles], refs[tiles], refs[tiles + 1]
        for j in range(tiles):
            scratch[rows * j : rows * j + rows, :] = ins[j][0].astype(jnp.float32)
        for c in range(tiles):
            out_ref[:, LANES * c : LANES * c + LANES] = scratch[
                pl.ds(c, rows, stride=tiles), :
            ].astype(jnp.bfloat16)

    return pl.pallas_call(
        kernel,
        grid_spec=pltpu.PrefetchScalarGridSpec(
            num_scalar_prefetch=1,
            grid=(groups,),
            in_specs=[
                pl.BlockSpec(
                    (1, rows, LANES), lambda g, positions, j=j: (positions[g * tiles + j], 0, 0)
                )
                for j in range(tiles)
            ],
            out_specs=pl.BlockSpec((rows, col_count), lambda g, positions: (g, 0)),
            scratch_shapes=[pltpu.VMEM((rows * tiles, LANES), jnp.float32)],
        ),
        out_shape=jax.ShapeDtypeStruct((groups * rows, col_count), jnp.bfloat16),
        compiler_params=params(),
    )(positions, *([gathered] * tiles))


def weight_grad_blocks(left_t, right, positions, slots_total, table, blocks_a_step):
    row_total, depth = left_t.shape
    col_count = right.shape[1]
    tiles = col_count // LANES
    piece_rows = 512
    even = tiles in (2, 4, 8, 16)
    step_rows = blocks_a_step * piece_rows // tiles
    steps = row_total // step_rows

    def kernel(positions_ref, left_ref, right_ref, *refs):
        if table is not None:
            refs = refs[1:]
        out_ref, product, staged, sem = refs
        g = pl.program_id(0)
        slot = lax.rem(g, 2)

        def settle(which):
            pltpu.make_async_copy(
                staged.at[which], out_ref.at[pl.ds(0, blocks_a_step)], sem.at[which]
            ).wait()

        @pl.when(g >= 2)
        def _():
            settle(slot)

        left = left_ref[...]
        if even:
            product[...] = jnp.dot(left, right_ref[...], preferred_element_type=jnp.float32)
            for tile in range(step_rows // TILE * tiles):
                row_tile, column = divmod(tile, tiles)
                block, row = divmod(TILE * tile, piece_rows)
                staged[slot, block, row : row + TILE, :] = product[
                    TILE * row_tile : TILE * row_tile + TILE, LANES * column : LANES * column + LANES
                ].astype(jnp.bfloat16)
        else:
            for c in range(0, tiles, 2):
                width = min(2, tiles - c)
                part = jnp.dot(
                    left,
                    right_ref[:, LANES * c : LANES * (c + width)],
                    preferred_element_type=jnp.float32,
                )
                for w in range(width):
                    product[pl.ds(c + w, step_rows, stride=tiles), :] = part[
                        :, LANES * w : LANES * w + LANES
                    ]
            for block in range(blocks_a_step):
                staged[slot, block] = product[
                    piece_rows * block : piece_rows * block + piece_rows, :
                ].astype(jnp.bfloat16)
        for block in range(blocks_a_step):
            pltpu.make_async_copy(
                staged.at[slot, block],
                out_ref.at[positions_ref[g * blocks_a_step + block]],
                sem.at[slot],
            ).start()

        @pl.when(g == steps - 1)
        def _():
            settle(slot)
            if steps > 1:
                settle(1 - slot)

    out_shape = jax.ShapeDtypeStruct((slots_total, piece_rows, LANES), jnp.bfloat16)
    operands = [positions, left_t, right]
    in_specs = [
        pl.BlockSpec((step_rows, depth), lambda g, positions: (g, 0)),
        pl.BlockSpec((depth, col_count), lambda g, positions: (0, 0)),
    ]
    aliases = {}
    if table is not None:
        operands.append(table)
        in_specs.append(pl.BlockSpec(memory_space=pl.ANY))
        aliases = {3: 0}
    product_shape = (step_rows, col_count) if even else (step_rows * tiles, LANES)
    return pl.pallas_call(
        kernel,
        grid_spec=pltpu.PrefetchScalarGridSpec(
            num_scalar_prefetch=1,
            grid=(steps,),
            in_specs=in_specs,
            out_specs=pl.BlockSpec(memory_space=pl.ANY),
            scratch_shapes=[
                pltpu.VMEM(product_shape, jnp.float32),
                pltpu.VMEM((2, blocks_a_step, piece_rows, LANES), jnp.bfloat16),
                pltpu.SemaphoreType.DMA((2,)),
            ],
        ),
        out_shape=out_shape,
        input_output_aliases=aliases,
        cost_estimate=pl.CostEstimate(
            flops=2 * row_total * depth * col_count,
            bytes_accessed=2 * row_total * col_count,
            transcendentals=0,
        ),
        compiler_params=params(),
    )(*operands)


def optimizer_update(
    reduced, slot_kinds, kinds_used, slot_masks, small_rates, master, moment_one, moment_two
):
    capacity, piece_size = master.shape
    chunks = piece_size // CHUNK
    rows = CHUNK // LANES
    slot_blocks = pl.cdiv(capacity, 8)

    def kernel(
        kinds_ref, reduced_ref, masks_ref, small_ref, master_ref, one_ref, two_ref,
        grad_out, master_out, one_out, two_out, low_out, scratch,
    ):
        first = pl.program_id(0) * 8
        for s in range(8):
            kind_now = kinds_ref[first + s]
            for kind in kinds_used:

                @pl.when(kind_now == kind)
                def _():
                    for tile in range(rows // TILE):
                        row_tile, column = divmod(tile, kind)
                        start = (row_tile * TILE * kind + column) * 8 + s
                        scratch[pl.ds(start, TILE, stride=8 * kind), :] = reduced_ref[
                            s, TILE * tile : TILE * tile + TILE, :
                        ].astype(jnp.float32)
        present = masks_ref[0] > 0.5
        is_small = masks_ref[1] > 0.5
        rate_rows = masks_ref[2]
        for j in range(rows):
            lanes = slice(LANES * j, LANES * j + LANES)
            grad = jnp.where(present, scratch[8 * j : 8 * j + 8, :], 0.0)
            rate = jnp.where(is_small, small_ref[:, lanes], rate_rows)
            master_now = master_ref[:, lanes]
            one_new = BETA_ONE * one_ref[:, lanes] + (1.0 - BETA_ONE) * grad
            two_new = BETA_TWO * two_ref[:, lanes] + (1.0 - BETA_TWO) * grad * grad
            first_hat = one_new / (1.0 - BETA_ONE**STEP)
            second_hat = two_new / (1.0 - BETA_TWO**STEP)
            master_new = master_now - rate * (
                first_hat / (jnp.sqrt(second_hat) + ADAM_EPSILON) + WEIGHT_DECAY * master_now
            )
            grad_out[:, lanes] = grad
            master_out[:, lanes] = master_new
            one_out[:, lanes] = one_new
            two_out[:, lanes] = two_new
            low_out[:, lanes] = master_new.astype(jnp.bfloat16)

    state_spec = pl.BlockSpec((8, CHUNK), lambda i, j, kinds: (i, j))
    wide = jax.ShapeDtypeStruct((capacity, piece_size), jnp.float32)
    return pl.pallas_call(
        kernel,
        grid_spec=pltpu.PrefetchScalarGridSpec(
            num_scalar_prefetch=1,
            grid=(slot_blocks, chunks),
            in_specs=[
                pl.BlockSpec((8, rows, LANES), lambda i, j, kinds: (i, j, 0)),
                pl.BlockSpec((3, 8, LANES), lambda i, j, kinds: (0, i, 0)),
                pl.BlockSpec((1, CHUNK), lambda i, j, kinds: (0, j)),
                state_spec,
                state_spec,
                state_spec,
            ],
            out_specs=[state_spec] * 5,
            scratch_shapes=[pltpu.VMEM((8 * rows, LANES), jnp.float32)],
        ),
        out_shape=[wide] * 4 + [jax.ShapeDtypeStruct((capacity, piece_size), jnp.bfloat16)],
        compiler_params=params(),
    )(slot_kinds, reduced, slot_masks, small_rates, master, moment_one, moment_two)


def weight_grad(left, right):
    return jnp.einsum("td,tc->dc", left, right, preferred_element_type=jnp.float32)


def back_product(grad_rows, weight):
    return jnp.dot(grad_rows, weight.T, preferred_element_type=jnp.float32)


def on_device(inputs, cotangent, owners, master, moment_one, moment_two):
    head_parts = lax.axis_size("head")
    seq_parts = lax.axis_size("seq")
    local_heads = HEADS // head_parts
    capacity, piece_size = master.shape
    piece_count = owners.shape[0]
    segments_list = shard_layout(local_heads, head_parts)
    slot_of_piece, piece_of_slot, present = piece_table(owners, seq_parts, capacity)
    my_index = lax.axis_index("seq")
    my_pieces = lax.dynamic_slice_in_dim(piece_of_slot, my_index * capacity, capacity)
    my_present = lax.dynamic_slice_in_dim(present, my_index * capacity, capacity)
    kind_table = piece_kinds(segments_list, piece_count, piece_size)
    kinds_used = sorted(set(kind_table.tolist()) | {1})
    slot_kinds = jnp.where(my_present, jnp.asarray(kind_table)[my_pieces], 1)
    slot_kinds = jnp.pad(slot_kinds, (0, -capacity % 8), constant_values=1)
    gathered = lax.all_gather(
        pack_blocks(master, slot_kinds, kinds_used), "seq", axis=0, tiled=True
    )
    counts = {name: r * c // piece_size for name, r, c, rate in segments_list[:8]}
    firsts = dict(zip(counts, np.cumsum([0] + list(counts.values())).tolist()))
    columns = {name: c for name, r, c, rate in segments_list}

    def positions_of(*names):
        return jnp.concatenate(
            [slot_of_piece[firsts[name] : firsts[name] + counts[name]] for name in names]
        )

    by_name = {}
    for name, blocks_a_step in (("wq", 4), ("wk", 4), ("wv", 8), ("wg", 8), ("wo", 8), ("wdown", 11)):
        by_name[name] = tiled_matrix(gathered, positions_of(name), columns[name], blocks_a_step)
    for name in ("wgate", "wup"):
        by_name[name] = spread_matrix(gathered, positions_of(name), columns[name])
    small_flat = lax.dynamic_index_in_dim(
        gathered, slot_of_piece[piece_count - 1], axis=0, keepdims=False
    ).reshape(-1)
    small_names, small_used = unpack(small_flat, segments_list[8:])
    by_name.update(small_names)
    row_count = inputs.shape[0]
    rim_width = KCONV - 1
    rows_full, back_full, first_norm_scale_factor, second_norm_scale_factor, norm_gain = (
        lax.all_gather(inputs, "head", axis=1, tiled=True),
        lax.all_gather(cotangent, "head", axis=1, tiled=True),
        lax.all_gather(by_name["gainone"].reshape(-1), "head", axis=0, tiled=True),
        lax.all_gather(by_name["gaintwo"].reshape(-1), "head", axis=0, tiled=True),
        lax.all_gather(by_name["wnorm"].reshape(-1), "head", axis=0, tiled=True),
    )
    first_norm_scale_factor = first_norm_scale_factor.astype(jnp.float32)
    second_norm_scale_factor = second_norm_scale_factor.astype(jnp.float32)
    rows_wide = rows_full.astype(jnp.float32)
    scale_one = lax.rsqrt(jnp.mean(rows_wide * rows_wide, axis=-1, keepdims=True) + NORM_EPSILON)
    normed = (rows_wide * scale_one * first_norm_scale_factor).astype(jnp.bfloat16)
    mixer_names = ("wq", "wk", "wv", "wg")
    projected = jnp.concatenate(
        [
            jnp.dot(normed, by_name[name], preferred_element_type=jnp.float32)
            for name in mixer_names
        ],
        axis=1,
    )
    conv_columns = local_heads * (2 * DK + DV)
    decay_weight = jnp.pad(by_name["wab"], ((0, 0), (0, LANES - 2 * local_heads)))
    decay_proj = jnp.dot(normed, decay_weight, preferred_element_type=jnp.float32)
    rim = shifted(projected[row_count - rim_width :, :conv_columns], "seq", 1)
    rim = jnp.pad(rim, ((8 - rim_width, 0), (0, 0)))
    taps = jnp.concatenate([by_name["cq"], by_name["ck"], by_name["cv"]], axis=1)
    taps = jnp.pad(taps.astype(jnp.float32), ((0, 8 - KCONV), (0, 0)))
    scalars = jnp.pad(
        jnp.concatenate([by_name["alog"], by_name["dtbias"]], axis=0).astype(jnp.float32),
        ((0, 6), (0, LANES - local_heads)),
    )
    solve, fresh, wy_keys, reach, zero_out, handoff = mixer_local(
        local_heads, projected, rim, taps, decay_proj, scalars
    )
    handoffs = lax.all_gather(handoff, "seq", axis=0, tiled=False)
    my_index_row = my_index.astype(jnp.int32).reshape(1)
    norm_row = norm_gain.astype(jnp.float32)[None, :]
    entering_state, recurred, gated_low = mixer_out(
        local_heads, my_index_row, handoffs, reach, zero_out, projected, norm_row
    )
    mixed = lax.psum_scatter(
        jnp.dot(gated_low, by_name["wo"], preferred_element_type=jnp.float32).astype(jnp.bfloat16),
        "head",
        scatter_dimension=1,
        tiled=True,
    ).astype(jnp.float32)
    inputs_wide = inputs.astype(jnp.float32)
    residual = inputs_wide + mixed
    resid_low = residual.astype(jnp.bfloat16)
    resid_full = lax.all_gather(resid_low, "head", axis=1, tiled=True).astype(jnp.float32)
    scale_two = lax.rsqrt(jnp.mean(resid_full * resid_full, axis=-1, keepdims=True) + NORM_EPSILON)
    hidden_in = (resid_full * scale_two * second_norm_scale_factor).astype(jnp.bfloat16)
    gate_mlp = jnp.dot(hidden_in, by_name["wgate"], preferred_element_type=jnp.float32)
    up_mlp = jnp.dot(hidden_in, by_name["wup"], preferred_element_type=jnp.float32)
    logistic_output_multiplier = jax.nn.sigmoid(gate_mlp)
    silu_gate = gate_mlp * logistic_output_multiplier
    hidden = (silu_gate * up_mlp).astype(jnp.bfloat16)
    mlp_out = lax.psum_scatter(
        jnp.dot(hidden, by_name["wdown"], preferred_element_type=jnp.float32).astype(jnp.bfloat16),
        "head",
        scatter_dimension=1,
        tiled=True,
    ).astype(jnp.float32)
    block_out = (residual + mlp_out).astype(jnp.bfloat16)
    d_hidden = back_product(back_full, by_name["wdown"])
    d_gate_mlp = (
        d_hidden
        * up_mlp
        * logistic_output_multiplier
        * (1.0 + gate_mlp * (1.0 - logistic_output_multiplier))
    ).astype(jnp.bfloat16)
    d_up_mlp = (d_hidden * silu_gate).astype(jnp.bfloat16)
    slots_total = seq_parts * capacity

    def store_grad(table, name, left, right, blocks_a_step):
        return weight_grad_blocks(
            left.T, right, positions_of(name), slots_total, table, blocks_a_step
        )

    grad_table = store_grad(None, "wdown", hidden, back_full, 11)
    grad_table = store_grad(grad_table, "wgate", hidden_in, d_gate_mlp, 11)
    grad_table = store_grad(grad_table, "wup", hidden_in, d_up_mlp, 11)
    d_hidden_in = back_product(d_gate_mlp, by_name["wgate"]) + back_product(
        d_up_mlp, by_name["wup"]
    )
    dot_two = jnp.sum(d_hidden_in * second_norm_scale_factor * resid_full, axis=-1, keepdims=True)
    d_hidden_mine, dot_two_sum = (
        lax.psum_scatter(
            d_hidden_in.astype(jnp.bfloat16), "head", scatter_dimension=1, tiled=True
        ).astype(jnp.float32),
        lax.psum_scatter(
            jnp.broadcast_to(dot_two, (row_count, head_parts)).astype(jnp.bfloat16),
            "head",
            scatter_dimension=1,
            tiled=True,
        ).astype(jnp.float32),
    )
    resid_mine = resid_low.astype(jnp.float32)
    gain_two_mine = by_name["gaintwo"].reshape(-1).astype(jnp.float32)
    grad_gaintwo = jnp.sum(d_hidden_mine * resid_mine * scale_two, axis=0, keepdims=True)
    d_resid = (
        cotangent.astype(jnp.float32)
        + scale_two * d_hidden_mine * gain_two_mine
        - scale_two**3 / D * resid_mine * dot_two_sum
    )
    back_mix_full = lax.all_gather(d_resid.astype(jnp.bfloat16), "head", axis=1, tiled=True)
    grad_table = store_grad(grad_table, "wo", gated_low, back_mix_full, 8)
    d_gated = back_product(back_mix_full, by_name["wo"])
    d_recurred, d_gate, norm_grad, d_entering = mixer_gate_back(
        local_heads, d_gated, recurred, projected, norm_row, reach
    )
    d_norm_gain = norm_grad[0]
    d_enterings = lax.all_gather(d_entering, "seq", axis=0, tiled=False)
    d_leaving = relay_back(local_heads, my_index_row, handoffs, d_enterings)
    d_conv, d_tail, d_rim, d_taps, d_decay_wide, d_scalars = mixer_back(
        local_heads,
        projected,
        rim,
        taps,
        decay_proj,
        scalars,
        solve,
        fresh,
        wy_keys,
        entering_state,
        d_recurred,
        d_leaving,
    )
    d_rim = shifted(d_rim[8 - rim_width :], "seq", -1)
    d_tail = d_tail + jnp.pad(d_rim, ((8 - rim_width, 0), (0, 0)))
    d_conv = lax.dynamic_update_slice(d_conv, d_tail.astype(jnp.bfloat16), (row_count - 8, 0))
    d_query = d_conv[:, : local_heads * DK]
    d_key = d_conv[:, local_heads * DK : 2 * local_heads * DK]
    d_value = d_conv[:, 2 * local_heads * DK :]
    d_decay = d_decay_wide[:, : 2 * local_heads].astype(jnp.bfloat16)
    d_conv_query = d_taps[:KCONV, : local_heads * DK]
    d_conv_key = d_taps[:KCONV, local_heads * DK : 2 * local_heads * DK]
    d_conv_value = d_taps[:KCONV, 2 * local_heads * DK :]
    d_log_rate = d_scalars[0, :local_heads]
    d_rate_bias = d_scalars[1, :local_heads]
    grad_table = store_grad(grad_table, "wg", normed, d_gate, 8)
    grad_table = store_grad(grad_table, "wv", normed, d_value, 8)
    grad_table = store_grad(grad_table, "wk", normed, d_key, 4)
    grad_table = store_grad(grad_table, "wq", normed, d_query, 4)
    grad_wab = weight_grad(normed, d_decay)
    d_normed = (
        back_product(d_query, by_name["wq"])
        + back_product(d_key, by_name["wk"])
        + back_product(d_value, by_name["wv"])
        + back_product(d_gate, by_name["wg"])
        + back_product(d_decay, by_name["wab"])
    )
    dot_one = jnp.sum(d_normed * first_norm_scale_factor * rows_wide, axis=-1, keepdims=True)
    d_normed_mine, dot_one_sum, grad_wnorm = (
        lax.psum_scatter(
            d_normed.astype(jnp.bfloat16), "head", scatter_dimension=1, tiled=True
        ).astype(jnp.float32),
        lax.psum_scatter(
            jnp.broadcast_to(dot_one, (row_count, head_parts)).astype(jnp.bfloat16),
            "head",
            scatter_dimension=1,
            tiled=True,
        ).astype(jnp.float32),
        lax.psum_scatter(
            d_norm_gain.astype(jnp.bfloat16), "head", scatter_dimension=0, tiled=True
        ).astype(jnp.float32),
    )
    gain_one_mine = by_name["gainone"].reshape(-1).astype(jnp.float32)
    grad_gainone = jnp.sum(d_normed_mine * inputs_wide * scale_one, axis=0, keepdims=True)
    input_grad = (
        d_resid
        + scale_one * d_normed_mine * gain_one_mine
        - scale_one**3 / D * inputs_wide * dot_one_sum
    )
    small_grads = [
        d_conv_query,
        d_conv_key,
        d_conv_value,
        grad_wab,
        d_log_rate,
        d_rate_bias,
        grad_gainone,
        grad_gaintwo,
        grad_wnorm,
    ]
    small_block = jnp.concatenate(
        [grad_now.astype(jnp.bfloat16).reshape(-1) for grad_now in small_grads]
        + [jnp.zeros((piece_size - small_used,), jnp.bfloat16)]
    ).reshape(1, -1, LANES)
    grad_table = lax.dynamic_update_slice(
        grad_table, small_block, (slot_of_piece[piece_count - 1], 0, 0)
    )
    reduced = lax.psum_scatter(grad_table, "seq", scatter_dimension=0, tiled=True)
    piece_rates, small_rates = rate_parts(segments_list, piece_count, piece_size)
    slot_masks = jnp.stack(
        [
            my_present.astype(jnp.float32),
            (my_present & (my_pieces == piece_count - 1)).astype(jnp.float32),
            jnp.where(my_present, jnp.asarray(piece_rates)[my_pieces], PAD_RATE),
        ]
    )
    slot_masks = jnp.pad(slot_masks, ((0, 0), (0, -capacity % 8)))
    slot_masks = jnp.broadcast_to(slot_masks[:, :, None], slot_masks.shape + (LANES,))
    grad_slots, master_new, moment_new, second_new, weights_low = optimizer_update(
        reduced,
        slot_kinds,
        kinds_used,
        slot_masks,
        jnp.asarray(small_rates)[None, :],
        master,
        moment_one,
        moment_two,
    )
    return (
        block_out,
        input_grad,
        grad_slots,
        master_new,
        moment_new,
        second_new,
        weights_low,
    )


def solution(mesh):
    return jax.shard_map(
        on_device,
        mesh=mesh,
        in_specs=(
            P("seq", "head"),
            P("seq", "head"),
            P(),
            P("seq", "head"),
            P("seq", "head"),
            P("seq", "head"),
        ),
        out_specs=(
            P("seq", "head"),
            P("seq", "head"),
            P("seq", "head"),
            P("seq", "head"),
            P("seq", "head"),
            P("seq", "head"),
            P("seq", "head"),
        ),
        check_vma=False,
    )
```

```python
import jax
import jax.numpy as jnp
import numpy as np
from jax import lax
from jax.experimental import pallas as pl
from jax.experimental.pallas import tpu as pltpu
from jax.sharding import PartitionSpec as P

D = 2048
HEADS = 16
DK = 128
DV = 256
FF = 5632
KCONV = 4
STEP = 5


EXACT_ARITHMETIC = lax.Precision.HIGHEST
NORM_EPSILON = 1e-06
UNIT_EPSILON = 1e-06
HEAD_EPSILON = 1e-05
ADAM_EPSILON = 1e-08
BETA_ONE = 0.5
BETA_TWO = 0.5
WEIGHT_DECAY = 0.1
PAD_RATE = 0.1


def shifted(block, axis, distance):
    devices = range(lax.axis_size(axis))
    route = [(i - distance, i) for i in devices if i - distance in devices]
    return lax.ppermute(block, axis, route)


def shard_layout(local_heads, head_parts):
    return [
        ("wq", D, local_heads * DK, 0.02),
        ("wk", D, local_heads * DK, 0.02),
        ("wv", D, local_heads * DV, 0.02),
        ("wg", D, local_heads * DV, 0.02),
        ("wo", local_heads * DV, D, 0.015),
        ("wgate", D, FF // head_parts, 0.02),
        ("wup", D, FF // head_parts, 0.02),
        ("wdown", FF // head_parts, D, 0.012),
        ("cq", KCONV, local_heads * DK, 0.4),
        ("ck", KCONV, local_heads * DK, 0.4),
        ("cv", KCONV, local_heads * DV, 0.4),
        ("wab", D, 2 * local_heads, 0.04),
        ("alog", 1, local_heads, 0.5),
        ("dtbias", 1, local_heads, 0.5),
        ("gainone", 1, D // head_parts, 0.1),
        ("gaintwo", 1, D // head_parts, 0.1),
        ("wnorm", 1, DV // head_parts, 0.1),
    ]


def piece_table(owners, seq_parts, capacity):
    piece_count = owners.shape[0]
    devices = jnp.arange(seq_parts, dtype=jnp.int32)
    onehot = (owners[:, None] == devices[None, :]).astype(jnp.int32)
    before = jnp.cumsum(onehot, axis=0) - onehot
    rank_within = jnp.sum(before * onehot, axis=1)
    slot_of_piece = owners * capacity + rank_within
    matches = slot_of_piece[None, :] == jnp.arange(seq_parts * capacity, dtype=jnp.int32)[:, None]
    present = jnp.any(matches, axis=1)
    piece_of_slot = jnp.sum(
        matches.astype(jnp.int32) * jnp.arange(piece_count, dtype=jnp.int32)[None, :], axis=1
    )
    return (slot_of_piece, piece_of_slot, present)


def unpack(flat_weights, segments_list):
    by_name = {}
    offset_now = 0
    for seg_name, row_count, col_count, seg_rate in segments_list:
        by_name[seg_name] = flat_weights[offset_now : offset_now + row_count * col_count].reshape(
            row_count, col_count
        )
        offset_now += row_count * col_count
    return (by_name, offset_now)


def rate_parts(segments_list, piece_count, piece_size):
    piece_rates = np.full(piece_count, PAD_RATE, np.float32)
    small_rates = np.full(piece_size, PAD_RATE, np.float32)
    offset_now = 0
    big_total = (piece_count - 1) * piece_size
    for seg_name, row_count, col_count, seg_rate in segments_list:
        seg_size = row_count * col_count
        if offset_now < big_total:
            piece_rates[offset_now // piece_size : (offset_now + seg_size) // piece_size] = seg_rate
        else:
            small_rates[offset_now - big_total : offset_now - big_total + seg_size] = seg_rate
        offset_now += seg_size
    return (piece_rates, small_rates)


def product(left, right, left_axis, right_axis, exact=True):
    return lax.dot_general(
        left,
        right,
        (((left_axis,), (right_axis,)), ((), ())),
        precision=EXACT_ARITHMETIC if exact else None,
        preferred_element_type=jnp.float32,
    )


def take_lane(wide, lane):
    lanes = lax.broadcasted_iota(jnp.int32, wide.shape, 1)
    return jnp.sum(jnp.where(lanes == lane, wide, 0.0), axis=1, keepdims=True)


def put_lane(column, lane):
    lanes = lax.broadcasted_iota(jnp.int32, (column.shape[0], 128), 1)
    return jnp.where(lanes == lane, column, 0.0)


def to_row(column, diagonal):
    return jnp.sum(jnp.where(diagonal, column, 0.0), axis=0, keepdims=True)


def convolved(extended, block_ref, rim_ref, taps_ref):
    row_count = block_ref.shape[0]
    extended[0:8, :] = rim_ref[...]
    extended[8 : 8 + row_count, :] = block_ref[...]
    first = 8 - (KCONV - 1)
    running = taps_ref[0:1, :] * extended[first : first + row_count, :]
    for tap in range(1, KCONV):
        running = running + taps_ref[tap : tap + 1, :] * extended[
            first + tap : first + tap + row_count, :
        ]
    return running


def decay_terms(head, local_heads, decay_ref, scalars_ref):
    row_count = decay_ref.shape[0]
    shape = (row_count, row_count)
    row_ids = lax.broadcasted_iota(jnp.int32, shape, 0)
    column_ids = lax.broadcasted_iota(jnp.int32, shape, 1)
    decay_in = take_lane(decay_ref[...], head) + take_lane(scalars_ref[1:2, :], head)
    rate = -jnp.exp(take_lane(scalars_ref[0:1, :], head))
    soft = jnp.maximum(decay_in, 0.0) + jnp.log1p(jnp.exp(-jnp.abs(decay_in)))
    logs = rate * soft
    beta = jax.nn.sigmoid(take_lane(decay_ref[...], head + local_heads))
    diagonal = row_ids == column_ids
    logs_row = to_row(logs, diagonal)
    upto = row_ids >= column_ids
    sums = jnp.sum(jnp.where(upto, logs_row, 0.0), axis=1, keepdims=True)
    sums_row = to_row(sums, diagonal)
    within = jnp.exp(jnp.where(upto, sums - sums_row, -1e30))
    return decay_in, rate, logs, beta, sums, within, row_ids, column_ids


def unit_rows(rows):
    scale = lax.rsqrt(jnp.sum(rows * rows, axis=-1, keepdims=True) + UNIT_EPSILON)
    return rows * scale, scale


def mixer_specs(local_heads, row_count):
    def spec(rows, width, first):
        return pl.BlockSpec((rows, width), lambda h, first=first: (0, first + h))

    def three(rows):
        return [
            spec(rows, DK, 0),
            spec(rows, DK, local_heads),
            spec(rows, DV, 2 * local_heads * DK // DV),
        ]

    whole = pl.BlockSpec((row_count, 128), lambda h: (0, 0))
    scalars = pl.BlockSpec((8, 128), lambda h: (0, 0))
    return three, whole, scalars


def per_head(*shape):
    return pl.BlockSpec((1,) + shape, lambda h: (h,) + (0,) * len(shape))


def mixer_local(local_heads, projected, rim, taps, decay_proj, scalars):
    row_count = projected.shape[0]
    three, whole, scalar_spec = mixer_specs(local_heads, row_count)

    def kernel(
        pq, pk, pv, rq, rk, rv, tq, tk, tv, decay_ref, scalars_ref,
        solve_ref, fresh_ref, wy_ref, reach_ref, zero_ref, handoff_ref, ext_q, ext_k, ext_v,
    ):
        head = pl.program_id(0)
        queries = unit_rows(jax.nn.silu(convolved(ext_q, pq, rq, tq)))[0] * DK ** (-0.5)
        key_rows = unit_rows(jax.nn.silu(convolved(ext_k, pk, rk, tk)))[0]
        values = jax.nn.silu(convolved(ext_v, pv, rv, tv))
        decay_in, rate, logs, beta, sums, within, row_ids, column_ids = decay_terms(
            head, local_heads, decay_ref, scalars_ref
        )
        gram = product(key_rows, key_rows, 1, 1)
        system = jnp.where(row_ids > column_ids, beta * gram * within, 0.0)
        solve = jnp.where(row_ids == column_ids, 1.0, 0.0)
        size = 1
        while size < row_count:
            lower = (row_ids // (2 * size) == column_ids // (2 * size)) & (
                row_ids // size != column_ids // size
            )
            part = jnp.where(lower, system, 0.0)
            if size == 1:
                solve = solve - part
            else:
                solve = solve - product(solve, product(part, solve, 1, 0), 1, 0)
            size *= 2
        grown = jnp.exp(sums)
        fresh = product(solve, beta * values, 1, 0)
        wy_keys = product(solve, (beta * grown) * key_rows, 1, 0)
        attention = product(queries, key_rows, 1, 1) * within
        last = sums[row_count - 1 : row_count, :]
        tail_keys = jnp.exp(last - sums) * key_rows
        eye = lax.broadcasted_iota(jnp.int32, (DK, DK), 0) == lax.broadcasted_iota(
            jnp.int32, (DK, DK), 1
        )
        solve_ref[0] = solve
        fresh_ref[0] = fresh
        wy_ref[0] = wy_keys
        reach_ref[0] = grown * queries - product(attention, wy_keys, 1, 0)
        zero_ref[0] = product(attention, fresh, 1, 0)
        handoff_ref[0, :, :DK] = (
            jnp.where(eye, jnp.exp(last), 0.0) - product(tail_keys, wy_keys, 0, 0)
        ).astype(jnp.bfloat16)
        handoff_ref[0, :, DK:] = product(tail_keys, fresh, 0, 0).astype(jnp.bfloat16)

    def out(*shape, kind=jnp.float32):
        return jax.ShapeDtypeStruct((local_heads,) + shape, kind)

    return pl.pallas_call(
        kernel,
        grid=(local_heads,),
        in_specs=three(row_count) + three(8) + three(8) + [whole, scalar_spec],
        out_specs=[
            per_head(row_count, row_count),
            per_head(row_count, DV),
            per_head(row_count, DK),
            per_head(row_count, DK),
            per_head(row_count, DV),
            per_head(DK, DK + DV),
        ],
        out_shape=[
            out(row_count, row_count),
            out(row_count, DV),
            out(row_count, DK),
            out(row_count, DK),
            out(row_count, DV),
            out(DK, DK + DV, kind=jnp.bfloat16),
        ],
        scratch_shapes=[
            pltpu.VMEM((row_count + 8, DK), jnp.float32),
            pltpu.VMEM((row_count + 8, DK), jnp.float32),
            pltpu.VMEM((row_count + 8, DV), jnp.float32),
        ],
        compiler_params=params(),
    )(*([projected] * 3), *([rim] * 3), *([taps] * 3), decay_proj, scalars)


def mixer_out(local_heads, my_index, base, handoffs, reach, zero_out, projected, norm_gain):
    row_count = projected.shape[0]
    gate_first = local_heads * (2 * DK + DV)

    def kernel(index_ref, base_ref, handoffs_ref, reach_ref, zero_ref, gate_ref, norm_ref, state_ref, out_ref, gated_ref):
        state_ref[...] = jnp.zeros_like(state_ref)

        def advance(j, carry):
            for h in range(local_heads):
                block = handoffs_ref[j ^ base_ref[0], h]
                state_ref[h] = product(
                    block[:, :DK].astype(jnp.float32), state_ref[h], 1, 0
                ) + block[:, DK:].astype(jnp.float32)
            return carry

        lax.fori_loop(0, index_ref[0], advance, 0)
        for h in range(local_heads):
            columns = slice(DV * h, DV * h + DV)
            out = zero_ref[h] + product(reach_ref[h], state_ref[h], 1, 0)
            normed = out * lax.rsqrt(jnp.mean(out * out, axis=-1, keepdims=True) + HEAD_EPSILON)
            out_ref[:, columns] = out
            gated_ref[:, columns] = (
                normed * norm_ref[...] * jax.nn.silu(gate_ref[:, columns])
            ).astype(jnp.bfloat16)

    vmem = pl.BlockSpec(memory_space=pltpu.VMEM)
    width = local_heads * DV
    return pl.pallas_call(
        kernel,
        grid=(1,),
        in_specs=[
            pl.BlockSpec(memory_space=pltpu.SMEM),
            pl.BlockSpec(memory_space=pltpu.SMEM),
            vmem,
            vmem,
            vmem,
            pl.BlockSpec((row_count, width), lambda i: (0, gate_first // width)),
            vmem,
        ],
        out_specs=[vmem, vmem, vmem],
        out_shape=[
            jax.ShapeDtypeStruct((local_heads, DK, DV), jnp.float32),
            jax.ShapeDtypeStruct((row_count, width), jnp.float32),
            jax.ShapeDtypeStruct((row_count, width), jnp.bfloat16),
        ],
        compiler_params=params(),
    )(my_index, base, handoffs, reach, zero_out, projected, norm_gain)


def mixer_gate_back(local_heads, d_gated, recurred, projected, norm_gain, reach):
    row_count = projected.shape[0]
    gate_first = local_heads * (2 * DK + DV) // DV

    def kernel(d_gated_ref, out_ref, gate_ref, norm_ref, reach_ref, d_out_ref, d_gate_ref, d_norm_ref, d_state_ref):
        out, gate, norm_row, d_gated_now = out_ref[...], gate_ref[...], norm_ref[...], d_gated_ref[...]
        scale = lax.rsqrt(jnp.mean(out * out, axis=-1, keepdims=True) + HEAD_EPSILON)
        normed = out * scale
        logistic = jax.nn.sigmoid(gate)
        silu = gate * logistic
        d_norm = jnp.sum(d_gated_now * normed * silu, axis=0, keepdims=True)

        @pl.when(pl.program_id(0) == 0)
        def _():
            d_norm_ref[...] = jnp.zeros_like(d_norm_ref)

        d_norm_ref[0:1, :] = d_norm_ref[0:1, :] + d_norm
        d_gate_ref[...] = (
            d_gated_now * normed * norm_row * logistic * (1.0 + gate * (1.0 - logistic))
        ).astype(jnp.bfloat16)
        d_normed = d_gated_now * norm_row * silu
        d_out = scale * d_normed - (scale * scale * scale) * out * jnp.mean(
            d_normed * out, axis=-1, keepdims=True
        )
        d_out_ref[...] = d_out
        d_state_ref[0] = product(reach_ref[0], d_out, 0, 0).astype(jnp.bfloat16)

    width = local_heads * DV
    block = pl.BlockSpec((row_count, DV), lambda h: (0, h))
    return pl.pallas_call(
        kernel,
        grid=(local_heads,),
        in_specs=[
            block,
            block,
            pl.BlockSpec((row_count, DV), lambda h: (0, gate_first + h)),
            pl.BlockSpec((1, DV), lambda h: (0, 0)),
            per_head(row_count, DK),
        ],
        out_specs=[block, block, pl.BlockSpec((8, DV), lambda h: (0, 0)), per_head(DK, DV)],
        out_shape=[
            jax.ShapeDtypeStruct((row_count, width), jnp.float32),
            jax.ShapeDtypeStruct((row_count, width), jnp.bfloat16),
            jax.ShapeDtypeStruct((8, DV), jnp.float32),
            jax.ShapeDtypeStruct((local_heads, DK, DV), jnp.bfloat16),
        ],
        compiler_params=params(),
    )(d_gated, recurred, projected, norm_gain, reach)


def relay_back(local_heads, my_index, base, handoffs, d_enterings):
    devices = handoffs.shape[0]

    def kernel(index_ref, base_ref, handoffs_ref, d_ref, state_ref):
        state_ref[...] = jnp.zeros_like(state_ref)

        def advance(step, carry):
            j = (devices - 1 - step) ^ base_ref[0]
            for h in range(local_heads):
                state_ref[h] = product(
                    handoffs_ref[j, h, :, :DK].astype(jnp.float32), state_ref[h], 0, 0
                ) + d_ref[j, h].astype(jnp.float32)
            return carry

        lax.fori_loop(0, devices - 1 - index_ref[0], advance, 0)

    vmem = pl.BlockSpec(memory_space=pltpu.VMEM)
    return pl.pallas_call(
        kernel,
        in_specs=[pl.BlockSpec(memory_space=pltpu.SMEM)] * 2 + [vmem, vmem],
        out_specs=vmem,
        out_shape=jax.ShapeDtypeStruct((local_heads, DK, DV), jnp.float32),
        compiler_params=params(),
    )(my_index, base, handoffs, d_enterings)


def conv_back(d_pre, extended, taps_ref, padded, d_block_ref, d_tail_ref, d_rim_ref, d_taps_ref):
    row_count = d_pre.shape[0]
    first = 8 - (KCONV - 1)
    padded[0:8, :] = jnp.zeros((8, d_pre.shape[1]), jnp.float32)
    padded[8 : 8 + row_count, :] = d_pre
    padded[8 + row_count : 16 + row_count, :] = jnp.zeros((8, d_pre.shape[1]), jnp.float32)
    total = None
    d_taps_ref[...] = jnp.zeros_like(d_taps_ref)
    for tap in range(KCONV):
        start = KCONV - 1 - tap
        term = taps_ref[tap : tap + 1, :] * padded[start : start + row_count + 8, :]
        total = term if total is None else total + term
        d_taps_ref[tap : tap + 1, :] = jnp.sum(
            d_pre * extended[first + tap : first + tap + row_count, :], axis=0, keepdims=True
        )
    d_rim_ref[...] = total[0:8, :]
    d_block_ref[...] = total[8:, :].astype(jnp.bfloat16)
    d_tail_ref[...] = total[row_count:, :]


def mixer_back(
    local_heads, projected, rim, taps, decay_proj, scalars,
    solve, fresh, wy_keys, entering_state, d_recurred, d_leaving,
):
    row_count = projected.shape[0]
    three, whole, scalar_spec = mixer_specs(local_heads, row_count)

    def kernel(
        pq, pk, pv, rq, rk, rv, tq, tk, tv, decay_ref, scalars_ref,
        solve_ref, fresh_ref, wy_ref, enter_ref, d_out_ref, d_leave_ref,
        dq_ref, dk_ref, dv_ref, tail_q, tail_k, tail_v, rim_q, rim_k, rim_v,
        taps_q, taps_k, taps_v, d_decay_ref, d_scalars_ref,
        ext_q, ext_k, ext_v, pad_k, pad_v,
    ):
        head = pl.program_id(0)

        @pl.when(head == 0)
        def _():
            d_decay_ref[...] = jnp.zeros_like(d_decay_ref)
            d_scalars_ref[...] = jnp.zeros_like(d_scalars_ref)

        pre_q = convolved(ext_q, pq, rq, tq)
        pre_k = convolved(ext_k, pk, rk, tk)
        pre_v = convolved(ext_v, pv, rv, tv)
        conv_q, conv_k = jax.nn.silu(pre_q), jax.nn.silu(pre_k)
        unit_q, scale_q = unit_rows(conv_q)
        queries = unit_q * DK ** (-0.5)
        key_rows, scale_k = unit_rows(conv_k)
        values = jax.nn.silu(pre_v)
        decay_in, rate, logs, beta, sums, within, row_ids, column_ids = decay_terms(
            head, local_heads, decay_ref, scalars_ref
        )
        strict = row_ids > column_ids
        grown = jnp.exp(sums)
        last = sums[row_count - 1 : row_count, :]
        tail = jnp.exp(last - sums)
        tail_keys = tail * key_rows
        gram = product(key_rows, key_rows, 1, 1)
        scores = jnp.where(strict, gram * within, 0.0)
        attention = product(queries, key_rows, 1, 1) * within
        enter, d_out, d_leave = enter_ref[0], d_out_ref[...], d_leave_ref[0]
        update = fresh_ref[0] - product(wy_ref[0], enter, 1, 0)
        d_update = product(attention, d_out, 0, 0) + product(tail_keys, d_leave, 1, 0)
        d_right = product(solve_ref[0], d_update, 0, 0)
        d_attention = product(d_out, update, 1, 1) * within
        d_system = -product(d_right, update, 1, 1)
        out_state = product(d_out, enter, 1, 1)
        right_state = product(d_right, enter, 1, 1)
        leave_update = product(update, d_leave, 1, 1)
        remainder = values - grown * product(key_rows, enter, 1, 0)
        d_values = beta * d_right
        d_beta = jnp.sum(d_right * remainder, axis=1, keepdims=True) + jnp.sum(
            d_system * scores, axis=1, keepdims=True
        )
        pair = beta * (d_system * scores)
        d_gram = jnp.where(strict, beta * d_system * within, 0.0)
        d_queries = grown * out_state + product(d_attention, key_rows, 1, 0)
        d_keys = (
            product(d_attention, queries, 0, 0)
            + product(d_gram, key_rows, 1, 0)
            + product(d_gram, key_rows, 0, 0)
            + tail * leave_update
            - (beta * grown) * right_state
        )
        both = pair + d_attention * product(queries, key_rows, 1, 1)
        tail_rows = jnp.sum(tail_keys * leave_update, axis=1, keepdims=True)
        diagonal = row_ids == column_ids
        columns = jnp.sum(both, axis=0, keepdims=True)
        d_sums = (
            jnp.sum(both, axis=1, keepdims=True)
            - jnp.sum(jnp.where(diagonal, columns, 0.0), axis=1, keepdims=True)
            + jnp.sum(out_state * (grown * queries), axis=1, keepdims=True)
            - jnp.sum(right_state * ((beta * grown) * key_rows), axis=1, keepdims=True)
            - tail_rows
        )
        d_last = jnp.exp(last) * jnp.sum(
            jnp.sum(d_leave * enter, axis=1, keepdims=True), axis=0, keepdims=True
        ) + jnp.sum(tail_rows, axis=0, keepdims=True)
        d_logs = d_last + jnp.sum(
            jnp.where(row_ids <= column_ids, to_row(d_sums, diagonal), 0.0), axis=1, keepdims=True
        )
        d_decay_in = d_logs * rate * jax.nn.sigmoid(decay_in)
        d_beta_in = d_beta * beta * (1.0 - beta)
        d_decay_ref[...] = (
            d_decay_ref[...]
            + put_lane(d_decay_in, head)
            + put_lane(d_beta_in, head + local_heads)
        )
        d_rate = jnp.sum(d_logs * logs, axis=0, keepdims=True)
        d_bias = jnp.sum(d_decay_in, axis=0, keepdims=True)
        d_scalars_ref[0:1, :] = d_scalars_ref[0:1, :] + put_lane(d_rate, head)
        d_scalars_ref[1:2, :] = d_scalars_ref[1:2, :] + put_lane(d_bias, head)

        def unit_back(d_unit, unit, scale):
            return scale * (d_unit - unit * jnp.sum(unit * d_unit, axis=1, keepdims=True))

        def silu_back(d_act, pre):
            logistic = jax.nn.sigmoid(pre)
            return d_act * logistic * (1.0 + pre * (1.0 - logistic))

        d_pre_q = silu_back(unit_back(d_queries * DK ** (-0.5), unit_q, scale_q), pre_q)
        conv_back(d_pre_q, ext_q, tq, pad_k, dq_ref, tail_q, rim_q, taps_q)
        d_pre_k = silu_back(unit_back(d_keys, key_rows, scale_k), pre_k)
        conv_back(d_pre_k, ext_k, tk, pad_k, dk_ref, tail_k, rim_k, taps_k)
        conv_back(silu_back(d_values, pre_v), ext_v, tv, pad_v, dv_ref, tail_v, rim_v, taps_v)

    def blocks(rows):
        return [
            pl.BlockSpec((rows, DK), lambda h: (0, h)),
            pl.BlockSpec((rows, DK), lambda h: (0, h)),
            pl.BlockSpec((rows, DV), lambda h: (0, h)),
        ]

    def shapes(rows, kind):
        return [
            jax.ShapeDtypeStruct((rows, local_heads * width), kind) for width in (DK, DK, DV)
        ]

    outs = pl.pallas_call(
        kernel,
        grid=(local_heads,),
        in_specs=three(row_count)
        + three(8)
        + three(8)
        + [
            whole,
            scalar_spec,
            per_head(row_count, row_count),
            per_head(row_count, DV),
            per_head(row_count, DK),
            per_head(DK, DV),
            pl.BlockSpec((row_count, DV), lambda h: (0, h)),
            per_head(DK, DV),
        ],
        out_specs=blocks(row_count) + blocks(8) * 3 + [whole, scalar_spec],
        out_shape=shapes(row_count, jnp.bfloat16)
        + shapes(8, jnp.float32) * 3
        + [
            jax.ShapeDtypeStruct((row_count, 128), jnp.float32),
            jax.ShapeDtypeStruct((8, 128), jnp.float32),
        ],
        scratch_shapes=[
            pltpu.VMEM((row_count + 8, DK), jnp.float32),
            pltpu.VMEM((row_count + 8, DK), jnp.float32),
            pltpu.VMEM((row_count + 8, DV), jnp.float32),
            pltpu.VMEM((row_count + 16, DK), jnp.float32),
            pltpu.VMEM((row_count + 16, DV), jnp.float32),
        ],
        compiler_params=params(),
    )(
        *([projected] * 3), *([rim] * 3), *([taps] * 3), decay_proj, scalars,
        solve, fresh, wy_keys, entering_state, d_recurred, d_leaving,
    )
    joined = [jnp.concatenate(outs[3 * i : 3 * i + 3], axis=1) for i in range(4)]
    return (*joined, outs[12], outs[13])


LANES = 128
CHUNK = 32768
TILE = 16
CAPACITY_UNIT = 44
FIRST_GATHER = 24
FIRST_REDUCE = 20
SECOND_REDUCE = 24
TABLE = 1 << 16
VMEM_LIMIT = 48 * 1024 * 1024


def params(**kwargs):
    return pltpu.CompilerParams(vmem_limit_bytes=VMEM_LIMIT, **kwargs)


def piece_kinds(segments_list, piece_count, piece_size):
    kinds = np.ones(piece_count, np.int32)
    offset_now = 0
    for seg_name, row_count, col_count, seg_rate in segments_list:
        if offset_now >= (piece_count - 1) * piece_size:
            break
        tiles = col_count // LANES
        if tiles in (2, 4, 8, 16):
            first = offset_now // piece_size
            kinds[first : first + row_count * col_count // piece_size] = tiles
        offset_now += row_count * col_count
    return kinds


def pack_blocks(master, slot_kinds, kinds_used, first_slot, slot_count):
    piece_size = master.shape[1]
    chunks = piece_size // CHUNK
    rows = CHUNK // LANES
    first_block = first_slot // 8
    slot_blocks = pl.cdiv(slot_count, 8)

    def kernel(kinds_ref, master_ref, out_ref, scratch):
        first = (first_block + pl.program_id(0)) * 8
        for j in range(rows):
            scratch[8 * j : 8 * j + 8, :] = master_ref[:, LANES * j : LANES * j + LANES]
        for s in range(8):
            kind_now = kinds_ref[first + s]
            for kind in kinds_used:

                @pl.when(kind_now == kind)
                def _():
                    for tile in range(rows // TILE):
                        row_tile, column = divmod(tile, kind)
                        start = (row_tile * TILE * kind + column) * 8 + s
                        out_ref[s, TILE * tile : TILE * tile + TILE, :] = scratch[
                            pl.ds(start, TILE, stride=8 * kind), :
                        ].astype(jnp.bfloat16)

    return pl.pallas_call(
        kernel,
        grid_spec=pltpu.PrefetchScalarGridSpec(
            num_scalar_prefetch=1,
            grid=(slot_blocks, chunks),
            in_specs=[pl.BlockSpec((8, CHUNK), lambda i, j, kinds: (first_block + i, j))],
            out_specs=pl.BlockSpec((8, rows, LANES), lambda i, j, kinds: (i, j, 0)),
            scratch_shapes=[pltpu.VMEM((8 * rows, LANES), jnp.float32)],
        ),
        out_shape=jax.ShapeDtypeStruct((slot_count, piece_size // LANES, LANES), jnp.bfloat16),
        compiler_params=params(),
    )(slot_kinds, master)


def reserve(shape, kind):
    def kernel(out_ref):
        pass

    return pl.pallas_call(
        kernel,
        out_specs=pl.BlockSpec(memory_space=pl.ANY),
        out_shape=jax.ShapeDtypeStruct(shape, kind),
        compiler_params=params(),
    )()


def assemble(tables, matrices, step_rows, rows_in=None):
    piece_rows = tables[0].shape[1]
    plans = []
    first_block, first_column = 0, 0
    for positions, col_count in matrices:
        tiles = col_count // LANES
        blocks = step_rows * tiles // piece_rows
        plans.append((first_block, first_column, tiles, blocks))
        first_block += blocks
        first_column += col_count
    blocks_a_step, width = first_block, first_column
    steps = matrices[0][0].shape[0] // plans[0][3]
    order = jnp.concatenate(
        [
            positions.reshape(steps, plan[3])
            for (positions, col_count), plan in zip(matrices, plans)
        ],
        axis=1,
    ).reshape(-1)
    uneven = [plan for plan in plans if piece_rows * plan[3] != step_rows * plan[2] or plan[2] not in (2, 4, 8, 16)]
    multiply = rows_in is not None

    def kernel(order_ref, *refs):
        if multiply:
            rows_ref, refs = refs[0], refs[1:]
        table_refs, refs = refs[: len(tables)], refs[len(tables) :]
        out_ref, refs = refs[0], refs[1:]
        if multiply:
            product_ref, refs = refs[0], refs[1:]
        buffer, sem, scratch = refs
        g = pl.program_id(0)
        slot = lax.rem(g, 2)

        def start(step, which):
            def one(j, carry):
                position = order_ref[step * blocks_a_step + j]
                for number, table_ref in enumerate(table_refs):

                    @pl.when(position // TABLE == number)
                    def _():
                        pltpu.make_async_copy(
                            table_ref.at[lax.rem(position, TABLE)],
                            buffer.at[which, j],
                            sem.at[which],
                        ).start()

                return carry

            lax.fori_loop(0, blocks_a_step, one, 0)

        @pl.when(g == 0)
        def _():
            start(0, 0)

        @pl.when(g + 1 < steps)
        def _():
            start(g + 1, 1 - slot)

        pltpu.make_async_copy(buffer.at[slot], buffer.at[slot], sem.at[slot]).wait()
        for plan in plans:
            first, left, tiles, blocks = plan
            if plan in uneven:
                for j in range(blocks):
                    scratch[piece_rows * j : piece_rows * j + piece_rows, :] = buffer[
                        slot, first + j
                    ].astype(jnp.float32)
                for c in range(tiles):
                    out_ref[:, left + LANES * c : left + LANES * c + LANES] = scratch[
                        pl.ds(c, step_rows, stride=tiles), :
                    ].astype(jnp.bfloat16)
                continue
            for j in range(blocks):
                for tile in range(piece_rows // TILE):
                    row_tile, column = divmod(tile, tiles)
                    row = piece_rows // tiles * j + TILE * row_tile
                    column = left + LANES * column
                    out_ref[row : row + TILE, column : column + LANES] = buffer[
                        slot, first + j, TILE * tile : TILE * tile + TILE, :
                    ]
        if multiply:
            part = jnp.dot(rows_ref[...], out_ref[...], preferred_element_type=jnp.float32)

            @pl.when(g == 0)
            def _():
                product_ref[...] = part

            @pl.when(g > 0)
            def _():
                product_ref[...] = product_ref[...] + part

    anywhere = pl.BlockSpec(memory_space=pl.ANY)
    in_specs = [anywhere for table in tables]
    operands = list(tables)
    out_specs = [pl.BlockSpec((step_rows, width), lambda g, order: (g, 0))]
    out_shape = [jax.ShapeDtypeStruct((steps * step_rows, width), jnp.bfloat16)]
    if multiply:
        row_count = rows_in.shape[0]
        in_specs.insert(0, pl.BlockSpec((row_count, step_rows), lambda g, order: (0, g)))
        operands.insert(0, rows_in)
        out_specs.append(pl.BlockSpec((row_count, width), lambda g, order: (0, 0)))
        out_shape.append(jax.ShapeDtypeStruct((row_count, width), jnp.float32))
    scratch_rows = max([plan[3] * piece_rows for plan in uneven], default=8)
    return pl.pallas_call(
        kernel,
        grid_spec=pltpu.PrefetchScalarGridSpec(
            num_scalar_prefetch=1,
            grid=(steps,),
            in_specs=in_specs,
            out_specs=out_specs,
            scratch_shapes=[
                pltpu.VMEM((2, blocks_a_step, piece_rows, LANES), jnp.bfloat16),
                pltpu.SemaphoreType.DMA((2,)),
                pltpu.VMEM((scratch_rows, LANES), jnp.float32),
            ],
        ),
        out_shape=out_shape,
        cost_estimate=pl.CostEstimate(
            flops=2 * steps * step_rows * width * (rows_in.shape[0] if multiply else 0),
            bytes_accessed=4 * steps * step_rows * width,
            transcendentals=0,
        ),
        compiler_params=params(),
    )(order, *operands)


def spread_products(my_part, parts, pairs):
    row_count = pairs[0][0].shape[0]
    total = pairs[0][1].shape[0 if pairs[0][2] else 1]
    width = total // parts

    def kernel(part_ref, *refs):
        ins, outs = refs[: 2 * len(pairs)], refs[2 * len(pairs) :]
        for m in range(parts):
            first = pl.multiple_of((part_ref[0] ^ m) * width, width)
            result = None
            for i, (left, right, transposed) in enumerate(pairs):
                if transposed:
                    block, axis = ins[2 * i + 1][pl.ds(first, width), :], 1
                else:
                    block, axis = ins[2 * i + 1][:, pl.ds(first, width)], 0
                part = lax.dot_general(
                    ins[2 * i][...],
                    block,
                    (((1,), (axis,)), ((), ())),
                    preferred_element_type=jnp.float32,
                )
                result = part if result is None else result + part
            outs[m][...] = result.astype(jnp.bfloat16)

    vmem = pl.BlockSpec(memory_space=pltpu.VMEM)
    flat = [array for left, right, transposed in pairs for array in (left, right)]
    return pl.pallas_call(
        kernel,
        in_specs=[pl.BlockSpec(memory_space=pltpu.SMEM)] + [vmem] * len(flat),
        out_specs=[vmem] * parts,
        out_shape=[jax.ShapeDtypeStruct((row_count, width), jnp.bfloat16)] * parts,
        cost_estimate=pl.CostEstimate(
            flops=2 * row_count * sum(pair[1].size for pair in pairs),
            bytes_accessed=2 * sum(pair[1].size for pair in pairs),
            transcendentals=0,
        ),
        compiler_params=params(),
    )(my_part, *flat)


def exchange(blocks, axis):
    devices = lax.axis_size(axis)
    return [blocks[0]] + [
        lax.ppermute(blocks[m], axis, [(i, i ^ m) for i in range(devices)])
        for m in range(1, devices)
    ]


def total_of(blocks):
    total = blocks[0].astype(jnp.float32)
    for block in blocks[1:]:
        total = total + block.astype(jnp.float32)
    return total


def sum_over(block, axis):
    return total_of(exchange([block] * lax.axis_size(axis), axis))


def in_order(blocks, my_part, axis):
    stacked = jnp.stack(blocks)
    return jnp.concatenate(
        [
            lax.dynamic_index_in_dim(stacked, my_part ^ j, 0, keepdims=False)
            for j in range(len(blocks))
        ],
        axis=axis,
    )


def gather_states(block):
    devices = lax.axis_size("seq")
    if devices != 8:
        return lax.all_gather(block, "seq", axis=0, tiled=False), jnp.zeros((1,), jnp.int32)

    def moved(array, mask):
        return lax.ppermute(array, "seq", [(i, i ^ mask) for i in range(devices)])

    chips = [block] + [moved(block, mask) for mask in (2, 4, 6)]
    pairs = [(chip, moved(chip, 1)) for chip in chips]
    rows = jnp.stack([array for pair in pairs for array in pair])
    return rows, lax.axis_index("seq").astype(jnp.int32).reshape(1)


def weight_grad_blocks(left_t, right, right_block, col_count, positions, tables, blocks_a_step):
    row_total, depth = left_t.shape
    tiles = col_count // LANES
    piece_rows = 512
    even = tiles in (2, 4, 8, 16)
    step_rows = blocks_a_step * piece_rows // tiles
    steps = row_total // step_rows

    def kernel(positions_ref, left_ref, right_ref, *refs):
        table_refs = refs[len(tables) : 2 * len(tables)]
        product, staged, sem = refs[2 * len(tables) :]
        g = pl.program_id(0)
        slot = lax.rem(g, 2)

        def settle(which):
            pltpu.make_async_copy(staged.at[which], staged.at[which], sem.at[which]).wait()

        @pl.when(g >= 2)
        def _():
            settle(slot)

        left = left_ref[...]
        if even:
            product[...] = jnp.dot(left, right_ref[...], preferred_element_type=jnp.float32)
            for tile in range(step_rows // TILE * tiles):
                row_tile, column = divmod(tile, tiles)
                block, row = divmod(TILE * tile, piece_rows)
                staged[slot, block, row : row + TILE, :] = product[
                    TILE * row_tile : TILE * row_tile + TILE, LANES * column : LANES * column + LANES
                ].astype(jnp.bfloat16)
        else:
            for c in range(0, tiles, 2):
                width = min(2, tiles - c)
                part = jnp.dot(
                    left,
                    right_ref[:, LANES * c : LANES * (c + width)],
                    preferred_element_type=jnp.float32,
                )
                for w in range(width):
                    product[pl.ds(c + w, step_rows, stride=tiles), :] = part[
                        :, LANES * w : LANES * w + LANES
                    ]
            for block in range(blocks_a_step):
                staged[slot, block] = product[
                    piece_rows * block : piece_rows * block + piece_rows, :
                ].astype(jnp.bfloat16)
        for block in range(blocks_a_step):
            position = positions_ref[g * blocks_a_step + block]

            for number, table_ref in enumerate(table_refs):

                @pl.when(position // TABLE == number)
                def _():
                    pltpu.make_async_copy(
                        staged.at[slot, block],
                        table_ref.at[lax.rem(position, TABLE)],
                        sem.at[slot],
                    ).start()

        @pl.when(g == steps - 1)
        def _():
            settle(slot)
            if steps > 1:
                settle(1 - slot)

    anywhere = pl.BlockSpec(memory_space=pl.ANY)
    in_specs = [
        pl.BlockSpec((step_rows, depth), lambda g, positions: (g, 0)),
        pl.BlockSpec((depth, col_count), lambda g, positions: (0, right_block)),
    ] + [anywhere for table in tables]
    product_shape = (step_rows, col_count) if even else (step_rows * tiles, LANES)
    return pl.pallas_call(
        kernel,
        grid_spec=pltpu.PrefetchScalarGridSpec(
            num_scalar_prefetch=1,
            grid=(steps,),
            in_specs=in_specs,
            out_specs=[anywhere for table in tables],
            scratch_shapes=[
                pltpu.VMEM(product_shape, jnp.float32),
                pltpu.VMEM((2, blocks_a_step, piece_rows, LANES), jnp.bfloat16),
                pltpu.SemaphoreType.DMA((2,)),
            ],
        ),
        out_shape=[jax.ShapeDtypeStruct(table.shape, table.dtype) for table in tables],
        input_output_aliases={3 + i: i for i in range(len(tables))},
        cost_estimate=pl.CostEstimate(
            flops=2 * row_total * depth * col_count,
            bytes_accessed=2 * row_total * col_count,
            transcendentals=0,
        ),
        compiler_params=params(),
    )(positions, left_t, right, *tables)


def optimizer_update(
    sources, slot_sources, slot_rows, slot_kinds, kinds_used, slot_masks, small_rates, master, moment_one, moment_two
):
    capacity, piece_size = master.shape
    chunks = piece_size // CHUNK
    rows = CHUNK // LANES
    slot_blocks = pl.cdiv(capacity, 8)

    steps = slot_blocks * chunks

    def kernel(kinds_ref, sources_ref, rows_ref, *refs):
        source_refs, refs = refs[: len(sources)], refs[len(sources) :]
        (
            masks_ref, small_ref, master_ref, one_ref, two_ref,
            grad_out, master_out, one_out, two_out, low_out, scratch, buffer, sem,
        ) = refs
        first = pl.program_id(0) * 8
        step = pl.program_id(0) * chunks + pl.program_id(1)
        slot = lax.rem(step, 2)

        def start(step, which):
            block, chunk = step // chunks, lax.rem(step, chunks)
            for s in range(8):
                for i, source_ref in enumerate(source_refs):

                    @pl.when(sources_ref[block * 8 + s] == i)
                    def _():
                        pltpu.make_async_copy(
                            source_ref.at[
                                rows_ref[block * 8 + s],
                                pl.ds(pl.multiple_of(chunk * rows, rows), rows),
                            ],
                            buffer.at[which, s],
                            sem.at[which],
                        ).start()

        @pl.when(step == 0)
        def _():
            start(0, 0)

        @pl.when(step + 1 < steps)
        def _():
            start(step + 1, 1 - slot)

        pltpu.make_async_copy(buffer.at[slot], buffer.at[slot], sem.at[slot]).wait()
        for s in range(8):
            kind_now = kinds_ref[first + s]
            for kind in kinds_used:

                @pl.when(kind_now == kind)
                def _():
                    for tile in range(rows // TILE):
                        row_tile, column = divmod(tile, kind)
                        start = (row_tile * TILE * kind + column) * 8 + s
                        scratch[pl.ds(start, TILE, stride=8 * kind), :] = buffer[
                            slot, s, TILE * tile : TILE * tile + TILE, :
                        ].astype(jnp.float32)
        present = masks_ref[0] > 0.5
        is_small = masks_ref[1] > 0.5
        rate_rows = masks_ref[2]
        for j in range(rows):
            lanes = slice(LANES * j, LANES * j + LANES)
            grad = jnp.where(present, scratch[8 * j : 8 * j + 8, :], 0.0)
            rate = jnp.where(is_small, small_ref[:, lanes], rate_rows)
            master_now = master_ref[:, lanes]
            one_new = BETA_ONE * one_ref[:, lanes] + (1.0 - BETA_ONE) * grad
            two_new = BETA_TWO * two_ref[:, lanes] + (1.0 - BETA_TWO) * grad * grad
            first_hat = one_new / (1.0 - BETA_ONE**STEP)
            second_hat = two_new / (1.0 - BETA_TWO**STEP)
            master_new = master_now - rate * (
                first_hat / (jnp.sqrt(second_hat) + ADAM_EPSILON) + WEIGHT_DECAY * master_now
            )
            grad_out[:, lanes] = grad
            master_out[:, lanes] = master_new
            one_out[:, lanes] = one_new
            two_out[:, lanes] = two_new
            low_out[:, lanes] = master_new.astype(jnp.bfloat16)

    state_spec = pl.BlockSpec((8, CHUNK), lambda i, j, *tables: (i, j))
    wide = jax.ShapeDtypeStruct((capacity, piece_size), jnp.float32)
    return pl.pallas_call(
        kernel,
        grid_spec=pltpu.PrefetchScalarGridSpec(
            num_scalar_prefetch=3,
            grid=(slot_blocks, chunks),
            in_specs=[pl.BlockSpec(memory_space=pl.ANY) for source in sources]
            + [
                pl.BlockSpec((3, 8, LANES), lambda i, j, *tables: (0, i, 0)),
                pl.BlockSpec((1, CHUNK), lambda i, j, *tables: (0, j)),
                state_spec,
                state_spec,
                state_spec,
            ],
            out_specs=[state_spec] * 5,
            scratch_shapes=[
                pltpu.VMEM((8 * rows, LANES), jnp.float32),
                pltpu.VMEM((2, 8, rows, LANES), jnp.bfloat16),
                pltpu.SemaphoreType.DMA((2,)),
            ],
        ),
        out_shape=[wide] * 4 + [jax.ShapeDtypeStruct((capacity, piece_size), jnp.bfloat16)],
        compiler_params=params(),
    )(
        slot_kinds, slot_sources, slot_rows, *sources,
        slot_masks, small_rates, master, moment_one, moment_two,
    )


def weight_grad(left, right):
    return jnp.einsum("td,tc->dc", left, right, preferred_element_type=jnp.float32)


def back_product(grad_rows, weight):
    return jnp.dot(grad_rows, weight.T, preferred_element_type=jnp.float32)


def gather_rest(packed, first, trips, most, extra_step):
    devices = lax.axis_size("seq")
    rows = devices * extra_step
    room = reserve((most * rows,) + packed.shape[1:], packed.dtype)

    def more(trip, table):
        part = lax.dynamic_slice_in_dim(packed, first + trip * extra_step, extra_step)
        part = lax.all_gather(part, "seq", axis=0, tiled=True)
        return lax.dynamic_update_slice_in_dim(table, part, trip * rows, axis=0)

    return lax.fori_loop(0, trips, more, room)


def reduce_rest(rest, trips, most, extra_step):
    devices = lax.axis_size("seq")
    rows = devices * extra_step
    room = reserve((most * extra_step,) + rest.shape[1:], rest.dtype)

    def more(trip, table):
        part = lax.dynamic_slice_in_dim(rest, trip * rows, rows)
        part = lax.psum_scatter(part, "seq", scatter_dimension=0, tiled=True)
        return lax.dynamic_update_slice_in_dim(table, part, trip * extra_step, axis=0)

    return lax.fori_loop(0, trips, more, room)


def on_device(inputs, cotangent, owners, master, moment_one, moment_two):
    head_parts = lax.axis_size("head")
    seq_parts = lax.axis_size("seq")
    local_heads = HEADS // head_parts
    capacity, piece_size = master.shape
    piece_count = owners.shape[0]
    row_count = inputs.shape[0]
    rim_width = KCONV - 1
    segments_list = shard_layout(local_heads, head_parts)
    columns = {name: c for name, r, c, rate in segments_list}
    counts = {name: r * c // piece_size for name, r, c, rate in segments_list[:8]}
    firsts = dict(zip(counts, np.cumsum([0] + list(counts.values())).tolist()))
    mixer_count = firsts["wgate"]
    big_count = piece_count - 1
    my_head = lax.axis_index("head").astype(jnp.int32)
    my_index = lax.axis_index("seq").astype(jnp.int32)
    my_head_row, my_index_row = my_head.reshape(1), my_index.reshape(1)

    onehot = (owners[:, None] == jnp.arange(seq_parts, dtype=jnp.int32)[None, :]).astype(jnp.int32)
    ranks = jnp.sum((jnp.cumsum(onehot, axis=0) - onehot) * onehot, axis=1)
    mixer_held = jnp.sum(onehot[:mixer_count], axis=0)
    mlp_held = jnp.sum(onehot[mixer_count:big_count], axis=0)
    padded = capacity + -capacity % 8
    small_rank = ranks[big_count]
    big_owners, big_ranks = owners[:big_count], ranks[:big_count]
    is_mixer = np.arange(big_count) < mixer_count
    held_there = jnp.sum(onehot[:big_count] * mixer_held[None, :], axis=1)

    def rest_row(over, owner):
        return over // extra_step * (seq_parts * extra_step) + owner * extra_step + over % extra_step

    early = -(-capacity * FIRST_GATHER // (8 * CAPACITY_UNIT)) * 8
    late = capacity - early
    extra_step = min(4, late)
    most_gather = -(-late // extra_step)
    trips_gather = jnp.maximum(-(-(jnp.max(mixer_held) - early) // extra_step), 0)
    early_row = big_owners * early + big_ranks
    mixer_fetch = jnp.where(
        big_ranks < early, early_row, TABLE + rest_row(big_ranks - early, big_owners)
    )
    mlp_fetch = jnp.where(
        big_ranks < early, TABLE + early_row, big_owners * late + big_ranks - early
    )
    first_room = -(-capacity * FIRST_REDUCE // CAPACITY_UNIT)
    second_room = -(-capacity * SECOND_REDUCE // CAPACITY_UNIT)
    most_reduce = -(-(capacity - second_room) // extra_step)
    second_held = mixer_held + jnp.maximum(mlp_held - first_room, 0)
    trips_reduce = jnp.maximum(-(-(jnp.max(second_held) - second_room) // extra_step), 0)
    mlp_ranks = big_ranks - held_there
    second_index = jnp.where(is_mixer, big_ranks, big_ranks - first_room)
    store = jnp.where(
        ~is_mixer & (mlp_ranks < first_room),
        big_owners * first_room + mlp_ranks,
        jnp.where(
            second_index < second_room,
            TABLE + big_owners * second_room + second_index,
            2 * TABLE + rest_row(second_index - second_room, big_owners),
        ),
    )
    small_owner = owners[big_count]

    def spots(table, name):
        return table[firsts[name] : firsts[name] + counts[name]]

    my_mixer = mixer_held[my_index]
    my_mlp = mlp_held[my_index]
    my_count = my_mixer + my_mlp
    slot_ids = jnp.arange(padded, dtype=jnp.int32)
    mine = owners == my_index
    matches = (mine[None, :] & (ranks[None, :] == slot_ids[:, None])).astype(jnp.int32)
    kind_table = piece_kinds(segments_list, piece_count, piece_size)
    piece_rates, small_rates = rate_parts(segments_list, piece_count, piece_size)
    present = jnp.sum(matches, axis=1)
    slot_kinds = 1 + jnp.sum(matches * jnp.asarray(kind_table - 1)[None, :], axis=1)
    slot_rates = PAD_RATE + jnp.sum(
        matches.astype(jnp.float32) * jnp.asarray(piece_rates - np.float32(PAD_RATE))[None, :], axis=1
    )
    is_small = matches[:, big_count]
    kinds_used = sorted(set(kind_table.tolist()) | {1})

    small_rows = -(-sum(r * c for name, r, c, rate in segments_list[8:]) // (TILE * LANES)) * TILE
    gain_width = D // head_parts
    norm_width = DV // head_parts
    gain_first = sum(r * c for name, r, c, rate in segments_list[8:14])
    my_small = lax.dynamic_slice(master, (small_rank, 0), (1, small_rows * LANES))
    my_small = my_small.astype(jnp.bfloat16)
    gains = my_small[:, gain_first : gain_first + 2 * gain_width + norm_width]
    gains = in_order(exchange([gains] * head_parts, "head"), my_head, 0)
    gains = jnp.concatenate(
        [
            gains[:, :gain_width].reshape(1, D),
            gains[:, gain_width : 2 * gain_width].reshape(1, D),
            gains[:, 2 * gain_width :].reshape(1, DV),
        ],
        axis=1,
    )
    rows_of_piece = piece_size // LANES
    small_width = small_rows * LANES
    small_part = jnp.concatenate([my_small, gains], axis=1).reshape(-1, LANES)
    small_table = lax.all_gather(small_part, "seq", axis=0, tiled=False)
    input_blocks = exchange([inputs] * head_parts, "head")
    early_part = pack_blocks(master, slot_kinds, kinds_used, 0, early)
    early_table = lax.all_gather(early_part, "seq", axis=0, tiled=True)
    late_part = pack_blocks(master, slot_kinds, kinds_used, early, late)
    back_blocks = exchange([cotangent] * head_parts, "head")
    rows_full = in_order(input_blocks, my_head, 1)
    back_full = in_order(back_blocks, my_head, 1)
    small_flat = lax.dynamic_index_in_dim(
        small_table, small_owner, axis=0, keepdims=False
    ).reshape(-1)
    by_name, small_used = unpack(small_flat, segments_list[8:])
    gains = small_flat[small_width:].astype(jnp.float32)[None, :]
    gain_one, gain_two, norm_row = gains[:, :D], gains[:, D : 2 * D], gains[:, 2 * D :]
    gain_one_mine = by_name["gainone"].astype(jnp.float32)
    gain_two_mine = by_name["gaintwo"].astype(jnp.float32)

    rows_wide = rows_full.astype(jnp.float32)
    scale_one = lax.rsqrt(jnp.mean(rows_wide * rows_wide, axis=-1, keepdims=True) + NORM_EPSILON)
    normed = (rows_wide * scale_one * gain_one).astype(jnp.bfloat16)

    decay_weight = jnp.pad(by_name["wab"], ((0, 0), (0, LANES - 2 * local_heads)))
    decay_proj = jnp.dot(normed, decay_weight, preferred_element_type=jnp.float32)
    taps = jnp.concatenate([by_name["cq"], by_name["ck"], by_name["cv"]], axis=1)
    taps = jnp.pad(taps.astype(jnp.float32), ((0, 8 - KCONV), (0, 0)))
    scalars = jnp.pad(
        jnp.concatenate([by_name["alog"], by_name["dtbias"]], axis=0).astype(jnp.float32),
        ((0, 6), (0, LANES - local_heads)),
    )

    beside = (
        trips_gather, late_part, normed, scale_one, decay_proj, decay_weight, taps, scalars,
        back_full, mixer_fetch, mlp_fetch, store, gain_two, norm_row,
    )
    early_table, beside = lax.optimization_barrier((early_table, beside))
    (
        trips_now, late_part, normed, scale_one, decay_proj, decay_weight, taps, scalars,
        back_full, mixer_fetch, mlp_fetch, store, gain_two, norm_row,
    ) = beside
    mixer_rest = gather_rest(late_part, 0, trips_now, most_gather, extra_step)
    late_table = lax.all_gather(late_part, "seq", axis=0, tiled=True)

    mixer_names = ("wq", "wk", "wv", "wg")
    mixer_weights, projected = assemble(
        [early_table, mixer_rest],
        [(spots(mixer_fetch, name), columns[name]) for name in mixer_names],
        512,
        normed,
    )
    conv_columns = local_heads * (2 * DK + DV)
    rim = shifted(projected[row_count - rim_width :, :conv_columns], "seq", 1)
    rim = jnp.pad(rim, ((8 - rim_width, 0), (0, 0)))
    solve, fresh, wy_keys, reach, zero_out, handoff = mixer_local(
        local_heads, projected, rim, taps, decay_proj, scalars
    )
    handoffs, base = gather_states(handoff)
    (out_weights,) = assemble(
        [early_table, mixer_rest], [(spots(mixer_fetch, "wo"), columns["wo"])], 256
    )
    entering_state, recurred, gated_low = mixer_out(
        local_heads, my_index_row, base, handoffs, reach, zero_out, projected, norm_row
    )
    mixed_parts = exchange(
        spread_products(my_head_row, head_parts, [(gated_low, out_weights, False)]), "head"
    )
    (down_weights,) = assemble(
        [late_table, early_table], [(spots(mlp_fetch, "wdown"), columns["wdown"])], 352
    )
    (mlp_weights,) = assemble(
        [late_table, early_table],
        [(spots(mlp_fetch, name), columns[name]) for name in ("wgate", "wup")],
        512,
    )
    mixed_parts, down_weights, mlp_weights = lax.optimization_barrier(
        (mixed_parts, down_weights, mlp_weights)
    )
    mixed = total_of(mixed_parts)
    inputs_wide = inputs.astype(jnp.float32)
    residual = inputs_wide + mixed
    resid_low = residual.astype(jnp.bfloat16)

    resid_blocks = exchange([resid_low] * head_parts, "head")
    resid_full = in_order(resid_blocks, my_head, 1).astype(jnp.float32)
    scale_two = lax.rsqrt(jnp.mean(resid_full * resid_full, axis=-1, keepdims=True) + NORM_EPSILON)
    hidden_in = (resid_full * scale_two * gain_two).astype(jnp.bfloat16)
    gate_up = jnp.dot(hidden_in, mlp_weights, preferred_element_type=jnp.float32)
    hidden_width = columns["wgate"]
    gate_mlp, up_mlp = gate_up[:, :hidden_width], gate_up[:, hidden_width:]
    logistic_output_multiplier = jax.nn.sigmoid(gate_mlp)
    silu_gate = gate_mlp * logistic_output_multiplier
    hidden = (silu_gate * up_mlp).astype(jnp.bfloat16)
    mlp_blocks = spread_products(my_head_row, head_parts, [(hidden, down_weights, False)])
    d_hidden = back_product(back_full, down_weights)
    d_gate_mlp = (
        d_hidden
        * up_mlp
        * logistic_output_multiplier
        * (1.0 + gate_mlp * (1.0 - logistic_output_multiplier))
    ).astype(jnp.bfloat16)
    d_up_mlp = (d_hidden * silu_gate).astype(jnp.bfloat16)
    d_gate_up = jnp.concatenate([d_gate_mlp, d_up_mlp], axis=1)
    def store_grad(tables, name, left_t, right, right_block, blocks_a_step):
        return weight_grad_blocks(
            left_t, right, right_block, columns[name], spots(store, name), tables, blocks_a_step
        )

    grad_tables = [
        reserve((rows, rows_of_piece, LANES), jnp.bfloat16)
        for rows in (
            seq_parts * first_room,
            seq_parts * second_room,
            most_reduce * seq_parts * extra_step,
        )
    ]
    grad_tables = store_grad(grad_tables, "wdown", hidden.T, back_full, 0, 11)
    hidden_in_t = hidden_in.T
    grad_tables = store_grad(grad_tables, "wgate", hidden_in_t, d_gate_up, 0, 11)
    grad_tables = store_grad(grad_tables, "wup", hidden_in_t, d_gate_up, 1, 11)
    grad_tables, d_gate_up = lax.optimization_barrier((grad_tables, d_gate_up))
    d_hidden_parts = exchange(
        spread_products(my_head_row, head_parts, [(d_gate_up, mlp_weights, True)]), "head"
    )
    first_reduced = lax.psum_scatter(grad_tables[0], "seq", scatter_dimension=0, tiled=True)
    grad_tables = grad_tables[1:]
    store = store - TABLE
    d_hidden_mine = total_of(d_hidden_parts)
    mlp_out = total_of(exchange(mlp_blocks, "head"))
    block_out = (residual + mlp_out).astype(jnp.bfloat16)

    resid_mine = resid_low.astype(jnp.float32)
    d_hidden_low = d_hidden_mine.astype(jnp.bfloat16)
    dot_mine = jnp.sum(d_hidden_mine * gain_two_mine * resid_mine, axis=-1)
    d_hidden_blocks = exchange([d_hidden_low] * head_parts, "head")
    dot_two = sum_over(dot_mine.reshape(-1, LANES), "head").reshape(row_count, 1)
    grad_gaintwo = jnp.sum(d_hidden_mine * resid_mine * scale_two, axis=0)
    d_resid = (
        cotangent.astype(jnp.float32)
        + scale_two * d_hidden_mine * gain_two_mine
        - scale_two**3 / D * resid_mine * dot_two
    )
    d_hidden_full = in_order(d_hidden_blocks, my_head, 1).astype(jnp.float32)
    back_mix_full = (
        back_full.astype(jnp.float32)
        + scale_two * d_hidden_full * gain_two
        - scale_two**3 / D * resid_full * dot_two
    ).astype(jnp.bfloat16)

    d_gated = back_product(back_mix_full, out_weights)
    d_recurred, d_gate, norm_grad, d_entering = mixer_gate_back(
        local_heads, d_gated, recurred, projected, norm_row, reach
    )
    d_enterings, base = gather_states(d_entering)
    normed_t = normed.T
    grad_tables = store_grad(grad_tables, "wo", gated_low.T, back_mix_full, 0, 8)
    grad_tables = store_grad(grad_tables, "wg", normed_t, d_gate, 0, 8)
    d_leaving = relay_back(local_heads, my_index_row, base, handoffs, d_enterings)
    d_conv, d_tail, d_rim, d_taps, d_decay_wide, d_scalars = mixer_back(
        local_heads,
        projected,
        rim,
        taps,
        decay_proj,
        scalars,
        solve,
        fresh,
        wy_keys,
        entering_state,
        d_recurred,
        d_leaving,
    )
    d_rim = shifted(d_rim[8 - rim_width :], "seq", -1)
    d_tail = d_tail + jnp.pad(d_rim, ((8 - rim_width, 0), (0, 0)))
    d_conv = lax.dynamic_update_slice(d_conv, d_tail.astype(jnp.bfloat16), (row_count - 8, 0))
    key_width = local_heads * DK
    grad_tables = store_grad(grad_tables, "wv", normed_t, d_conv, 1, 8)
    grad_tables = store_grad(grad_tables, "wk", normed_t, d_conv, 1, 4)
    grad_tables = store_grad(grad_tables, "wq", normed_t, d_conv, 0, 4)
    second_table, first_reduced = lax.optimization_barrier((grad_tables[0], first_reduced))
    second_reduced = lax.psum_scatter(second_table, "seq", scatter_dimension=0, tiled=True)
    d_decay = d_decay_wide.astype(jnp.bfloat16)
    grad_wab = weight_grad(normed, d_decay)[:, : 2 * local_heads]
    d_projected = jnp.concatenate([d_conv, d_gate], axis=1)
    d_normed_mine = total_of(
        exchange(
            spread_products(
                my_head_row,
                head_parts,
                [(d_projected, mixer_weights, True), (d_decay, decay_weight, True)],
            ),
            "head",
        )
    )
    dot_one = jnp.sum(d_normed_mine * gain_one_mine * inputs_wide, axis=-1)
    sums = sum_over(
        jnp.concatenate([dot_one.reshape(-1, LANES), norm_grad[0].reshape(-1, LANES)]), "head"
    )
    dot_one = sums[: row_count // LANES].reshape(row_count, 1)
    grad_wnorm = lax.dynamic_slice_in_dim(
        sums[row_count // LANES :].reshape(-1), my_head * norm_width, norm_width
    )
    grad_gainone = jnp.sum(d_normed_mine * inputs_wide * scale_one, axis=0)
    input_grad = (
        d_resid
        + scale_one * d_normed_mine * gain_one_mine
        - scale_one**3 / D * inputs_wide * dot_one
    )

    small_grads = [
        d_taps[:KCONV, :key_width],
        d_taps[:KCONV, key_width : 2 * key_width],
        d_taps[:KCONV, 2 * key_width :],
        grad_wab,
        d_scalars[0, :local_heads],
        d_scalars[1, :local_heads],
        grad_gainone,
        grad_gaintwo,
        grad_wnorm,
    ]
    small_block = jnp.concatenate(
        [grad_now.reshape(-1) for grad_now in small_grads]
        + [jnp.zeros((small_rows * LANES - small_used,), jnp.float32)]
    ).reshape(-1, LANES)
    mask = 1
    while mask < seq_parts:
        small_block = small_block + lax.ppermute(
            small_block, "seq", [(i, i ^ mask) for i in range(seq_parts)]
        )
        mask *= 2
    small_block = jnp.pad(
        small_block.astype(jnp.bfloat16), ((0, rows_of_piece - small_rows), (0, 0))
    )[None]

    trips_now, second_reduced, rest_grads = lax.optimization_barrier(
        (trips_reduce, second_reduced, grad_tables[1])
    )
    rest_reduced = reduce_rest(rest_grads, trips_now, most_reduce, extra_step)
    my_first = slot_ids - my_mixer
    in_first = (my_first >= 0) & (my_first < first_room)
    my_second = jnp.where(my_first >= 0, slot_ids - first_room, slot_ids)
    slot_sources = jnp.where(in_first, 0, jnp.where(my_second < second_room, 1, 2))
    slot_rows = jnp.where(
        in_first, my_first, jnp.where(my_second < second_room, my_second, my_second - second_room)
    )
    slot_sources = jnp.where(present > 0, jnp.where(is_small > 0, 3, slot_sources), 0)
    slot_rows = jnp.where(is_small > 0, 0, slot_rows)
    slot_rows = jnp.where(present > 0, slot_rows, 0)
    slot_masks = jnp.stack([present.astype(jnp.float32), is_small.astype(jnp.float32), slot_rates])
    slot_masks = jnp.broadcast_to(slot_masks[:, :, None], slot_masks.shape + (LANES,))
    grad_slots, master_new, moment_new, second_new, weights_low = optimizer_update(
        [first_reduced, second_reduced, rest_reduced, small_block],
        slot_sources,
        slot_rows,
        slot_kinds,
        kinds_used,
        slot_masks,
        jnp.asarray(small_rates)[None, :],
        master,
        moment_one,
        moment_two,
    )
    return (
        block_out,
        input_grad,
        grad_slots,
        master_new,
        moment_new,
        second_new,
        weights_low,
    )


def solution(mesh):
    return jax.shard_map(
        on_device,
        mesh=mesh,
        in_specs=(
            P("seq", "head"),
            P("seq", "head"),
            P(),
            P("seq", "head"),
            P("seq", "head"),
            P("seq", "head"),
        ),
        out_specs=(
            P("seq", "head"),
            P("seq", "head"),
            P("seq", "head"),
            P("seq", "head"),
            P("seq", "head"),
            P("seq", "head"),
            P("seq", "head"),
        ),
        check_vma=False,
    )
```

```python
import jax
import jax.numpy as jnp
import numpy as np
from jax import lax
from jax.experimental import pallas as pl
from jax.experimental.pallas import tpu as pltpu
from jax.sharding import PartitionSpec as P

D = 2048
HEADS = 16
DK = 128
DV = 256
FF = 5632
KCONV = 4
STEP = 5


EXACT_ARITHMETIC = lax.Precision.HIGHEST
NORM_EPSILON = 1e-06
UNIT_EPSILON = 1e-06
HEAD_EPSILON = 1e-05
ADAM_EPSILON = 1e-08
BETA_ONE = 0.5
BETA_TWO = 0.5
WEIGHT_DECAY = 0.1
PAD_RATE = 0.1


def shifted(block, axis, distance):
    devices = range(lax.axis_size(axis))
    route = [(i - distance, i) for i in devices if i - distance in devices]
    return lax.ppermute(block, axis, route)


def shard_layout(local_heads, head_parts):
    return [
        ("wq", D, local_heads * DK, 0.02),
        ("wk", D, local_heads * DK, 0.02),
        ("wv", D, local_heads * DV, 0.02),
        ("wg", D, local_heads * DV, 0.02),
        ("wo", local_heads * DV, D, 0.015),
        ("wgate", D, FF // head_parts, 0.02),
        ("wup", D, FF // head_parts, 0.02),
        ("wdown", FF // head_parts, D, 0.012),
        ("cq", KCONV, local_heads * DK, 0.4),
        ("ck", KCONV, local_heads * DK, 0.4),
        ("cv", KCONV, local_heads * DV, 0.4),
        ("wab", D, 2 * local_heads, 0.04),
        ("alog", 1, local_heads, 0.5),
        ("dtbias", 1, local_heads, 0.5),
        ("gainone", 1, D // head_parts, 0.1),
        ("gaintwo", 1, D // head_parts, 0.1),
        ("wnorm", 1, DV // head_parts, 0.1),
    ]


def piece_table(owners, seq_parts, capacity):
    piece_count = owners.shape[0]
    devices = jnp.arange(seq_parts, dtype=jnp.int32)
    onehot = (owners[:, None] == devices[None, :]).astype(jnp.int32)
    before = jnp.cumsum(onehot, axis=0) - onehot
    rank_within = jnp.sum(before * onehot, axis=1)
    slot_of_piece = owners * capacity + rank_within
    matches = slot_of_piece[None, :] == jnp.arange(seq_parts * capacity, dtype=jnp.int32)[:, None]
    present = jnp.any(matches, axis=1)
    piece_of_slot = jnp.sum(
        matches.astype(jnp.int32) * jnp.arange(piece_count, dtype=jnp.int32)[None, :], axis=1
    )
    return (slot_of_piece, piece_of_slot, present)


def unpack(flat_weights, segments_list):
    by_name = {}
    offset_now = 0
    for seg_name, row_count, col_count, seg_rate in segments_list:
        by_name[seg_name] = flat_weights[offset_now : offset_now + row_count * col_count].reshape(
            row_count, col_count
        )
        offset_now += row_count * col_count
    return (by_name, offset_now)


def rate_parts(segments_list, piece_count, piece_size):
    piece_rates = np.full(piece_count, PAD_RATE, np.float32)
    small_rates = np.full(piece_size, PAD_RATE, np.float32)
    offset_now = 0
    big_total = (piece_count - 1) * piece_size
    for seg_name, row_count, col_count, seg_rate in segments_list:
        seg_size = row_count * col_count
        if offset_now < big_total:
            piece_rates[offset_now // piece_size : (offset_now + seg_size) // piece_size] = seg_rate
        else:
            small_rates[offset_now - big_total : offset_now - big_total + seg_size] = seg_rate
        offset_now += seg_size
    return (piece_rates, small_rates)


HEADS_A_STEP = 1


def product(left, right, left_axis, right_axis, exact=False):
    def dot(a, b):
        return lax.dot_general(
            a,
            b,
            (((left_axis,), (right_axis,)), ((), ())),
            preferred_element_type=jnp.float32,
        )

    left_low, right_low = left.astype(jnp.bfloat16), right.astype(jnp.bfloat16)
    if not exact:
        return dot(left_low, right_low)
    left_rest = (left - left_low.astype(jnp.float32)).astype(jnp.bfloat16)
    right_rest = (right - right_low.astype(jnp.float32)).astype(jnp.bfloat16)
    return dot(left_low, right_low) + (dot(left_low, right_rest) + dot(left_rest, right_low))


def take_lane(wide, lane):
    lanes = lax.broadcasted_iota(jnp.int32, wide.shape, 1)
    return jnp.sum(jnp.where(lanes == lane, wide, 0.0), axis=1, keepdims=True)


def put_lane(column, lane):
    lanes = lax.broadcasted_iota(jnp.int32, (column.shape[0], 128), 1)
    return jnp.where(lanes == lane, column, 0.0)


def to_row(column, diagonal):
    return jnp.sum(jnp.where(diagonal, column, 0.0), axis=0, keepdims=True)


def convolved(extended, block_ref, rim_ref, taps_ref, columns):
    row_count = block_ref.shape[0]
    extended[0:8, :] = rim_ref[:, columns]
    extended[8 : 8 + row_count, :] = block_ref[:, columns]
    first = 8 - (KCONV - 1)
    running = taps_ref[0:1, columns] * extended[first : first + row_count, :]
    for tap in range(1, KCONV):
        running = running + taps_ref[tap : tap + 1, columns] * extended[
            first + tap : first + tap + row_count, :
        ]
    return running


def decay_terms(head, local_heads, decay_ref, scalars_ref):
    row_count = decay_ref.shape[0]
    shape = (row_count, row_count)
    row_ids = lax.broadcasted_iota(jnp.int32, shape, 0)
    column_ids = lax.broadcasted_iota(jnp.int32, shape, 1)
    decay_in = take_lane(decay_ref[...], head) + take_lane(scalars_ref[1:2, :], head)
    rate = -jnp.exp(take_lane(scalars_ref[0:1, :], head))
    soft = jnp.maximum(decay_in, 0.0) + jnp.log1p(jnp.exp(-jnp.abs(decay_in)))
    logs = rate * soft
    beta = jax.nn.sigmoid(take_lane(decay_ref[...], head + local_heads))
    diagonal = row_ids == column_ids
    logs_row = to_row(logs, diagonal)
    upto = row_ids >= column_ids
    sums = jnp.sum(jnp.where(upto, logs_row, 0.0), axis=1, keepdims=True)
    sums_row = to_row(sums, diagonal)
    within = jnp.exp(jnp.where(upto, sums - sums_row, -1e30))
    return decay_in, rate, logs, beta, sums, within, row_ids, column_ids


def unit_rows(rows):
    scale = lax.rsqrt(jnp.sum(rows * rows, axis=-1, keepdims=True) + UNIT_EPSILON)
    return rows * scale, scale


def mixer_specs(local_heads, row_count):
    def spec(rows, width, first):
        return pl.BlockSpec((rows, width), lambda h, first=first // width: (0, first + h))

    def three(rows):
        return [
            spec(rows, HEADS_A_STEP * DK, 0),
            spec(rows, HEADS_A_STEP * DK, local_heads * DK),
            spec(rows, HEADS_A_STEP * DV, 2 * local_heads * DK),
        ]

    whole = pl.BlockSpec((row_count, 128), lambda h: (0, 0))
    scalars = pl.BlockSpec((8, 128), lambda h: (0, 0))
    return three, whole, scalars


def per_head(*shape):
    return pl.BlockSpec((HEADS_A_STEP,) + shape, lambda h: (h,) + (0,) * len(shape))


def head_columns(sub):
    return slice(DK * sub, DK * sub + DK), slice(DV * sub, DV * sub + DV)


def mixer_local(local_heads, projected, rim, taps, decay_proj, scalars):
    row_count = projected.shape[0]
    three, whole, scalar_spec = mixer_specs(local_heads, row_count)

    def kernel(
        pq, pk, pv, rq, rk, rv, tq, tk, tv, decay_ref, scalars_ref,
        solve_ref, fresh_ref, wy_ref, reach_ref, zero_ref, handoff_ref, ext_q, ext_k, ext_v,
    ):
        for sub in range(HEADS_A_STEP):
            head = pl.program_id(0) * HEADS_A_STEP + sub
            narrow, wide = head_columns(sub)
            queries = unit_rows(jax.nn.silu(convolved(ext_q.at[sub], pq, rq, tq, narrow)))[0] * DK ** (-0.5)
            key_rows = unit_rows(jax.nn.silu(convolved(ext_k.at[sub], pk, rk, tk, narrow)))[0]
            values = jax.nn.silu(convolved(ext_v.at[sub], pv, rv, tv, wide))
            decay_in, rate, logs, beta, sums, within, row_ids, column_ids = decay_terms(
                head, local_heads, decay_ref, scalars_ref
            )
            gram = product(key_rows, key_rows, 1, 1, True)
            system = jnp.where(row_ids > column_ids, beta * gram * within, 0.0)
            solve = jnp.where(row_ids == column_ids, 1.0, 0.0)
            size = 1
            while size < row_count:
                lower = (row_ids // (2 * size) == column_ids // (2 * size)) & (
                    row_ids // size != column_ids // size
                )
                part = jnp.where(lower, system, 0.0)
                if size == 1:
                    solve = solve - part
                else:
                    solve = solve - product(solve, product(part, solve, 1, 0), 1, 0)
                size *= 2
            unit = jnp.where(row_ids == column_ids, 1.0, 0.0)
            remainder = (unit - solve) - product(system, solve, 1, 0, True)
            solve = solve + product(solve, remainder, 1, 0)
            grown = jnp.exp(sums)
            fresh = product(solve, beta * values, 1, 0, True)
            wy_keys = product(solve, (beta * grown) * key_rows, 1, 0, True)
            attention = product(queries, key_rows, 1, 1) * within
            last = sums[row_count - 1 : row_count, :]
            tail_keys = jnp.exp(last - sums) * key_rows
            eye = lax.broadcasted_iota(jnp.int32, (DK, DK), 0) == lax.broadcasted_iota(
                jnp.int32, (DK, DK), 1
            )
            solve_ref[sub] = solve
            fresh_ref[sub] = fresh
            wy_ref[sub] = wy_keys
            reach_ref[sub] = grown * queries - product(attention, wy_keys, 1, 0)
            zero_ref[sub] = product(attention, fresh, 1, 0)
            handoff_ref[sub, :, :DK] = (
                jnp.where(eye, jnp.exp(last), 0.0) - product(tail_keys, wy_keys, 0, 0)
            ).astype(jnp.bfloat16)
            handoff_ref[sub, :, DK:] = product(tail_keys, fresh, 0, 0).astype(jnp.bfloat16)

    def out(*shape, kind=jnp.float32):
        return jax.ShapeDtypeStruct((local_heads,) + shape, kind)

    return pl.pallas_call(
        kernel,
        grid=(local_heads // HEADS_A_STEP,),
        in_specs=three(row_count) + three(8) + three(8) + [whole, scalar_spec],
        out_specs=[
            per_head(row_count, row_count),
            per_head(row_count, DV),
            per_head(row_count, DK),
            per_head(row_count, DK),
            per_head(row_count, DV),
            per_head(DK, DK + DV),
        ],
        out_shape=[
            out(row_count, row_count),
            out(row_count, DV),
            out(row_count, DK),
            out(row_count, DK),
            out(row_count, DV),
            out(DK, DK + DV, kind=jnp.bfloat16),
        ],
        scratch_shapes=[
            pltpu.VMEM((HEADS_A_STEP, row_count + 8, DK), jnp.float32),
            pltpu.VMEM((HEADS_A_STEP, row_count + 8, DK), jnp.float32),
            pltpu.VMEM((HEADS_A_STEP, row_count + 8, DV), jnp.float32),
        ],
        compiler_params=params(),
    )(*([projected] * 3), *([rim] * 3), *([taps] * 3), decay_proj, scalars)


def mixer_out(local_heads, my_index, base, handoffs, reach, zero_out, projected, norm_gain):
    row_count = projected.shape[0]
    gate_first = local_heads * (2 * DK + DV)

    def kernel(index_ref, base_ref, handoffs_ref, reach_ref, zero_ref, gate_ref, norm_ref, state_ref, out_ref, gated_ref):
        state_ref[...] = jnp.zeros_like(state_ref)

        def advance(j, carry):
            for h in range(local_heads):
                block = handoffs_ref[j ^ base_ref[0], h]
                state_ref[h] = product(
                    block[:, :DK].astype(jnp.float32), state_ref[h], 1, 0
                ) + block[:, DK:].astype(jnp.float32)
            return carry

        lax.fori_loop(0, index_ref[0], advance, 0)
        for h in range(local_heads):
            columns = slice(DV * h, DV * h + DV)
            out = zero_ref[h] + product(reach_ref[h], state_ref[h], 1, 0)
            normed = out * lax.rsqrt(jnp.mean(out * out, axis=-1, keepdims=True) + HEAD_EPSILON)
            out_ref[:, columns] = out
            gated_ref[:, columns] = (
                normed * norm_ref[...] * jax.nn.silu(gate_ref[:, columns])
            ).astype(jnp.bfloat16)

    vmem = pl.BlockSpec(memory_space=pltpu.VMEM)
    width = local_heads * DV
    return pl.pallas_call(
        kernel,
        grid=(1,),
        in_specs=[
            pl.BlockSpec(memory_space=pltpu.SMEM),
            pl.BlockSpec(memory_space=pltpu.SMEM),
            vmem,
            vmem,
            vmem,
            pl.BlockSpec((row_count, width), lambda i: (0, gate_first // width)),
            vmem,
        ],
        out_specs=[vmem, vmem, vmem],
        out_shape=[
            jax.ShapeDtypeStruct((local_heads, DK, DV), jnp.float32),
            jax.ShapeDtypeStruct((row_count, width), jnp.float32),
            jax.ShapeDtypeStruct((row_count, width), jnp.bfloat16),
        ],
        compiler_params=params(),
    )(my_index, base, handoffs, reach, zero_out, projected, norm_gain)


def mixer_gate_back(local_heads, d_gated, recurred, projected, norm_gain, reach):
    row_count = projected.shape[0]
    gate_first = local_heads * (2 * DK + DV) // DV

    def kernel(d_gated_ref, out_ref, gate_ref, norm_ref, reach_ref, d_out_ref, d_gate_ref, d_norm_ref, d_state_ref):
        out, gate, norm_row, d_gated_now = out_ref[...], gate_ref[...], norm_ref[...], d_gated_ref[...]
        scale = lax.rsqrt(jnp.mean(out * out, axis=-1, keepdims=True) + HEAD_EPSILON)
        normed = out * scale
        logistic = jax.nn.sigmoid(gate)
        silu = gate * logistic
        d_norm = jnp.sum(d_gated_now * normed * silu, axis=0, keepdims=True)

        @pl.when(pl.program_id(0) == 0)
        def _():
            d_norm_ref[...] = jnp.zeros_like(d_norm_ref)

        d_norm_ref[0:1, :] = d_norm_ref[0:1, :] + d_norm
        d_gate_ref[...] = (
            d_gated_now * normed * norm_row * logistic * (1.0 + gate * (1.0 - logistic))
        ).astype(jnp.bfloat16)
        d_normed = d_gated_now * norm_row * silu
        d_out = scale * d_normed - (scale * scale * scale) * out * jnp.mean(
            d_normed * out, axis=-1, keepdims=True
        )
        d_out_ref[...] = d_out
        d_state_ref[0] = product(reach_ref[0], d_out, 0, 0).astype(jnp.bfloat16)

    width = local_heads * DV
    block = pl.BlockSpec((row_count, DV), lambda h: (0, h))
    return pl.pallas_call(
        kernel,
        grid=(local_heads,),
        in_specs=[
            block,
            block,
            pl.BlockSpec((row_count, DV), lambda h: (0, gate_first + h)),
            pl.BlockSpec((1, DV), lambda h: (0, 0)),
            pl.BlockSpec((1, row_count, DK), lambda h: (h, 0, 0)),
        ],
        out_specs=[
            block,
            block,
            pl.BlockSpec((8, DV), lambda h: (0, 0)),
            pl.BlockSpec((1, DK, DV), lambda h: (h, 0, 0)),
        ],
        out_shape=[
            jax.ShapeDtypeStruct((row_count, width), jnp.float32),
            jax.ShapeDtypeStruct((row_count, width), jnp.bfloat16),
            jax.ShapeDtypeStruct((8, DV), jnp.float32),
            jax.ShapeDtypeStruct((local_heads, DK, DV), jnp.bfloat16),
        ],
        compiler_params=params(),
    )(d_gated, recurred, projected, norm_gain, reach)


def relay_back(local_heads, my_index, base, handoffs, d_enterings):
    devices = handoffs.shape[0]

    def kernel(index_ref, base_ref, handoffs_ref, d_ref, state_ref):
        state_ref[...] = jnp.zeros_like(state_ref)

        def advance(step, carry):
            j = (devices - 1 - step) ^ base_ref[0]
            for h in range(local_heads):
                state_ref[h] = product(
                    handoffs_ref[j, h, :, :DK].astype(jnp.float32), state_ref[h], 0, 0
                ) + d_ref[j, h].astype(jnp.float32)
            return carry

        lax.fori_loop(0, devices - 1 - index_ref[0], advance, 0)

    vmem = pl.BlockSpec(memory_space=pltpu.VMEM)
    return pl.pallas_call(
        kernel,
        in_specs=[pl.BlockSpec(memory_space=pltpu.SMEM)] * 2 + [vmem, vmem],
        out_specs=vmem,
        out_shape=jax.ShapeDtypeStruct((local_heads, DK, DV), jnp.float32),
        compiler_params=params(),
    )(my_index, base, handoffs, d_enterings)


def conv_back(
    d_pre, extended, taps_ref, padded, d_block_ref, d_tail_ref, d_rim_ref, d_taps_ref, columns
):
    row_count = d_pre.shape[0]
    first = 8 - (KCONV - 1)
    padded[0:8, :] = jnp.zeros((8, d_pre.shape[1]), jnp.float32)
    padded[8 : 8 + row_count, :] = d_pre
    padded[8 + row_count : 16 + row_count, :] = jnp.zeros((8, d_pre.shape[1]), jnp.float32)
    total = None
    d_taps_ref[:, columns] = jnp.zeros((8, d_pre.shape[1]), jnp.float32)
    for tap in range(KCONV):
        start = KCONV - 1 - tap
        term = taps_ref[tap : tap + 1, columns] * padded[start : start + row_count + 8, :]
        total = term if total is None else total + term
        d_taps_ref[tap : tap + 1, columns] = jnp.sum(
            d_pre * extended[first + tap : first + tap + row_count, :], axis=0, keepdims=True
        )
    d_rim_ref[:, columns] = total[0:8, :]
    d_block_ref[:, columns] = total[8:, :].astype(jnp.bfloat16)
    d_tail_ref[:, columns] = total[row_count:, :]


def mixer_back(
    local_heads, projected, rim, taps, decay_proj, scalars,
    solve, fresh, wy_keys, entering_state, d_recurred, d_leaving,
):
    row_count = projected.shape[0]
    three, whole, scalar_spec = mixer_specs(local_heads, row_count)

    def kernel(
        pq, pk, pv, rq, rk, rv, tq, tk, tv, decay_ref, scalars_ref,
        solve_ref, fresh_ref, wy_ref, enter_ref, d_out_ref, d_leave_ref,
        dq_ref, dk_ref, dv_ref, tail_q, tail_k, tail_v, rim_q, rim_k, rim_v,
        taps_q, taps_k, taps_v, d_decay_ref, d_scalars_ref,
        ext_q, ext_k, ext_v, pad_q, pad_k, pad_v,
    ):
        @pl.when(pl.program_id(0) == 0)
        def _():
            d_decay_ref[...] = jnp.zeros_like(d_decay_ref)
            d_scalars_ref[...] = jnp.zeros_like(d_scalars_ref)

        for sub in range(HEADS_A_STEP):
            head = pl.program_id(0) * HEADS_A_STEP + sub
            narrow, wide = head_columns(sub)
            pre_q = convolved(ext_q.at[sub], pq, rq, tq, narrow)
            pre_k = convolved(ext_k.at[sub], pk, rk, tk, narrow)
            pre_v = convolved(ext_v.at[sub], pv, rv, tv, wide)
            conv_q, conv_k = jax.nn.silu(pre_q), jax.nn.silu(pre_k)
            unit_q, scale_q = unit_rows(conv_q)
            queries = unit_q * DK ** (-0.5)
            key_rows, scale_k = unit_rows(conv_k)
            values = jax.nn.silu(pre_v)
            decay_in, rate, logs, beta, sums, within, row_ids, column_ids = decay_terms(
                head, local_heads, decay_ref, scalars_ref
            )
            strict = row_ids > column_ids
            grown = jnp.exp(sums)
            last = sums[row_count - 1 : row_count, :]
            tail = jnp.exp(last - sums)
            tail_keys = tail * key_rows
            gram = product(key_rows, key_rows, 1, 1, True)
            scores = jnp.where(strict, gram * within, 0.0)
            attention = product(queries, key_rows, 1, 1) * within
            enter, d_out, d_leave = enter_ref[sub], d_out_ref[:, wide], d_leave_ref[sub]
            update = fresh_ref[sub] - product(wy_ref[sub], enter, 1, 0)
            d_update = product(attention, d_out, 0, 0) + product(tail_keys, d_leave, 1, 0)
            d_right = product(solve_ref[sub], d_update, 0, 0, True)
            d_attention = product(d_out, update, 1, 1) * within
            d_system = -product(d_right, update, 1, 1)
            out_state = product(d_out, enter, 1, 1)
            right_state = product(d_right, enter, 1, 1)
            leave_update = product(update, d_leave, 1, 1)
            remainder = values - grown * product(key_rows, enter, 1, 0)
            d_values = beta * d_right
            d_beta = jnp.sum(d_right * remainder, axis=1, keepdims=True) + jnp.sum(
                d_system * scores, axis=1, keepdims=True
            )
            pair = beta * (d_system * scores)
            d_gram = jnp.where(strict, beta * d_system * within, 0.0)
            d_queries = grown * out_state + product(d_attention, key_rows, 1, 0)
            d_keys = (
                product(d_attention, queries, 0, 0)
                + product(d_gram, key_rows, 1, 0)
                + product(d_gram, key_rows, 0, 0)
                + tail * leave_update
                - (beta * grown) * right_state
            )
            both = pair + d_attention * product(queries, key_rows, 1, 1)
            tail_rows = jnp.sum(tail_keys * leave_update, axis=1, keepdims=True)
            diagonal = row_ids == column_ids
            columns = jnp.sum(both, axis=0, keepdims=True)
            d_sums = (
                jnp.sum(both, axis=1, keepdims=True)
                - jnp.sum(jnp.where(diagonal, columns, 0.0), axis=1, keepdims=True)
                + jnp.sum(out_state * (grown * queries), axis=1, keepdims=True)
                - jnp.sum(right_state * ((beta * grown) * key_rows), axis=1, keepdims=True)
                - tail_rows
            )
            d_last = jnp.exp(last) * jnp.sum(
                jnp.sum(d_leave * enter, axis=1, keepdims=True), axis=0, keepdims=True
            ) + jnp.sum(tail_rows, axis=0, keepdims=True)
            d_logs = d_last + jnp.sum(
                jnp.where(row_ids <= column_ids, to_row(d_sums, diagonal), 0.0), axis=1, keepdims=True
            )
            d_decay_in = d_logs * rate * jax.nn.sigmoid(decay_in)
            d_beta_in = d_beta * beta * (1.0 - beta)
            d_decay_ref[...] = (
                d_decay_ref[...]
                + put_lane(d_decay_in, head)
                + put_lane(d_beta_in, head + local_heads)
            )
            d_rate = jnp.sum(d_logs * logs, axis=0, keepdims=True)
            d_bias = jnp.sum(d_decay_in, axis=0, keepdims=True)
            d_scalars_ref[0:1, :] = d_scalars_ref[0:1, :] + put_lane(d_rate, head)
            d_scalars_ref[1:2, :] = d_scalars_ref[1:2, :] + put_lane(d_bias, head)

            def unit_back(d_unit, unit, scale):
                return scale * (d_unit - unit * jnp.sum(unit * d_unit, axis=1, keepdims=True))

            def silu_back(d_act, pre):
                logistic = jax.nn.sigmoid(pre)
                return d_act * logistic * (1.0 + pre * (1.0 - logistic))

            d_pre_q = silu_back(unit_back(d_queries * DK ** (-0.5), unit_q, scale_q), pre_q)
            conv_back(d_pre_q, ext_q.at[sub], tq, pad_q.at[sub], dq_ref, tail_q, rim_q, taps_q, narrow)
            d_pre_k = silu_back(unit_back(d_keys, key_rows, scale_k), pre_k)
            conv_back(d_pre_k, ext_k.at[sub], tk, pad_k.at[sub], dk_ref, tail_k, rim_k, taps_k, narrow)
            conv_back(
                silu_back(d_values, pre_v), ext_v.at[sub], tv, pad_v.at[sub],
                dv_ref, tail_v, rim_v, taps_v, wide,
            )

    def blocks(rows):
        return [
            pl.BlockSpec((rows, HEADS_A_STEP * width), lambda h: (0, h)) for width in (DK, DK, DV)
        ]

    def shapes(rows, kind):
        return [
            jax.ShapeDtypeStruct((rows, local_heads * width), kind) for width in (DK, DK, DV)
        ]

    outs = pl.pallas_call(
        kernel,
        grid=(local_heads // HEADS_A_STEP,),
        in_specs=three(row_count)
        + three(8)
        + three(8)
        + [
            whole,
            scalar_spec,
            per_head(row_count, row_count),
            per_head(row_count, DV),
            per_head(row_count, DK),
            per_head(DK, DV),
            pl.BlockSpec((row_count, HEADS_A_STEP * DV), lambda h: (0, h)),
            per_head(DK, DV),
        ],
        out_specs=blocks(row_count) + blocks(8) * 3 + [whole, scalar_spec],
        out_shape=shapes(row_count, jnp.bfloat16)
        + shapes(8, jnp.float32) * 3
        + [
            jax.ShapeDtypeStruct((row_count, 128), jnp.float32),
            jax.ShapeDtypeStruct((8, 128), jnp.float32),
        ],
        scratch_shapes=[
            pltpu.VMEM((HEADS_A_STEP, row_count + 8, DK), jnp.float32),
            pltpu.VMEM((HEADS_A_STEP, row_count + 8, DK), jnp.float32),
            pltpu.VMEM((HEADS_A_STEP, row_count + 8, DV), jnp.float32),
            pltpu.VMEM((HEADS_A_STEP, row_count + 16, DK), jnp.float32),
            pltpu.VMEM((HEADS_A_STEP, row_count + 16, DK), jnp.float32),
            pltpu.VMEM((HEADS_A_STEP, row_count + 16, DV), jnp.float32),
        ],
        compiler_params=params(),
    )(
        *([projected] * 3), *([rim] * 3), *([taps] * 3), decay_proj, scalars,
        solve, fresh, wy_keys, entering_state, d_recurred, d_leaving,
    )
    joined = [jnp.concatenate(outs[3 * i : 3 * i + 3], axis=1) for i in range(4)]
    return (*joined, outs[12], outs[13])


LANES = 128
CHUNK = 32768
TILE = 16
CAPACITY_UNIT = 44
FIRST_GATHER = 24
FIRST_REDUCE = 16
SECOND_REDUCE = 24
SECOND_GATHER = 16
TABLE = 1 << 16
VMEM_LIMIT = 48 * 1024 * 1024


def params(**kwargs):
    return pltpu.CompilerParams(vmem_limit_bytes=VMEM_LIMIT, **kwargs)


def piece_kinds(segments_list, piece_count, piece_size):
    kinds = np.ones(piece_count, np.int32)
    offset_now = 0
    for seg_name, row_count, col_count, seg_rate in segments_list:
        if offset_now >= (piece_count - 1) * piece_size:
            break
        tiles = col_count // LANES
        if tiles in (2, 4, 8, 16):
            first = offset_now // piece_size
            kinds[first : first + row_count * col_count // piece_size] = tiles
        offset_now += row_count * col_count
    return kinds


def pack_blocks(master, slot_kinds, kinds_used, first_slot, slot_count):
    piece_size = master.shape[1]
    chunks = piece_size // CHUNK
    rows = CHUNK // LANES
    first_block = first_slot // 8
    slot_blocks = pl.cdiv(slot_count, 8)

    def kernel(kinds_ref, master_ref, out_ref, scratch):
        first = (first_block + pl.program_id(0)) * 8
        for j in range(rows):
            scratch[8 * j : 8 * j + 8, :] = master_ref[:, LANES * j : LANES * j + LANES]
        for s in range(8):
            kind_now = kinds_ref[first + s]
            for kind in kinds_used:

                @pl.when(kind_now == kind)
                def _():
                    for tile in range(rows // TILE):
                        row_tile, column = divmod(tile, kind)
                        start = (row_tile * TILE * kind + column) * 8 + s
                        out_ref[s, TILE * tile : TILE * tile + TILE, :] = scratch[
                            pl.ds(start, TILE, stride=8 * kind), :
                        ].astype(jnp.bfloat16)

    return pl.pallas_call(
        kernel,
        grid_spec=pltpu.PrefetchScalarGridSpec(
            num_scalar_prefetch=1,
            grid=(slot_blocks, chunks),
            in_specs=[pl.BlockSpec((8, CHUNK), lambda i, j, kinds: (first_block + i, j))],
            out_specs=pl.BlockSpec((8, rows, LANES), lambda i, j, kinds: (i, j, 0)),
            scratch_shapes=[pltpu.VMEM((8 * rows, LANES), jnp.float32)],
        ),
        out_shape=jax.ShapeDtypeStruct((slot_count, piece_size // LANES, LANES), jnp.bfloat16),
        compiler_params=params(),
    )(slot_kinds, master)


def reserve(shape, kind):
    def kernel(out_ref):
        pass

    return pl.pallas_call(
        kernel,
        out_specs=pl.BlockSpec(memory_space=pl.ANY),
        out_shape=jax.ShapeDtypeStruct(shape, kind),
        compiler_params=params(),
    )()


def assemble(tables, matrices, step_rows, rows_in=None):
    piece_rows = tables[0].shape[1]
    plans = []
    first_block, first_column = 0, 0
    for positions, col_count in matrices:
        tiles = col_count // LANES
        blocks = step_rows * tiles // piece_rows
        plans.append((first_block, first_column, tiles, blocks))
        first_block += blocks
        first_column += col_count
    blocks_a_step, width = first_block, first_column
    steps = matrices[0][0].shape[0] // plans[0][3]
    order = jnp.concatenate(
        [
            positions.reshape(steps, plan[3])
            for (positions, col_count), plan in zip(matrices, plans)
        ],
        axis=1,
    ).reshape(-1)
    uneven = [plan for plan in plans if piece_rows * plan[3] != step_rows * plan[2] or plan[2] not in (2, 4, 8, 16)]
    multiply = rows_in is not None

    def kernel(order_ref, *refs):
        if multiply:
            rows_ref, refs = refs[0], refs[1:]
        table_refs, refs = refs[: len(tables)], refs[len(tables) :]
        out_ref, refs = refs[0], refs[1:]
        if multiply:
            product_ref, refs = refs[0], refs[1:]
        buffer, sem, scratch = refs
        g = pl.program_id(0)
        slot = lax.rem(g, 2)

        def start(step, which):
            def one(j, carry):
                position = order_ref[step * blocks_a_step + j]
                for number, table_ref in enumerate(table_refs):

                    @pl.when(position // TABLE == number)
                    def _():
                        pltpu.make_async_copy(
                            table_ref.at[lax.rem(position, TABLE)],
                            buffer.at[which, j],
                            sem.at[which],
                        ).start()

                return carry

            lax.fori_loop(0, blocks_a_step, one, 0)

        @pl.when(g == 0)
        def _():
            start(0, 0)

        @pl.when(g + 1 < steps)
        def _():
            start(g + 1, 1 - slot)

        pltpu.make_async_copy(buffer.at[slot], buffer.at[slot], sem.at[slot]).wait()
        for plan in plans:
            first, left, tiles, blocks = plan
            if plan in uneven:
                for j in range(blocks):
                    scratch[piece_rows * j : piece_rows * j + piece_rows, :] = buffer[
                        slot, first + j
                    ].astype(jnp.float32)
                for c in range(tiles):
                    out_ref[:, left + LANES * c : left + LANES * c + LANES] = scratch[
                        pl.ds(c, step_rows, stride=tiles), :
                    ].astype(jnp.bfloat16)
                continue
            for j in range(blocks):
                for tile in range(piece_rows // TILE):
                    row_tile, column = divmod(tile, tiles)
                    row = piece_rows // tiles * j + TILE * row_tile
                    column = left + LANES * column
                    out_ref[row : row + TILE, column : column + LANES] = buffer[
                        slot, first + j, TILE * tile : TILE * tile + TILE, :
                    ]
        if multiply:
            part = jnp.dot(rows_ref[...], out_ref[...], preferred_element_type=jnp.float32)

            @pl.when(g == 0)
            def _():
                product_ref[...] = part

            @pl.when(g > 0)
            def _():
                product_ref[...] = product_ref[...] + part

    anywhere = pl.BlockSpec(memory_space=pl.ANY)
    in_specs = [anywhere for table in tables]
    operands = list(tables)
    out_specs = [pl.BlockSpec((step_rows, width), lambda g, order: (g, 0))]
    out_shape = [jax.ShapeDtypeStruct((steps * step_rows, width), jnp.bfloat16)]
    if multiply:
        row_count = rows_in.shape[0]
        in_specs.insert(0, pl.BlockSpec((row_count, step_rows), lambda g, order: (0, g)))
        operands.insert(0, rows_in)
        out_specs.append(pl.BlockSpec((row_count, width), lambda g, order: (0, 0)))
        out_shape.append(jax.ShapeDtypeStruct((row_count, width), jnp.float32))
    scratch_rows = max([plan[3] * piece_rows for plan in uneven], default=8)
    return pl.pallas_call(
        kernel,
        grid_spec=pltpu.PrefetchScalarGridSpec(
            num_scalar_prefetch=1,
            grid=(steps,),
            in_specs=in_specs,
            out_specs=out_specs,
            scratch_shapes=[
                pltpu.VMEM((2, blocks_a_step, piece_rows, LANES), jnp.bfloat16),
                pltpu.SemaphoreType.DMA((2,)),
                pltpu.VMEM((scratch_rows, LANES), jnp.float32),
            ],
        ),
        out_shape=out_shape,
        cost_estimate=pl.CostEstimate(
            flops=2 * steps * step_rows * width * (rows_in.shape[0] if multiply else 0),
            bytes_accessed=4 * steps * step_rows * width,
            transcendentals=0,
        ),
        compiler_params=params(),
    )(order, *operands)


def spread_products(my_part, parts, pairs):
    row_count = pairs[0][0].shape[0]
    total = pairs[0][1].shape[0 if pairs[0][2] else 1]
    width = total // parts

    def kernel(part_ref, *refs):
        ins, outs = refs[: 2 * len(pairs)], refs[2 * len(pairs) :]
        for m in range(parts):
            first = pl.multiple_of((part_ref[0] ^ m) * width, width)
            result = None
            for i, (left, right, transposed) in enumerate(pairs):
                if transposed:
                    block, axis = ins[2 * i + 1][pl.ds(first, width), :], 1
                else:
                    block, axis = ins[2 * i + 1][:, pl.ds(first, width)], 0
                part = lax.dot_general(
                    ins[2 * i][...],
                    block,
                    (((1,), (axis,)), ((), ())),
                    preferred_element_type=jnp.float32,
                )
                result = part if result is None else result + part
            outs[m][...] = result.astype(jnp.bfloat16)

    vmem = pl.BlockSpec(memory_space=pltpu.VMEM)
    flat = [array for left, right, transposed in pairs for array in (left, right)]
    return pl.pallas_call(
        kernel,
        in_specs=[pl.BlockSpec(memory_space=pltpu.SMEM)] + [vmem] * len(flat),
        out_specs=[vmem] * parts,
        out_shape=[jax.ShapeDtypeStruct((row_count, width), jnp.bfloat16)] * parts,
        cost_estimate=pl.CostEstimate(
            flops=2 * row_count * sum(pair[1].size for pair in pairs),
            bytes_accessed=2 * sum(pair[1].size for pair in pairs),
            transcendentals=0,
        ),
        compiler_params=params(),
    )(my_part, *flat)


def exchange(blocks, axis):
    devices = lax.axis_size(axis)
    return [blocks[0]] + [
        lax.ppermute(blocks[m], axis, [(i, i ^ m) for i in range(devices)])
        for m in range(1, devices)
    ]


def total_of(blocks):
    total = blocks[0].astype(jnp.float32)
    for block in blocks[1:]:
        total = total + block.astype(jnp.float32)
    return total


def sum_over(block, axis):
    return total_of(exchange([block] * lax.axis_size(axis), axis))


def in_order(blocks, my_part, axis):
    stacked = jnp.stack(blocks)
    return jnp.concatenate(
        [
            lax.dynamic_index_in_dim(stacked, my_part ^ j, 0, keepdims=False)
            for j in range(len(blocks))
        ],
        axis=axis,
    )


def gather_states(block):
    devices = lax.axis_size("seq")
    if devices != 8:
        return lax.all_gather(block, "seq", axis=0, tiled=False), jnp.zeros((1,), jnp.int32)

    def moved(array, mask):
        return lax.ppermute(array, "seq", [(i, i ^ mask) for i in range(devices)])

    chips = [block] + [moved(block, mask) for mask in (2, 4, 6)]
    pairs = [(chip, moved(chip, 1)) for chip in chips]
    rows = jnp.stack([array for pair in pairs for array in pair])
    return rows, lax.axis_index("seq").astype(jnp.int32).reshape(1)


def weight_grad_blocks(left_t, right, right_block, col_count, positions, tables, blocks_a_step):
    row_total, depth = left_t.shape
    tiles = col_count // LANES
    piece_rows = 512
    even = tiles in (2, 4, 8, 16)
    step_rows = blocks_a_step * piece_rows // tiles
    steps = row_total // step_rows

    def kernel(positions_ref, left_ref, right_ref, *refs):
        table_refs = refs[len(tables) : 2 * len(tables)]
        product, staged, sem = refs[2 * len(tables) :]
        g = pl.program_id(0)
        slot = lax.rem(g, 2)

        def settle(which):
            pltpu.make_async_copy(staged.at[which], staged.at[which], sem.at[which]).wait()

        @pl.when(g >= 2)
        def _():
            settle(slot)

        left = left_ref[...]
        if even:
            product[...] = jnp.dot(left, right_ref[...], preferred_element_type=jnp.float32)
            for tile in range(step_rows // TILE * tiles):
                row_tile, column = divmod(tile, tiles)
                block, row = divmod(TILE * tile, piece_rows)
                staged[slot, block, row : row + TILE, :] = product[
                    TILE * row_tile : TILE * row_tile + TILE, LANES * column : LANES * column + LANES
                ].astype(jnp.bfloat16)
        else:
            for c in range(0, tiles, 2):
                width = min(2, tiles - c)
                part = jnp.dot(
                    left,
                    right_ref[:, LANES * c : LANES * (c + width)],
                    preferred_element_type=jnp.float32,
                )
                for w in range(width):
                    product[pl.ds(c + w, step_rows, stride=tiles), :] = part[
                        :, LANES * w : LANES * w + LANES
                    ]
            for block in range(blocks_a_step):
                staged[slot, block] = product[
                    piece_rows * block : piece_rows * block + piece_rows, :
                ].astype(jnp.bfloat16)
        for block in range(blocks_a_step):
            position = positions_ref[g * blocks_a_step + block]

            for number, table_ref in enumerate(table_refs):

                @pl.when(position // TABLE == number)
                def _():
                    pltpu.make_async_copy(
                        staged.at[slot, block],
                        table_ref.at[lax.rem(position, TABLE)],
                        sem.at[slot],
                    ).start()

        @pl.when(g == steps - 1)
        def _():
            settle(slot)
            if steps > 1:
                settle(1 - slot)

    anywhere = pl.BlockSpec(memory_space=pl.ANY)
    in_specs = [
        pl.BlockSpec((step_rows, depth), lambda g, positions: (g, 0)),
        pl.BlockSpec((depth, col_count), lambda g, positions: (0, right_block)),
    ] + [anywhere for table in tables]
    product_shape = (step_rows, col_count) if even else (step_rows * tiles, LANES)
    return pl.pallas_call(
        kernel,
        grid_spec=pltpu.PrefetchScalarGridSpec(
            num_scalar_prefetch=1,
            grid=(steps,),
            in_specs=in_specs,
            out_specs=[anywhere for table in tables],
            scratch_shapes=[
                pltpu.VMEM(product_shape, jnp.float32),
                pltpu.VMEM((2, blocks_a_step, piece_rows, LANES), jnp.bfloat16),
                pltpu.SemaphoreType.DMA((2,)),
            ],
        ),
        out_shape=[jax.ShapeDtypeStruct(table.shape, table.dtype) for table in tables],
        input_output_aliases={3 + i: i for i in range(len(tables))},
        cost_estimate=pl.CostEstimate(
            flops=2 * row_total * depth * col_count,
            bytes_accessed=2 * row_total * col_count,
            transcendentals=0,
        ),
        compiler_params=params(),
    )(positions, left_t, right, *tables)


def optimizer_update(
    sources, slot_sources, slot_rows, slot_kinds, kinds_used, slot_masks, small_rates,
    master, moment_one, moment_two, first_block, earlier,
):
    capacity, piece_size = master.shape
    chunks = piece_size // CHUNK
    rows = CHUNK // LANES
    slot_blocks = pl.cdiv(capacity, 8)
    steps = slot_blocks * chunks

    def steps_here(first):
        return (first if earlier else slot_blocks - first) * chunks

    def place(step, first):
        now = jnp.minimum(step, jnp.maximum(steps_here(first) - 1, 0))
        block, chunk = now // chunks, lax.rem(now, chunks)
        return (block if earlier else slot_blocks - 1 - block), chunk

    def kernel(first_ref, kinds_ref, sources_ref, rows_ref, *refs):
        source_refs, refs = refs[: len(sources)], refs[len(sources) :]
        masks_ref, small_ref, master_ref, one_ref, two_ref = refs[:5]
        refs = refs[5 + len(earlier) :]
        grad_out, master_out, one_out, two_out, low_out, scratch, buffer, sem = refs
        step = pl.program_id(0)
        count = jnp.maximum(steps_here(first_ref[0]), 1)
        first = place(step, first_ref[0])[0] * 8
        slot = lax.rem(step, 2)

        def start(step, which):
            block, chunk = place(step, first_ref[0])
            for s in range(8):
                for i, source_ref in enumerate(source_refs):

                    @pl.when(sources_ref[block * 8 + s] == i)
                    def _():
                        pltpu.make_async_copy(
                            source_ref.at[
                                rows_ref[block * 8 + s],
                                pl.ds(pl.multiple_of(chunk * rows, rows), rows),
                            ],
                            buffer.at[which, s],
                            sem.at[which],
                        ).start()

                @pl.when(sources_ref[block * 8 + s] >= len(sources))
                def _():
                    pltpu.make_async_copy(
                        source_refs[0].at[0, pl.ds(0, rows)], buffer.at[which, s], sem.at[which]
                    ).start()

        @pl.when(step == 0)
        def _():
            start(0, 0)

        @pl.when(step + 1 < count)
        def _():
            start(step + 1, 1 - slot)

        @pl.when(step < count)
        def _():
            pltpu.make_async_copy(buffer.at[slot], buffer.at[slot], sem.at[slot]).wait()
            for s in range(8):
                kind_now = kinds_ref[first + s]
                for kind in kinds_used:

                    @pl.when(kind_now == kind)
                    def _():
                        for tile in range(rows // TILE):
                            row_tile, column = divmod(tile, kind)
                            start_row = (row_tile * TILE * kind + column) * 8 + s
                            scratch[pl.ds(start_row, TILE, stride=8 * kind), :] = buffer[
                                slot, s, TILE * tile : TILE * tile + TILE, :
                            ].astype(jnp.float32)

            present = masks_ref[0] > 0.5
            is_small = masks_ref[1] > 0.5
            rate_rows = masks_ref[2]
            for j in range(rows):
                lanes = slice(LANES * j, LANES * j + LANES)
                grad = jnp.where(present, scratch[8 * j : 8 * j + 8, :], 0.0)
                rate = jnp.where(is_small, small_ref[:, lanes], rate_rows)
                master_now = master_ref[:, lanes]
                one_new = BETA_ONE * one_ref[:, lanes] + (1.0 - BETA_ONE) * grad
                two_new = BETA_TWO * two_ref[:, lanes] + (1.0 - BETA_TWO) * grad * grad
                first_hat = one_new / (1.0 - BETA_ONE**STEP)
                second_hat = two_new / (1.0 - BETA_TWO**STEP)
                master_new = master_now - rate * (
                    first_hat / (jnp.sqrt(second_hat) + ADAM_EPSILON) + WEIGHT_DECAY * master_now
                )
                grad_out[:, lanes] = grad
                master_out[:, lanes] = master_new
                one_out[:, lanes] = one_new
                two_out[:, lanes] = two_new
                low_out[:, lanes] = master_new.astype(jnp.bfloat16)

    state_spec = pl.BlockSpec((8, CHUNK), lambda t, first, *tables: place(t, first[0]))
    anywhere = pl.BlockSpec(memory_space=pl.ANY)
    wide = jax.ShapeDtypeStruct((capacity, piece_size), jnp.float32)
    operands = [*sources, slot_masks, small_rates, master, moment_one, moment_two, *earlier]
    return pl.pallas_call(
        kernel,
        grid_spec=pltpu.PrefetchScalarGridSpec(
            num_scalar_prefetch=4,
            grid=(steps,),
            in_specs=[anywhere for source in sources]
            + [
                pl.BlockSpec((3, 8, LANES), lambda t, first, *tables: (0, place(t, first[0])[0], 0)),
                pl.BlockSpec((1, CHUNK), lambda t, first, *tables: (0, place(t, first[0])[1])),
                state_spec,
                state_spec,
                state_spec,
            ]
            + [anywhere for array in earlier],
            out_specs=[state_spec] * 5,
            scratch_shapes=[
                pltpu.VMEM((8 * rows, LANES), jnp.float32),
                pltpu.VMEM((2, 8, rows, LANES), jnp.bfloat16),
                pltpu.SemaphoreType.DMA((2,)),
            ],
        ),
        out_shape=[wide] * 4 + [jax.ShapeDtypeStruct((capacity, piece_size), jnp.bfloat16)],
        input_output_aliases={
            4 + len(operands) - len(earlier) + i: i for i in range(len(earlier))
        },
        cost_estimate=pl.CostEstimate(
            flops=20 * master.size,
            bytes_accessed=16 * master.size,
            transcendentals=2 * master.size,
        ),
        compiler_params=pltpu.CompilerParams(vmem_limit_bytes=24 * 1024 * 1024),
    )(first_block, slot_kinds, slot_sources, slot_rows, *operands)


def weight_grad(left, right):
    return jnp.einsum("td,tc->dc", left, right, preferred_element_type=jnp.float32)


def back_product(grad_rows, weight):
    return jnp.dot(grad_rows, weight.T, preferred_element_type=jnp.float32)


def gather_rest(packed, first, trips, most, extra_step):
    devices = lax.axis_size("seq")
    rows = devices * extra_step
    room = reserve((most * rows,) + packed.shape[1:], packed.dtype)

    def more(trip, table):
        part = lax.dynamic_slice_in_dim(packed, first + trip * extra_step, extra_step)
        part = lax.all_gather(part, "seq", axis=0, tiled=True)
        return lax.dynamic_update_slice_in_dim(table, part, trip * rows, axis=0)

    return lax.fori_loop(0, trips, more, room)


def reduce_rest(rest, trips, most, extra_step):
    devices = lax.axis_size("seq")
    rows = devices * extra_step
    room = reserve((most * extra_step,) + rest.shape[1:], rest.dtype)

    def more(trip, table):
        part = lax.dynamic_slice_in_dim(rest, trip * rows, rows)
        part = lax.psum_scatter(part, "seq", scatter_dimension=0, tiled=True)
        return lax.dynamic_update_slice_in_dim(table, part, trip * extra_step, axis=0)

    return lax.fori_loop(0, trips, more, room)


def bring_spilled(reduced, first, trips, most, step):
    devices = lax.axis_size("seq")
    room = reserve((most * step,) + reduced.shape[1:], reduced.dtype)

    def more(trip, table):
        part = lax.dynamic_slice_in_dim(reduced, first + trip * step, step)
        part = lax.ppermute(part, "seq", [(i, i ^ 1) for i in range(devices)])
        return lax.dynamic_update_slice_in_dim(table, part, trip * step, axis=0)

    return lax.fori_loop(0, trips, more, room)


def on_device(inputs, cotangent, owners, master, moment_one, moment_two):
    head_parts = lax.axis_size("head")
    seq_parts = lax.axis_size("seq")
    local_heads = HEADS // head_parts
    capacity, piece_size = master.shape
    piece_count = owners.shape[0]
    row_count = inputs.shape[0]
    rim_width = KCONV - 1
    segments_list = shard_layout(local_heads, head_parts)
    columns = {name: c for name, r, c, rate in segments_list}
    counts = {name: r * c // piece_size for name, r, c, rate in segments_list[:8]}
    firsts = dict(zip(counts, np.cumsum([0] + list(counts.values())).tolist()))
    mixer_count = firsts["wgate"]
    big_count = piece_count - 1
    my_head = lax.axis_index("head").astype(jnp.int32)
    my_index = lax.axis_index("seq").astype(jnp.int32)
    my_head_row, my_index_row = my_head.reshape(1), my_index.reshape(1)

    onehot = (owners[:, None] == jnp.arange(seq_parts, dtype=jnp.int32)[None, :]).astype(jnp.int32)
    ranks = jnp.sum((jnp.cumsum(onehot, axis=0) - onehot) * onehot, axis=1)
    mixer_held = jnp.sum(onehot[:mixer_count], axis=0)
    mlp_held = jnp.sum(onehot[mixer_count:big_count], axis=0)
    padded = capacity + -capacity % 8
    small_rank = ranks[big_count]
    big_owners, big_ranks = owners[:big_count], ranks[:big_count]

    def rest_row(over, owner):
        return over // extra_step * (seq_parts * extra_step) + owner * extra_step + over % extra_step

    early = -(-capacity * FIRST_GATHER // (8 * CAPACITY_UNIT)) * 8
    late = capacity - early
    late_room = min(late, -(-capacity * SECOND_GATHER // CAPACITY_UNIT))
    extra_step = 2 if late % 2 == 0 else 1
    most_gather = -(-late // extra_step)
    trips_gather = jnp.maximum(-(-(jnp.max(mixer_held) - early) // extra_step), 0)
    early_row = big_owners * early + big_ranks
    mixer_fetch = jnp.where(
        big_ranks < early, early_row, TABLE + rest_row(big_ranks - early, big_owners)
    )
    neighbours = np.arange(seq_parts) ^ 1
    late_held = jnp.maximum(mixer_held + mlp_held - early, 0)
    late_spare = jnp.maximum(late_room - late_held[neighbours], 0)
    late_over = jnp.maximum(late_held - late_room, 0)
    trips_late = -(-jnp.max(jnp.maximum(late_over - late_spare, 0)) // extra_step)
    spare_there = jnp.sum(onehot[:big_count] * late_spare[None, :], axis=1)
    past = big_ranks - early - late_room
    rest_trip = (past - spare_there) // extra_step
    rest_start = late_room + spare_there + rest_trip * extra_step
    rest_start = jnp.minimum(rest_start, late - extra_step)
    mlp_fetch = jnp.where(
        big_ranks < early,
        TABLE + early_row,
        jnp.where(
            past < 0,
            big_owners * late_room + big_ranks - early,
            jnp.where(
                past < spare_there,
                (big_owners ^ 1) * late_room + late_room - spare_there + past,
                2 * TABLE
                + rest_trip * (seq_parts * extra_step)
                + big_owners * extra_step
                + big_ranks - early - rest_start,
            ),
        ),
    )
    first_room = -(-capacity * FIRST_REDUCE // CAPACITY_UNIT)
    second_room = -(-capacity * SECOND_REDUCE // CAPACITY_UNIT)
    most_reduce = -(-(capacity - second_room) // extra_step)
    second_held = mixer_held + jnp.maximum(mlp_held - first_room, 0)
    second_there = jnp.sum(onehot[:big_count] * second_held[None, :], axis=1)
    room_there = jnp.maximum(second_room - second_held[neighbours], 0)
    over_held = jnp.maximum(second_held - second_room, 0)
    spill_step = min(4, second_room)
    most_spill = -(-min(second_room, capacity - second_room) // spill_step)
    trips_spill = -(-jnp.max(jnp.minimum(over_held, room_there)) // spill_step)
    trips_reduce = -(-jnp.max(jnp.maximum(over_held - room_there, 0)) // extra_step)
    second_over = big_ranks - second_room
    spare = jnp.sum(onehot[:big_count] * room_there[None, :], axis=1)
    store = jnp.where(
        big_ranks >= second_there,
        big_owners * first_room + big_ranks - second_there,
        jnp.where(
            second_over < 0,
            TABLE + big_owners * second_room + big_ranks,
            jnp.where(
                second_over < spare,
                TABLE + (big_owners ^ 1) * second_room + (second_room - spare) + second_over,
                2 * TABLE + rest_row(second_over - spare, big_owners),
            ),
        ),
    )
    small_owner = owners[big_count]

    def spots(table, name):
        return table[firsts[name] : firsts[name] + counts[name]]

    my_spare_here = room_there[my_index ^ 1]
    my_mixer = mixer_held[my_index]
    my_mlp = mlp_held[my_index]
    my_count = my_mixer + my_mlp
    slot_ids = jnp.arange(padded, dtype=jnp.int32)
    mine = owners == my_index
    matches = (mine[None, :] & (ranks[None, :] == slot_ids[:, None])).astype(jnp.int32)
    kind_table = piece_kinds(segments_list, piece_count, piece_size)
    piece_rates, small_rates = rate_parts(segments_list, piece_count, piece_size)
    present = jnp.sum(matches, axis=1)
    slot_kinds = 1 + jnp.sum(matches * jnp.asarray(kind_table - 1)[None, :], axis=1)
    slot_rates = PAD_RATE + jnp.sum(
        matches.astype(jnp.float32) * jnp.asarray(piece_rates - np.float32(PAD_RATE))[None, :], axis=1
    )
    is_small = matches[:, big_count]
    kinds_used = sorted(set(kind_table.tolist()) | {1})

    small_rows = -(-sum(r * c for name, r, c, rate in segments_list[8:]) // (TILE * LANES)) * TILE
    gain_width = D // head_parts
    norm_width = DV // head_parts
    gain_first = sum(r * c for name, r, c, rate in segments_list[8:14])
    my_small = lax.dynamic_slice(master, (small_rank, 0), (1, small_rows * LANES))
    my_small = my_small.astype(jnp.bfloat16)
    gains = my_small[:, gain_first : gain_first + 2 * gain_width + norm_width]
    gains = in_order(exchange([gains] * head_parts, "head"), my_head, 0)
    gains = jnp.concatenate(
        [
            gains[:, :gain_width].reshape(1, D),
            gains[:, gain_width : 2 * gain_width].reshape(1, D),
            gains[:, 2 * gain_width :].reshape(1, DV),
        ],
        axis=1,
    )
    rows_of_piece = piece_size // LANES
    small_width = small_rows * LANES
    small_part = jnp.concatenate([my_small, gains], axis=1).reshape(-1, LANES)
    small_table, small_base = gather_states(small_part)
    input_blocks = exchange([inputs] * head_parts, "head")
    early_part = pack_blocks(master, slot_kinds, kinds_used, 0, early)
    early_table = lax.all_gather(early_part, "seq", axis=0, tiled=True)
    late_part = pack_blocks(master, slot_kinds, kinds_used, early, late)
    late_send = late_part[:late_room]
    if late_room < late:
        guests = lax.ppermute(
            late_part[late_room:], "seq", [(i, i ^ 1) for i in range(seq_parts)]
        )
        late_send = lax.dynamic_update_slice_in_dim(
            late_part, guests, late_held[my_index], axis=0
        )[:late_room]
    back_blocks = exchange([cotangent] * head_parts, "head")
    rows_full = in_order(input_blocks, my_head, 1)
    back_full = in_order(back_blocks, my_head, 1)
    small_flat = lax.dynamic_index_in_dim(
        small_table, small_owner ^ small_base[0], axis=0, keepdims=False
    ).reshape(-1)
    by_name, small_used = unpack(small_flat, segments_list[8:])
    gains = small_flat[small_width:].astype(jnp.float32)[None, :]
    gain_one, gain_two, norm_row = gains[:, :D], gains[:, D : 2 * D], gains[:, 2 * D :]
    gain_one_mine = by_name["gainone"].astype(jnp.float32)
    gain_two_mine = by_name["gaintwo"].astype(jnp.float32)

    rows_wide = rows_full.astype(jnp.float32)
    scale_one = lax.rsqrt(jnp.mean(rows_wide * rows_wide, axis=-1, keepdims=True) + NORM_EPSILON)
    normed = (rows_wide * scale_one * gain_one).astype(jnp.bfloat16)

    decay_weight = jnp.pad(by_name["wab"], ((0, 0), (0, LANES - 2 * local_heads)))
    decay_proj = jnp.dot(normed, decay_weight, preferred_element_type=jnp.float32)
    taps = jnp.concatenate([by_name["cq"], by_name["ck"], by_name["cv"]], axis=1)
    taps = jnp.pad(taps.astype(jnp.float32), ((0, 8 - KCONV), (0, 0)))
    scalars = jnp.pad(
        jnp.concatenate([by_name["alog"], by_name["dtbias"]], axis=0).astype(jnp.float32),
        ((0, 6), (0, LANES - local_heads)),
    )

    beside = (
        trips_gather, late_part, late_send, normed, scale_one, decay_proj, decay_weight, taps, scalars,
        back_full, mixer_fetch, mlp_fetch, store, gain_two, norm_row,
    )
    early_table, beside = lax.optimization_barrier((early_table, beside))
    (
        trips_now, late_part, late_send, normed, scale_one, decay_proj, decay_weight, taps, scalars,
        back_full, mixer_fetch, mlp_fetch, store, gain_two, norm_row,
    ) = beside
    mixer_rest = gather_rest(late_part, 0, trips_now, most_gather, extra_step)
    late_table = lax.all_gather(late_send, "seq", axis=0, tiled=True)

    mixer_names = ("wq", "wk", "wv", "wg")
    mixer_weights, projected = assemble(
        [early_table, mixer_rest],
        [(spots(mixer_fetch, name), columns[name]) for name in mixer_names],
        512,
        normed,
    )
    conv_columns = local_heads * (2 * DK + DV)
    rim = shifted(projected[row_count - rim_width :, :conv_columns], "seq", 1)
    rim = jnp.pad(rim, ((8 - rim_width, 0), (0, 0)))
    solve, fresh, wy_keys, reach, zero_out, handoff = mixer_local(
        local_heads, projected, rim, taps, decay_proj, scalars
    )
    handoffs, base = gather_states(handoff)
    (out_weights,) = assemble(
        [early_table, mixer_rest], [(spots(mixer_fetch, "wo"), columns["wo"])], 256
    )
    entering_state, recurred, gated_low = mixer_out(
        local_heads, my_index_row, base, handoffs, reach, zero_out, projected, norm_row
    )
    mixed_parts = exchange(
        spread_products(my_head_row, head_parts, [(gated_low, out_weights, False)]), "head"
    )
    mixed = total_of(mixed_parts)
    inputs_wide = inputs.astype(jnp.float32)
    residual = inputs_wide + mixed
    resid_low = residual.astype(jnp.bfloat16)

    resid_blocks = exchange([resid_low] * head_parts, "head")
    trips_now, late_table = lax.optimization_barrier((trips_late, late_table))
    late_rest = gather_rest(
        late_part, late_room + late_spare[my_index], trips_now, most_gather, extra_step
    )
    mlp_tables = [late_table, early_table, late_rest]
    (down_weights,) = assemble(
        mlp_tables, [(spots(mlp_fetch, "wdown"), columns["wdown"])], 352
    )
    (mlp_weights,) = assemble(
        mlp_tables,
        [(spots(mlp_fetch, name), columns[name]) for name in ("wgate", "wup")],
        512,
    )
    resid_blocks, down_weights, mlp_weights = lax.optimization_barrier(
        (resid_blocks, down_weights, mlp_weights)
    )
    resid_full = in_order(resid_blocks, my_head, 1).astype(jnp.float32)
    scale_two = lax.rsqrt(jnp.mean(resid_full * resid_full, axis=-1, keepdims=True) + NORM_EPSILON)
    hidden_in = (resid_full * scale_two * gain_two).astype(jnp.bfloat16)
    gate_up = jnp.dot(hidden_in, mlp_weights, preferred_element_type=jnp.float32)
    hidden_width = columns["wgate"]
    gate_mlp, up_mlp = gate_up[:, :hidden_width], gate_up[:, hidden_width:]
    logistic_output_multiplier = jax.nn.sigmoid(gate_mlp)
    silu_gate = gate_mlp * logistic_output_multiplier
    hidden = (silu_gate * up_mlp).astype(jnp.bfloat16)
    mlp_blocks = spread_products(my_head_row, head_parts, [(hidden, down_weights, False)])
    d_hidden = back_product(back_full, down_weights)
    d_gate_mlp = (
        d_hidden
        * up_mlp
        * logistic_output_multiplier
        * (1.0 + gate_mlp * (1.0 - logistic_output_multiplier))
    ).astype(jnp.bfloat16)
    d_up_mlp = (d_hidden * silu_gate).astype(jnp.bfloat16)
    d_gate_up = jnp.concatenate([d_gate_mlp, d_up_mlp], axis=1)
    def store_grad(tables, name, left_t, right, right_block, blocks_a_step):
        return weight_grad_blocks(
            left_t, right, right_block, columns[name], spots(store, name), tables, blocks_a_step
        )

    grad_tables = [
        reserve((rows, rows_of_piece, LANES), jnp.bfloat16)
        for rows in (
            seq_parts * first_room,
            seq_parts * second_room,
            most_reduce * seq_parts * extra_step,
        )
    ]
    grad_tables = store_grad(grad_tables, "wdown", hidden.T, back_full, 0, 11)
    hidden_in_t = hidden_in.T
    grad_tables = store_grad(grad_tables, "wgate", hidden_in_t, d_gate_up, 0, 11)
    grad_tables = store_grad(grad_tables, "wup", hidden_in_t, d_gate_up, 1, 11)
    grad_tables, d_gate_up = lax.optimization_barrier((grad_tables, d_gate_up))
    d_hidden_parts = exchange(
        spread_products(my_head_row, head_parts, [(d_gate_up, mlp_weights, True)]), "head"
    )
    first_reduced = lax.psum_scatter(grad_tables[0], "seq", scatter_dimension=0, tiled=True)
    grad_tables = grad_tables[1:]
    store = store - TABLE
    d_hidden_mine = total_of(d_hidden_parts)
    mlp_out = total_of(exchange(mlp_blocks, "head"))
    block_out = (residual + mlp_out).astype(jnp.bfloat16)

    resid_mine = resid_low.astype(jnp.float32)
    d_hidden_low = d_hidden_mine.astype(jnp.bfloat16)
    dot_mine = jnp.sum(d_hidden_mine * gain_two_mine * resid_mine, axis=-1)
    d_hidden_blocks = exchange([d_hidden_low] * head_parts, "head")
    dot_two = sum_over(dot_mine.reshape(-1, LANES), "head").reshape(row_count, 1)
    grad_gaintwo = jnp.sum(d_hidden_mine * resid_mine * scale_two, axis=0)
    d_resid = (
        cotangent.astype(jnp.float32)
        + scale_two * d_hidden_mine * gain_two_mine
        - scale_two**3 / D * resid_mine * dot_two
    )
    d_hidden_full = in_order(d_hidden_blocks, my_head, 1).astype(jnp.float32)
    back_mix_full = (
        back_full.astype(jnp.float32)
        + scale_two * d_hidden_full * gain_two
        - scale_two**3 / D * resid_full * dot_two
    ).astype(jnp.bfloat16)

    d_gated = back_product(back_mix_full, out_weights)
    d_recurred, d_gate, norm_grad, d_entering = mixer_gate_back(
        local_heads, d_gated, recurred, projected, norm_row, reach
    )
    d_enterings, base = gather_states(d_entering)
    normed_t = normed.T
    grad_tables = store_grad(grad_tables, "wo", gated_low.T, back_mix_full, 0, 8)
    grad_tables = store_grad(grad_tables, "wg", normed_t, d_gate, 0, 8)
    d_leaving = relay_back(local_heads, my_index_row, base, handoffs, d_enterings)
    d_conv, d_tail, d_rim, d_taps, d_decay_wide, d_scalars = mixer_back(
        local_heads,
        projected,
        rim,
        taps,
        decay_proj,
        scalars,
        solve,
        fresh,
        wy_keys,
        entering_state,
        d_recurred,
        d_leaving,
    )
    d_rim = shifted(d_rim[8 - rim_width :], "seq", -1)
    d_tail = d_tail + jnp.pad(d_rim, ((8 - rim_width, 0), (0, 0)))
    d_conv = lax.dynamic_update_slice(d_conv, d_tail.astype(jnp.bfloat16), (row_count - 8, 0))
    key_width = local_heads * DK
    grad_tables = store_grad(grad_tables, "wv", normed_t, d_conv, 1, 8)
    grad_tables = store_grad(grad_tables, "wk", normed_t, d_conv, 1, 4)
    grad_tables = store_grad(grad_tables, "wq", normed_t, d_conv, 0, 4)
    second_table, first_reduced = lax.optimization_barrier((grad_tables[0], first_reduced))
    second_reduced = lax.psum_scatter(second_table, "seq", scatter_dimension=0, tiled=True)
    d_decay = d_decay_wide.astype(jnp.bfloat16)
    grad_wab = weight_grad(normed, d_decay)[:, : 2 * local_heads]
    d_projected = jnp.concatenate([d_conv, d_gate], axis=1)
    d_normed_mine = total_of(
        exchange(
            spread_products(
                my_head_row,
                head_parts,
                [(d_projected, mixer_weights, True), (d_decay, decay_weight, True)],
            ),
            "head",
        )
    )
    dot_one = jnp.sum(d_normed_mine * gain_one_mine * inputs_wide, axis=-1)
    sums = sum_over(
        jnp.concatenate([dot_one.reshape(-1, LANES), norm_grad[0].reshape(-1, LANES)]), "head"
    )
    dot_one = sums[: row_count // LANES].reshape(row_count, 1)
    grad_wnorm = lax.dynamic_slice_in_dim(
        sums[row_count // LANES :].reshape(-1), my_head * norm_width, norm_width
    )
    grad_gainone = jnp.sum(d_normed_mine * inputs_wide * scale_one, axis=0)
    input_grad = (
        d_resid
        + scale_one * d_normed_mine * gain_one_mine
        - scale_one**3 / D * inputs_wide * dot_one
    )

    small_grads = [
        d_taps[:KCONV, :key_width],
        d_taps[:KCONV, key_width : 2 * key_width],
        d_taps[:KCONV, 2 * key_width :],
        grad_wab,
        d_scalars[0, :local_heads],
        d_scalars[1, :local_heads],
        grad_gainone,
        grad_gaintwo,
        grad_wnorm,
    ]
    small_block = jnp.concatenate(
        [grad_now.reshape(-1) for grad_now in small_grads]
        + [jnp.zeros((small_rows * LANES - small_used,), jnp.float32)]
    ).reshape(-1, LANES)
    mask = 1
    while mask < seq_parts:
        small_block = small_block + lax.ppermute(
            small_block, "seq", [(i, i ^ mask) for i in range(seq_parts)]
        )
        mask *= 2
    small_block = jnp.pad(
        small_block.astype(jnp.bfloat16), ((0, rows_of_piece - small_rows), (0, 0))
    )[None]

    trips_now, second_reduced, rest_grads = lax.optimization_barrier(
        (trips_reduce, second_reduced, grad_tables[1])
    )
    rest_reduced = reduce_rest(rest_grads, trips_now, most_reduce, extra_step)
    spilled = bring_spilled(
        second_reduced, second_room - my_spare_here, trips_spill, most_spill, spill_step
    )
    my_held = second_held[my_index]
    in_first = slot_ids >= my_held
    my_over = slot_ids - second_room
    my_spare = room_there[my_index]
    spill_trip = my_over // spill_step
    there = second_room - my_spare + spill_trip * spill_step
    spill_shift = there - jnp.minimum(there, second_room - spill_step)
    slot_sources = jnp.where(
        in_first, 0, jnp.where(my_over < 0, 2, jnp.where(my_over < my_spare, 3, 4))
    )
    slot_rows = jnp.where(
        in_first,
        slot_ids - my_held,
        jnp.where(
            my_over < 0,
            slot_ids,
            jnp.where(my_over < my_spare, my_over + spill_shift, my_over - my_spare),
        ),
    )
    slot_sources = jnp.where(present > 0, jnp.where(is_small > 0, 1, slot_sources), 0)
    slot_rows = jnp.where(is_small > 0, 0, slot_rows)
    slot_rows = jnp.where(present > 0, slot_rows, 0)
    slot_masks = jnp.stack([present.astype(jnp.float32), is_small.astype(jnp.float32), slot_rates])
    slot_masks = jnp.broadcast_to(slot_masks[:, :, None], slot_masks.shape + (LANES,))
    first_block = jnp.minimum((my_held + 7) // 8, padded // 8).astype(jnp.int32).reshape(1)

    def update(sources, earlier):
        return optimizer_update(
            sources,
            slot_sources,
            slot_rows,
            slot_kinds,
            kinds_used,
            slot_masks,
            jnp.asarray(small_rates)[None, :],
            master,
            moment_one,
            moment_two,
            first_block,
            earlier,
        )

    partly = update([first_reduced, small_block], [])
    grad_slots, master_new, moment_new, second_new, weights_low = update(
        [first_reduced, small_block, second_reduced, spilled, rest_reduced], partly
    )
    return (
        block_out,
        input_grad,
        grad_slots,
        master_new,
        moment_new,
        second_new,
        weights_low,
    )


def solution(mesh):
    return jax.shard_map(
        on_device,
        mesh=mesh,
        in_specs=(
            P("seq", "head"),
            P("seq", "head"),
            P(),
            P("seq", "head"),
            P("seq", "head"),
            P("seq", "head"),
        ),
        out_specs=(
            P("seq", "head"),
            P("seq", "head"),
            P("seq", "head"),
            P("seq", "head"),
            P("seq", "head"),
            P("seq", "head"),
            P("seq", "head"),
        ),
        check_vma=False,
    )
```

```python
import jax
import jax.numpy as jnp
import numpy as np
from jax import lax
from jax.experimental import pallas as pl
from jax.experimental.pallas import tpu as pltpu
from jax.sharding import PartitionSpec as P

D = 2048
HEADS = 16
DK = 128
DV = 256
FF = 5632
KCONV = 4
STEP = 5


EXACT_ARITHMETIC = lax.Precision.HIGHEST
NORM_EPSILON = 1e-06
UNIT_EPSILON = 1e-06
HEAD_EPSILON = 1e-05
ADAM_EPSILON = 1e-08
BETA_ONE = 0.5
BETA_TWO = 0.5
WEIGHT_DECAY = 0.1
PAD_RATE = 0.1


def shifted(block, axis, distance):
    devices = range(lax.axis_size(axis))
    route = [(i - distance, i) for i in devices if i - distance in devices]
    return lax.ppermute(block, axis, route)


def shard_layout(local_heads, head_parts):
    return [
        ("wq", D, local_heads * DK, 0.02),
        ("wk", D, local_heads * DK, 0.02),
        ("wv", D, local_heads * DV, 0.02),
        ("wg", D, local_heads * DV, 0.02),
        ("wo", local_heads * DV, D, 0.015),
        ("wgate", D, FF // head_parts, 0.02),
        ("wup", D, FF // head_parts, 0.02),
        ("wdown", FF // head_parts, D, 0.012),
        ("cq", KCONV, local_heads * DK, 0.4),
        ("ck", KCONV, local_heads * DK, 0.4),
        ("cv", KCONV, local_heads * DV, 0.4),
        ("wab", D, 2 * local_heads, 0.04),
        ("alog", 1, local_heads, 0.5),
        ("dtbias", 1, local_heads, 0.5),
        ("gainone", 1, D // head_parts, 0.1),
        ("gaintwo", 1, D // head_parts, 0.1),
        ("wnorm", 1, DV // head_parts, 0.1),
    ]


def piece_table(owners, seq_parts, capacity):
    piece_count = owners.shape[0]
    devices = jnp.arange(seq_parts, dtype=jnp.int32)
    onehot = (owners[:, None] == devices[None, :]).astype(jnp.int32)
    before = jnp.cumsum(onehot, axis=0) - onehot
    rank_within = jnp.sum(before * onehot, axis=1)
    slot_of_piece = owners * capacity + rank_within
    matches = slot_of_piece[None, :] == jnp.arange(seq_parts * capacity, dtype=jnp.int32)[:, None]
    present = jnp.any(matches, axis=1)
    piece_of_slot = jnp.sum(
        matches.astype(jnp.int32) * jnp.arange(piece_count, dtype=jnp.int32)[None, :], axis=1
    )
    return (slot_of_piece, piece_of_slot, present)


def unpack(flat_weights, segments_list):
    by_name = {}
    offset_now = 0
    for seg_name, row_count, col_count, seg_rate in segments_list:
        by_name[seg_name] = flat_weights[offset_now : offset_now + row_count * col_count].reshape(
            row_count, col_count
        )
        offset_now += row_count * col_count
    return (by_name, offset_now)


def rate_parts(segments_list, piece_count, piece_size):
    piece_rates = np.full(piece_count, PAD_RATE, np.float32)
    small_rates = np.full(piece_size, PAD_RATE, np.float32)
    offset_now = 0
    big_total = (piece_count - 1) * piece_size
    for seg_name, row_count, col_count, seg_rate in segments_list:
        seg_size = row_count * col_count
        if offset_now < big_total:
            piece_rates[offset_now // piece_size : (offset_now + seg_size) // piece_size] = seg_rate
        else:
            small_rates[offset_now - big_total : offset_now - big_total + seg_size] = seg_rate
        offset_now += seg_size
    return (piece_rates, small_rates)


HEADS_A_STEP = 1


def product(left, right, left_axis, right_axis, exact=False):
    def dot(a, b):
        return lax.dot_general(
            a,
            b,
            (((left_axis,), (right_axis,)), ((), ())),
            preferred_element_type=jnp.float32,
        )

    left_low, right_low = left.astype(jnp.bfloat16), right.astype(jnp.bfloat16)
    if not exact:
        return dot(left_low, right_low)
    left_rest = (left - left_low.astype(jnp.float32)).astype(jnp.bfloat16)
    right_rest = (right - right_low.astype(jnp.float32)).astype(jnp.bfloat16)
    return dot(left_low, right_low) + (dot(left_low, right_rest) + dot(left_rest, right_low))


def take_lane(wide, lane):
    lanes = lax.broadcasted_iota(jnp.int32, wide.shape, 1)
    return jnp.sum(jnp.where(lanes == lane, wide, 0.0), axis=1, keepdims=True)


def put_lane(column, lane):
    lanes = lax.broadcasted_iota(jnp.int32, (column.shape[0], 128), 1)
    return jnp.where(lanes == lane, column, 0.0)


def to_row(column, diagonal):
    return jnp.sum(jnp.where(diagonal, column, 0.0), axis=0, keepdims=True)


def convolved(extended, taps_ref, columns):
    row_count = extended.shape[0] - RIM
    first = RIM - (KCONV - 1)
    running = taps_ref[0:1, columns] * extended[first : first + row_count, columns]
    for tap in range(1, KCONV):
        running = running + taps_ref[tap : tap + 1, columns] * extended[
            first + tap : first + tap + row_count, columns
        ]
    return running


def decay_terms(head, local_heads, decay_ref, scalars_ref):
    row_count = decay_ref.shape[0]
    shape = (row_count, row_count)
    row_ids = lax.broadcasted_iota(jnp.int32, shape, 0)
    column_ids = lax.broadcasted_iota(jnp.int32, shape, 1)
    decay_in = take_lane(decay_ref[...], head) + take_lane(scalars_ref[1:2, :], head)
    rate = -jnp.exp(take_lane(scalars_ref[0:1, :], head))
    soft = jnp.maximum(decay_in, 0.0) + jnp.log1p(jnp.exp(-jnp.abs(decay_in)))
    logs = rate * soft
    beta = jax.nn.sigmoid(take_lane(decay_ref[...], head + local_heads))
    diagonal = row_ids == column_ids
    logs_row = to_row(logs, diagonal)
    upto = row_ids >= column_ids
    sums = jnp.sum(jnp.where(upto, logs_row, 0.0), axis=1, keepdims=True)
    sums_row = to_row(sums, diagonal)
    within = jnp.exp(jnp.where(upto, sums - sums_row, -1e30))
    return decay_in, rate, logs, beta, sums, within, row_ids, column_ids


def unit_rows(rows):
    scale = lax.rsqrt(jnp.sum(rows * rows, axis=-1, keepdims=True) + UNIT_EPSILON)
    return rows * scale, scale


def mixer_specs(local_heads, row_count):
    def spec(rows, width, first):
        width *= HEADS_A_STEP
        return pl.BlockSpec((rows, width), lambda h, first=first // width: (0, first + h))

    def query(rows):
        return spec(rows, DK, 0)

    def key(rows):
        return spec(rows, DK, local_heads * DV)

    def value(rows):
        return spec(rows, DV, 0)

    whole = pl.BlockSpec((row_count, 128), lambda h: (0, 0))
    scalars = pl.BlockSpec((8, 128), lambda h: (0, 0))
    return query, key, value, whole, scalars


def per_head(*shape):
    return pl.BlockSpec((HEADS_A_STEP,) + shape, lambda h: (h,) + (0,) * len(shape))


def head_columns(sub):
    return slice(DK * sub, DK * sub + DK), slice(DV * sub, DV * sub + DV)


def mixer_local(local_heads, value_key, taps, decay_proj, scalars):
    row_count = value_key.shape[0] - RIM
    query, key, value, whole, scalar_spec = mixer_specs(local_heads, row_count)

    def kernel(
        pv, pk, tv, tk, decay_ref, scalars_ref, solve_ref, fresh_ref, wy_ref, handoff_ref
    ):
        for sub in range(HEADS_A_STEP):
            head = pl.program_id(0) * HEADS_A_STEP + sub
            narrow, wide = head_columns(sub)
            key_rows = unit_rows(jax.nn.silu(convolved(pk, tk, narrow)))[0]
            values = jax.nn.silu(convolved(pv, tv, wide))
            decay_in, rate, logs, beta, sums, within, row_ids, column_ids = decay_terms(
                head, local_heads, decay_ref, scalars_ref
            )
            gram = product(key_rows, key_rows, 1, 1, True)
            system = jnp.where(row_ids > column_ids, beta * gram * within, 0.0)
            unit = jnp.where(row_ids == column_ids, 1.0, 0.0)
            solve = unit
            size = 1
            while size < row_count:
                lower = (row_ids // (2 * size) == column_ids // (2 * size)) & (
                    row_ids // size != column_ids // size
                )
                part = jnp.where(lower, system, 0.0)
                if size == 1:
                    solve = solve - part
                else:
                    solve = solve - product(solve, product(part, solve, 1, 0), 1, 0)
                size *= 2
            remainder = (unit - solve) - product(system, solve, 1, 0, True)
            solve = solve + product(solve, remainder, 1, 0)
            grown = jnp.exp(sums)
            fresh = product(solve, beta * values, 1, 0, True)
            wy_keys = product(solve, (beta * grown) * key_rows, 1, 0, True)
            last = sums[row_count - 1 : row_count, :]
            tail_keys = jnp.exp(last - sums) * key_rows
            eye = lax.broadcasted_iota(jnp.int32, (DK, DK), 0) == lax.broadcasted_iota(
                jnp.int32, (DK, DK), 1
            )
            solve_ref[sub] = solve
            fresh_ref[sub] = fresh
            wy_ref[sub] = wy_keys
            handoff_ref[sub, :, :DK] = (
                jnp.where(eye, jnp.exp(last), 0.0) - product(tail_keys, wy_keys, 0, 0)
            ).astype(jnp.bfloat16)
            handoff_ref[sub, :, DK:] = product(tail_keys, fresh, 0, 0).astype(jnp.bfloat16)

    def out(*shape, kind=jnp.float32):
        return jax.ShapeDtypeStruct((local_heads,) + shape, kind)

    return pl.pallas_call(
        kernel,
        grid=(local_heads // HEADS_A_STEP,),
        in_specs=[
            value(RIM + row_count), key(RIM + row_count), value(8), key(8), whole, scalar_spec,
        ],
        out_specs=[
            per_head(row_count, row_count),
            per_head(row_count, DV),
            per_head(row_count, DK),
            per_head(DK, DK + DV),
        ],
        out_shape=[
            out(row_count, row_count),
            out(row_count, DV),
            out(row_count, DK),
            out(DK, DK + DV, kind=jnp.bfloat16),
        ],
        compiler_params=params(),
    )(value_key, value_key, taps, taps, decay_proj, scalars)


def mixer_reach(local_heads, query_gate, value_key, query_taps, taps, decay_proj, scalars, fresh, wy_keys):
    row_count = value_key.shape[0] - RIM
    query, key, value, whole, scalar_spec = mixer_specs(local_heads, row_count)

    def kernel(pq, pk, tq, tk, decay_ref, scalars_ref, fresh_ref, wy_ref, reach_ref, zero_ref):
        for sub in range(HEADS_A_STEP):
            head = pl.program_id(0) * HEADS_A_STEP + sub
            narrow, wide = head_columns(sub)
            queries = unit_rows(jax.nn.silu(convolved(pq, tq, narrow)))[0] * DK ** (-0.5)
            key_rows = unit_rows(jax.nn.silu(convolved(pk, tk, narrow)))[0]
            decay_in, rate, logs, beta, sums, within, row_ids, column_ids = decay_terms(
                head, local_heads, decay_ref, scalars_ref
            )
            attention = product(queries, key_rows, 1, 1) * within
            reach_ref[sub] = jnp.exp(sums) * queries - product(attention, wy_ref[sub], 1, 0)
            zero_ref[sub] = product(attention, fresh_ref[sub], 1, 0)

    return pl.pallas_call(
        kernel,
        grid=(local_heads // HEADS_A_STEP,),
        in_specs=[
            query(RIM + row_count), key(RIM + row_count), query(8), key(8), whole, scalar_spec,
            per_head(row_count, DV),
            per_head(row_count, DK),
        ],
        out_specs=[per_head(row_count, DK), per_head(row_count, DV)],
        out_shape=[
            jax.ShapeDtypeStruct((local_heads, row_count, DK), jnp.float32),
            jax.ShapeDtypeStruct((local_heads, row_count, DV), jnp.float32),
        ],
        compiler_params=params(),
    )(query_gate, value_key, query_taps, taps, decay_proj, scalars, fresh, wy_keys)


def advance_state(block, state, back):
    moved = product(block[:, :DK].astype(jnp.float32), state, 0 if back else 1, 0)
    return moved, block[:, DK:].astype(jnp.float32)


def chain_all(local_heads, my_index, handoffs, inputs, back):
    devices = handoffs.shape[0]

    def kernel(index_ref, handoffs_ref, inputs_ref, state_ref):
        state_ref[...] = jnp.zeros_like(state_ref)

        def advance(step, carry):
            j = devices - 1 - step if back else step
            for h in range(local_heads):
                moved, added = advance_state(handoffs_ref[j, h], state_ref[h], back)
                if back:
                    added = inputs_ref[j, h].astype(jnp.float32)
                state_ref[h] = moved + added
            return carry

        count = devices - 1 - index_ref[0] if back else index_ref[0]
        lax.fori_loop(0, count, advance, 0)

    vmem = pl.BlockSpec(memory_space=pltpu.VMEM)
    return pl.pallas_call(
        kernel,
        in_specs=[pl.BlockSpec(memory_space=pltpu.SMEM), vmem, vmem],
        out_specs=vmem,
        out_shape=jax.ShapeDtypeStruct((local_heads, DK, DV), jnp.float32),
        compiler_params=params(),
    )(my_index, handoffs, inputs)


def join_cores(local_heads, my_index, mine, theirs, inputs):
    half = local_heads // 2

    def kernel(index_ref, mine_ref, theirs_ref, *refs):
        out_ref = refs[-1]
        core = lax.rem(index_ref[0], 2)
        for i in range(half):
            h = core * half + i
            own, other = mine_ref[h], theirs_ref[h]
            first = jnp.where(core == 0, own, other)
            second = jnp.where(core == 0, other, own)
            if inputs:
                own, other = refs[0][h], refs[1][h]
                early = jnp.where(core == 0, own, other).astype(jnp.float32)
                late = jnp.where(core == 0, other, own).astype(jnp.float32)
                out_ref[i] = (advance_state(first, late, True)[0] + early).astype(jnp.bfloat16)
                continue
            moved, added = advance_state(second, first.astype(jnp.float32), False)
            out_ref[i, :, :DK] = moved[:, :DK].astype(jnp.bfloat16)
            out_ref[i, :, DK:] = (moved[:, DK:] + added).astype(jnp.bfloat16)

    vmem = pl.BlockSpec(memory_space=pltpu.VMEM)
    return pl.pallas_call(
        kernel,
        in_specs=[pl.BlockSpec(memory_space=pltpu.SMEM)] + [vmem] * (2 + len(inputs)),
        out_specs=vmem,
        out_shape=jax.ShapeDtypeStruct((half, DK, DV if inputs else DK + DV), jnp.bfloat16),
        compiler_params=params(),
    )(my_index, mine, theirs, *inputs)


def chain_chips(local_heads, my_index, theirs, chips, their_input, chip_inputs):
    half = local_heads // 2
    masks = len(chips) // 2
    back = their_input is not None
    flat = [theirs, *chips] + ([their_input, *chip_inputs] if back else [])

    def kernel(index_ref, *refs):
        state_ref = refs[-1]
        state_ref[...] = jnp.zeros_like(state_ref)
        core, chip = lax.rem(index_ref[0], 2), index_ref[0] // 2
        offset = 1 + len(chips)

        def update(h, block, extra):
            moved, added = advance_state(block, state_ref[h], back)
            state_ref[h] = moved + (extra.astype(jnp.float32) if back else added)

        order = range(masks, 0, -1) if back else range(masks)
        for other in order:
            for mask in range(1, masks + 1):
                here = (other ^ chip) == mask

                @pl.when(here & ((other > chip) if back else (other < chip)))
                def _():
                    for h in range(local_heads):
                        mine = core == h // half
                        pair = [refs[1 + 2 * (mask - 1) + i][h % half] for i in range(2)]
                        extra = None
                        if back:
                            extra = [
                                refs[offset + 1 + 2 * (mask - 1) + i][h % half] for i in range(2)
                            ]
                            extra = jnp.where(mine, *extra)
                        update(h, jnp.where(mine, *pair), extra)

        @pl.when(core == (0 if back else 1))
        def _():
            for h in range(local_heads):
                update(h, refs[0][h], refs[offset][h] if back else None)

    vmem = pl.BlockSpec(memory_space=pltpu.VMEM)
    return pl.pallas_call(
        kernel,
        in_specs=[pl.BlockSpec(memory_space=pltpu.SMEM)] + [vmem] * len(flat),
        out_specs=vmem,
        out_shape=jax.ShapeDtypeStruct((local_heads, DK, DV), jnp.float32),
        compiler_params=params(),
    )(my_index, *flat)


def moved_by(array, mask):
    return lax.ppermute(array, "seq", [(i, i ^ mask) for i in range(lax.axis_size("seq"))])


def pass_chips(block, beside):
    arrived = [moved_by(block, mask) for mask in (2, 4, 6)]
    arrived, beside = lax.optimization_barrier((arrived, beside))
    return [array for part in arrived for array in (part, moved_by(part, 1))], beside


def entering(local_heads, my_index, handoff, beside):
    if lax.axis_size("seq") != 8:
        handoffs = lax.all_gather(handoff, "seq", axis=0, tiled=False)
        return chain_all(local_heads, my_index, handoffs, handoffs, False), handoffs, beside
    theirs = moved_by(handoff, 1)
    chips, beside = pass_chips(join_cores(local_heads, my_index, handoff, theirs, []), beside)
    state = chain_chips(local_heads, my_index, theirs, chips, None, [])
    return state, (handoff, theirs, chips), beside


def leaving(local_heads, my_index, d_entering, kept, beside):
    if lax.axis_size("seq") != 8:
        inputs = lax.all_gather(d_entering, "seq", axis=0, tiled=False)
        return chain_all(local_heads, my_index, kept, inputs, True), beside
    handoff, theirs, chips = kept
    their_input = moved_by(d_entering, 1)
    joined = join_cores(local_heads, my_index, handoff, theirs, [d_entering, their_input])
    inputs, beside = pass_chips(joined, beside)
    return chain_chips(local_heads, my_index, theirs, chips, their_input, inputs), beside


def mixer_out(local_heads, entering_state, reach, zero_out, query_gate, norm_gain):
    row_count = query_gate.shape[0] - RIM
    gate_first = local_heads * DK

    def kernel(state_ref, reach_ref, zero_ref, gate_ref, norm_ref, out_ref, gated_ref):
        for h in range(local_heads):
            columns = slice(DV * h, DV * h + DV)
            out = zero_ref[h] + product(reach_ref[h], state_ref[h], 1, 0)
            normed = out * lax.rsqrt(jnp.mean(out * out, axis=-1, keepdims=True) + HEAD_EPSILON)
            out_ref[:, columns] = out
            gate = gate_ref[RIM:, gate_first + DV * h : gate_first + DV * h + DV]
            gated_ref[:, columns] = (normed * norm_ref[...] * jax.nn.silu(gate)).astype(
                jnp.bfloat16
            )

    vmem = pl.BlockSpec(memory_space=pltpu.VMEM)
    width = local_heads * DV
    return pl.pallas_call(
        kernel,
        in_specs=[vmem] * 5,
        out_specs=[vmem, vmem],
        out_shape=[
            jax.ShapeDtypeStruct((row_count, width), jnp.float32),
            jax.ShapeDtypeStruct((row_count, width), jnp.bfloat16),
        ],
        compiler_params=params(),
    )(entering_state, reach, zero_out, query_gate, norm_gain)


def mixer_gate_back(local_heads, d_gated, recurred, query_gate, norm_gain, reach):
    row_count = query_gate.shape[0] - RIM
    gate_first = local_heads * DK // DV

    def kernel(d_gated_ref, out_ref, gate_ref, norm_ref, reach_ref, d_out_ref, d_gate_ref, d_norm_ref, d_state_ref):
        out, gate, norm_row, d_gated_now = (
            out_ref[...], gate_ref[RIM:, :], norm_ref[...], d_gated_ref[...]
        )
        scale = lax.rsqrt(jnp.mean(out * out, axis=-1, keepdims=True) + HEAD_EPSILON)
        normed = out * scale
        logistic = jax.nn.sigmoid(gate)
        silu = gate * logistic
        d_norm = jnp.sum(d_gated_now * normed * silu, axis=0, keepdims=True)

        @pl.when(pl.program_id(0) == 0)
        def _():
            d_norm_ref[...] = jnp.zeros_like(d_norm_ref)

        d_norm_ref[0:1, :] = d_norm_ref[0:1, :] + d_norm
        d_gate_ref[...] = (
            d_gated_now * normed * norm_row * logistic * (1.0 + gate * (1.0 - logistic))
        ).astype(jnp.bfloat16)
        d_normed = d_gated_now * norm_row * silu
        d_out = scale * d_normed - (scale * scale * scale) * out * jnp.mean(
            d_normed * out, axis=-1, keepdims=True
        )
        d_out_ref[...] = d_out
        d_state_ref[0] = product(reach_ref[0], d_out, 0, 0).astype(jnp.bfloat16)

    width = local_heads * DV
    block = pl.BlockSpec((row_count, DV), lambda h: (0, h))
    return pl.pallas_call(
        kernel,
        grid=(local_heads,),
        in_specs=[
            block,
            block,
            pl.BlockSpec((RIM + row_count, DV), lambda h: (0, gate_first + h)),
            pl.BlockSpec((1, DV), lambda h: (0, 0)),
            pl.BlockSpec((1, row_count, DK), lambda h: (h, 0, 0)),
        ],
        out_specs=[
            block,
            block,
            pl.BlockSpec((8, DV), lambda h: (0, 0)),
            pl.BlockSpec((1, DK, DV), lambda h: (h, 0, 0)),
        ],
        out_shape=[
            jax.ShapeDtypeStruct((row_count, width), jnp.float32),
            jax.ShapeDtypeStruct((row_count, width), jnp.bfloat16),
            jax.ShapeDtypeStruct((8, DV), jnp.float32),
            jax.ShapeDtypeStruct((local_heads, DK, DV), jnp.bfloat16),
        ],
        compiler_params=params(),
    )(d_gated, recurred, query_gate, norm_gain, reach)


def conv_back(
    d_pre, extended, taps_ref, padded, d_block_ref, d_tail_ref, d_rim_ref, d_taps_ref, columns
):
    row_count = d_pre.shape[0]
    first = RIM - (KCONV - 1)
    padded[0:8, :] = jnp.zeros((8, d_pre.shape[1]), jnp.float32)
    padded[8 : 8 + row_count, :] = d_pre
    padded[8 + row_count : 16 + row_count, :] = jnp.zeros((8, d_pre.shape[1]), jnp.float32)
    total = None
    d_taps_ref[:, columns] = jnp.zeros((8, d_pre.shape[1]), jnp.float32)
    for tap in range(KCONV):
        start = KCONV - 1 - tap
        term = taps_ref[tap : tap + 1, columns] * padded[start : start + row_count + 8, :]
        total = term if total is None else total + term
        d_taps_ref[tap : tap + 1, columns] = jnp.sum(
            d_pre * extended[first + tap : first + tap + row_count, columns], axis=0, keepdims=True
        )
    d_rim_ref[:, columns] = total[0:8, :]
    d_block_ref[:, columns] = total[8:, :].astype(jnp.bfloat16)
    d_tail_ref[:, columns] = total[row_count:, :]


def mixer_back(
    local_heads, query_gate, value_key, query_taps, taps, decay_proj, scalars,
    solve, fresh, wy_keys, entering_state, d_recurred, d_leaving,
):
    row_count = value_key.shape[0] - RIM
    query, key, value, whole, scalar_spec = mixer_specs(local_heads, row_count)

    def kernel(
        pq, pk, pv, tq, tk, tv, decay_ref, scalars_ref,
        solve_ref, fresh_ref, wy_ref, enter_ref, d_out_ref, d_leave_ref,
        dq_ref, dk_ref, dv_ref, tail_q, tail_k, tail_v, rim_q, rim_k, rim_v,
        taps_q, taps_k, taps_v, d_decay_ref, d_scalars_ref,
        pad_q, pad_k, pad_v,
    ):
        @pl.when(pl.program_id(0) == 0)
        def _():
            d_decay_ref[...] = jnp.zeros_like(d_decay_ref)
            d_scalars_ref[...] = jnp.zeros_like(d_scalars_ref)

        for sub in range(HEADS_A_STEP):
            head = pl.program_id(0) * HEADS_A_STEP + sub
            narrow, wide = head_columns(sub)
            pre_q = convolved(pq, tq, narrow)
            pre_k = convolved(pk, tk, narrow)
            pre_v = convolved(pv, tv, wide)
            conv_q, conv_k = jax.nn.silu(pre_q), jax.nn.silu(pre_k)
            unit_q, scale_q = unit_rows(conv_q)
            queries = unit_q * DK ** (-0.5)
            key_rows, scale_k = unit_rows(conv_k)
            values = jax.nn.silu(pre_v)
            decay_in, rate, logs, beta, sums, within, row_ids, column_ids = decay_terms(
                head, local_heads, decay_ref, scalars_ref
            )
            strict = row_ids > column_ids
            grown = jnp.exp(sums)
            last = sums[row_count - 1 : row_count, :]
            tail = jnp.exp(last - sums)
            tail_keys = tail * key_rows
            gram = product(key_rows, key_rows, 1, 1, True)
            scores = jnp.where(strict, gram * within, 0.0)
            attention = product(queries, key_rows, 1, 1) * within
            enter, d_out, d_leave = enter_ref[sub], d_out_ref[:, wide], d_leave_ref[sub]
            update = fresh_ref[sub] - product(wy_ref[sub], enter, 1, 0)
            d_update = product(attention, d_out, 0, 0) + product(tail_keys, d_leave, 1, 0)
            d_right = product(solve_ref[sub], d_update, 0, 0, True)
            d_attention = product(d_out, update, 1, 1) * within
            d_system = -product(d_right, update, 1, 1)
            out_state = product(d_out, enter, 1, 1)
            right_state = product(d_right, enter, 1, 1)
            leave_update = product(update, d_leave, 1, 1)
            remainder = values - grown * product(key_rows, enter, 1, 0)
            d_values = beta * d_right
            d_beta = jnp.sum(d_right * remainder, axis=1, keepdims=True) + jnp.sum(
                d_system * scores, axis=1, keepdims=True
            )
            pair = beta * (d_system * scores)
            d_gram = jnp.where(strict, beta * d_system * within, 0.0)
            d_queries = grown * out_state + product(d_attention, key_rows, 1, 0)
            d_keys = (
                product(d_attention, queries, 0, 0)
                + product(d_gram, key_rows, 1, 0)
                + product(d_gram, key_rows, 0, 0)
                + tail * leave_update
                - (beta * grown) * right_state
            )
            both = pair + d_attention * product(queries, key_rows, 1, 1)
            tail_rows = jnp.sum(tail_keys * leave_update, axis=1, keepdims=True)
            diagonal = row_ids == column_ids
            columns = jnp.sum(both, axis=0, keepdims=True)
            d_sums = (
                jnp.sum(both, axis=1, keepdims=True)
                - jnp.sum(jnp.where(diagonal, columns, 0.0), axis=1, keepdims=True)
                + jnp.sum(out_state * (grown * queries), axis=1, keepdims=True)
                - jnp.sum(right_state * ((beta * grown) * key_rows), axis=1, keepdims=True)
                - tail_rows
            )
            d_last = jnp.exp(last) * jnp.sum(
                jnp.sum(d_leave * enter, axis=1, keepdims=True), axis=0, keepdims=True
            ) + jnp.sum(tail_rows, axis=0, keepdims=True)
            d_logs = d_last + jnp.sum(
                jnp.where(row_ids <= column_ids, to_row(d_sums, diagonal), 0.0), axis=1, keepdims=True
            )
            d_decay_in = d_logs * rate * jax.nn.sigmoid(decay_in)
            d_beta_in = d_beta * beta * (1.0 - beta)
            d_decay_ref[...] = (
                d_decay_ref[...]
                + put_lane(d_decay_in, head)
                + put_lane(d_beta_in, head + local_heads)
            )
            d_rate = jnp.sum(d_logs * logs, axis=0, keepdims=True)
            d_bias = jnp.sum(d_decay_in, axis=0, keepdims=True)
            d_scalars_ref[0:1, :] = d_scalars_ref[0:1, :] + put_lane(d_rate, head)
            d_scalars_ref[1:2, :] = d_scalars_ref[1:2, :] + put_lane(d_bias, head)

            def unit_back(d_unit, unit, scale):
                return scale * (d_unit - unit * jnp.sum(unit * d_unit, axis=1, keepdims=True))

            def silu_back(d_act, pre):
                logistic = jax.nn.sigmoid(pre)
                return d_act * logistic * (1.0 + pre * (1.0 - logistic))

            d_pre_q = silu_back(unit_back(d_queries * DK ** (-0.5), unit_q, scale_q), pre_q)
            conv_back(d_pre_q, pq, tq, pad_q.at[sub], dq_ref, tail_q, rim_q, taps_q, narrow)
            d_pre_k = silu_back(unit_back(d_keys, key_rows, scale_k), pre_k)
            conv_back(d_pre_k, pk, tk, pad_k.at[sub], dk_ref, tail_k, rim_k, taps_k, narrow)
            conv_back(
                silu_back(d_values, pre_v), pv, tv, pad_v.at[sub],
                dv_ref, tail_v, rim_v, taps_v, wide,
            )

    def blocks(rows):
        return [
            pl.BlockSpec((rows, HEADS_A_STEP * width), lambda h: (0, h)) for width in (DK, DK, DV)
        ]

    def shapes(rows, kind):
        return [
            jax.ShapeDtypeStruct((rows, local_heads * width), kind) for width in (DK, DK, DV)
        ]

    outs = pl.pallas_call(
        kernel,
        grid=(local_heads // HEADS_A_STEP,),
        in_specs=[each(RIM + row_count) for each in (query, key, value)]
        + [each(8) for each in (query, key, value)]
        + [
            whole,
            scalar_spec,
            per_head(row_count, row_count),
            per_head(row_count, DV),
            per_head(row_count, DK),
            per_head(DK, DV),
            pl.BlockSpec((row_count, HEADS_A_STEP * DV), lambda h: (0, h)),
            per_head(DK, DV),
        ],
        out_specs=blocks(row_count) + blocks(8) * 3 + [whole, scalar_spec],
        out_shape=shapes(row_count, jnp.bfloat16)
        + shapes(8, jnp.float32) * 3
        + [
            jax.ShapeDtypeStruct((row_count, 128), jnp.float32),
            jax.ShapeDtypeStruct((8, 128), jnp.float32),
        ],
        scratch_shapes=[
            pltpu.VMEM((HEADS_A_STEP, row_count + 16, DK), jnp.float32),
            pltpu.VMEM((HEADS_A_STEP, row_count + 16, DK), jnp.float32),
            pltpu.VMEM((HEADS_A_STEP, row_count + 16, DV), jnp.float32),
        ],
        compiler_params=params(),
    )(
        query_gate, value_key, value_key, query_taps, taps, taps, decay_proj, scalars,
        solve, fresh, wy_keys, entering_state, d_recurred, d_leaving,
    )
    joined = [
        (outs[3 * i], jnp.concatenate([outs[3 * i + 2], outs[3 * i + 1]], axis=1))
        for i in range(4)
    ]
    return (*joined, outs[12], outs[13])


LANES = 128
CHUNK = 32768
TILE = 16
CAPACITY_UNIT = 44
FIRST_GATHER = 24
FIRST_REDUCE = 16
SECOND_REDUCE = 24
SECOND_GATHER = 16
RIM = 16
TABLE = 1 << 16
VMEM_LIMIT = 48 * 1024 * 1024


def params(**kwargs):
    return pltpu.CompilerParams(vmem_limit_bytes=VMEM_LIMIT, **kwargs)


def piece_kinds(segments_list, piece_count, piece_size):
    kinds = np.ones(piece_count, np.int32)
    offset_now = 0
    for seg_name, row_count, col_count, seg_rate in segments_list:
        if offset_now >= (piece_count - 1) * piece_size:
            break
        tiles = col_count // LANES
        if tiles in (2, 4, 8, 16):
            first = offset_now // piece_size
            kinds[first : first + row_count * col_count // piece_size] = tiles
        offset_now += row_count * col_count
    return kinds


def pack_blocks(master, slot_kinds, kinds_used, first_slot, slot_count):
    piece_size = master.shape[1]
    chunks = piece_size // CHUNK
    rows = CHUNK // LANES
    first_block = first_slot // 8
    slot_blocks = pl.cdiv(slot_count, 8)

    def kernel(kinds_ref, master_ref, out_ref, scratch):
        first = (first_block + pl.program_id(0)) * 8
        for j in range(rows):
            scratch[8 * j : 8 * j + 8, :] = master_ref[:, LANES * j : LANES * j + LANES]
        for s in range(8):
            kind_now = kinds_ref[first + s]
            for kind in kinds_used:

                @pl.when(kind_now == kind)
                def _():
                    for tile in range(rows // TILE):
                        row_tile, column = divmod(tile, kind)
                        start = (row_tile * TILE * kind + column) * 8 + s
                        out_ref[s, TILE * tile : TILE * tile + TILE, :] = scratch[
                            pl.ds(start, TILE, stride=8 * kind), :
                        ].astype(jnp.bfloat16)

    return pl.pallas_call(
        kernel,
        grid_spec=pltpu.PrefetchScalarGridSpec(
            num_scalar_prefetch=1,
            grid=(slot_blocks, chunks),
            in_specs=[pl.BlockSpec((8, CHUNK), lambda i, j, kinds: (first_block + i, j))],
            out_specs=pl.BlockSpec((8, rows, LANES), lambda i, j, kinds: (i, j, 0)),
            scratch_shapes=[pltpu.VMEM((8 * rows, LANES), jnp.float32)],
        ),
        out_shape=jax.ShapeDtypeStruct((slot_count, piece_size // LANES, LANES), jnp.bfloat16),
        compiler_params=params(),
    )(slot_kinds, master)


def reserve(shape, kind):
    def kernel(out_ref):
        pass

    return pl.pallas_call(
        kernel,
        out_specs=pl.BlockSpec(memory_space=pl.ANY),
        out_shape=jax.ShapeDtypeStruct(shape, kind),
        compiler_params=params(),
    )()


def assemble(tables, matrices, step_rows, rows_in=None):
    piece_rows = tables[0].shape[1]
    plans = []
    first_block, first_column = 0, 0
    for positions, col_count in matrices:
        tiles = col_count // LANES
        blocks = step_rows * tiles // piece_rows
        plans.append((first_block, first_column, tiles, blocks))
        first_block += blocks
        first_column += col_count
    blocks_a_step, width = first_block, first_column
    steps = matrices[0][0].shape[0] // plans[0][3]
    order = jnp.concatenate(
        [
            positions.reshape(steps, plan[3])
            for (positions, col_count), plan in zip(matrices, plans)
        ],
        axis=1,
    ).reshape(-1)
    uneven = [plan for plan in plans if piece_rows * plan[3] != step_rows * plan[2] or plan[2] not in (2, 4, 8, 16)]
    multiply = rows_in is not None

    def kernel(order_ref, *refs):
        if multiply:
            rows_ref, refs = refs[0], refs[1:]
        table_refs, refs = refs[: len(tables)], refs[len(tables) :]
        out_ref, refs = refs[0], refs[1:]
        if multiply:
            product_ref, refs = refs[0], refs[1:]
        buffer, sem, scratch = refs
        g = pl.program_id(0)
        slot = lax.rem(g, 2)

        def start(step, which):
            def one(j, carry):
                position = order_ref[step * blocks_a_step + j]
                for number, table_ref in enumerate(table_refs):

                    @pl.when(position // TABLE == number)
                    def _():
                        pltpu.make_async_copy(
                            table_ref.at[lax.rem(position, TABLE)],
                            buffer.at[which, j],
                            sem.at[which],
                        ).start()

                return carry

            lax.fori_loop(0, blocks_a_step, one, 0)

        @pl.when(g == 0)
        def _():
            start(0, 0)

        @pl.when(g + 1 < steps)
        def _():
            start(g + 1, 1 - slot)

        pltpu.make_async_copy(buffer.at[slot], buffer.at[slot], sem.at[slot]).wait()
        for plan in plans:
            first, left, tiles, blocks = plan
            if plan in uneven:
                for j in range(blocks):
                    scratch[piece_rows * j : piece_rows * j + piece_rows, :] = buffer[
                        slot, first + j
                    ].astype(jnp.float32)
                for c in range(tiles):
                    out_ref[:, left + LANES * c : left + LANES * c + LANES] = scratch[
                        pl.ds(c, step_rows, stride=tiles), :
                    ].astype(jnp.bfloat16)
                continue
            for j in range(blocks):
                for tile in range(piece_rows // TILE):
                    row_tile, column = divmod(tile, tiles)
                    row = piece_rows // tiles * j + TILE * row_tile
                    column = left + LANES * column
                    out_ref[row : row + TILE, column : column + LANES] = buffer[
                        slot, first + j, TILE * tile : TILE * tile + TILE, :
                    ]
        if multiply:
            part = jnp.dot(rows_ref[...], out_ref[...], preferred_element_type=jnp.float32)

            @pl.when(g == 0)
            def _():
                product_ref[...] = part

            @pl.when(g > 0)
            def _():
                product_ref[...] = product_ref[...] + part

    anywhere = pl.BlockSpec(memory_space=pl.ANY)
    in_specs = [anywhere for table in tables]
    operands = list(tables)
    out_specs = [pl.BlockSpec((step_rows, width), lambda g, order: (g, 0))]
    out_shape = [jax.ShapeDtypeStruct((steps * step_rows, width), jnp.bfloat16)]
    if multiply:
        row_count = rows_in.shape[0]
        in_specs.insert(0, pl.BlockSpec((row_count, step_rows), lambda g, order: (0, g)))
        operands.insert(0, rows_in)
        out_specs.append(pl.BlockSpec((row_count, width), lambda g, order: (0, 0)))
        out_shape.append(jax.ShapeDtypeStruct((row_count, width), jnp.float32))
    scratch_rows = max([plan[3] * piece_rows for plan in uneven], default=8)
    return pl.pallas_call(
        kernel,
        grid_spec=pltpu.PrefetchScalarGridSpec(
            num_scalar_prefetch=1,
            grid=(steps,),
            in_specs=in_specs,
            out_specs=out_specs,
            scratch_shapes=[
                pltpu.VMEM((2, blocks_a_step, piece_rows, LANES), jnp.bfloat16),
                pltpu.SemaphoreType.DMA((2,)),
                pltpu.VMEM((scratch_rows, LANES), jnp.float32),
            ],
        ),
        out_shape=out_shape,
        cost_estimate=pl.CostEstimate(
            flops=2 * steps * step_rows * width * (rows_in.shape[0] if multiply else 0),
            bytes_accessed=4 * steps * step_rows * width,
            transcendentals=0,
        ),
        compiler_params=params(),
    )(order, *operands)


def spread_products(my_part, parts, pairs):
    row_count = pairs[0][0][0].shape[0]
    total = pairs[0][1].shape[0 if pairs[0][2] else 1]
    width = total // parts

    def kernel(part_ref, *refs):
        ins, outs = list(refs[:-parts]), refs[-parts:]
        for m in range(parts):
            first = pl.multiple_of((part_ref[0] ^ m) * width, width)
            result, place = None, 0
            for lefts, right, transposed in pairs:
                left_refs, right_ref = ins[place : place + len(lefts)], ins[place + len(lefts)]
                place += len(lefts) + 1
                depth = 0
                for left_ref in left_refs:
                    inner = slice(depth, depth + left_ref.shape[1])
                    depth += left_ref.shape[1]
                    if transposed:
                        block, axis = right_ref[pl.ds(first, width), inner], 1
                    else:
                        block, axis = right_ref[inner, pl.ds(first, width)], 0
                    part = lax.dot_general(
                        left_ref[...],
                        block,
                        (((1,), (axis,)), ((), ())),
                        preferred_element_type=jnp.float32,
                    )
                    result = part if result is None else result + part
            outs[m][...] = result.astype(jnp.bfloat16)

    vmem = pl.BlockSpec(memory_space=pltpu.VMEM)
    flat = [array for lefts, right, transposed in pairs for array in (*lefts, right)]
    return pl.pallas_call(
        kernel,
        in_specs=[pl.BlockSpec(memory_space=pltpu.SMEM)] + [vmem] * len(flat),
        out_specs=[vmem] * parts,
        out_shape=[jax.ShapeDtypeStruct((row_count, width), jnp.bfloat16)] * parts,
        cost_estimate=pl.CostEstimate(
            flops=2 * row_count * sum(pair[1].size for pair in pairs),
            bytes_accessed=2 * sum(pair[1].size for pair in pairs),
            transcendentals=0,
        ),
        compiler_params=params(),
    )(my_part, *flat)


def exchange(blocks, axis):
    devices = lax.axis_size(axis)
    return [blocks[0]] + [
        lax.ppermute(blocks[m], axis, [(i, i ^ m) for i in range(devices)])
        for m in range(1, devices)
    ]


def total_of(blocks):
    total = blocks[0].astype(jnp.float32)
    for block in blocks[1:]:
        total = total + block.astype(jnp.float32)
    return total


def sum_over(block, axis):
    return total_of(exchange([block] * lax.axis_size(axis), axis))


def in_order(blocks, my_part, axis):
    stacked = jnp.stack(blocks)
    return jnp.concatenate(
        [
            lax.dynamic_index_in_dim(stacked, my_part ^ j, 0, keepdims=False)
            for j in range(len(blocks))
        ],
        axis=axis,
    )


def gather_states(block):
    devices = lax.axis_size("seq")
    if devices != 8:
        return lax.all_gather(block, "seq", axis=0, tiled=False), jnp.zeros((1,), jnp.int32)

    def moved(array, mask):
        return lax.ppermute(array, "seq", [(i, i ^ mask) for i in range(devices)])

    chips = [block] + [moved(block, mask) for mask in (2, 4, 6)]
    pairs = [(chip, moved(chip, 1)) for chip in chips]
    rows = jnp.stack([array for pair in pairs for array in pair])
    return rows, lax.axis_index("seq").astype(jnp.int32).reshape(1)


def weight_grad_blocks(left_t, right, right_block, col_count, positions, tables, blocks_a_step):
    row_total, depth = left_t.shape
    tiles = col_count // LANES
    piece_rows = 512
    even = tiles in (2, 4, 8, 16)
    step_rows = blocks_a_step * piece_rows // tiles
    steps = row_total // step_rows

    def kernel(positions_ref, left_ref, right_ref, *refs):
        table_refs = refs[len(tables) : 2 * len(tables)]
        product, staged, sem = refs[2 * len(tables) :]
        g = pl.program_id(0)
        slot = lax.rem(g, 2)

        def settle(which):
            pltpu.make_async_copy(staged.at[which], staged.at[which], sem.at[which]).wait()

        @pl.when(g >= 2)
        def _():
            settle(slot)

        left = left_ref[...]
        if even:
            product[...] = jnp.dot(left, right_ref[...], preferred_element_type=jnp.float32)
            for tile in range(step_rows // TILE * tiles):
                row_tile, column = divmod(tile, tiles)
                block, row = divmod(TILE * tile, piece_rows)
                staged[slot, block, row : row + TILE, :] = product[
                    TILE * row_tile : TILE * row_tile + TILE, LANES * column : LANES * column + LANES
                ].astype(jnp.bfloat16)
        else:
            for c in range(0, tiles, 2):
                width = min(2, tiles - c)
                part = jnp.dot(
                    left,
                    right_ref[:, LANES * c : LANES * (c + width)],
                    preferred_element_type=jnp.float32,
                )
                for w in range(width):
                    product[pl.ds(c + w, step_rows, stride=tiles), :] = part[
                        :, LANES * w : LANES * w + LANES
                    ]
            for block in range(blocks_a_step):
                staged[slot, block] = product[
                    piece_rows * block : piece_rows * block + piece_rows, :
                ].astype(jnp.bfloat16)
        for block in range(blocks_a_step):
            position = positions_ref[g * blocks_a_step + block]

            for number, table_ref in enumerate(table_refs):

                @pl.when(position // TABLE == number)
                def _():
                    pltpu.make_async_copy(
                        staged.at[slot, block],
                        table_ref.at[lax.rem(position, TABLE)],
                        sem.at[slot],
                    ).start()

        @pl.when(g == steps - 1)
        def _():
            settle(slot)
            if steps > 1:
                settle(1 - slot)

    anywhere = pl.BlockSpec(memory_space=pl.ANY)
    in_specs = [
        pl.BlockSpec((step_rows, depth), lambda g, positions: (g, 0)),
        pl.BlockSpec((depth, col_count), lambda g, positions: (0, right_block)),
    ] + [anywhere for table in tables]
    product_shape = (step_rows, col_count) if even else (step_rows * tiles, LANES)
    return pl.pallas_call(
        kernel,
        grid_spec=pltpu.PrefetchScalarGridSpec(
            num_scalar_prefetch=1,
            grid=(steps,),
            in_specs=in_specs,
            out_specs=[anywhere for table in tables],
            scratch_shapes=[
                pltpu.VMEM(product_shape, jnp.float32),
                pltpu.VMEM((2, blocks_a_step, piece_rows, LANES), jnp.bfloat16),
                pltpu.SemaphoreType.DMA((2,)),
            ],
        ),
        out_shape=[jax.ShapeDtypeStruct(table.shape, table.dtype) for table in tables],
        input_output_aliases={3 + i: i for i in range(len(tables))},
        cost_estimate=pl.CostEstimate(
            flops=2 * row_total * depth * col_count,
            bytes_accessed=2 * row_total * col_count,
            transcendentals=0,
        ),
        compiler_params=params(),
    )(positions, left_t, right, *tables)


def optimizer_update(
    sources, slot_sources, slot_rows, slot_kinds, kinds_used, slot_masks, small_rates,
    master, moment_one, moment_two, first_block, earlier,
):
    capacity, piece_size = master.shape
    chunks = piece_size // CHUNK
    rows = CHUNK // LANES
    slot_blocks = pl.cdiv(capacity, 8)
    steps = slot_blocks * chunks

    def steps_here(first):
        return (first if earlier else slot_blocks - first) * chunks

    def place(step, first):
        now = jnp.minimum(step, jnp.maximum(steps_here(first) - 1, 0))
        block, chunk = now // chunks, lax.rem(now, chunks)
        return (block if earlier else slot_blocks - 1 - block), chunk

    def kernel(first_ref, kinds_ref, sources_ref, rows_ref, *refs):
        source_refs, refs = refs[: len(sources)], refs[len(sources) :]
        masks_ref, small_ref, master_ref, one_ref, two_ref = refs[:5]
        refs = refs[5 + len(earlier) :]
        grad_out, master_out, one_out, two_out, low_out, scratch, buffer, sem = refs
        step = pl.program_id(0)
        count = jnp.maximum(steps_here(first_ref[0]), 1)
        first = place(step, first_ref[0])[0] * 8
        slot = lax.rem(step, 2)

        def start(step, which):
            block, chunk = place(step, first_ref[0])
            for s in range(8):
                for i, source_ref in enumerate(source_refs):

                    @pl.when(sources_ref[block * 8 + s] == i)
                    def _():
                        pltpu.make_async_copy(
                            source_ref.at[
                                rows_ref[block * 8 + s],
                                pl.ds(pl.multiple_of(chunk * rows, rows), rows),
                            ],
                            buffer.at[which, s],
                            sem.at[which],
                        ).start()

                @pl.when(sources_ref[block * 8 + s] >= len(sources))
                def _():
                    pltpu.make_async_copy(
                        source_refs[0].at[0, pl.ds(0, rows)], buffer.at[which, s], sem.at[which]
                    ).start()

        @pl.when(step == 0)
        def _():
            start(0, 0)

        @pl.when(step + 1 < count)
        def _():
            start(step + 1, 1 - slot)

        @pl.when(step < count)
        def _():
            pltpu.make_async_copy(buffer.at[slot], buffer.at[slot], sem.at[slot]).wait()
            for s in range(8):
                kind_now = kinds_ref[first + s]
                for kind in kinds_used:

                    @pl.when(kind_now == kind)
                    def _():
                        for tile in range(rows // TILE):
                            row_tile, column = divmod(tile, kind)
                            start_row = (row_tile * TILE * kind + column) * 8 + s
                            scratch[pl.ds(start_row, TILE, stride=8 * kind), :] = buffer[
                                slot, s, TILE * tile : TILE * tile + TILE, :
                            ].astype(jnp.float32)

            present = masks_ref[0] > 0.5
            is_small = masks_ref[1] > 0.5
            rate_rows = masks_ref[2]
            for j in range(rows):
                lanes = slice(LANES * j, LANES * j + LANES)
                grad = jnp.where(present, scratch[8 * j : 8 * j + 8, :], 0.0)
                rate = jnp.where(is_small, small_ref[:, lanes], rate_rows)
                master_now = master_ref[:, lanes]
                one_new = BETA_ONE * one_ref[:, lanes] + (1.0 - BETA_ONE) * grad
                two_new = BETA_TWO * two_ref[:, lanes] + (1.0 - BETA_TWO) * grad * grad
                first_hat = one_new / (1.0 - BETA_ONE**STEP)
                second_hat = two_new / (1.0 - BETA_TWO**STEP)
                master_new = master_now - rate * (
                    first_hat / (jnp.sqrt(second_hat) + ADAM_EPSILON) + WEIGHT_DECAY * master_now
                )
                grad_out[:, lanes] = grad
                master_out[:, lanes] = master_new
                one_out[:, lanes] = one_new
                two_out[:, lanes] = two_new
                low_out[:, lanes] = master_new.astype(jnp.bfloat16)

    state_spec = pl.BlockSpec((8, CHUNK), lambda t, first, *tables: place(t, first[0]))
    anywhere = pl.BlockSpec(memory_space=pl.ANY)
    wide = jax.ShapeDtypeStruct((capacity, piece_size), jnp.float32)
    operands = [*sources, slot_masks, small_rates, master, moment_one, moment_two, *earlier]
    return pl.pallas_call(
        kernel,
        grid_spec=pltpu.PrefetchScalarGridSpec(
            num_scalar_prefetch=4,
            grid=(steps,),
            in_specs=[anywhere for source in sources]
            + [
                pl.BlockSpec((3, 8, LANES), lambda t, first, *tables: (0, place(t, first[0])[0], 0)),
                pl.BlockSpec((1, CHUNK), lambda t, first, *tables: (0, place(t, first[0])[1])),
                state_spec,
                state_spec,
                state_spec,
            ]
            + [anywhere for array in earlier],
            out_specs=[state_spec] * 5,
            scratch_shapes=[
                pltpu.VMEM((8 * rows, LANES), jnp.float32),
                pltpu.VMEM((2, 8, rows, LANES), jnp.bfloat16),
                pltpu.SemaphoreType.DMA((2,)),
            ],
        ),
        out_shape=[wide] * 4 + [jax.ShapeDtypeStruct((capacity, piece_size), jnp.bfloat16)],
        input_output_aliases={
            4 + len(operands) - len(earlier) + i: i for i in range(len(earlier))
        },
        cost_estimate=pl.CostEstimate(
            flops=20 * master.size,
            bytes_accessed=16 * master.size,
            transcendentals=2 * master.size,
        ),
        compiler_params=params(),
    )(first_block, slot_kinds, slot_sources, slot_rows, *operands)


def weight_grad(left, right):
    return jnp.einsum("td,tc->dc", left, right, preferred_element_type=jnp.float32)


def back_product(grad_rows, weight):
    return jnp.dot(grad_rows, weight.T, preferred_element_type=jnp.float32)


def gather_rest(packed, first, trips, most, extra_step):
    devices = lax.axis_size("seq")
    rows = devices * extra_step
    room = reserve((most * rows,) + packed.shape[1:], packed.dtype)

    def more(trip, table):
        part = lax.dynamic_slice_in_dim(packed, first + trip * extra_step, extra_step)
        part = lax.all_gather(part, "seq", axis=0, tiled=True)
        return lax.dynamic_update_slice_in_dim(table, part, trip * rows, axis=0)

    return lax.fori_loop(0, trips, more, room)


def reduce_rest(rest, trips, most, extra_step):
    devices = lax.axis_size("seq")
    rows = devices * extra_step
    room = reserve((most * extra_step,) + rest.shape[1:], rest.dtype)

    def more(trip, table):
        part = lax.dynamic_slice_in_dim(rest, trip * rows, rows)
        part = lax.psum_scatter(part, "seq", scatter_dimension=0, tiled=True)
        return lax.dynamic_update_slice_in_dim(table, part, trip * extra_step, axis=0)

    return lax.fori_loop(0, trips, more, room)


def bring_spilled(reduced, first, trips, most, step):
    devices = lax.axis_size("seq")
    room = reserve((most * step,) + reduced.shape[1:], reduced.dtype)

    def more(trip, table):
        part = lax.dynamic_slice_in_dim(reduced, first + trip * step, step)
        part = lax.ppermute(part, "seq", [(i, i ^ 1) for i in range(devices)])
        return lax.dynamic_update_slice_in_dim(table, part, trip * step, axis=0)

    return lax.fori_loop(0, trips, more, room)


def on_device(inputs, cotangent, owners, master, moment_one, moment_two):
    head_parts = lax.axis_size("head")
    seq_parts = lax.axis_size("seq")
    local_heads = HEADS // head_parts
    capacity, piece_size = master.shape
    piece_count = owners.shape[0]
    row_count = inputs.shape[0]
    rim_width = KCONV - 1
    segments_list = shard_layout(local_heads, head_parts)
    columns = {name: c for name, r, c, rate in segments_list}
    counts = {name: r * c // piece_size for name, r, c, rate in segments_list[:8]}
    firsts = dict(zip(counts, np.cumsum([0] + list(counts.values())).tolist()))
    mixer_count = firsts["wgate"]
    big_count = piece_count - 1
    my_head = lax.axis_index("head").astype(jnp.int32)
    my_index = lax.axis_index("seq").astype(jnp.int32)
    my_head_row, my_index_row = my_head.reshape(1), my_index.reshape(1)

    onehot = (owners[:, None] == jnp.arange(seq_parts, dtype=jnp.int32)[None, :]).astype(jnp.int32)
    ranks = jnp.sum((jnp.cumsum(onehot, axis=0) - onehot) * onehot, axis=1)
    mixer_held = jnp.sum(onehot[:mixer_count], axis=0)
    mlp_held = jnp.sum(onehot[mixer_count:big_count], axis=0)
    padded = capacity + -capacity % 8
    small_rank = ranks[big_count]
    big_owners, big_ranks = owners[:big_count], ranks[:big_count]

    def rest_row(over, owner):
        return over // extra_step * (seq_parts * extra_step) + owner * extra_step + over % extra_step

    early = -(-capacity * FIRST_GATHER // (8 * CAPACITY_UNIT)) * 8
    late = capacity - early
    late_room = min(late, -(-capacity * SECOND_GATHER // CAPACITY_UNIT))
    extra_step = 2 if late % 2 == 0 else 1
    most_gather = -(-late // extra_step)
    trips_gather = jnp.maximum(-(-(jnp.max(mixer_held) - early) // extra_step), 0)
    early_row = big_owners * early + big_ranks
    mixer_fetch = jnp.where(
        big_ranks < early, early_row, TABLE + rest_row(big_ranks - early, big_owners)
    )
    neighbours = np.arange(seq_parts) ^ 1
    late_held = jnp.maximum(mixer_held + mlp_held - early, 0)
    late_spare = jnp.maximum(late_room - late_held[neighbours], 0)
    late_over = jnp.maximum(late_held - late_room, 0)
    trips_late = -(-jnp.max(jnp.maximum(late_over - late_spare, 0)) // extra_step)
    spare_there = jnp.sum(onehot[:big_count] * late_spare[None, :], axis=1)
    past = big_ranks - early - late_room
    rest_trip = (past - spare_there) // extra_step
    rest_start = late_room + spare_there + rest_trip * extra_step
    rest_start = jnp.minimum(rest_start, late - extra_step)
    mlp_fetch = jnp.where(
        big_ranks < early,
        TABLE + early_row,
        jnp.where(
            past < 0,
            big_owners * late_room + big_ranks - early,
            jnp.where(
                past < spare_there,
                (big_owners ^ 1) * late_room + late_room - spare_there + past,
                2 * TABLE
                + rest_trip * (seq_parts * extra_step)
                + big_owners * extra_step
                + big_ranks - early - rest_start,
            ),
        ),
    )
    first_room = -(-capacity * FIRST_REDUCE // CAPACITY_UNIT)
    second_room = -(-capacity * SECOND_REDUCE // CAPACITY_UNIT)
    most_reduce = -(-(capacity - second_room) // extra_step)
    second_held = mixer_held + jnp.maximum(mlp_held - first_room, 0)
    second_there = jnp.sum(onehot[:big_count] * second_held[None, :], axis=1)
    room_there = jnp.maximum(second_room - second_held[neighbours], 0)
    over_held = jnp.maximum(second_held - second_room, 0)
    spill_step = min(4, second_room)
    most_spill = -(-min(second_room, capacity - second_room) // spill_step)
    trips_spill = -(-jnp.max(jnp.minimum(over_held, room_there)) // spill_step)
    trips_reduce = -(-jnp.max(jnp.maximum(over_held - room_there, 0)) // extra_step)
    second_over = big_ranks - second_room
    spare = jnp.sum(onehot[:big_count] * room_there[None, :], axis=1)
    store = jnp.where(
        big_ranks >= second_there,
        big_owners * first_room + big_ranks - second_there,
        jnp.where(
            second_over < 0,
            TABLE + big_owners * second_room + big_ranks,
            jnp.where(
                second_over < spare,
                TABLE + (big_owners ^ 1) * second_room + (second_room - spare) + second_over,
                2 * TABLE + rest_row(second_over - spare, big_owners),
            ),
        ),
    )
    small_owner = owners[big_count]

    def spots(table, name):
        return table[firsts[name] : firsts[name] + counts[name]]

    my_spare_here = room_there[my_index ^ 1]
    my_mixer = mixer_held[my_index]
    my_mlp = mlp_held[my_index]
    my_count = my_mixer + my_mlp
    slot_ids = jnp.arange(padded, dtype=jnp.int32)
    mine = owners == my_index
    matches = (mine[None, :] & (ranks[None, :] == slot_ids[:, None])).astype(jnp.int32)
    kind_table = piece_kinds(segments_list, piece_count, piece_size)
    piece_rates, small_rates = rate_parts(segments_list, piece_count, piece_size)
    present = jnp.sum(matches, axis=1)
    slot_kinds = 1 + jnp.sum(matches * jnp.asarray(kind_table - 1)[None, :], axis=1)
    slot_rates = PAD_RATE + jnp.sum(
        matches.astype(jnp.float32) * jnp.asarray(piece_rates - np.float32(PAD_RATE))[None, :], axis=1
    )
    is_small = matches[:, big_count]
    kinds_used = sorted(set(kind_table.tolist()) | {1})

    small_rows = -(-sum(r * c for name, r, c, rate in segments_list[8:]) // (TILE * LANES)) * TILE
    gain_width = D // head_parts
    norm_width = DV // head_parts
    gain_first = sum(r * c for name, r, c, rate in segments_list[8:14])
    my_small = lax.dynamic_slice(master, (small_rank, 0), (1, small_rows * LANES))
    my_small = my_small.astype(jnp.bfloat16)
    gains = my_small[:, gain_first : gain_first + 2 * gain_width + norm_width]
    gains = in_order(exchange([gains] * head_parts, "head"), my_head, 0)
    gains = jnp.concatenate(
        [
            gains[:, :gain_width].reshape(1, D),
            gains[:, gain_width : 2 * gain_width].reshape(1, D),
            gains[:, 2 * gain_width :].reshape(1, DV),
        ],
        axis=1,
    )
    rows_of_piece = piece_size // LANES
    small_width = small_rows * LANES
    small_part = jnp.concatenate([my_small, gains], axis=1).reshape(-1, LANES)
    small_table, small_base = gather_states(small_part)
    input_blocks = exchange([inputs] * head_parts, "head")
    early_part = pack_blocks(master, slot_kinds, kinds_used, 0, early)
    early_table = lax.all_gather(early_part, "seq", axis=0, tiled=True)
    late_part = pack_blocks(master, slot_kinds, kinds_used, early, late)
    late_send = late_part[:late_room]
    if late_room < late:
        guests = lax.ppermute(
            late_part[late_room:], "seq", [(i, i ^ 1) for i in range(seq_parts)]
        )
        late_send = lax.dynamic_update_slice_in_dim(
            late_part, guests, late_held[my_index], axis=0
        )[:late_room]
    back_blocks = exchange([cotangent] * head_parts, "head")
    rows_full = in_order(input_blocks, my_head, 1)
    back_full = in_order(back_blocks, my_head, 1)
    small_flat = lax.dynamic_index_in_dim(
        small_table, small_owner ^ small_base[0], axis=0, keepdims=False
    ).reshape(-1)
    by_name, small_used = unpack(small_flat, segments_list[8:])
    gains = small_flat[small_width:].astype(jnp.float32)[None, :]
    gain_one, gain_two, norm_row = gains[:, :D], gains[:, D : 2 * D], gains[:, 2 * D :]
    gain_one_mine = by_name["gainone"].astype(jnp.float32)
    gain_two_mine = by_name["gaintwo"].astype(jnp.float32)

    rows_wide = rows_full.astype(jnp.float32)
    scale_one = lax.rsqrt(jnp.mean(rows_wide * rows_wide, axis=-1, keepdims=True) + NORM_EPSILON)
    normed = (rows_wide * scale_one * gain_one).astype(jnp.bfloat16)
    normed_ext = jnp.concatenate([shifted(normed[row_count - RIM :], "seq", 1), normed], axis=0)

    decay_weight = jnp.pad(by_name["wab"], ((0, 0), (0, LANES - 2 * local_heads)))
    decay_proj = jnp.dot(normed, decay_weight, preferred_element_type=jnp.float32)
    taps = jnp.concatenate([by_name["cv"], by_name["ck"]], axis=1)
    taps = jnp.pad(taps.astype(jnp.float32), ((0, 8 - KCONV), (0, 0)))
    query_taps = jnp.pad(by_name["cq"].astype(jnp.float32), ((0, 8 - KCONV), (0, 0)))
    scalars = jnp.pad(
        jnp.concatenate([by_name["alog"], by_name["dtbias"]], axis=0).astype(jnp.float32),
        ((0, 6), (0, LANES - local_heads)),
    )

    beside = (
        trips_gather, late_part, late_send, normed, normed_ext, scale_one, decay_proj, decay_weight, taps, query_taps, scalars,
        back_full, mixer_fetch, mlp_fetch, store, gain_two, norm_row,
    )
    early_table, beside = lax.optimization_barrier((early_table, beside))
    (
        trips_now, late_part, late_send, normed, normed_ext, scale_one, decay_proj, decay_weight, taps, query_taps, scalars,
        back_full, mixer_fetch, mlp_fetch, store, gain_two, norm_row,
    ) = beside
    mixer_rest = gather_rest(late_part, 0, trips_now, most_gather, extra_step)
    late_table = lax.all_gather(late_send, "seq", axis=0, tiled=True)

    value_key_weights, value_key = assemble(
        [early_table, mixer_rest],
        [(spots(mixer_fetch, name), columns[name]) for name in ("wv", "wk")],
        512,
        normed_ext,
    )
    solve, fresh, wy_keys, handoff = mixer_local(
        local_heads, value_key, taps, decay_proj, scalars
    )
    query_gate_weights, query_gate = assemble(
        [early_table, mixer_rest],
        [(spots(mixer_fetch, name), columns[name]) for name in ("wq", "wg")],
        512,
        normed_ext,
    )
    reach, zero_out = mixer_reach(
        local_heads, query_gate, value_key, query_taps, taps, decay_proj, scalars, fresh, wy_keys
    )
    (out_weights,) = assemble(
        [early_table, mixer_rest], [(spots(mixer_fetch, "wo"), columns["wo"])], 256
    )
    entering_state, kept_states, beside = entering(
        local_heads,
        my_index_row,
        handoff,
        (query_gate_weights, query_gate, reach, zero_out, out_weights),
    )
    query_gate_weights, query_gate, reach, zero_out, out_weights = beside
    recurred, gated_low = mixer_out(
        local_heads, entering_state, reach, zero_out, query_gate, norm_row
    )
    mixed_parts = exchange(
        spread_products(my_head_row, head_parts, [((gated_low,), out_weights, False)]), "head"
    )
    mixed = total_of(mixed_parts)
    inputs_wide = inputs.astype(jnp.float32)
    residual = inputs_wide + mixed
    resid_low = residual.astype(jnp.bfloat16)

    resid_blocks = exchange([resid_low] * head_parts, "head")
    trips_now, late_table = lax.optimization_barrier((trips_late, late_table))
    late_rest = gather_rest(
        late_part, late_room + late_spare[my_index], trips_now, most_gather, extra_step
    )
    mlp_tables = [late_table, early_table, late_rest]
    (down_weights,) = assemble(
        mlp_tables, [(spots(mlp_fetch, "wdown"), columns["wdown"])], 352
    )
    (mlp_weights,) = assemble(
        mlp_tables,
        [(spots(mlp_fetch, name), columns[name]) for name in ("wgate", "wup")],
        512,
    )
    resid_blocks, down_weights, mlp_weights = lax.optimization_barrier(
        (resid_blocks, down_weights, mlp_weights)
    )
    resid_full = in_order(resid_blocks, my_head, 1).astype(jnp.float32)
    scale_two = lax.rsqrt(jnp.mean(resid_full * resid_full, axis=-1, keepdims=True) + NORM_EPSILON)
    hidden_in = (resid_full * scale_two * gain_two).astype(jnp.bfloat16)
    gate_up = jnp.dot(hidden_in, mlp_weights, preferred_element_type=jnp.float32)
    hidden_width = columns["wgate"]
    gate_mlp, up_mlp = gate_up[:, :hidden_width], gate_up[:, hidden_width:]
    logistic_output_multiplier = jax.nn.sigmoid(gate_mlp)
    silu_gate = gate_mlp * logistic_output_multiplier
    hidden = (silu_gate * up_mlp).astype(jnp.bfloat16)
    mlp_blocks = spread_products(my_head_row, head_parts, [((hidden,), down_weights, False)])
    d_hidden = back_product(back_full, down_weights)
    d_gate_mlp = (
        d_hidden
        * up_mlp
        * logistic_output_multiplier
        * (1.0 + gate_mlp * (1.0 - logistic_output_multiplier))
    ).astype(jnp.bfloat16)
    d_up_mlp = (d_hidden * silu_gate).astype(jnp.bfloat16)
    def store_grad(tables, name, left_t, right, right_block, blocks_a_step):
        return weight_grad_blocks(
            left_t, right, right_block, columns[name], spots(store, name), tables, blocks_a_step
        )

    grad_tables = [
        reserve((rows, rows_of_piece, LANES), jnp.bfloat16)
        for rows in (
            seq_parts * first_room,
            seq_parts * second_room,
            most_reduce * seq_parts * extra_step,
        )
    ]
    grad_tables = store_grad(grad_tables, "wdown", hidden.T, back_full, 0, 11)
    hidden_in_t = hidden_in.T
    grad_tables = store_grad(grad_tables, "wgate", hidden_in_t, d_gate_mlp, 0, 11)
    grad_tables = store_grad(grad_tables, "wup", hidden_in_t, d_up_mlp, 0, 11)
    grad_tables, d_gate_mlp, d_up_mlp = lax.optimization_barrier(
        (grad_tables, d_gate_mlp, d_up_mlp)
    )
    d_hidden_parts = exchange(
        spread_products(my_head_row, head_parts, [((d_gate_mlp, d_up_mlp), mlp_weights, True)]), "head"
    )
    first_reduced = lax.psum_scatter(grad_tables[0], "seq", scatter_dimension=0, tiled=True)
    grad_tables = grad_tables[1:]
    store = store - TABLE
    d_hidden_mine = total_of(d_hidden_parts)
    mlp_out = total_of(exchange(mlp_blocks, "head"))
    block_out = (residual + mlp_out).astype(jnp.bfloat16)

    resid_mine = resid_low.astype(jnp.float32)
    d_hidden_low = d_hidden_mine.astype(jnp.bfloat16)
    dot_mine = jnp.sum(d_hidden_mine * gain_two_mine * resid_mine, axis=-1)
    d_hidden_blocks = exchange([d_hidden_low] * head_parts, "head")
    dot_two = sum_over(dot_mine.reshape(-1, LANES), "head").reshape(row_count, 1)
    grad_gaintwo = jnp.sum(d_hidden_mine * resid_mine * scale_two, axis=0)
    d_resid = (
        cotangent.astype(jnp.float32)
        + scale_two * d_hidden_mine * gain_two_mine
        - scale_two**3 / D * resid_mine * dot_two
    )
    d_hidden_full = in_order(d_hidden_blocks, my_head, 1).astype(jnp.float32)
    back_mix_full = (
        back_full.astype(jnp.float32)
        + scale_two * d_hidden_full * gain_two
        - scale_two**3 / D * resid_full * dot_two
    ).astype(jnp.bfloat16)

    d_gated = back_product(back_mix_full, out_weights)
    d_recurred, d_gate, norm_grad, d_entering = mixer_gate_back(
        local_heads, d_gated, recurred, query_gate, norm_row, reach
    )
    normed_t = normed.T
    grad_tables = store_grad(grad_tables, "wo", gated_low.T, back_mix_full, 0, 8)
    grad_tables = store_grad(grad_tables, "wg", normed_t, d_gate, 0, 8)
    d_leaving, grad_tables = leaving(local_heads, my_index_row, d_entering, kept_states, grad_tables)
    d_conv, d_tail, d_rim, d_taps, d_decay_wide, d_scalars = mixer_back(
        local_heads,
        query_gate,
        value_key,
        query_taps,
        taps,
        decay_proj,
        scalars,
        solve,
        fresh,
        wy_keys,
        entering_state,
        d_recurred,
        d_leaving,
    )
    d_rims = shifted(tuple(part[8 - rim_width :] for part in d_rim), "seq", -1)

    def with_rim(whole, tail, rim_grad):
        tail = tail + jnp.pad(rim_grad, ((8 - rim_width, 0), (0, 0)))
        return lax.dynamic_update_slice(whole, tail.astype(jnp.bfloat16), (row_count - 8, 0))

    d_query, d_value_key = (
        with_rim(*parts) for parts in zip(d_conv, d_tail, d_rims)
    )
    grad_tables = store_grad(grad_tables, "wv", normed_t, d_value_key, 0, 8)
    grad_tables = store_grad(grad_tables, "wk", normed_t, d_value_key, 2, 4)
    grad_tables = store_grad(grad_tables, "wq", normed_t, d_query, 0, 4)
    second_table, first_reduced = lax.optimization_barrier((grad_tables[0], first_reduced))
    second_reduced = lax.psum_scatter(second_table, "seq", scatter_dimension=0, tiled=True)
    d_decay = d_decay_wide.astype(jnp.bfloat16)
    grad_wab = weight_grad(normed, d_decay)[:, : 2 * local_heads]
    d_normed_mine = total_of(
        exchange(
            spread_products(
                my_head_row,
                head_parts,
                [
                    ((d_value_key,), value_key_weights, True),
                    ((d_query, d_gate), query_gate_weights, True),
                    ((d_decay,), decay_weight, True),
                ],
            ),
            "head",
        )
    )
    dot_one = jnp.sum(d_normed_mine * gain_one_mine * inputs_wide, axis=-1)
    sums = sum_over(
        jnp.concatenate([dot_one.reshape(-1, LANES), norm_grad[0].reshape(-1, LANES)]), "head"
    )
    dot_one = sums[: row_count // LANES].reshape(row_count, 1)
    grad_wnorm = lax.dynamic_slice_in_dim(
        sums[row_count // LANES :].reshape(-1), my_head * norm_width, norm_width
    )
    grad_gainone = jnp.sum(d_normed_mine * inputs_wide * scale_one, axis=0)
    input_grad = (
        d_resid
        + scale_one * d_normed_mine * gain_one_mine
        - scale_one**3 / D * inputs_wide * dot_one
    )

    small_grads = [
        d_taps[0][:KCONV],
        d_taps[1][:KCONV, local_heads * DV :],
        d_taps[1][:KCONV, : local_heads * DV],
        grad_wab,
        d_scalars[0, :local_heads],
        d_scalars[1, :local_heads],
        grad_gainone,
        grad_gaintwo,
        grad_wnorm,
    ]
    small_block = jnp.concatenate(
        [grad_now.reshape(-1) for grad_now in small_grads]
        + [jnp.zeros((small_rows * LANES - small_used,), jnp.float32)]
    ).reshape(-1, LANES)
    mask = 1
    while mask < seq_parts:
        small_block = small_block + lax.ppermute(
            small_block, "seq", [(i, i ^ mask) for i in range(seq_parts)]
        )
        mask *= 2
    small_block = jnp.pad(
        small_block.astype(jnp.bfloat16), ((0, rows_of_piece - small_rows), (0, 0))
    )[None]

    trips_now, second_reduced, rest_grads = lax.optimization_barrier(
        (trips_reduce, second_reduced, grad_tables[1])
    )
    rest_reduced = reduce_rest(rest_grads, trips_now, most_reduce, extra_step)
    spilled = bring_spilled(
        second_reduced, second_room - my_spare_here, trips_spill, most_spill, spill_step
    )
    my_held = second_held[my_index]
    in_first = slot_ids >= my_held
    my_over = slot_ids - second_room
    my_spare = room_there[my_index]
    spill_trip = my_over // spill_step
    there = second_room - my_spare + spill_trip * spill_step
    spill_shift = there - jnp.minimum(there, second_room - spill_step)
    slot_sources = jnp.where(
        in_first, 0, jnp.where(my_over < 0, 2, jnp.where(my_over < my_spare, 3, 4))
    )
    slot_rows = jnp.where(
        in_first,
        slot_ids - my_held,
        jnp.where(
            my_over < 0,
            slot_ids,
            jnp.where(my_over < my_spare, my_over + spill_shift, my_over - my_spare),
        ),
    )
    slot_sources = jnp.where(present > 0, jnp.where(is_small > 0, 1, slot_sources), 0)
    slot_rows = jnp.where(is_small > 0, 0, slot_rows)
    slot_rows = jnp.where(present > 0, slot_rows, 0)
    slot_masks = jnp.stack([present.astype(jnp.float32), is_small.astype(jnp.float32), slot_rates])
    slot_masks = jnp.broadcast_to(slot_masks[:, :, None], slot_masks.shape + (LANES,))
    first_block = jnp.minimum((my_held + 7) // 8, padded // 8).astype(jnp.int32).reshape(1)

    def update(sources, earlier):
        return optimizer_update(
            sources,
            slot_sources,
            slot_rows,
            slot_kinds,
            kinds_used,
            slot_masks,
            jnp.asarray(small_rates)[None, :],
            master,
            moment_one,
            moment_two,
            first_block,
            earlier,
        )

    partly = update([first_reduced, small_block], [])
    grad_slots, master_new, moment_new, second_new, weights_low = update(
        [first_reduced, small_block, second_reduced, spilled, rest_reduced], partly
    )
    return (
        block_out,
        input_grad,
        grad_slots,
        master_new,
        moment_new,
        second_new,
        weights_low,
    )


def solution(mesh):
    return jax.shard_map(
        on_device,
        mesh=mesh,
        in_specs=(
            P("seq", "head"),
            P("seq", "head"),
            P(),
            P("seq", "head"),
            P("seq", "head"),
            P("seq", "head"),
        ),
        out_specs=(
            P("seq", "head"),
            P("seq", "head"),
            P("seq", "head"),
            P("seq", "head"),
            P("seq", "head"),
            P("seq", "head"),
            P("seq", "head"),
        ),
        check_vma=False,
    )
```

```python
import jax
import jax.numpy as jnp
import numpy as np
from jax import lax
from jax.experimental import pallas as pl
from jax.experimental.pallas import tpu as pltpu
from jax.sharding import PartitionSpec as P

D = 2048
HEADS = 16
DK = 128
DV = 256
FF = 5632
KCONV = 4
STEP = 5


EXACT_ARITHMETIC = lax.Precision.HIGHEST
NORM_EPSILON = 1e-06
UNIT_EPSILON = 1e-06
HEAD_EPSILON = 1e-05
ADAM_EPSILON = 1e-08
BETA_ONE = 0.5
BETA_TWO = 0.5
WEIGHT_DECAY = 0.1
PAD_RATE = 0.1


def shifted(block, axis, distance):
    devices = range(lax.axis_size(axis))
    route = [(i - distance, i) for i in devices if i - distance in devices]
    return lax.ppermute(block, axis, route)


def shard_layout(local_heads, head_parts):
    return [
        ("wq", D, local_heads * DK, 0.02),
        ("wk", D, local_heads * DK, 0.02),
        ("wv", D, local_heads * DV, 0.02),
        ("wg", D, local_heads * DV, 0.02),
        ("wo", local_heads * DV, D, 0.015),
        ("wgate", D, FF // head_parts, 0.02),
        ("wup", D, FF // head_parts, 0.02),
        ("wdown", FF // head_parts, D, 0.012),
        ("cq", KCONV, local_heads * DK, 0.4),
        ("ck", KCONV, local_heads * DK, 0.4),
        ("cv", KCONV, local_heads * DV, 0.4),
        ("wab", D, 2 * local_heads, 0.04),
        ("alog", 1, local_heads, 0.5),
        ("dtbias", 1, local_heads, 0.5),
        ("gainone", 1, D // head_parts, 0.1),
        ("gaintwo", 1, D // head_parts, 0.1),
        ("wnorm", 1, DV // head_parts, 0.1),
    ]


def piece_table(owners, seq_parts, capacity):
    piece_count = owners.shape[0]
    devices = jnp.arange(seq_parts, dtype=jnp.int32)
    onehot = (owners[:, None] == devices[None, :]).astype(jnp.int32)
    before = jnp.cumsum(onehot, axis=0) - onehot
    rank_within = jnp.sum(before * onehot, axis=1)
    slot_of_piece = owners * capacity + rank_within
    matches = slot_of_piece[None, :] == jnp.arange(seq_parts * capacity, dtype=jnp.int32)[:, None]
    present = jnp.any(matches, axis=1)
    piece_of_slot = jnp.sum(
        matches.astype(jnp.int32) * jnp.arange(piece_count, dtype=jnp.int32)[None, :], axis=1
    )
    return (slot_of_piece, piece_of_slot, present)


def unpack(flat_weights, segments_list):
    by_name = {}
    offset_now = 0
    for seg_name, row_count, col_count, seg_rate in segments_list:
        by_name[seg_name] = flat_weights[offset_now : offset_now + row_count * col_count].reshape(
            row_count, col_count
        )
        offset_now += row_count * col_count
    return (by_name, offset_now)


def rate_parts(segments_list, piece_count, piece_size):
    piece_rates = np.full(piece_count, PAD_RATE, np.float32)
    small_rates = np.full(piece_size, PAD_RATE, np.float32)
    offset_now = 0
    big_total = (piece_count - 1) * piece_size
    for seg_name, row_count, col_count, seg_rate in segments_list:
        seg_size = row_count * col_count
        if offset_now < big_total:
            piece_rates[offset_now // piece_size : (offset_now + seg_size) // piece_size] = seg_rate
        else:
            small_rates[offset_now - big_total : offset_now - big_total + seg_size] = seg_rate
        offset_now += seg_size
    return (piece_rates, small_rates)


HEADS_A_STEP = 1


def product(left, right, left_axis, right_axis, exact=False):
    def dot(a, b):
        return lax.dot_general(
            a,
            b,
            (((left_axis,), (right_axis,)), ((), ())),
            preferred_element_type=jnp.float32,
        )

    left_low, right_low = left.astype(jnp.bfloat16), right.astype(jnp.bfloat16)
    if not exact:
        return dot(left_low, right_low)
    left_rest = (left - left_low.astype(jnp.float32)).astype(jnp.bfloat16)
    right_rest = (right - right_low.astype(jnp.float32)).astype(jnp.bfloat16)
    return dot(left_low, right_low) + (dot(left_low, right_rest) + dot(left_rest, right_low))


def take_lane(wide, lane):
    lanes = lax.broadcasted_iota(jnp.int32, wide.shape, 1)
    return jnp.sum(jnp.where(lanes == lane, wide, 0.0), axis=1, keepdims=True)


def put_lane(column, lane):
    lanes = lax.broadcasted_iota(jnp.int32, (column.shape[0], 128), 1)
    return jnp.where(lanes == lane, column, 0.0)


def to_row(column, diagonal):
    return jnp.sum(jnp.where(diagonal, column, 0.0), axis=0, keepdims=True)


def convolved(extended, taps_ref, columns):
    row_count = extended.shape[0] - RIM
    first = RIM - (KCONV - 1)
    running = taps_ref[0:1, columns] * extended[first : first + row_count, columns]
    for tap in range(1, KCONV):
        running = running + taps_ref[tap : tap + 1, columns] * extended[
            first + tap : first + tap + row_count, columns
        ]
    return running


def decay_terms(head, local_heads, decay_ref, scalars_ref):
    row_count = decay_ref.shape[0]
    shape = (row_count, row_count)
    row_ids = lax.broadcasted_iota(jnp.int32, shape, 0)
    column_ids = lax.broadcasted_iota(jnp.int32, shape, 1)
    decay_in = take_lane(decay_ref[...], head) + take_lane(scalars_ref[1:2, :], head)
    rate = -jnp.exp(take_lane(scalars_ref[0:1, :], head))
    soft = jnp.maximum(decay_in, 0.0) + jnp.log1p(jnp.exp(-jnp.abs(decay_in)))
    logs = rate * soft
    beta = jax.nn.sigmoid(take_lane(decay_ref[...], head + local_heads))
    diagonal = row_ids == column_ids
    logs_row = to_row(logs, diagonal)
    upto = row_ids >= column_ids
    sums = jnp.sum(jnp.where(upto, logs_row, 0.0), axis=1, keepdims=True)
    sums_row = to_row(sums, diagonal)
    within = jnp.exp(jnp.where(upto, sums - sums_row, -1e30))
    return decay_in, rate, logs, beta, sums, within, row_ids, column_ids


def unit_rows(rows):
    scale = lax.rsqrt(jnp.sum(rows * rows, axis=-1, keepdims=True) + UNIT_EPSILON)
    return rows * scale, scale


def mixer_specs(local_heads, row_count):
    def spec(rows, width, first):
        width *= HEADS_A_STEP
        return pl.BlockSpec((rows, width), lambda h, first=first // width: (0, first + h))

    def query(rows):
        return spec(rows, DK, 0)

    def key(rows):
        return spec(rows, DK, local_heads * DV)

    def value(rows):
        return spec(rows, DV, 0)

    whole = pl.BlockSpec((row_count, 128), lambda h: (0, 0))
    scalars = pl.BlockSpec((8, 128), lambda h: (0, 0))
    return query, key, value, whole, scalars


def per_head(*shape):
    return pl.BlockSpec((HEADS_A_STEP,) + shape, lambda h: (h,) + (0,) * len(shape))


def head_columns(sub):
    return slice(DK * sub, DK * sub + DK), slice(DV * sub, DV * sub + DV)


def mixer_local(local_heads, value_key, taps, decay_proj, scalars):
    row_count = value_key.shape[0] - RIM
    query, key, value, whole, scalar_spec = mixer_specs(local_heads, row_count)

    def kernel(
        pv, pk, tv, tk, decay_ref, scalars_ref, solve_ref, fresh_ref, wy_ref, handoff_ref
    ):
        for sub in range(HEADS_A_STEP):
            head = pl.program_id(0) * HEADS_A_STEP + sub
            narrow, wide = head_columns(sub)
            key_rows = unit_rows(jax.nn.silu(convolved(pk, tk, narrow)))[0]
            values = jax.nn.silu(convolved(pv, tv, wide))
            decay_in, rate, logs, beta, sums, within, row_ids, column_ids = decay_terms(
                head, local_heads, decay_ref, scalars_ref
            )
            gram = product(key_rows, key_rows, 1, 1, True)
            system = jnp.where(row_ids > column_ids, beta * gram * within, 0.0)
            unit = jnp.where(row_ids == column_ids, 1.0, 0.0)
            solve = unit
            size = 1
            while size < row_count:
                lower = (row_ids // (2 * size) == column_ids // (2 * size)) & (
                    row_ids // size != column_ids // size
                )
                part = jnp.where(lower, system, 0.0)
                if size == 1:
                    solve = solve - part
                else:
                    solve = solve - product(solve, product(part, solve, 1, 0), 1, 0)
                size *= 2
            remainder = (unit - solve) - product(system, solve, 1, 0, True)
            solve = solve + product(solve, remainder, 1, 0)
            grown = jnp.exp(sums)
            fresh = product(solve, beta * values, 1, 0, True)
            wy_keys = product(solve, (beta * grown) * key_rows, 1, 0, True)
            last = sums[row_count - 1 : row_count, :]
            tail_keys = jnp.exp(last - sums) * key_rows
            eye = lax.broadcasted_iota(jnp.int32, (DK, DK), 0) == lax.broadcasted_iota(
                jnp.int32, (DK, DK), 1
            )
            solve_ref[sub] = solve
            fresh_ref[sub] = fresh
            wy_ref[sub] = wy_keys
            handoff_ref[sub, :, :DK] = (
                jnp.where(eye, jnp.exp(last), 0.0) - product(tail_keys, wy_keys, 0, 0)
            ).astype(jnp.bfloat16)
            handoff_ref[sub, :, DK:] = product(tail_keys, fresh, 0, 0).astype(jnp.bfloat16)

    def out(*shape, kind=jnp.float32):
        return jax.ShapeDtypeStruct((local_heads,) + shape, kind)

    return pl.pallas_call(
        kernel,
        grid=(local_heads // HEADS_A_STEP,),
        in_specs=[
            value(RIM + row_count), key(RIM + row_count), value(8), key(8), whole, scalar_spec,
        ],
        out_specs=[
            per_head(row_count, row_count),
            per_head(row_count, DV),
            per_head(row_count, DK),
            per_head(DK, DK + DV),
        ],
        out_shape=[
            out(row_count, row_count),
            out(row_count, DV),
            out(row_count, DK),
            out(DK, DK + DV, kind=jnp.bfloat16),
        ],
        compiler_params=params(),
    )(value_key, value_key, taps, taps, decay_proj, scalars)


def mixer_reach(local_heads, query_gate, value_key, query_taps, taps, decay_proj, scalars, fresh, wy_keys):
    row_count = value_key.shape[0] - RIM
    query, key, value, whole, scalar_spec = mixer_specs(local_heads, row_count)

    def kernel(pq, pk, tq, tk, decay_ref, scalars_ref, fresh_ref, wy_ref, reach_ref, zero_ref):
        for sub in range(HEADS_A_STEP):
            head = pl.program_id(0) * HEADS_A_STEP + sub
            narrow, wide = head_columns(sub)
            queries = unit_rows(jax.nn.silu(convolved(pq, tq, narrow)))[0] * DK ** (-0.5)
            key_rows = unit_rows(jax.nn.silu(convolved(pk, tk, narrow)))[0]
            decay_in, rate, logs, beta, sums, within, row_ids, column_ids = decay_terms(
                head, local_heads, decay_ref, scalars_ref
            )
            attention = product(queries, key_rows, 1, 1) * within
            reach_ref[sub] = jnp.exp(sums) * queries - product(attention, wy_ref[sub], 1, 0)
            zero_ref[sub] = product(attention, fresh_ref[sub], 1, 0)

    return pl.pallas_call(
        kernel,
        grid=(local_heads // HEADS_A_STEP,),
        in_specs=[
            query(RIM + row_count), key(RIM + row_count), query(8), key(8), whole, scalar_spec,
            per_head(row_count, DV),
            per_head(row_count, DK),
        ],
        out_specs=[per_head(row_count, DK), per_head(row_count, DV)],
        out_shape=[
            jax.ShapeDtypeStruct((local_heads, row_count, DK), jnp.float32),
            jax.ShapeDtypeStruct((local_heads, row_count, DV), jnp.float32),
        ],
        compiler_params=params(),
    )(query_gate, value_key, query_taps, taps, decay_proj, scalars, fresh, wy_keys)


def advance_state(block, state, back):
    moved = product(block[:, :DK].astype(jnp.float32), state, 0 if back else 1, 0)
    return moved, block[:, DK:].astype(jnp.float32)


def chain_all(local_heads, my_index, handoffs, inputs, back):
    devices = handoffs.shape[0]

    def kernel(index_ref, handoffs_ref, inputs_ref, state_ref):
        state_ref[...] = jnp.zeros_like(state_ref)

        def advance(step, carry):
            j = devices - 1 - step if back else step
            for h in range(local_heads):
                moved, added = advance_state(handoffs_ref[j, h], state_ref[h], back)
                if back:
                    added = inputs_ref[j, h].astype(jnp.float32)
                state_ref[h] = moved + added
            return carry

        count = devices - 1 - index_ref[0] if back else index_ref[0]
        lax.fori_loop(0, count, advance, 0)

    vmem = pl.BlockSpec(memory_space=pltpu.VMEM)
    return pl.pallas_call(
        kernel,
        in_specs=[pl.BlockSpec(memory_space=pltpu.SMEM), vmem, vmem],
        out_specs=vmem,
        out_shape=jax.ShapeDtypeStruct((local_heads, DK, DV), jnp.float32),
        compiler_params=params(),
    )(my_index, handoffs, inputs)


def join_cores(local_heads, my_index, mine, theirs, inputs):
    half = local_heads // 2

    def kernel(index_ref, mine_ref, theirs_ref, *refs):
        out_ref = refs[-1]
        core = lax.rem(index_ref[0], 2)
        for i in range(half):
            h = core * half + i
            own, other = mine_ref[h], theirs_ref[h]
            first = jnp.where(core == 0, own, other)
            second = jnp.where(core == 0, other, own)
            if inputs:
                own, other = refs[0][h], refs[1][h]
                early = jnp.where(core == 0, own, other).astype(jnp.float32)
                late = jnp.where(core == 0, other, own).astype(jnp.float32)
                out_ref[i] = (advance_state(first, late, True)[0] + early).astype(jnp.bfloat16)
                continue
            moved, added = advance_state(second, first.astype(jnp.float32), False)
            out_ref[i, :, :DK] = moved[:, :DK].astype(jnp.bfloat16)
            out_ref[i, :, DK:] = (moved[:, DK:] + added).astype(jnp.bfloat16)

    vmem = pl.BlockSpec(memory_space=pltpu.VMEM)
    return pl.pallas_call(
        kernel,
        in_specs=[pl.BlockSpec(memory_space=pltpu.SMEM)] + [vmem] * (2 + len(inputs)),
        out_specs=vmem,
        out_shape=jax.ShapeDtypeStruct((half, DK, DV if inputs else DK + DV), jnp.bfloat16),
        compiler_params=params(),
    )(my_index, mine, theirs, *inputs)


def chain_chips(local_heads, my_index, theirs, chips, their_input, chip_inputs):
    half = local_heads // 2
    masks = len(chips) // 2
    back = their_input is not None
    flat = [theirs, *chips] + ([their_input, *chip_inputs] if back else [])

    def kernel(index_ref, *refs):
        state_ref = refs[-1]
        state_ref[...] = jnp.zeros_like(state_ref)
        core, chip = lax.rem(index_ref[0], 2), index_ref[0] // 2
        offset = 1 + len(chips)

        def update(h, block, extra):
            moved, added = advance_state(block, state_ref[h], back)
            state_ref[h] = moved + (extra.astype(jnp.float32) if back else added)

        order = range(masks, 0, -1) if back else range(masks)
        for other in order:
            for mask in range(1, masks + 1):
                here = (other ^ chip) == mask

                @pl.when(here & ((other > chip) if back else (other < chip)))
                def _():
                    for h in range(local_heads):
                        mine = core == h // half
                        pair = [refs[1 + 2 * (mask - 1) + i][h % half] for i in range(2)]
                        extra = None
                        if back:
                            extra = [
                                refs[offset + 1 + 2 * (mask - 1) + i][h % half] for i in range(2)
                            ]
                            extra = jnp.where(mine, *extra)
                        update(h, jnp.where(mine, *pair), extra)

        @pl.when(core == (0 if back else 1))
        def _():
            for h in range(local_heads):
                update(h, refs[0][h], refs[offset][h] if back else None)

    vmem = pl.BlockSpec(memory_space=pltpu.VMEM)
    return pl.pallas_call(
        kernel,
        in_specs=[pl.BlockSpec(memory_space=pltpu.SMEM)] + [vmem] * len(flat),
        out_specs=vmem,
        out_shape=jax.ShapeDtypeStruct((local_heads, DK, DV), jnp.float32),
        compiler_params=params(),
    )(my_index, *flat)


def moved_by(array, mask):
    return lax.ppermute(array, "seq", [(i, i ^ mask) for i in range(lax.axis_size("seq"))])


def pass_chips(block, beside):
    arrived = [moved_by(block, mask) for mask in (2, 4, 6)]
    arrived, beside = lax.optimization_barrier((arrived, beside))
    return [array for part in arrived for array in (part, moved_by(part, 1))], beside


def entering(local_heads, my_index, handoff, beside):
    if lax.axis_size("seq") != 8:
        handoffs = lax.all_gather(handoff, "seq", axis=0, tiled=False)
        return chain_all(local_heads, my_index, handoffs, handoffs, False), handoffs, beside
    theirs = moved_by(handoff, 1)
    chips, beside = pass_chips(join_cores(local_heads, my_index, handoff, theirs, []), beside)
    state = chain_chips(local_heads, my_index, theirs, chips, None, [])
    return state, (handoff, theirs, chips), beside


def leaving(local_heads, my_index, d_entering, kept, beside):
    if lax.axis_size("seq") != 8:
        inputs = lax.all_gather(d_entering, "seq", axis=0, tiled=False)
        return chain_all(local_heads, my_index, kept, inputs, True), beside
    handoff, theirs, chips = kept
    their_input = moved_by(d_entering, 1)
    joined = join_cores(local_heads, my_index, handoff, theirs, [d_entering, their_input])
    inputs, beside = pass_chips(joined, beside)
    return chain_chips(local_heads, my_index, theirs, chips, their_input, inputs), beside


def mixer_out(local_heads, entering_state, reach, zero_out, query_gate, norm_gain):
    row_count = query_gate.shape[0] - RIM
    gate_first = local_heads * DK

    def kernel(state_ref, reach_ref, zero_ref, gate_ref, norm_ref, out_ref, gated_ref):
        for h in range(local_heads):
            columns = slice(DV * h, DV * h + DV)
            out = zero_ref[h] + product(reach_ref[h], state_ref[h], 1, 0)
            normed = out * lax.rsqrt(jnp.mean(out * out, axis=-1, keepdims=True) + HEAD_EPSILON)
            out_ref[:, columns] = out
            gate = gate_ref[RIM:, gate_first + DV * h : gate_first + DV * h + DV]
            gated_ref[:, columns] = (normed * norm_ref[...] * jax.nn.silu(gate)).astype(
                jnp.bfloat16
            )

    vmem = pl.BlockSpec(memory_space=pltpu.VMEM)
    width = local_heads * DV
    return pl.pallas_call(
        kernel,
        in_specs=[vmem] * 5,
        out_specs=[vmem, vmem],
        out_shape=[
            jax.ShapeDtypeStruct((row_count, width), jnp.float32),
            jax.ShapeDtypeStruct((row_count, width), jnp.bfloat16),
        ],
        compiler_params=params(),
    )(entering_state, reach, zero_out, query_gate, norm_gain)


def mixer_gate_back(local_heads, d_gated, recurred, query_gate, norm_gain, reach):
    row_count = query_gate.shape[0] - RIM
    gate_first = local_heads * DK // DV

    def kernel(d_gated_ref, out_ref, gate_ref, norm_ref, reach_ref, d_out_ref, d_gate_ref, d_norm_ref, d_state_ref):
        out, gate, norm_row, d_gated_now = (
            out_ref[...], gate_ref[RIM:, :], norm_ref[...], d_gated_ref[...]
        )
        scale = lax.rsqrt(jnp.mean(out * out, axis=-1, keepdims=True) + HEAD_EPSILON)
        normed = out * scale
        logistic = jax.nn.sigmoid(gate)
        silu = gate * logistic
        d_norm = jnp.sum(d_gated_now * normed * silu, axis=0, keepdims=True)

        @pl.when(pl.program_id(0) == 0)
        def _():
            d_norm_ref[...] = jnp.zeros_like(d_norm_ref)

        d_norm_ref[0:1, :] = d_norm_ref[0:1, :] + d_norm
        d_gate_ref[...] = (
            d_gated_now * normed * norm_row * logistic * (1.0 + gate * (1.0 - logistic))
        ).astype(jnp.bfloat16)
        d_normed = d_gated_now * norm_row * silu
        d_out = scale * d_normed - (scale * scale * scale) * out * jnp.mean(
            d_normed * out, axis=-1, keepdims=True
        )
        d_out_ref[...] = d_out
        d_state_ref[0] = product(reach_ref[0], d_out, 0, 0).astype(jnp.bfloat16)

    width = local_heads * DV
    block = pl.BlockSpec((row_count, DV), lambda h: (0, h))
    return pl.pallas_call(
        kernel,
        grid=(local_heads,),
        in_specs=[
            block,
            block,
            pl.BlockSpec((RIM + row_count, DV), lambda h: (0, gate_first + h)),
            pl.BlockSpec((1, DV), lambda h: (0, 0)),
            pl.BlockSpec((1, row_count, DK), lambda h: (h, 0, 0)),
        ],
        out_specs=[
            block,
            block,
            pl.BlockSpec((8, DV), lambda h: (0, 0)),
            pl.BlockSpec((1, DK, DV), lambda h: (h, 0, 0)),
        ],
        out_shape=[
            jax.ShapeDtypeStruct((row_count, width), jnp.float32),
            jax.ShapeDtypeStruct((row_count, width), jnp.bfloat16),
            jax.ShapeDtypeStruct((8, DV), jnp.float32),
            jax.ShapeDtypeStruct((local_heads, DK, DV), jnp.bfloat16),
        ],
        compiler_params=params(),
    )(d_gated, recurred, query_gate, norm_gain, reach)


def conv_back(
    d_pre, extended, taps_ref, padded, d_block_ref, d_tail_ref, d_rim_ref, d_taps_ref, columns
):
    row_count = d_pre.shape[0]
    first = RIM - (KCONV - 1)
    padded[0:8, :] = jnp.zeros((8, d_pre.shape[1]), jnp.float32)
    padded[8 : 8 + row_count, :] = d_pre
    padded[8 + row_count : 16 + row_count, :] = jnp.zeros((8, d_pre.shape[1]), jnp.float32)
    total = None
    d_taps_ref[:, columns] = jnp.zeros((8, d_pre.shape[1]), jnp.float32)
    for tap in range(KCONV):
        start = KCONV - 1 - tap
        term = taps_ref[tap : tap + 1, columns] * padded[start : start + row_count + 8, :]
        total = term if total is None else total + term
        d_taps_ref[tap : tap + 1, columns] = jnp.sum(
            d_pre * extended[first + tap : first + tap + row_count, columns], axis=0, keepdims=True
        )
    d_rim_ref[:, columns] = total[0:8, :]
    d_block_ref[:, columns] = total[8:, :].astype(jnp.bfloat16)
    d_tail_ref[:, columns] = total[row_count:, :]


def mixer_back(
    local_heads, query_gate, value_key, query_taps, taps, decay_proj, scalars,
    solve, fresh, wy_keys, entering_state, d_recurred, d_leaving,
):
    row_count = value_key.shape[0] - RIM
    query, key, value, whole, scalar_spec = mixer_specs(local_heads, row_count)

    def kernel(
        pq, pk, pv, tq, tk, tv, decay_ref, scalars_ref,
        solve_ref, fresh_ref, wy_ref, enter_ref, d_out_ref, d_leave_ref,
        dq_ref, dk_ref, dv_ref, tail_q, tail_k, tail_v, rim_q, rim_k, rim_v,
        taps_q, taps_k, taps_v, d_decay_ref, d_scalars_ref,
        pad_q, pad_k, pad_v,
    ):
        @pl.when(pl.program_id(0) == 0)
        def _():
            d_decay_ref[...] = jnp.zeros_like(d_decay_ref)
            d_scalars_ref[...] = jnp.zeros_like(d_scalars_ref)

        for sub in range(HEADS_A_STEP):
            head = pl.program_id(0) * HEADS_A_STEP + sub
            narrow, wide = head_columns(sub)
            pre_q = convolved(pq, tq, narrow)
            pre_k = convolved(pk, tk, narrow)
            pre_v = convolved(pv, tv, wide)
            conv_q, conv_k = jax.nn.silu(pre_q), jax.nn.silu(pre_k)
            unit_q, scale_q = unit_rows(conv_q)
            queries = unit_q * DK ** (-0.5)
            key_rows, scale_k = unit_rows(conv_k)
            values = jax.nn.silu(pre_v)
            decay_in, rate, logs, beta, sums, within, row_ids, column_ids = decay_terms(
                head, local_heads, decay_ref, scalars_ref
            )
            strict = row_ids > column_ids
            grown = jnp.exp(sums)
            last = sums[row_count - 1 : row_count, :]
            tail = jnp.exp(last - sums)
            tail_keys = tail * key_rows
            gram = product(key_rows, key_rows, 1, 1, True)
            scores = jnp.where(strict, gram * within, 0.0)
            attention = product(queries, key_rows, 1, 1) * within
            enter, d_out, d_leave = enter_ref[sub], d_out_ref[:, wide], d_leave_ref[sub]
            update = fresh_ref[sub] - product(wy_ref[sub], enter, 1, 0)
            d_update = product(attention, d_out, 0, 0) + product(tail_keys, d_leave, 1, 0)
            d_right = product(solve_ref[sub], d_update, 0, 0, True)
            d_attention = product(d_out, update, 1, 1) * within
            d_system = -product(d_right, update, 1, 1)
            out_state = product(d_out, enter, 1, 1)
            right_state = product(d_right, enter, 1, 1)
            leave_update = product(update, d_leave, 1, 1)
            remainder = values - grown * product(key_rows, enter, 1, 0)
            d_values = beta * d_right
            d_beta = jnp.sum(d_right * remainder, axis=1, keepdims=True) + jnp.sum(
                d_system * scores, axis=1, keepdims=True
            )
            pair = beta * (d_system * scores)
            d_gram = jnp.where(strict, beta * d_system * within, 0.0)
            d_queries = grown * out_state + product(d_attention, key_rows, 1, 0)
            d_keys = (
                product(d_attention, queries, 0, 0)
                + product(d_gram, key_rows, 1, 0)
                + product(d_gram, key_rows, 0, 0)
                + tail * leave_update
                - (beta * grown) * right_state
            )
            both = pair + d_attention * product(queries, key_rows, 1, 1)
            tail_rows = jnp.sum(tail_keys * leave_update, axis=1, keepdims=True)
            diagonal = row_ids == column_ids
            columns = jnp.sum(both, axis=0, keepdims=True)
            d_sums = (
                jnp.sum(both, axis=1, keepdims=True)
                - jnp.sum(jnp.where(diagonal, columns, 0.0), axis=1, keepdims=True)
                + jnp.sum(out_state * (grown * queries), axis=1, keepdims=True)
                - jnp.sum(right_state * ((beta * grown) * key_rows), axis=1, keepdims=True)
                - tail_rows
            )
            d_last = jnp.exp(last) * jnp.sum(
                jnp.sum(d_leave * enter, axis=1, keepdims=True), axis=0, keepdims=True
            ) + jnp.sum(tail_rows, axis=0, keepdims=True)
            d_logs = d_last + jnp.sum(
                jnp.where(row_ids <= column_ids, to_row(d_sums, diagonal), 0.0), axis=1, keepdims=True
            )
            d_decay_in = d_logs * rate * jax.nn.sigmoid(decay_in)
            d_beta_in = d_beta * beta * (1.0 - beta)
            d_decay_ref[...] = (
                d_decay_ref[...]
                + put_lane(d_decay_in, head)
                + put_lane(d_beta_in, head + local_heads)
            )
            d_rate = jnp.sum(d_logs * logs, axis=0, keepdims=True)
            d_bias = jnp.sum(d_decay_in, axis=0, keepdims=True)
            d_scalars_ref[0:1, :] = d_scalars_ref[0:1, :] + put_lane(d_rate, head)
            d_scalars_ref[1:2, :] = d_scalars_ref[1:2, :] + put_lane(d_bias, head)

            def unit_back(d_unit, unit, scale):
                return scale * (d_unit - unit * jnp.sum(unit * d_unit, axis=1, keepdims=True))

            def silu_back(d_act, pre):
                logistic = jax.nn.sigmoid(pre)
                return d_act * logistic * (1.0 + pre * (1.0 - logistic))

            d_pre_q = silu_back(unit_back(d_queries * DK ** (-0.5), unit_q, scale_q), pre_q)
            conv_back(d_pre_q, pq, tq, pad_q.at[sub], dq_ref, tail_q, rim_q, taps_q, narrow)
            d_pre_k = silu_back(unit_back(d_keys, key_rows, scale_k), pre_k)
            conv_back(d_pre_k, pk, tk, pad_k.at[sub], dk_ref, tail_k, rim_k, taps_k, narrow)
            conv_back(
                silu_back(d_values, pre_v), pv, tv, pad_v.at[sub],
                dv_ref, tail_v, rim_v, taps_v, wide,
            )

    def blocks(rows):
        return [
            pl.BlockSpec((rows, HEADS_A_STEP * width), lambda h: (0, h)) for width in (DK, DK, DV)
        ]

    def shapes(rows, kind):
        return [
            jax.ShapeDtypeStruct((rows, local_heads * width), kind) for width in (DK, DK, DV)
        ]

    outs = pl.pallas_call(
        kernel,
        grid=(local_heads // HEADS_A_STEP,),
        in_specs=[each(RIM + row_count) for each in (query, key, value)]
        + [each(8) for each in (query, key, value)]
        + [
            whole,
            scalar_spec,
            per_head(row_count, row_count),
            per_head(row_count, DV),
            per_head(row_count, DK),
            per_head(DK, DV),
            pl.BlockSpec((row_count, HEADS_A_STEP * DV), lambda h: (0, h)),
            per_head(DK, DV),
        ],
        out_specs=blocks(row_count) + blocks(8) * 3 + [whole, scalar_spec],
        out_shape=shapes(row_count, jnp.bfloat16)
        + shapes(8, jnp.float32) * 3
        + [
            jax.ShapeDtypeStruct((row_count, 128), jnp.float32),
            jax.ShapeDtypeStruct((8, 128), jnp.float32),
        ],
        scratch_shapes=[
            pltpu.VMEM((HEADS_A_STEP, row_count + 16, DK), jnp.float32),
            pltpu.VMEM((HEADS_A_STEP, row_count + 16, DK), jnp.float32),
            pltpu.VMEM((HEADS_A_STEP, row_count + 16, DV), jnp.float32),
        ],
        compiler_params=params(),
    )(
        query_gate, value_key, value_key, query_taps, taps, taps, decay_proj, scalars,
        solve, fresh, wy_keys, entering_state, d_recurred, d_leaving,
    )
    joined = [
        (outs[3 * i], jnp.concatenate([outs[3 * i + 2], outs[3 * i + 1]], axis=1))
        for i in range(4)
    ]
    return (*joined, outs[12], outs[13])


LANES = 128
CHUNK = 32768
TILE = 16
CAPACITY_UNIT = 44
FIRST_GATHER = 24
FIRST_REDUCE = 16
SECOND_REDUCE = 20
SECOND_GATHER = 16
RIM = 16
TABLE = 1 << 16
VMEM_LIMIT = 48 * 1024 * 1024


def params(**kwargs):
    return pltpu.CompilerParams(vmem_limit_bytes=VMEM_LIMIT, **kwargs)


def piece_kinds(segments_list, piece_count, piece_size):
    kinds = np.ones(piece_count, np.int32)
    offset_now = 0
    for seg_name, row_count, col_count, seg_rate in segments_list:
        if offset_now >= (piece_count - 1) * piece_size:
            break
        tiles = col_count // LANES
        if tiles in (2, 4, 8, 16):
            first = offset_now // piece_size
            kinds[first : first + row_count * col_count // piece_size] = tiles
        offset_now += row_count * col_count
    return kinds


def pack_blocks(master, slot_kinds, kinds_used, first_slot, slot_count):
    piece_size = master.shape[1]
    chunks = piece_size // CHUNK
    rows = CHUNK // LANES
    first_block = first_slot // 8
    slot_blocks = pl.cdiv(slot_count, 8)

    def kernel(kinds_ref, master_ref, out_ref, scratch):
        first = (first_block + pl.program_id(0)) * 8
        for j in range(rows):
            scratch[8 * j : 8 * j + 8, :] = master_ref[:, LANES * j : LANES * j + LANES]
        for s in range(8):
            kind_now = kinds_ref[first + s]
            for kind in kinds_used:

                @pl.when(kind_now == kind)
                def _():
                    for tile in range(rows // TILE):
                        row_tile, column = divmod(tile, kind)
                        start = (row_tile * TILE * kind + column) * 8 + s
                        out_ref[s, TILE * tile : TILE * tile + TILE, :] = scratch[
                            pl.ds(start, TILE, stride=8 * kind), :
                        ].astype(jnp.bfloat16)

    return pl.pallas_call(
        kernel,
        grid_spec=pltpu.PrefetchScalarGridSpec(
            num_scalar_prefetch=1,
            grid=(slot_blocks, chunks),
            in_specs=[pl.BlockSpec((8, CHUNK), lambda i, j, kinds: (first_block + i, j))],
            out_specs=pl.BlockSpec((8, rows, LANES), lambda i, j, kinds: (i, j, 0)),
            scratch_shapes=[pltpu.VMEM((8 * rows, LANES), jnp.float32)],
        ),
        out_shape=jax.ShapeDtypeStruct((slot_count, piece_size // LANES, LANES), jnp.bfloat16),
        compiler_params=params(),
    )(slot_kinds, master)


def reserve(shape, kind):
    def kernel(out_ref):
        pass

    return pl.pallas_call(
        kernel,
        out_specs=pl.BlockSpec(memory_space=pl.ANY),
        out_shape=jax.ShapeDtypeStruct(shape, kind),
        compiler_params=params(),
    )()


def assemble(tables, matrices, step_rows, rows_in=None):
    piece_rows = tables[0].shape[1]
    plans = []
    first_block, first_column = 0, 0
    for positions, col_count in matrices:
        tiles = col_count // LANES
        blocks = step_rows * tiles // piece_rows
        plans.append((first_block, first_column, tiles, blocks))
        first_block += blocks
        first_column += col_count
    blocks_a_step, width = first_block, first_column
    steps = matrices[0][0].shape[0] // plans[0][3]
    order = jnp.concatenate(
        [
            positions.reshape(steps, plan[3])
            for (positions, col_count), plan in zip(matrices, plans)
        ],
        axis=1,
    ).reshape(-1)
    uneven = [plan for plan in plans if piece_rows * plan[3] != step_rows * plan[2] or plan[2] not in (2, 4, 8, 16)]
    multiply = rows_in is not None

    def kernel(order_ref, *refs):
        if multiply:
            rows_ref, refs = refs[0], refs[1:]
        table_refs, refs = refs[: len(tables)], refs[len(tables) :]
        out_ref, refs = refs[0], refs[1:]
        if multiply:
            product_ref, refs = refs[0], refs[1:]
        buffer, sem, scratch = refs
        g = pl.program_id(0)
        slot = lax.rem(g, 2)

        def start(step, which):
            def one(j, carry):
                position = order_ref[step * blocks_a_step + j]
                for number, table_ref in enumerate(table_refs):

                    @pl.when(position // TABLE == number)
                    def _():
                        pltpu.make_async_copy(
                            table_ref.at[lax.rem(position, TABLE)],
                            buffer.at[which, j],
                            sem.at[which],
                        ).start()

                return carry

            lax.fori_loop(0, blocks_a_step, one, 0)

        @pl.when(g == 0)
        def _():
            start(0, 0)

        @pl.when(g + 1 < steps)
        def _():
            start(g + 1, 1 - slot)

        pltpu.make_async_copy(buffer.at[slot], buffer.at[slot], sem.at[slot]).wait()
        for plan in plans:
            first, left, tiles, blocks = plan
            if plan in uneven:
                for j in range(blocks):
                    scratch[piece_rows * j : piece_rows * j + piece_rows, :] = buffer[
                        slot, first + j
                    ].astype(jnp.float32)
                for c in range(tiles):
                    out_ref[:, left + LANES * c : left + LANES * c + LANES] = scratch[
                        pl.ds(c, step_rows, stride=tiles), :
                    ].astype(jnp.bfloat16)
                continue
            for j in range(blocks):
                for tile in range(piece_rows // TILE):
                    row_tile, column = divmod(tile, tiles)
                    row = piece_rows // tiles * j + TILE * row_tile
                    column = left + LANES * column
                    out_ref[row : row + TILE, column : column + LANES] = buffer[
                        slot, first + j, TILE * tile : TILE * tile + TILE, :
                    ]
        if multiply:
            part = jnp.dot(rows_ref[...], out_ref[...], preferred_element_type=jnp.float32)

            @pl.when(g == 0)
            def _():
                product_ref[...] = part

            @pl.when(g > 0)
            def _():
                product_ref[...] = product_ref[...] + part

    anywhere = pl.BlockSpec(memory_space=pl.ANY)
    in_specs = [anywhere for table in tables]
    operands = list(tables)
    out_specs = [pl.BlockSpec((step_rows, width), lambda g, order: (g, 0))]
    out_shape = [jax.ShapeDtypeStruct((steps * step_rows, width), jnp.bfloat16)]
    if multiply:
        row_count = rows_in.shape[0]
        in_specs.insert(0, pl.BlockSpec((row_count, step_rows), lambda g, order: (0, g)))
        operands.insert(0, rows_in)
        out_specs.append(pl.BlockSpec((row_count, width), lambda g, order: (0, 0)))
        out_shape.append(jax.ShapeDtypeStruct((row_count, width), jnp.float32))
    scratch_rows = max([plan[3] * piece_rows for plan in uneven], default=8)
    return pl.pallas_call(
        kernel,
        grid_spec=pltpu.PrefetchScalarGridSpec(
            num_scalar_prefetch=1,
            grid=(steps,),
            in_specs=in_specs,
            out_specs=out_specs,
            scratch_shapes=[
                pltpu.VMEM((2, blocks_a_step, piece_rows, LANES), jnp.bfloat16),
                pltpu.SemaphoreType.DMA((2,)),
                pltpu.VMEM((scratch_rows, LANES), jnp.float32),
            ],
        ),
        out_shape=out_shape,
        cost_estimate=pl.CostEstimate(
            flops=2 * steps * step_rows * width * (rows_in.shape[0] if multiply else 0),
            bytes_accessed=4 * steps * step_rows * width,
            transcendentals=0,
        ),
        compiler_params=params(),
    )(order, *operands)


def spread_products(my_part, parts, pairs):
    row_count = pairs[0][0][0].shape[0]
    total = pairs[0][1].shape[0 if pairs[0][2] else 1]
    width = total // parts

    def kernel(part_ref, *refs):
        ins, outs = list(refs[:-parts]), refs[-parts:]
        for m in range(parts):
            first = pl.multiple_of((part_ref[0] ^ m) * width, width)
            result, place = None, 0
            for lefts, right, transposed in pairs:
                left_refs, right_ref = ins[place : place + len(lefts)], ins[place + len(lefts)]
                place += len(lefts) + 1
                depth = 0
                for left_ref in left_refs:
                    inner = slice(depth, depth + left_ref.shape[1])
                    depth += left_ref.shape[1]
                    if transposed:
                        block, axis = right_ref[pl.ds(first, width), inner], 1
                    else:
                        block, axis = right_ref[inner, pl.ds(first, width)], 0
                    part = lax.dot_general(
                        left_ref[...],
                        block,
                        (((1,), (axis,)), ((), ())),
                        preferred_element_type=jnp.float32,
                    )
                    result = part if result is None else result + part
            outs[m][...] = result.astype(jnp.bfloat16)

    vmem = pl.BlockSpec(memory_space=pltpu.VMEM)
    flat = [array for lefts, right, transposed in pairs for array in (*lefts, right)]
    return pl.pallas_call(
        kernel,
        in_specs=[pl.BlockSpec(memory_space=pltpu.SMEM)] + [vmem] * len(flat),
        out_specs=[vmem] * parts,
        out_shape=[jax.ShapeDtypeStruct((row_count, width), jnp.bfloat16)] * parts,
        cost_estimate=pl.CostEstimate(
            flops=2 * row_count * sum(pair[1].size for pair in pairs),
            bytes_accessed=2 * sum(pair[1].size for pair in pairs),
            transcendentals=0,
        ),
        compiler_params=params(),
    )(my_part, *flat)


def exchange(blocks, axis):
    devices = lax.axis_size(axis)
    return [blocks[0]] + [
        lax.ppermute(blocks[m], axis, [(i, i ^ m) for i in range(devices)])
        for m in range(1, devices)
    ]


def total_of(blocks):
    total = blocks[0].astype(jnp.float32)
    for block in blocks[1:]:
        total = total + block.astype(jnp.float32)
    return total


def sum_over(block, axis):
    return total_of(exchange([block] * lax.axis_size(axis), axis))


def in_order(blocks, my_part, axis):
    stacked = jnp.stack(blocks)
    return jnp.concatenate(
        [
            lax.dynamic_index_in_dim(stacked, my_part ^ j, 0, keepdims=False)
            for j in range(len(blocks))
        ],
        axis=axis,
    )


def gather_states(block):
    devices = lax.axis_size("seq")
    if devices != 8:
        return lax.all_gather(block, "seq", axis=0, tiled=False), jnp.zeros((1,), jnp.int32)

    def moved(array, mask):
        return lax.ppermute(array, "seq", [(i, i ^ mask) for i in range(devices)])

    chips = [block] + [moved(block, mask) for mask in (2, 4, 6)]
    pairs = [(chip, moved(chip, 1)) for chip in chips]
    rows = jnp.stack([array for pair in pairs for array in pair])
    return rows, lax.axis_index("seq").astype(jnp.int32).reshape(1)


def weight_grad_blocks(left_t, right, right_block, col_count, positions, tables, blocks_a_step):
    row_total, depth = left_t.shape
    tiles = col_count // LANES
    piece_rows = 512
    even = tiles in (2, 4, 8, 16)
    step_rows = blocks_a_step * piece_rows // tiles
    steps = row_total // step_rows

    def kernel(positions_ref, left_ref, right_ref, *refs):
        table_refs = refs[len(tables) : 2 * len(tables)]
        product, staged, sem = refs[2 * len(tables) :]
        g = pl.program_id(0)
        slot = lax.rem(g, 2)

        def settle(which):
            pltpu.make_async_copy(staged.at[which], staged.at[which], sem.at[which]).wait()

        @pl.when(g >= 2)
        def _():
            settle(slot)

        left = left_ref[...]
        if even:
            product[...] = jnp.dot(left, right_ref[...], preferred_element_type=jnp.float32)
            for tile in range(step_rows // TILE * tiles):
                row_tile, column = divmod(tile, tiles)
                block, row = divmod(TILE * tile, piece_rows)
                staged[slot, block, row : row + TILE, :] = product[
                    TILE * row_tile : TILE * row_tile + TILE, LANES * column : LANES * column + LANES
                ].astype(jnp.bfloat16)
        else:
            for c in range(0, tiles, 2):
                width = min(2, tiles - c)
                part = jnp.dot(
                    left,
                    right_ref[:, LANES * c : LANES * (c + width)],
                    preferred_element_type=jnp.float32,
                )
                for w in range(width):
                    product[pl.ds(c + w, step_rows, stride=tiles), :] = part[
                        :, LANES * w : LANES * w + LANES
                    ]
            for block in range(blocks_a_step):
                staged[slot, block] = product[
                    piece_rows * block : piece_rows * block + piece_rows, :
                ].astype(jnp.bfloat16)
        for block in range(blocks_a_step):
            position = positions_ref[g * blocks_a_step + block]

            for number, table_ref in enumerate(table_refs):

                @pl.when(position // TABLE == number)
                def _():
                    pltpu.make_async_copy(
                        staged.at[slot, block],
                        table_ref.at[lax.rem(position, TABLE)],
                        sem.at[slot],
                    ).start()

        @pl.when(g == steps - 1)
        def _():
            settle(slot)
            if steps > 1:
                settle(1 - slot)

    anywhere = pl.BlockSpec(memory_space=pl.ANY)
    in_specs = [
        pl.BlockSpec((step_rows, depth), lambda g, positions: (g, 0)),
        pl.BlockSpec((depth, col_count), lambda g, positions: (0, right_block)),
    ] + [anywhere for table in tables]
    product_shape = (step_rows, col_count) if even else (step_rows * tiles, LANES)
    return pl.pallas_call(
        kernel,
        grid_spec=pltpu.PrefetchScalarGridSpec(
            num_scalar_prefetch=1,
            grid=(steps,),
            in_specs=in_specs,
            out_specs=[anywhere for table in tables],
            scratch_shapes=[
                pltpu.VMEM(product_shape, jnp.float32),
                pltpu.VMEM((2, blocks_a_step, piece_rows, LANES), jnp.bfloat16),
                pltpu.SemaphoreType.DMA((2,)),
            ],
        ),
        out_shape=[jax.ShapeDtypeStruct(table.shape, table.dtype) for table in tables],
        input_output_aliases={3 + i: i for i in range(len(tables))},
        cost_estimate=pl.CostEstimate(
            flops=2 * row_total * depth * col_count,
            bytes_accessed=2 * row_total * col_count,
            transcendentals=0,
        ),
        compiler_params=params(),
    )(positions, left_t, right, *tables)


def optimizer_update(
    sources, slot_sources, slot_rows, slot_kinds, kinds_used, slot_masks, small_rates,
    master, moment_one, moment_two, block_range, most_blocks, earlier,
):
    capacity, piece_size = master.shape
    chunks = piece_size // CHUNK
    rows = CHUNK // LANES
    last_block = pl.cdiv(capacity, 8) - 1
    steps = most_blocks * chunks

    def place(step, first, end):
        now = jnp.minimum(step, jnp.maximum((end - first) * chunks - 1, 0))
        return jnp.minimum(first + now // chunks, last_block), lax.rem(now, chunks)

    def kernel(range_ref, kinds_ref, sources_ref, rows_ref, *refs):
        source_refs, refs = refs[: len(sources)], refs[len(sources) :]
        masks_ref, small_ref, master_ref, one_ref, two_ref = refs[:5]
        refs = refs[5 + len(earlier) :]
        grad_out, master_out, one_out, two_out, low_out, scratch, buffer, sem = refs
        step = pl.program_id(0)
        count = jnp.maximum((range_ref[1] - range_ref[0]) * chunks, 1)
        first = place(step, range_ref[0], range_ref[1])[0] * 8
        slot = lax.rem(step, 2)

        def start(step, which):
            block, chunk = place(step, range_ref[0], range_ref[1])
            for s in range(8):
                for i, source_ref in enumerate(source_refs):

                    @pl.when(sources_ref[block * 8 + s] == i)
                    def _():
                        pltpu.make_async_copy(
                            source_ref.at[
                                rows_ref[block * 8 + s],
                                pl.ds(pl.multiple_of(chunk * rows, rows), rows),
                            ],
                            buffer.at[which, s],
                            sem.at[which],
                        ).start()

                @pl.when(sources_ref[block * 8 + s] >= len(sources))
                def _():
                    pltpu.make_async_copy(
                        source_refs[0].at[0, pl.ds(0, rows)], buffer.at[which, s], sem.at[which]
                    ).start()

        @pl.when(step == 0)
        def _():
            start(0, 0)

        @pl.when(step + 1 < count)
        def _():
            start(step + 1, 1 - slot)

        @pl.when(step < count)
        def _():
            pltpu.make_async_copy(buffer.at[slot], buffer.at[slot], sem.at[slot]).wait()
            for s in range(8):
                kind_now = kinds_ref[first + s]
                for kind in kinds_used:

                    @pl.when(kind_now == kind)
                    def _():
                        for tile in range(rows // TILE):
                            row_tile, column = divmod(tile, kind)
                            start_row = (row_tile * TILE * kind + column) * 8 + s
                            scratch[pl.ds(start_row, TILE, stride=8 * kind), :] = buffer[
                                slot, s, TILE * tile : TILE * tile + TILE, :
                            ].astype(jnp.float32)

            present = masks_ref[0] > 0.5
            is_small = masks_ref[1] > 0.5
            rate_rows = masks_ref[2]
            for j in range(rows):
                lanes = slice(LANES * j, LANES * j + LANES)
                grad = jnp.where(present, scratch[8 * j : 8 * j + 8, :], 0.0)
                rate = jnp.where(is_small, small_ref[:, lanes], rate_rows)
                master_now = master_ref[:, lanes]
                one_new = BETA_ONE * one_ref[:, lanes] + (1.0 - BETA_ONE) * grad
                two_new = BETA_TWO * two_ref[:, lanes] + (1.0 - BETA_TWO) * grad * grad
                first_hat = one_new / (1.0 - BETA_ONE**STEP)
                second_hat = two_new / (1.0 - BETA_TWO**STEP)
                master_new = master_now - rate * (
                    first_hat / (jnp.sqrt(second_hat) + ADAM_EPSILON) + WEIGHT_DECAY * master_now
                )
                grad_out[:, lanes] = grad
                master_out[:, lanes] = master_new
                one_out[:, lanes] = one_new
                two_out[:, lanes] = two_new
                low_out[:, lanes] = master_new.astype(jnp.bfloat16)

    state_spec = pl.BlockSpec((8, CHUNK), lambda t, ends, *tables: place(t, ends[0], ends[1]))
    anywhere = pl.BlockSpec(memory_space=pl.ANY)
    wide = jax.ShapeDtypeStruct((capacity, piece_size), jnp.float32)
    operands = [*sources, slot_masks, small_rates, master, moment_one, moment_two, *earlier]
    return pl.pallas_call(
        kernel,
        grid_spec=pltpu.PrefetchScalarGridSpec(
            num_scalar_prefetch=4,
            grid=(steps,),
            in_specs=[pl.BlockSpec(memory_space=pltpu.HBM) for source in sources]
            + [
                pl.BlockSpec((3, 8, LANES), lambda t, ends, *tables: (0, place(t, ends[0], ends[1])[0], 0)),
                pl.BlockSpec((1, CHUNK), lambda t, ends, *tables: (0, place(t, ends[0], ends[1])[1])),
                state_spec,
                state_spec,
                state_spec,
            ]
            + [anywhere for array in earlier],
            out_specs=[state_spec] * 5,
            scratch_shapes=[
                pltpu.VMEM((8 * rows, LANES), jnp.float32),
                pltpu.VMEM((2, 8, rows, LANES), jnp.bfloat16),
                pltpu.SemaphoreType.DMA((2,)),
            ],
        ),
        out_shape=[wide] * 4 + [jax.ShapeDtypeStruct((capacity, piece_size), jnp.bfloat16)],
        input_output_aliases={
            4 + len(operands) - len(earlier) + i: i for i in range(len(earlier))
        },
        cost_estimate=pl.CostEstimate(
            flops=20 * most_blocks * 8 * piece_size,
            bytes_accessed=16 * most_blocks * 8 * piece_size,
            transcendentals=2 * most_blocks * 8 * piece_size,
        ),
        compiler_params=params(),
    )(block_range, slot_kinds, slot_sources, slot_rows, *operands)


def weight_grad(left, right):
    return jnp.einsum("td,tc->dc", left, right, preferred_element_type=jnp.float32)


def back_product(grad_rows, weight):
    return jnp.dot(grad_rows, weight.T, preferred_element_type=jnp.float32)


def gather_rest(packed, first, trips, most, extra_step):
    devices = lax.axis_size("seq")
    rows = devices * extra_step
    room = reserve((most * rows,) + packed.shape[1:], packed.dtype)

    def more(trip, table):
        part = lax.dynamic_slice_in_dim(packed, first + trip * extra_step, extra_step)
        if devices != 8:
            part = lax.all_gather(part, "seq", axis=0, tiled=True)
            return lax.dynamic_update_slice_in_dim(table, part, trip * rows, axis=0)
        me = lax.axis_index("seq").astype(jnp.int32)
        chips = [part] + [moved_by(part, mask) for mask in (2, 4, 6)]
        for mask, chip in zip((0, 2, 4, 6), chips):
            for core, block in ((0, chip), (1, moved_by(chip, 1))):
                place = trip * rows + (me ^ (mask + core)) * extra_step
                table = lax.dynamic_update_slice_in_dim(table, block, place, axis=0)
        return table

    return lax.fori_loop(0, trips, more, room)


def reduce_rest(rest, trips, most, extra_step):
    devices = lax.axis_size("seq")
    rows = devices * extra_step
    room = reserve((most * extra_step,) + rest.shape[1:], rest.dtype)

    def more(trip, table):
        part = lax.dynamic_slice_in_dim(rest, trip * rows, rows)
        part = lax.psum_scatter(part, "seq", scatter_dimension=0, tiled=True)
        return lax.dynamic_update_slice_in_dim(table, part, trip * extra_step, axis=0)

    return lax.fori_loop(0, trips, more, room)


def on_device(inputs, cotangent, owners, master, moment_one, moment_two):
    head_parts = lax.axis_size("head")
    seq_parts = lax.axis_size("seq")
    local_heads = HEADS // head_parts
    capacity, piece_size = master.shape
    piece_count = owners.shape[0]
    row_count = inputs.shape[0]
    rim_width = KCONV - 1
    segments_list = shard_layout(local_heads, head_parts)
    columns = {name: c for name, r, c, rate in segments_list}
    counts = {name: r * c // piece_size for name, r, c, rate in segments_list[:8]}
    firsts = dict(zip(counts, np.cumsum([0] + list(counts.values())).tolist()))
    mixer_count = firsts["wgate"]
    big_count = piece_count - 1
    my_head = lax.axis_index("head").astype(jnp.int32)
    my_index = lax.axis_index("seq").astype(jnp.int32)
    my_head_row, my_index_row = my_head.reshape(1), my_index.reshape(1)

    onehot = (owners[:, None] == jnp.arange(seq_parts, dtype=jnp.int32)[None, :]).astype(jnp.int32)
    ranks = jnp.sum((jnp.cumsum(onehot, axis=0) - onehot) * onehot, axis=1)
    mixer_held = jnp.sum(onehot[:mixer_count], axis=0)
    mlp_held = jnp.sum(onehot[mixer_count:big_count], axis=0)
    padded = capacity + -capacity % 8
    small_rank = ranks[big_count]
    big_owners, big_ranks = owners[:big_count], ranks[:big_count]

    def rest_row(over, owner):
        return over // extra_step * (seq_parts * extra_step) + owner * extra_step + over % extra_step

    early = -(-capacity * FIRST_GATHER // (8 * CAPACITY_UNIT)) * 8
    late = capacity - early
    late_room = min(late, -(-capacity * SECOND_GATHER // CAPACITY_UNIT))
    extra_step = 2 if late % 2 == 0 else 1
    most_gather = -(-late // extra_step)
    trips_gather = jnp.maximum(-(-(jnp.max(mixer_held) - early) // extra_step), 0)
    early_row = big_owners * early + big_ranks
    mixer_fetch = jnp.where(
        big_ranks < early, early_row, TABLE + rest_row(big_ranks - early, big_owners)
    )
    neighbours = np.arange(seq_parts) ^ 1
    late_held = jnp.maximum(mixer_held + mlp_held - early, 0)
    late_spare = jnp.maximum(late_room - late_held[neighbours], 0)
    late_over = jnp.maximum(late_held - late_room, 0)
    trips_late = -(-jnp.max(jnp.maximum(late_over - late_spare, 0)) // extra_step)
    spare_there = jnp.sum(onehot[:big_count] * late_spare[None, :], axis=1)
    past = big_ranks - early - late_room
    rest_trip = (past - spare_there) // extra_step
    rest_start = late_room + spare_there + rest_trip * extra_step
    rest_start = jnp.minimum(rest_start, late - extra_step)
    mlp_fetch = jnp.where(
        big_ranks < early,
        TABLE + early_row,
        jnp.where(
            past < 0,
            big_owners * late_room + big_ranks - early,
            jnp.where(
                past < spare_there,
                (big_owners ^ 1) * late_room + late_room - spare_there + past,
                2 * TABLE
                + rest_trip * (seq_parts * extra_step)
                + big_owners * extra_step
                + big_ranks - early - rest_start,
            ),
        ),
    )
    first_room = -(-capacity * FIRST_REDUCE // CAPACITY_UNIT)
    second_room = -(-capacity * SECOND_REDUCE // CAPACITY_UNIT)
    most_reduce = -(-(capacity - second_room) // extra_step)
    second_held = mixer_held + jnp.maximum(mlp_held - first_room, 0)
    second_there = jnp.sum(onehot[:big_count] * second_held[None, :], axis=1)
    spill_plan, spill_taken = [], jnp.zeros_like(second_held)
    hosted = jnp.zeros_like(second_held)
    over_held = jnp.maximum(second_held - second_room, 0)
    for mask, most in (((1, 6), (2, 4), (4, 4), (6, 4)) if seq_parts == 8 else ((1, 4),)):
        most = min(most, second_room)
        partner = np.arange(seq_parts) ^ mask
        free = jnp.maximum(second_room - second_held - hosted, 0)[partner]
        take = jnp.minimum(jnp.minimum(over_held - spill_taken, most - hosted[partner]), free)
        take = jnp.maximum(take, 0)
        first_row = second_room - hosted[partner] - take
        spill_plan.append((mask, most, spill_taken, take, first_row))
        spill_taken = spill_taken + take
        hosted = hosted + take[partner]
    trips_reduce = -(-jnp.max(over_held - spill_taken) // extra_step)

    def of_owner(values):
        return jnp.sum(onehot[:big_count] * values[None, :], axis=1)

    second_over = big_ranks - second_room
    second_spot = jnp.where(
        second_over < 0,
        TABLE + big_owners * second_room + big_ranks,
        2 * TABLE + rest_row(second_over - of_owner(spill_taken), big_owners),
    )
    for mask, most, before, take, first_row in spill_plan:
        inside = second_over - of_owner(before)
        second_spot = jnp.where(
            (inside >= 0) & (inside < of_owner(take)),
            TABLE + (big_owners ^ mask) * second_room + of_owner(first_row) + inside,
            second_spot,
        )
    store = jnp.where(
        big_ranks >= second_there,
        big_owners * first_room + big_ranks - second_there,
        second_spot,
    )
    small_owner = owners[big_count]

    def spots(table, name):
        return table[firsts[name] : firsts[name] + counts[name]]

    my_mixer = mixer_held[my_index]
    my_mlp = mlp_held[my_index]
    my_count = my_mixer + my_mlp
    slot_ids = jnp.arange(padded, dtype=jnp.int32)
    mine = owners == my_index
    matches = (mine[None, :] & (ranks[None, :] == slot_ids[:, None])).astype(jnp.int32)
    kind_table = piece_kinds(segments_list, piece_count, piece_size)
    piece_rates, small_rates = rate_parts(segments_list, piece_count, piece_size)
    present = jnp.sum(matches, axis=1)
    slot_kinds = 1 + jnp.sum(matches * jnp.asarray(kind_table - 1)[None, :], axis=1)
    slot_rates = PAD_RATE + jnp.sum(
        matches.astype(jnp.float32) * jnp.asarray(piece_rates - np.float32(PAD_RATE))[None, :], axis=1
    )
    is_small = matches[:, big_count]
    kinds_used = sorted(set(kind_table.tolist()) | {1})
    my_held = second_held[my_index]
    in_first = slot_ids >= my_held
    my_over = slot_ids - second_room
    rest_source = 3 + len(spill_plan)
    slot_sources = jnp.where(my_over < 0, 2, rest_source)
    slot_rows = jnp.where(my_over < 0, slot_ids, my_over - spill_taken[my_index])
    for number, (mask, most, before, take, first_row) in enumerate(spill_plan):
        inside = my_over - before[my_index]
        here = (inside >= 0) & (inside < take[my_index])
        slot_sources = jnp.where(here, 3 + number, slot_sources)
        slot_rows = jnp.where(
            here, first_row[my_index] + inside - (second_room - most), slot_rows
        )
    slot_sources = jnp.where(in_first, 0, slot_sources)
    slot_rows = jnp.where(in_first, slot_ids - my_held, slot_rows)
    slot_sources = jnp.where(present > 0, jnp.where(is_small > 0, 1, slot_sources), 0)
    slot_rows = jnp.where(is_small > 0, 0, slot_rows)
    slot_rows = jnp.where(present > 0, slot_rows, 0)
    slot_masks = jnp.stack([present.astype(jnp.float32), is_small.astype(jnp.float32), slot_rates])
    slot_masks = jnp.broadcast_to(slot_masks[:, :, None], slot_masks.shape + (LANES,))
    all_blocks = padded // 8
    plain_blocks = second_room // 8
    from_first = jnp.clip((my_held + 7) // 8, plain_blocks, all_blocks).astype(jnp.int32)
    ranges = [
        jnp.stack([from_first, jnp.int32(all_blocks)]),
        jnp.array([0, plain_blocks], jnp.int32),
        jnp.stack([jnp.int32(plain_blocks), jnp.maximum(from_first, plain_blocks + 1)]),
    ]

    small_rows = -(-sum(r * c for name, r, c, rate in segments_list[8:]) // (TILE * LANES)) * TILE
    gain_width = D // head_parts
    norm_width = DV // head_parts
    gain_first = sum(r * c for name, r, c, rate in segments_list[8:14])
    my_small = lax.dynamic_slice(master, (small_rank, 0), (1, small_rows * LANES))
    my_small = my_small.astype(jnp.bfloat16)
    gains = my_small[:, gain_first : gain_first + 2 * gain_width + norm_width]
    gains = in_order(exchange([gains] * head_parts, "head"), my_head, 0)
    gains = jnp.concatenate(
        [
            gains[:, :gain_width].reshape(1, D),
            gains[:, gain_width : 2 * gain_width].reshape(1, D),
            gains[:, 2 * gain_width :].reshape(1, DV),
        ],
        axis=1,
    )
    rows_of_piece = piece_size // LANES
    small_width = small_rows * LANES
    small_part = jnp.concatenate([my_small, gains], axis=1).reshape(-1, LANES)
    small_table, small_base = gather_states(small_part)
    input_blocks = exchange([inputs] * head_parts, "head")
    early_part = pack_blocks(master, slot_kinds, kinds_used, 0, early)
    early_table = lax.all_gather(early_part, "seq", axis=0, tiled=True)
    late_part = pack_blocks(master, slot_kinds, kinds_used, early, late)
    late_send = late_part[:late_room]
    if late_room < late:
        guests = lax.ppermute(
            late_part[late_room:], "seq", [(i, i ^ 1) for i in range(seq_parts)]
        )
        late_send = lax.dynamic_update_slice_in_dim(
            late_part, guests, late_held[my_index], axis=0
        )[:late_room]
    back_blocks = exchange([cotangent] * head_parts, "head")
    rows_full = in_order(input_blocks, my_head, 1)
    back_full = in_order(back_blocks, my_head, 1)
    small_flat = lax.dynamic_index_in_dim(
        small_table, small_owner ^ small_base[0], axis=0, keepdims=False
    ).reshape(-1)
    by_name, small_used = unpack(small_flat, segments_list[8:])
    gains = small_flat[small_width:].astype(jnp.float32)[None, :]
    gain_one, gain_two, norm_row = gains[:, :D], gains[:, D : 2 * D], gains[:, 2 * D :]
    gain_one_mine = by_name["gainone"].astype(jnp.float32)
    gain_two_mine = by_name["gaintwo"].astype(jnp.float32)

    rows_wide = rows_full.astype(jnp.float32)
    scale_one = lax.rsqrt(jnp.mean(rows_wide * rows_wide, axis=-1, keepdims=True) + NORM_EPSILON)
    normed = (rows_wide * scale_one * gain_one).astype(jnp.bfloat16)
    normed_ext = jnp.concatenate([shifted(normed[row_count - RIM :], "seq", 1), normed], axis=0)

    decay_weight = jnp.pad(by_name["wab"], ((0, 0), (0, LANES - 2 * local_heads)))
    decay_proj = jnp.dot(normed, decay_weight, preferred_element_type=jnp.float32)
    taps = jnp.concatenate([by_name["cv"], by_name["ck"]], axis=1)
    taps = jnp.pad(taps.astype(jnp.float32), ((0, 8 - KCONV), (0, 0)))
    query_taps = jnp.pad(by_name["cq"].astype(jnp.float32), ((0, 8 - KCONV), (0, 0)))
    scalars = jnp.pad(
        jnp.concatenate([by_name["alog"], by_name["dtbias"]], axis=0).astype(jnp.float32),
        ((0, 6), (0, LANES - local_heads)),
    )

    beside = (
        trips_gather, late_part, late_send, normed, normed_ext, scale_one, decay_proj, decay_weight, taps, query_taps, scalars,
        back_full, mixer_fetch, mlp_fetch, store, gain_two, norm_row,
        slot_sources, slot_rows, slot_masks, ranges, trips_late, trips_reduce,
    )
    early_table, beside = lax.optimization_barrier((early_table, beside))
    (
        trips_now, late_part, late_send, normed, normed_ext, scale_one, decay_proj, decay_weight, taps, query_taps, scalars,
        back_full, mixer_fetch, mlp_fetch, store, gain_two, norm_row,
        slot_sources, slot_rows, slot_masks, ranges, trips_late, trips_reduce,
    ) = beside
    mixer_rest = gather_rest(late_part, 0, trips_now, most_gather, extra_step)
    late_table = lax.all_gather(late_send, "seq", axis=0, tiled=True)

    value_key_weights, value_key = assemble(
        [early_table, mixer_rest],
        [(spots(mixer_fetch, name), columns[name]) for name in ("wv", "wk")],
        512,
        normed_ext,
    )
    solve, fresh, wy_keys, handoff = mixer_local(
        local_heads, value_key, taps, decay_proj, scalars
    )
    query_gate_weights, query_gate = assemble(
        [early_table, mixer_rest],
        [(spots(mixer_fetch, name), columns[name]) for name in ("wq", "wg")],
        512,
        normed_ext,
    )
    reach, zero_out = mixer_reach(
        local_heads, query_gate, value_key, query_taps, taps, decay_proj, scalars, fresh, wy_keys
    )
    (out_weights,) = assemble(
        [early_table, mixer_rest], [(spots(mixer_fetch, "wo"), columns["wo"])], 256
    )
    entering_state, kept_states, beside = entering(
        local_heads,
        my_index_row,
        handoff,
        (query_gate_weights, query_gate, reach, zero_out, out_weights),
    )
    query_gate_weights, query_gate, reach, zero_out, out_weights = beside
    recurred, gated_low = mixer_out(
        local_heads, entering_state, reach, zero_out, query_gate, norm_row
    )
    mixed_parts = exchange(
        spread_products(my_head_row, head_parts, [((gated_low,), out_weights, False)]), "head"
    )
    mixed = total_of(mixed_parts)
    inputs_wide = inputs.astype(jnp.float32)
    residual = inputs_wide + mixed
    resid_low = residual.astype(jnp.bfloat16)

    resid_blocks = exchange([resid_low] * head_parts, "head")
    trips_now, late_table = lax.optimization_barrier((trips_late, late_table))
    late_rest = gather_rest(
        late_part, late_room + late_spare[my_index], trips_now, most_gather, extra_step
    )
    mlp_tables = [late_table, early_table, late_rest]
    (down_weights,) = assemble(
        mlp_tables, [(spots(mlp_fetch, "wdown"), columns["wdown"])], 352
    )
    (mlp_weights,) = assemble(
        mlp_tables,
        [(spots(mlp_fetch, name), columns[name]) for name in ("wgate", "wup")],
        512,
    )
    resid_blocks, down_weights, mlp_weights = lax.optimization_barrier(
        (resid_blocks, down_weights, mlp_weights)
    )
    resid_full = in_order(resid_blocks, my_head, 1).astype(jnp.float32)
    scale_two = lax.rsqrt(jnp.mean(resid_full * resid_full, axis=-1, keepdims=True) + NORM_EPSILON)
    hidden_in = (resid_full * scale_two * gain_two).astype(jnp.bfloat16)
    gate_up = jnp.dot(hidden_in, mlp_weights, preferred_element_type=jnp.float32)
    hidden_width = columns["wgate"]
    gate_mlp, up_mlp = gate_up[:, :hidden_width], gate_up[:, hidden_width:]
    logistic_output_multiplier = jax.nn.sigmoid(gate_mlp)
    silu_gate = gate_mlp * logistic_output_multiplier
    hidden = (silu_gate * up_mlp).astype(jnp.bfloat16)
    mlp_blocks = spread_products(my_head_row, head_parts, [((hidden,), down_weights, False)])
    d_hidden = back_product(back_full, down_weights)
    d_gate_mlp = (
        d_hidden
        * up_mlp
        * logistic_output_multiplier
        * (1.0 + gate_mlp * (1.0 - logistic_output_multiplier))
    ).astype(jnp.bfloat16)
    d_up_mlp = (d_hidden * silu_gate).astype(jnp.bfloat16)
    def store_grad(tables, name, left_t, right, right_block, blocks_a_step):
        return weight_grad_blocks(
            left_t, right, right_block, columns[name], spots(store, name), tables, blocks_a_step
        )

    grad_tables = [
        reserve((rows, rows_of_piece, LANES), jnp.bfloat16)
        for rows in (
            seq_parts * first_room,
            seq_parts * second_room,
            most_reduce * seq_parts * extra_step,
        )
    ]
    grad_tables = store_grad(grad_tables, "wdown", hidden.T, back_full, 0, 11)
    hidden_in_t = hidden_in.T
    grad_tables = store_grad(grad_tables, "wgate", hidden_in_t, d_gate_mlp, 0, 11)
    grad_tables = store_grad(grad_tables, "wup", hidden_in_t, d_up_mlp, 0, 11)
    grad_tables, d_gate_mlp, d_up_mlp = lax.optimization_barrier(
        (grad_tables, d_gate_mlp, d_up_mlp)
    )
    d_hidden_parts = exchange(
        spread_products(my_head_row, head_parts, [((d_gate_mlp, d_up_mlp), mlp_weights, True)]), "head"
    )
    first_reduced = lax.psum_scatter(grad_tables[0], "seq", scatter_dimension=0, tiled=True)
    grad_tables = grad_tables[1:]
    store = store - TABLE
    d_hidden_mine = total_of(d_hidden_parts)

    resid_mine = resid_low.astype(jnp.float32)
    d_hidden_low = d_hidden_mine.astype(jnp.bfloat16)
    dot_mine = jnp.sum(d_hidden_mine * gain_two_mine * resid_mine, axis=-1)
    d_hidden_blocks = exchange([d_hidden_low] * head_parts, "head")
    dot_two = sum_over(dot_mine.reshape(-1, LANES), "head").reshape(row_count, 1)
    grad_gaintwo = jnp.sum(d_hidden_mine * resid_mine * scale_two, axis=0)
    d_resid = (
        cotangent.astype(jnp.float32)
        + scale_two * d_hidden_mine * gain_two_mine
        - scale_two**3 / D * resid_mine * dot_two
    )
    d_hidden_full = in_order(d_hidden_blocks, my_head, 1).astype(jnp.float32)
    back_mix_full = (
        back_full.astype(jnp.float32)
        + scale_two * d_hidden_full * gain_two
        - scale_two**3 / D * resid_full * dot_two
    ).astype(jnp.bfloat16)

    d_gated = back_product(back_mix_full, out_weights)
    d_recurred, d_gate, norm_grad, d_entering = mixer_gate_back(
        local_heads, d_gated, recurred, query_gate, norm_row, reach
    )
    normed_t = normed.T
    grad_tables = store_grad(grad_tables, "wo", gated_low.T, back_mix_full, 0, 8)
    grad_tables = store_grad(grad_tables, "wg", normed_t, d_gate, 0, 8)
    d_leaving, (grad_tables, mlp_blocks) = leaving(
        local_heads, my_index_row, d_entering, kept_states, (grad_tables, mlp_blocks)
    )
    mlp_parts = exchange(mlp_blocks, "head")
    d_conv, d_tail, d_rim, d_taps, d_decay_wide, d_scalars = mixer_back(
        local_heads,
        query_gate,
        value_key,
        query_taps,
        taps,
        decay_proj,
        scalars,
        solve,
        fresh,
        wy_keys,
        entering_state,
        d_recurred,
        d_leaving,
    )
    d_rims = shifted(tuple(part[8 - rim_width :] for part in d_rim), "seq", -1)

    def with_rim(whole, tail, rim_grad):
        tail = tail + jnp.pad(rim_grad, ((8 - rim_width, 0), (0, 0)))
        return lax.dynamic_update_slice(whole, tail.astype(jnp.bfloat16), (row_count - 8, 0))

    d_query, d_value_key = (
        with_rim(*parts) for parts in zip(d_conv, d_tail, d_rims)
    )
    grad_tables = store_grad(grad_tables, "wv", normed_t, d_value_key, 0, 8)
    grad_tables = store_grad(grad_tables, "wk", normed_t, d_value_key, 2, 4)
    grad_tables = store_grad(grad_tables, "wq", normed_t, d_query, 0, 4)
    second_table, first_reduced, mlp_parts = lax.optimization_barrier(
        (grad_tables[0], first_reduced, mlp_parts)
    )
    block_out = (residual + total_of(mlp_parts)).astype(jnp.bfloat16)
    second_reduced = lax.psum_scatter(second_table, "seq", scatter_dimension=0, tiled=True)
    d_decay = d_decay_wide.astype(jnp.bfloat16)
    grad_wab = weight_grad(normed, d_decay)[:, : 2 * local_heads]
    d_normed_mine = total_of(
        exchange(
            spread_products(
                my_head_row,
                head_parts,
                [
                    ((d_value_key,), value_key_weights, True),
                    ((d_query, d_gate), query_gate_weights, True),
                    ((d_decay,), decay_weight, True),
                ],
            ),
            "head",
        )
    )
    dot_one = jnp.sum(d_normed_mine * gain_one_mine * inputs_wide, axis=-1)
    sums = sum_over(
        jnp.concatenate([dot_one.reshape(-1, LANES), norm_grad[0].reshape(-1, LANES)]), "head"
    )
    dot_one = sums[: row_count // LANES].reshape(row_count, 1)
    grad_wnorm = lax.dynamic_slice_in_dim(
        sums[row_count // LANES :].reshape(-1), my_head * norm_width, norm_width
    )
    grad_gainone = jnp.sum(d_normed_mine * inputs_wide * scale_one, axis=0)
    input_grad = (
        d_resid
        + scale_one * d_normed_mine * gain_one_mine
        - scale_one**3 / D * inputs_wide * dot_one
    )

    small_grads = [
        d_taps[0][:KCONV],
        d_taps[1][:KCONV, local_heads * DV :],
        d_taps[1][:KCONV, : local_heads * DV],
        grad_wab,
        d_scalars[0, :local_heads],
        d_scalars[1, :local_heads],
        grad_gainone,
        grad_gaintwo,
        grad_wnorm,
    ]
    small_block = jnp.concatenate(
        [grad_now.reshape(-1) for grad_now in small_grads]
        + [jnp.zeros((small_rows * LANES - small_used,), jnp.float32)]
    ).reshape(-1, LANES)
    mask = 1
    while mask < seq_parts:
        small_block = small_block + lax.ppermute(
            small_block, "seq", [(i, i ^ mask) for i in range(seq_parts)]
        )
        mask *= 2
    small_block = jnp.pad(
        small_block.astype(jnp.bfloat16), ((0, rows_of_piece - small_rows), (0, 0))
    )[None]

    def update(sources, block_range, most_blocks, earlier):
        return optimizer_update(
            sources,
            slot_sources,
            slot_rows,
            slot_kinds,
            kinds_used,
            slot_masks,
            jnp.asarray(small_rates)[None, :],
            master,
            moment_one,
            moment_two,
            block_range,
            most_blocks,
            earlier,
        )

    done = update([first_reduced, small_block], ranges[0], all_blocks - plain_blocks, [])
    done, second_reduced, input_grad, block_out = lax.optimization_barrier(
        (done, second_reduced, input_grad, block_out)
    )
    spilled = []
    for mask, most, before, take, first_row in spill_plan:
        spilled.append(moved_by(second_reduced[second_room - most :], mask))
    sources = [first_reduced, small_block, second_reduced]
    if plain_blocks:
        done = update(sources, ranges[1], plain_blocks, done)
    done, spilled, rest_grads, trips_now = lax.optimization_barrier(
        (done, spilled, grad_tables[1], trips_reduce)
    )
    rest_reduced = reduce_rest(rest_grads, trips_now, most_reduce, extra_step)
    grad_slots, master_new, moment_new, second_new, weights_low = update(
        sources + spilled + [rest_reduced],
        ranges[2],
        all_blocks - plain_blocks,
        done,
    )
    return (
        block_out,
        input_grad,
        grad_slots,
        master_new,
        moment_new,
        second_new,
        weights_low,
    )


def solution(mesh):
    return jax.shard_map(
        on_device,
        mesh=mesh,
        in_specs=(
            P("seq", "head"),
            P("seq", "head"),
            P(),
            P("seq", "head"),
            P("seq", "head"),
            P("seq", "head"),
        ),
        out_specs=(
            P("seq", "head"),
            P("seq", "head"),
            P("seq", "head"),
            P("seq", "head"),
            P("seq", "head"),
            P("seq", "head"),
            P("seq", "head"),
        ),
        check_vma=False,
    )
```

```python
import jax
import jax.numpy as jnp
import numpy as np
from jax import lax
from jax.experimental import pallas as pl
from jax.experimental.pallas import tpu as pltpu
from jax.sharding import PartitionSpec as P

D = 2048
HEADS = 16
DK = 128
DV = 256
FF = 5632
KCONV = 4
STEP = 5


EXACT_ARITHMETIC = lax.Precision.HIGHEST
NORM_EPSILON = 1e-06
UNIT_EPSILON = 1e-06
HEAD_EPSILON = 1e-05
ADAM_EPSILON = 1e-08
BETA_ONE = 0.5
BETA_TWO = 0.5
WEIGHT_DECAY = 0.1
PAD_RATE = 0.1


def shifted(block, axis, distance):
    devices = range(lax.axis_size(axis))
    route = [(i - distance, i) for i in devices if i - distance in devices]
    return lax.ppermute(block, axis, route)


def shard_layout(local_heads, head_parts):
    return [
        ("wq", D, local_heads * DK, 0.02),
        ("wk", D, local_heads * DK, 0.02),
        ("wv", D, local_heads * DV, 0.02),
        ("wg", D, local_heads * DV, 0.02),
        ("wo", local_heads * DV, D, 0.015),
        ("wgate", D, FF // head_parts, 0.02),
        ("wup", D, FF // head_parts, 0.02),
        ("wdown", FF // head_parts, D, 0.012),
        ("cq", KCONV, local_heads * DK, 0.4),
        ("ck", KCONV, local_heads * DK, 0.4),
        ("cv", KCONV, local_heads * DV, 0.4),
        ("wab", D, 2 * local_heads, 0.04),
        ("alog", 1, local_heads, 0.5),
        ("dtbias", 1, local_heads, 0.5),
        ("gainone", 1, D // head_parts, 0.1),
        ("gaintwo", 1, D // head_parts, 0.1),
        ("wnorm", 1, DV // head_parts, 0.1),
    ]


def piece_table(owners, seq_parts, capacity):
    piece_count = owners.shape[0]
    devices = jnp.arange(seq_parts, dtype=jnp.int32)
    onehot = (owners[:, None] == devices[None, :]).astype(jnp.int32)
    before = jnp.cumsum(onehot, axis=0) - onehot
    rank_within = jnp.sum(before * onehot, axis=1)
    slot_of_piece = owners * capacity + rank_within
    matches = slot_of_piece[None, :] == jnp.arange(seq_parts * capacity, dtype=jnp.int32)[:, None]
    present = jnp.any(matches, axis=1)
    piece_of_slot = jnp.sum(
        matches.astype(jnp.int32) * jnp.arange(piece_count, dtype=jnp.int32)[None, :], axis=1
    )
    return (slot_of_piece, piece_of_slot, present)


def unpack(flat_weights, segments_list):
    by_name = {}
    offset_now = 0
    for seg_name, row_count, col_count, seg_rate in segments_list:
        by_name[seg_name] = flat_weights[offset_now : offset_now + row_count * col_count].reshape(
            row_count, col_count
        )
        offset_now += row_count * col_count
    return (by_name, offset_now)


def rate_parts(segments_list, piece_count, piece_size):
    piece_rates = np.full(piece_count, PAD_RATE, np.float32)
    small_rates = np.full(piece_size, PAD_RATE, np.float32)
    offset_now = 0
    big_total = (piece_count - 1) * piece_size
    for seg_name, row_count, col_count, seg_rate in segments_list:
        seg_size = row_count * col_count
        if offset_now < big_total:
            piece_rates[offset_now // piece_size : (offset_now + seg_size) // piece_size] = seg_rate
        else:
            small_rates[offset_now - big_total : offset_now - big_total + seg_size] = seg_rate
        offset_now += seg_size
    return (piece_rates, small_rates)


HEADS_A_STEP = 1


def product(left, right, left_axis, right_axis, exact=False):
    def dot(a, b):
        return lax.dot_general(
            a,
            b,
            (((left_axis,), (right_axis,)), ((), ())),
            preferred_element_type=jnp.float32,
        )

    left_low, right_low = left.astype(jnp.bfloat16), right.astype(jnp.bfloat16)
    if not exact:
        return dot(left_low, right_low)
    left_rest = (left - left_low.astype(jnp.float32)).astype(jnp.bfloat16)
    right_rest = (right - right_low.astype(jnp.float32)).astype(jnp.bfloat16)
    return dot(left_low, right_low) + (dot(left_low, right_rest) + dot(left_rest, right_low))


def take_lane(wide, lane):
    lanes = lax.broadcasted_iota(jnp.int32, wide.shape, 1)
    return jnp.sum(jnp.where(lanes == lane, wide, 0.0), axis=1, keepdims=True)


def put_lane(column, lane):
    lanes = lax.broadcasted_iota(jnp.int32, (column.shape[0], 128), 1)
    return jnp.where(lanes == lane, column, 0.0)


def to_row(column, diagonal):
    return jnp.sum(jnp.where(diagonal, column, 0.0), axis=0, keepdims=True)


def convolved(extended, taps_ref, columns):
    row_count = extended.shape[0] - RIM
    first = RIM - (KCONV - 1)
    running = taps_ref[0:1, columns] * extended[first : first + row_count, columns]
    for tap in range(1, KCONV):
        running = running + taps_ref[tap : tap + 1, columns] * extended[
            first + tap : first + tap + row_count, columns
        ]
    return running


def decay_terms(head, local_heads, decay_ref, scalars_ref):
    row_count = decay_ref.shape[0]
    shape = (row_count, row_count)
    row_ids = lax.broadcasted_iota(jnp.int32, shape, 0)
    column_ids = lax.broadcasted_iota(jnp.int32, shape, 1)
    decay_in = take_lane(decay_ref[...], head) + take_lane(scalars_ref[1:2, :], head)
    rate = -jnp.exp(take_lane(scalars_ref[0:1, :], head))
    soft = jnp.maximum(decay_in, 0.0) + jnp.log1p(jnp.exp(-jnp.abs(decay_in)))
    logs = rate * soft
    beta = jax.nn.sigmoid(take_lane(decay_ref[...], head + local_heads))
    diagonal = row_ids == column_ids
    logs_row = to_row(logs, diagonal)
    upto = row_ids >= column_ids
    sums = jnp.sum(jnp.where(upto, logs_row, 0.0), axis=1, keepdims=True)
    sums_row = to_row(sums, diagonal)
    within = jnp.exp(jnp.where(upto, sums - sums_row, -1e30))
    return decay_in, rate, logs, beta, sums, within, row_ids, column_ids


def unit_rows(rows):
    scale = lax.rsqrt(jnp.sum(rows * rows, axis=-1, keepdims=True) + UNIT_EPSILON)
    return rows * scale, scale


def mixer_specs(local_heads, row_count):
    def spec(rows, width, first):
        width *= HEADS_A_STEP
        return pl.BlockSpec((rows, width), lambda h, first=first // width: (0, first + h))

    def query(rows):
        return spec(rows, DK, 0)

    def key(rows):
        return spec(rows, DK, local_heads * DV)

    def value(rows):
        return spec(rows, DV, 0)

    whole = pl.BlockSpec((row_count, 128), lambda h: (0, 0))
    scalars = pl.BlockSpec((8, 128), lambda h: (0, 0))
    return query, key, value, whole, scalars


def per_head(*shape):
    return pl.BlockSpec((HEADS_A_STEP,) + shape, lambda h: (h,) + (0,) * len(shape))


def head_columns(sub):
    return slice(DK * sub, DK * sub + DK), slice(DV * sub, DV * sub + DV)


def mixer_local(local_heads, value_key, taps, decay_proj, scalars):
    row_count = value_key.shape[0] - RIM
    query, key, value, whole, scalar_spec = mixer_specs(local_heads, row_count)

    def kernel(
        pv, pk, tv, tk, decay_ref, scalars_ref, solve_ref, fresh_ref, wy_ref, handoff_ref
    ):
        for sub in range(HEADS_A_STEP):
            head = pl.program_id(0) * HEADS_A_STEP + sub
            narrow, wide = head_columns(sub)
            key_rows = unit_rows(jax.nn.silu(convolved(pk, tk, narrow)))[0]
            values = jax.nn.silu(convolved(pv, tv, wide))
            decay_in, rate, logs, beta, sums, within, row_ids, column_ids = decay_terms(
                head, local_heads, decay_ref, scalars_ref
            )
            gram = product(key_rows, key_rows, 1, 1, True)
            system = jnp.where(row_ids > column_ids, beta * gram * within, 0.0)
            unit = jnp.where(row_ids == column_ids, 1.0, 0.0)
            solve = unit
            size = 1
            while size < row_count:
                lower = (row_ids // (2 * size) == column_ids // (2 * size)) & (
                    row_ids // size != column_ids // size
                )
                part = jnp.where(lower, system, 0.0)
                if size == 1:
                    solve = solve - part
                else:
                    solve = solve - product(solve, product(part, solve, 1, 0), 1, 0)
                size *= 2
            remainder = (unit - solve) - product(system, solve, 1, 0, True)
            solve = solve + product(solve, remainder, 1, 0)
            grown = jnp.exp(sums)
            fresh = product(solve, beta * values, 1, 0, True)
            wy_keys = product(solve, (beta * grown) * key_rows, 1, 0, True)
            last = sums[row_count - 1 : row_count, :]
            tail_keys = jnp.exp(last - sums) * key_rows
            eye = lax.broadcasted_iota(jnp.int32, (DK, DK), 0) == lax.broadcasted_iota(
                jnp.int32, (DK, DK), 1
            )
            solve_ref[sub] = solve
            fresh_ref[sub] = fresh
            wy_ref[sub] = wy_keys
            handoff_ref[sub, :, :DK] = (
                jnp.where(eye, jnp.exp(last), 0.0) - product(tail_keys, wy_keys, 0, 0)
            ).astype(jnp.bfloat16)
            handoff_ref[sub, :, DK:] = product(tail_keys, fresh, 0, 0).astype(jnp.bfloat16)

    def out(*shape, kind=jnp.float32):
        return jax.ShapeDtypeStruct((local_heads,) + shape, kind)

    return pl.pallas_call(
        kernel,
        grid=(local_heads // HEADS_A_STEP,),
        in_specs=[
            value(RIM + row_count), key(RIM + row_count), value(8), key(8), whole, scalar_spec,
        ],
        out_specs=[
            per_head(row_count, row_count),
            per_head(row_count, DV),
            per_head(row_count, DK),
            per_head(DK, DK + DV),
        ],
        out_shape=[
            out(row_count, row_count),
            out(row_count, DV),
            out(row_count, DK),
            out(DK, DK + DV, kind=jnp.bfloat16),
        ],
        compiler_params=params(),
    )(value_key, value_key, taps, taps, decay_proj, scalars)


def mixer_reach(local_heads, query_gate, value_key, query_taps, taps, decay_proj, scalars, fresh, wy_keys):
    row_count = value_key.shape[0] - RIM
    query, key, value, whole, scalar_spec = mixer_specs(local_heads, row_count)

    def kernel(pq, pk, tq, tk, decay_ref, scalars_ref, fresh_ref, wy_ref, reach_ref, zero_ref):
        for sub in range(HEADS_A_STEP):
            head = pl.program_id(0) * HEADS_A_STEP + sub
            narrow, wide = head_columns(sub)
            queries = unit_rows(jax.nn.silu(convolved(pq, tq, narrow)))[0] * DK ** (-0.5)
            key_rows = unit_rows(jax.nn.silu(convolved(pk, tk, narrow)))[0]
            decay_in, rate, logs, beta, sums, within, row_ids, column_ids = decay_terms(
                head, local_heads, decay_ref, scalars_ref
            )
            attention = product(queries, key_rows, 1, 1) * within
            reach_ref[sub] = jnp.exp(sums) * queries - product(attention, wy_ref[sub], 1, 0)
            zero_ref[sub] = product(attention, fresh_ref[sub], 1, 0)

    return pl.pallas_call(
        kernel,
        grid=(local_heads // HEADS_A_STEP,),
        in_specs=[
            query(RIM + row_count), key(RIM + row_count), query(8), key(8), whole, scalar_spec,
            per_head(row_count, DV),
            per_head(row_count, DK),
        ],
        out_specs=[per_head(row_count, DK), per_head(row_count, DV)],
        out_shape=[
            jax.ShapeDtypeStruct((local_heads, row_count, DK), jnp.float32),
            jax.ShapeDtypeStruct((local_heads, row_count, DV), jnp.float32),
        ],
        compiler_params=params(),
    )(query_gate, value_key, query_taps, taps, decay_proj, scalars, fresh, wy_keys)


def advance_state(block, state, back):
    moved = product(block[:, :DK].astype(jnp.float32), state, 0 if back else 1, 0)
    return moved, block[:, DK:].astype(jnp.float32)


def chain_all(local_heads, my_index, handoffs, inputs, back):
    devices = handoffs.shape[0]

    def kernel(index_ref, handoffs_ref, inputs_ref, state_ref):
        state_ref[...] = jnp.zeros_like(state_ref)

        def advance(step, carry):
            j = devices - 1 - step if back else step
            for h in range(local_heads):
                moved, added = advance_state(handoffs_ref[j, h], state_ref[h], back)
                if back:
                    added = inputs_ref[j, h].astype(jnp.float32)
                state_ref[h] = moved + added
            return carry

        count = devices - 1 - index_ref[0] if back else index_ref[0]
        lax.fori_loop(0, count, advance, 0)

    vmem = pl.BlockSpec(memory_space=pltpu.VMEM)
    return pl.pallas_call(
        kernel,
        in_specs=[pl.BlockSpec(memory_space=pltpu.SMEM), vmem, vmem],
        out_specs=vmem,
        out_shape=jax.ShapeDtypeStruct((local_heads, DK, DV), jnp.float32),
        compiler_params=params(),
    )(my_index, handoffs, inputs)


def join_cores(local_heads, my_index, mine, theirs, inputs):
    half = local_heads // 2

    def kernel(index_ref, mine_ref, theirs_ref, *refs):
        out_ref = refs[-1]
        core = lax.rem(index_ref[0], 2)
        for i in range(half):
            h = core * half + i
            own, other = mine_ref[h], theirs_ref[h]
            first = jnp.where(core == 0, own, other)
            second = jnp.where(core == 0, other, own)
            if inputs:
                own, other = refs[0][h], refs[1][h]
                early = jnp.where(core == 0, own, other).astype(jnp.float32)
                late = jnp.where(core == 0, other, own).astype(jnp.float32)
                out_ref[i] = (advance_state(first, late, True)[0] + early).astype(jnp.bfloat16)
                continue
            moved, added = advance_state(second, first.astype(jnp.float32), False)
            out_ref[i, :, :DK] = moved[:, :DK].astype(jnp.bfloat16)
            out_ref[i, :, DK:] = (moved[:, DK:] + added).astype(jnp.bfloat16)

    vmem = pl.BlockSpec(memory_space=pltpu.VMEM)
    return pl.pallas_call(
        kernel,
        in_specs=[pl.BlockSpec(memory_space=pltpu.SMEM)] + [vmem] * (2 + len(inputs)),
        out_specs=vmem,
        out_shape=jax.ShapeDtypeStruct((half, DK, DV if inputs else DK + DV), jnp.bfloat16),
        compiler_params=params(),
    )(my_index, mine, theirs, *inputs)


def chain_chips(local_heads, my_index, theirs, chips, their_input, chip_inputs):
    half = local_heads // 2
    masks = len(chips) // 2
    back = their_input is not None
    flat = [theirs, *chips] + ([their_input, *chip_inputs] if back else [])

    def kernel(index_ref, *refs):
        state_ref = refs[-1]
        state_ref[...] = jnp.zeros_like(state_ref)
        core, chip = lax.rem(index_ref[0], 2), index_ref[0] // 2
        offset = 1 + len(chips)

        def update(h, block, extra):
            moved, added = advance_state(block, state_ref[h], back)
            state_ref[h] = moved + (extra.astype(jnp.float32) if back else added)

        order = range(masks, 0, -1) if back else range(masks)
        for other in order:
            for mask in range(1, masks + 1):
                here = (other ^ chip) == mask

                @pl.when(here & ((other > chip) if back else (other < chip)))
                def _():
                    for h in range(local_heads):
                        mine = core == h // half
                        pair = [refs[1 + 2 * (mask - 1) + i][h % half] for i in range(2)]
                        extra = None
                        if back:
                            extra = [
                                refs[offset + 1 + 2 * (mask - 1) + i][h % half] for i in range(2)
                            ]
                            extra = jnp.where(mine, *extra)
                        update(h, jnp.where(mine, *pair), extra)

        @pl.when(core == (0 if back else 1))
        def _():
            for h in range(local_heads):
                update(h, refs[0][h], refs[offset][h] if back else None)

    vmem = pl.BlockSpec(memory_space=pltpu.VMEM)
    return pl.pallas_call(
        kernel,
        in_specs=[pl.BlockSpec(memory_space=pltpu.SMEM)] + [vmem] * len(flat),
        out_specs=vmem,
        out_shape=jax.ShapeDtypeStruct((local_heads, DK, DV), jnp.float32),
        compiler_params=params(),
    )(my_index, *flat)


def moved_by(array, mask):
    return lax.ppermute(array, "seq", [(i, i ^ mask) for i in range(lax.axis_size("seq"))])


def pass_chips(block, beside):
    arrived = [moved_by(block, mask) for mask in (2, 4, 6)]
    arrived, beside = lax.optimization_barrier((arrived, beside))
    return [array for part in arrived for array in (part, moved_by(part, 1))], beside


def entering(local_heads, my_index, handoff, beside):
    if lax.axis_size("seq") != 8:
        handoffs = lax.all_gather(handoff, "seq", axis=0, tiled=False)
        return chain_all(local_heads, my_index, handoffs, handoffs, False), handoffs, beside
    theirs = moved_by(handoff, 1)
    chips, beside = pass_chips(join_cores(local_heads, my_index, handoff, theirs, []), beside)
    state = chain_chips(local_heads, my_index, theirs, chips, None, [])
    return state, (handoff, theirs, chips), beside


def leaving(local_heads, my_index, d_entering, kept, beside):
    if lax.axis_size("seq") != 8:
        inputs = lax.all_gather(d_entering, "seq", axis=0, tiled=False)
        return chain_all(local_heads, my_index, kept, inputs, True), beside
    handoff, theirs, chips = kept
    their_input = moved_by(d_entering, 1)
    joined = join_cores(local_heads, my_index, handoff, theirs, [d_entering, their_input])
    inputs, beside = pass_chips(joined, beside)
    return chain_chips(local_heads, my_index, theirs, chips, their_input, inputs), beside


def mixer_out(local_heads, entering_state, reach, zero_out, query_gate, norm_gain):
    row_count = query_gate.shape[0] - RIM
    gate_first = local_heads * DK

    def kernel(state_ref, reach_ref, zero_ref, gate_ref, norm_ref, out_ref, gated_ref):
        for h in range(local_heads):
            columns = slice(DV * h, DV * h + DV)
            out = zero_ref[h] + product(reach_ref[h], state_ref[h], 1, 0)
            normed = out * lax.rsqrt(jnp.mean(out * out, axis=-1, keepdims=True) + HEAD_EPSILON)
            out_ref[:, columns] = out
            gate = gate_ref[RIM:, gate_first + DV * h : gate_first + DV * h + DV]
            gated_ref[:, columns] = (normed * norm_ref[...] * jax.nn.silu(gate)).astype(
                jnp.bfloat16
            )

    vmem = pl.BlockSpec(memory_space=pltpu.VMEM)
    width = local_heads * DV
    return pl.pallas_call(
        kernel,
        in_specs=[vmem] * 5,
        out_specs=[vmem, vmem],
        out_shape=[
            jax.ShapeDtypeStruct((row_count, width), jnp.float32),
            jax.ShapeDtypeStruct((row_count, width), jnp.bfloat16),
        ],
        compiler_params=params(),
    )(entering_state, reach, zero_out, query_gate, norm_gain)


def mixer_gate_back(local_heads, d_gated, recurred, query_gate, norm_gain, reach):
    row_count = query_gate.shape[0] - RIM
    gate_first = local_heads * DK // DV

    def kernel(d_gated_ref, out_ref, gate_ref, norm_ref, reach_ref, d_out_ref, d_gate_ref, d_norm_ref, d_state_ref):
        out, gate, norm_row, d_gated_now = (
            out_ref[...], gate_ref[RIM:, :], norm_ref[...], d_gated_ref[...]
        )
        scale = lax.rsqrt(jnp.mean(out * out, axis=-1, keepdims=True) + HEAD_EPSILON)
        normed = out * scale
        logistic = jax.nn.sigmoid(gate)
        silu = gate * logistic
        d_norm = jnp.sum(d_gated_now * normed * silu, axis=0, keepdims=True)

        @pl.when(pl.program_id(0) == 0)
        def _():
            d_norm_ref[...] = jnp.zeros_like(d_norm_ref)

        d_norm_ref[0:1, :] = d_norm_ref[0:1, :] + d_norm
        d_gate_ref[...] = (
            d_gated_now * normed * norm_row * logistic * (1.0 + gate * (1.0 - logistic))
        ).astype(jnp.bfloat16)
        d_normed = d_gated_now * norm_row * silu
        d_out = scale * d_normed - (scale * scale * scale) * out * jnp.mean(
            d_normed * out, axis=-1, keepdims=True
        )
        d_out_ref[...] = d_out
        d_state_ref[0] = product(reach_ref[0], d_out, 0, 0).astype(jnp.bfloat16)

    width = local_heads * DV
    block = pl.BlockSpec((row_count, DV), lambda h: (0, h))
    return pl.pallas_call(
        kernel,
        grid=(local_heads,),
        in_specs=[
            block,
            block,
            pl.BlockSpec((RIM + row_count, DV), lambda h: (0, gate_first + h)),
            pl.BlockSpec((1, DV), lambda h: (0, 0)),
            pl.BlockSpec((1, row_count, DK), lambda h: (h, 0, 0)),
        ],
        out_specs=[
            block,
            block,
            pl.BlockSpec((8, DV), lambda h: (0, 0)),
            pl.BlockSpec((1, DK, DV), lambda h: (h, 0, 0)),
        ],
        out_shape=[
            jax.ShapeDtypeStruct((row_count, width), jnp.float32),
            jax.ShapeDtypeStruct((row_count, width), jnp.bfloat16),
            jax.ShapeDtypeStruct((8, DV), jnp.float32),
            jax.ShapeDtypeStruct((local_heads, DK, DV), jnp.bfloat16),
        ],
        compiler_params=params(),
    )(d_gated, recurred, query_gate, norm_gain, reach)


def conv_back(
    d_pre, extended, taps_ref, padded, d_block_ref, d_tail_ref, d_rim_ref, d_taps_ref, columns
):
    row_count = d_pre.shape[0]
    first = RIM - (KCONV - 1)
    padded[0:8, :] = jnp.zeros((8, d_pre.shape[1]), jnp.float32)
    padded[8 : 8 + row_count, :] = d_pre
    padded[8 + row_count : 16 + row_count, :] = jnp.zeros((8, d_pre.shape[1]), jnp.float32)
    total = None
    d_taps_ref[:, columns] = jnp.zeros((8, d_pre.shape[1]), jnp.float32)
    for tap in range(KCONV):
        start = KCONV - 1 - tap
        term = taps_ref[tap : tap + 1, columns] * padded[start : start + row_count + 8, :]
        total = term if total is None else total + term
        d_taps_ref[tap : tap + 1, columns] = jnp.sum(
            d_pre * extended[first + tap : first + tap + row_count, columns], axis=0, keepdims=True
        )
    d_rim_ref[:, columns] = total[0:8, :]
    d_block_ref[:, columns] = total[8:, :].astype(jnp.bfloat16)
    d_tail_ref[:, columns] = total[row_count:, :]


def mixer_back(
    local_heads, query_gate, value_key, query_taps, taps, decay_proj, scalars,
    solve, fresh, wy_keys, entering_state, d_recurred, d_leaving,
):
    row_count = value_key.shape[0] - RIM
    query, key, value, whole, scalar_spec = mixer_specs(local_heads, row_count)

    def kernel(
        pq, pk, pv, tq, tk, tv, decay_ref, scalars_ref,
        solve_ref, fresh_ref, wy_ref, enter_ref, d_out_ref, d_leave_ref,
        dq_ref, dk_ref, dv_ref, tail_q, tail_k, tail_v, rim_q, rim_k, rim_v,
        taps_q, taps_k, taps_v, d_decay_ref, d_scalars_ref,
        pad_q, pad_k, pad_v,
    ):
        @pl.when(pl.program_id(0) == 0)
        def _():
            d_decay_ref[...] = jnp.zeros_like(d_decay_ref)
            d_scalars_ref[...] = jnp.zeros_like(d_scalars_ref)

        for sub in range(HEADS_A_STEP):
            head = pl.program_id(0) * HEADS_A_STEP + sub
            narrow, wide = head_columns(sub)
            pre_q = convolved(pq, tq, narrow)
            pre_k = convolved(pk, tk, narrow)
            pre_v = convolved(pv, tv, wide)
            conv_q, conv_k = jax.nn.silu(pre_q), jax.nn.silu(pre_k)
            unit_q, scale_q = unit_rows(conv_q)
            queries = unit_q * DK ** (-0.5)
            key_rows, scale_k = unit_rows(conv_k)
            values = jax.nn.silu(pre_v)
            decay_in, rate, logs, beta, sums, within, row_ids, column_ids = decay_terms(
                head, local_heads, decay_ref, scalars_ref
            )
            strict = row_ids > column_ids
            grown = jnp.exp(sums)
            last = sums[row_count - 1 : row_count, :]
            tail = jnp.exp(last - sums)
            tail_keys = tail * key_rows
            gram = product(key_rows, key_rows, 1, 1, True)
            scores = jnp.where(strict, gram * within, 0.0)
            attention = product(queries, key_rows, 1, 1) * within
            enter, d_out, d_leave = enter_ref[sub], d_out_ref[:, wide], d_leave_ref[sub]
            update = fresh_ref[sub] - product(wy_ref[sub], enter, 1, 0)
            d_update = product(attention, d_out, 0, 0) + product(tail_keys, d_leave, 1, 0)
            d_right = product(solve_ref[sub], d_update, 0, 0, True)
            d_attention = product(d_out, update, 1, 1) * within
            d_system = -product(d_right, update, 1, 1)
            out_state = product(d_out, enter, 1, 1)
            right_state = product(d_right, enter, 1, 1)
            leave_update = product(update, d_leave, 1, 1)
            remainder = values - grown * product(key_rows, enter, 1, 0)
            d_values = beta * d_right
            d_beta = jnp.sum(d_right * remainder, axis=1, keepdims=True) + jnp.sum(
                d_system * scores, axis=1, keepdims=True
            )
            pair = beta * (d_system * scores)
            d_gram = jnp.where(strict, beta * d_system * within, 0.0)
            d_queries = grown * out_state + product(d_attention, key_rows, 1, 0)
            d_keys = (
                product(d_attention, queries, 0, 0)
                + product(d_gram, key_rows, 1, 0)
                + product(d_gram, key_rows, 0, 0)
                + tail * leave_update
                - (beta * grown) * right_state
            )
            both = pair + d_attention * product(queries, key_rows, 1, 1)
            tail_rows = jnp.sum(tail_keys * leave_update, axis=1, keepdims=True)
            diagonal = row_ids == column_ids
            columns = jnp.sum(both, axis=0, keepdims=True)
            d_sums = (
                jnp.sum(both, axis=1, keepdims=True)
                - jnp.sum(jnp.where(diagonal, columns, 0.0), axis=1, keepdims=True)
                + jnp.sum(out_state * (grown * queries), axis=1, keepdims=True)
                - jnp.sum(right_state * ((beta * grown) * key_rows), axis=1, keepdims=True)
                - tail_rows
            )
            d_last = jnp.exp(last) * jnp.sum(
                jnp.sum(d_leave * enter, axis=1, keepdims=True), axis=0, keepdims=True
            ) + jnp.sum(tail_rows, axis=0, keepdims=True)
            d_logs = d_last + jnp.sum(
                jnp.where(row_ids <= column_ids, to_row(d_sums, diagonal), 0.0), axis=1, keepdims=True
            )
            d_decay_in = d_logs * rate * jax.nn.sigmoid(decay_in)
            d_beta_in = d_beta * beta * (1.0 - beta)
            d_decay_ref[...] = (
                d_decay_ref[...]
                + put_lane(d_decay_in, head)
                + put_lane(d_beta_in, head + local_heads)
            )
            d_rate = jnp.sum(d_logs * logs, axis=0, keepdims=True)
            d_bias = jnp.sum(d_decay_in, axis=0, keepdims=True)
            d_scalars_ref[0:1, :] = d_scalars_ref[0:1, :] + put_lane(d_rate, head)
            d_scalars_ref[1:2, :] = d_scalars_ref[1:2, :] + put_lane(d_bias, head)

            def unit_back(d_unit, unit, scale):
                return scale * (d_unit - unit * jnp.sum(unit * d_unit, axis=1, keepdims=True))

            def silu_back(d_act, pre):
                logistic = jax.nn.sigmoid(pre)
                return d_act * logistic * (1.0 + pre * (1.0 - logistic))

            d_pre_q = silu_back(unit_back(d_queries * DK ** (-0.5), unit_q, scale_q), pre_q)
            conv_back(d_pre_q, pq, tq, pad_q.at[sub], dq_ref, tail_q, rim_q, taps_q, narrow)
            d_pre_k = silu_back(unit_back(d_keys, key_rows, scale_k), pre_k)
            conv_back(d_pre_k, pk, tk, pad_k.at[sub], dk_ref, tail_k, rim_k, taps_k, narrow)
            conv_back(
                silu_back(d_values, pre_v), pv, tv, pad_v.at[sub],
                dv_ref, tail_v, rim_v, taps_v, wide,
            )

    def blocks(rows):
        return [
            pl.BlockSpec((rows, HEADS_A_STEP * width), lambda h: (0, h)) for width in (DK, DK, DV)
        ]

    def shapes(rows, kind):
        return [
            jax.ShapeDtypeStruct((rows, local_heads * width), kind) for width in (DK, DK, DV)
        ]

    outs = pl.pallas_call(
        kernel,
        grid=(local_heads // HEADS_A_STEP,),
        in_specs=[each(RIM + row_count) for each in (query, key, value)]
        + [each(8) for each in (query, key, value)]
        + [
            whole,
            scalar_spec,
            per_head(row_count, row_count),
            per_head(row_count, DV),
            per_head(row_count, DK),
            per_head(DK, DV),
            pl.BlockSpec((row_count, HEADS_A_STEP * DV), lambda h: (0, h)),
            per_head(DK, DV),
        ],
        out_specs=blocks(row_count) + blocks(8) * 3 + [whole, scalar_spec],
        out_shape=shapes(row_count, jnp.bfloat16)
        + shapes(8, jnp.float32) * 3
        + [
            jax.ShapeDtypeStruct((row_count, 128), jnp.float32),
            jax.ShapeDtypeStruct((8, 128), jnp.float32),
        ],
        scratch_shapes=[
            pltpu.VMEM((HEADS_A_STEP, row_count + 16, DK), jnp.float32),
            pltpu.VMEM((HEADS_A_STEP, row_count + 16, DK), jnp.float32),
            pltpu.VMEM((HEADS_A_STEP, row_count + 16, DV), jnp.float32),
        ],
        compiler_params=params(),
    )(
        query_gate, value_key, value_key, query_taps, taps, taps, decay_proj, scalars,
        solve, fresh, wy_keys, entering_state, d_recurred, d_leaving,
    )
    joined = [
        (outs[3 * i], jnp.concatenate([outs[3 * i + 2], outs[3 * i + 1]], axis=1))
        for i in range(4)
    ]
    return (*joined, outs[12], outs[13])


LANES = 128
CHUNK = 32768
TILE = 16
CAPACITY_UNIT = 44
FIRST_GATHER = 24
FIRST_REDUCE = 16
SECOND_REDUCE = 20
SECOND_GATHER = 16
RIM = 16
TABLE = 1 << 16
VMEM_LIMIT = 48 * 1024 * 1024


def params(**kwargs):
    return pltpu.CompilerParams(vmem_limit_bytes=VMEM_LIMIT, **kwargs)


def piece_kinds(segments_list, piece_count, piece_size):
    kinds = np.ones(piece_count, np.int32)
    offset_now = 0
    for seg_name, row_count, col_count, seg_rate in segments_list:
        if offset_now >= (piece_count - 1) * piece_size:
            break
        tiles = col_count // LANES
        if tiles in (2, 4, 8, 16):
            first = offset_now // piece_size
            kinds[first : first + row_count * col_count // piece_size] = tiles
        offset_now += row_count * col_count
    return kinds


def pack_blocks(master, slot_kinds, kinds_used, first_slot, slot_count):
    piece_size = master.shape[1]
    chunks = piece_size // CHUNK
    rows = CHUNK // LANES
    first_block = first_slot // 8
    slot_blocks = pl.cdiv(slot_count, 8)

    def kernel(kinds_ref, master_ref, out_ref, scratch):
        first = (first_block + pl.program_id(0)) * 8
        for j in range(rows):
            scratch[8 * j : 8 * j + 8, :] = master_ref[:, LANES * j : LANES * j + LANES]
        for s in range(8):
            kind_now = kinds_ref[first + s]
            for kind in kinds_used:

                @pl.when(kind_now == kind)
                def _():
                    for tile in range(rows // TILE):
                        row_tile, column = divmod(tile, kind)
                        start = (row_tile * TILE * kind + column) * 8 + s
                        out_ref[s, TILE * tile : TILE * tile + TILE, :] = scratch[
                            pl.ds(start, TILE, stride=8 * kind), :
                        ].astype(jnp.bfloat16)

    return pl.pallas_call(
        kernel,
        grid_spec=pltpu.PrefetchScalarGridSpec(
            num_scalar_prefetch=1,
            grid=(slot_blocks, chunks),
            in_specs=[pl.BlockSpec((8, CHUNK), lambda i, j, kinds: (first_block + i, j))],
            out_specs=pl.BlockSpec((8, rows, LANES), lambda i, j, kinds: (i, j, 0)),
            scratch_shapes=[pltpu.VMEM((8 * rows, LANES), jnp.float32)],
        ),
        out_shape=jax.ShapeDtypeStruct((slot_count, piece_size // LANES, LANES), jnp.bfloat16),
        compiler_params=params(),
    )(slot_kinds, master)


def reserve(shape, kind):
    def kernel(out_ref):
        pass

    return pl.pallas_call(
        kernel,
        out_specs=pl.BlockSpec(memory_space=pl.ANY),
        out_shape=jax.ShapeDtypeStruct(shape, kind),
        compiler_params=params(),
    )()


def assemble(tables, matrices, step_rows, rows_in=None):
    piece_rows = tables[0].shape[1]
    plans = []
    first_block, first_column = 0, 0
    for positions, col_count in matrices:
        tiles = col_count // LANES
        blocks = step_rows * tiles // piece_rows
        plans.append((first_block, first_column, tiles, blocks))
        first_block += blocks
        first_column += col_count
    blocks_a_step, width = first_block, first_column
    steps = matrices[0][0].shape[0] // plans[0][3]
    order = jnp.concatenate(
        [
            positions.reshape(steps, plan[3])
            for (positions, col_count), plan in zip(matrices, plans)
        ],
        axis=1,
    ).reshape(-1)
    uneven = [plan for plan in plans if piece_rows * plan[3] != step_rows * plan[2] or plan[2] not in (2, 4, 8, 16)]
    multiply = rows_in is not None

    def kernel(order_ref, *refs):
        if multiply:
            rows_ref, refs = refs[0], refs[1:]
        table_refs, refs = refs[: len(tables)], refs[len(tables) :]
        out_ref, refs = refs[0], refs[1:]
        if multiply:
            product_ref, refs = refs[0], refs[1:]
        buffer, sem, scratch = refs
        g = pl.program_id(0)
        slot = lax.rem(g, 2)

        def start(step, which):
            def one(j, carry):
                position = order_ref[step * blocks_a_step + j]
                for number, table_ref in enumerate(table_refs):

                    @pl.when(position // TABLE == number)
                    def _():
                        pltpu.make_async_copy(
                            table_ref.at[lax.rem(position, TABLE)],
                            buffer.at[which, j],
                            sem.at[which],
                        ).start()

                return carry

            lax.fori_loop(0, blocks_a_step, one, 0)

        @pl.when(g == 0)
        def _():
            start(0, 0)

        @pl.when(g + 1 < steps)
        def _():
            start(g + 1, 1 - slot)

        pltpu.make_async_copy(buffer.at[slot], buffer.at[slot], sem.at[slot]).wait()
        for plan in plans:
            first, left, tiles, blocks = plan
            if plan in uneven:
                for j in range(blocks):
                    scratch[piece_rows * j : piece_rows * j + piece_rows, :] = buffer[
                        slot, first + j
                    ].astype(jnp.float32)
                for c in range(tiles):
                    out_ref[:, left + LANES * c : left + LANES * c + LANES] = scratch[
                        pl.ds(c, step_rows, stride=tiles), :
                    ].astype(jnp.bfloat16)
                continue
            for j in range(blocks):
                for tile in range(piece_rows // TILE):
                    row_tile, column = divmod(tile, tiles)
                    row = piece_rows // tiles * j + TILE * row_tile
                    column = left + LANES * column
                    out_ref[row : row + TILE, column : column + LANES] = buffer[
                        slot, first + j, TILE * tile : TILE * tile + TILE, :
                    ]
        if multiply:
            part = jnp.dot(rows_ref[...], out_ref[...], preferred_element_type=jnp.float32)

            @pl.when(g == 0)
            def _():
                product_ref[...] = part

            @pl.when(g > 0)
            def _():
                product_ref[...] = product_ref[...] + part

    anywhere = pl.BlockSpec(memory_space=pl.ANY)
    in_specs = [anywhere for table in tables]
    operands = list(tables)
    out_specs = [pl.BlockSpec((step_rows, width), lambda g, order: (g, 0))]
    out_shape = [jax.ShapeDtypeStruct((steps * step_rows, width), jnp.bfloat16)]
    if multiply:
        row_count = rows_in.shape[0]
        in_specs.insert(0, pl.BlockSpec((row_count, step_rows), lambda g, order: (0, g)))
        operands.insert(0, rows_in)
        out_specs.append(pl.BlockSpec((row_count, width), lambda g, order: (0, 0)))
        out_shape.append(jax.ShapeDtypeStruct((row_count, width), jnp.float32))
    scratch_rows = max([plan[3] * piece_rows for plan in uneven], default=8)
    return pl.pallas_call(
        kernel,
        grid_spec=pltpu.PrefetchScalarGridSpec(
            num_scalar_prefetch=1,
            grid=(steps,),
            in_specs=in_specs,
            out_specs=out_specs,
            scratch_shapes=[
                pltpu.VMEM((2, blocks_a_step, piece_rows, LANES), jnp.bfloat16),
                pltpu.SemaphoreType.DMA((2,)),
                pltpu.VMEM((scratch_rows, LANES), jnp.float32),
            ],
        ),
        out_shape=out_shape,
        cost_estimate=pl.CostEstimate(
            flops=2 * steps * step_rows * width * (rows_in.shape[0] if multiply else 0),
            bytes_accessed=4 * steps * step_rows * width,
            transcendentals=0,
        ),
        compiler_params=params(),
    )(order, *operands)


def spread_products(my_part, parts, pairs):
    row_count = pairs[0][0][0].shape[0]
    total = pairs[0][1].shape[0 if pairs[0][2] else 1]
    width = total // parts

    def kernel(part_ref, *refs):
        ins, outs = list(refs[:-parts]), refs[-parts:]
        for m in range(parts):
            first = pl.multiple_of((part_ref[0] ^ m) * width, width)
            result, place = None, 0
            for lefts, right, transposed in pairs:
                left_refs, right_ref = ins[place : place + len(lefts)], ins[place + len(lefts)]
                place += len(lefts) + 1
                depth = 0
                for left_ref in left_refs:
                    inner = slice(depth, depth + left_ref.shape[1])
                    depth += left_ref.shape[1]
                    if transposed:
                        block, axis = right_ref[pl.ds(first, width), inner], 1
                    else:
                        block, axis = right_ref[inner, pl.ds(first, width)], 0
                    part = lax.dot_general(
                        left_ref[...],
                        block,
                        (((1,), (axis,)), ((), ())),
                        preferred_element_type=jnp.float32,
                    )
                    result = part if result is None else result + part
            outs[m][...] = result.astype(jnp.bfloat16)

    vmem = pl.BlockSpec(memory_space=pltpu.VMEM)
    flat = [array for lefts, right, transposed in pairs for array in (*lefts, right)]
    return pl.pallas_call(
        kernel,
        in_specs=[pl.BlockSpec(memory_space=pltpu.SMEM)] + [vmem] * len(flat),
        out_specs=[vmem] * parts,
        out_shape=[jax.ShapeDtypeStruct((row_count, width), jnp.bfloat16)] * parts,
        cost_estimate=pl.CostEstimate(
            flops=2 * row_count * sum(pair[1].size for pair in pairs),
            bytes_accessed=2 * sum(pair[1].size for pair in pairs),
            transcendentals=0,
        ),
        compiler_params=params(),
    )(my_part, *flat)


def stored(array):
    def kernel(in_ref, out_ref):
        out_ref[...] = in_ref[...]

    return pl.pallas_call(
        kernel,
        out_shape=jax.ShapeDtypeStruct(array.shape, array.dtype),
        compiler_params=params(),
    )(array)


def exchange(blocks, axis):
    devices = lax.axis_size(axis)
    return [blocks[0]] + [
        lax.ppermute(blocks[m], axis, [(i, i ^ m) for i in range(devices)])
        for m in range(1, devices)
    ]


def total_of(blocks):
    total = blocks[0].astype(jnp.float32)
    for block in blocks[1:]:
        total = total + block.astype(jnp.float32)
    return total


def sum_over(block, axis):
    return total_of(exchange([block] * lax.axis_size(axis), axis))


def in_order(blocks, my_part, axis):
    stacked = jnp.stack(blocks)
    return jnp.concatenate(
        [
            lax.dynamic_index_in_dim(stacked, my_part ^ j, 0, keepdims=False)
            for j in range(len(blocks))
        ],
        axis=axis,
    )


def gather_states(block):
    devices = lax.axis_size("seq")
    if devices != 8:
        return lax.all_gather(block, "seq", axis=0, tiled=False), jnp.zeros((1,), jnp.int32)

    def moved(array, mask):
        return lax.ppermute(array, "seq", [(i, i ^ mask) for i in range(devices)])

    chips = [block] + [moved(block, mask) for mask in (2, 4, 6)]
    pairs = [(chip, moved(chip, 1)) for chip in chips]
    rows = jnp.stack([array for pair in pairs for array in pair])
    return rows, lax.axis_index("seq").astype(jnp.int32).reshape(1)


def weight_grad_blocks(left_t, right, right_block, col_count, positions, tables, blocks_a_step):
    row_total, depth = left_t.shape
    tiles = col_count // LANES
    piece_rows = 512
    even = tiles in (2, 4, 8, 16)
    step_rows = blocks_a_step * piece_rows // tiles
    steps = row_total // step_rows

    def kernel(positions_ref, left_ref, right_ref, *refs):
        table_refs = refs[len(tables) : 2 * len(tables)]
        product, staged, sem = refs[2 * len(tables) :]
        g = pl.program_id(0)
        slot = lax.rem(g, 2)

        def settle(which):
            pltpu.make_async_copy(staged.at[which], staged.at[which], sem.at[which]).wait()

        @pl.when(g >= 2)
        def _():
            settle(slot)

        left = left_ref[...]
        if even:
            product[...] = jnp.dot(left, right_ref[...], preferred_element_type=jnp.float32)
            for tile in range(step_rows // TILE * tiles):
                row_tile, column = divmod(tile, tiles)
                block, row = divmod(TILE * tile, piece_rows)
                staged[slot, block, row : row + TILE, :] = product[
                    TILE * row_tile : TILE * row_tile + TILE, LANES * column : LANES * column + LANES
                ].astype(jnp.bfloat16)
        else:
            for c in range(0, tiles, 2):
                width = min(2, tiles - c)
                part = jnp.dot(
                    left,
                    right_ref[:, LANES * c : LANES * (c + width)],
                    preferred_element_type=jnp.float32,
                )
                for w in range(width):
                    product[pl.ds(c + w, step_rows, stride=tiles), :] = part[
                        :, LANES * w : LANES * w + LANES
                    ]
            for block in range(blocks_a_step):
                staged[slot, block] = product[
                    piece_rows * block : piece_rows * block + piece_rows, :
                ].astype(jnp.bfloat16)
        for block in range(blocks_a_step):
            position = positions_ref[g * blocks_a_step + block]

            for number, table_ref in enumerate(table_refs):

                @pl.when(position // TABLE == number)
                def _():
                    pltpu.make_async_copy(
                        staged.at[slot, block],
                        table_ref.at[lax.rem(position, TABLE)],
                        sem.at[slot],
                    ).start()

        @pl.when(g == steps - 1)
        def _():
            settle(slot)
            if steps > 1:
                settle(1 - slot)

    anywhere = pl.BlockSpec(memory_space=pl.ANY)
    in_specs = [
        pl.BlockSpec((step_rows, depth), lambda g, positions: (g, 0)),
        pl.BlockSpec((depth, col_count), lambda g, positions: (0, right_block)),
    ] + [anywhere for table in tables]
    product_shape = (step_rows, col_count) if even else (step_rows * tiles, LANES)
    return pl.pallas_call(
        kernel,
        grid_spec=pltpu.PrefetchScalarGridSpec(
            num_scalar_prefetch=1,
            grid=(steps,),
            in_specs=in_specs,
            out_specs=[anywhere for table in tables],
            scratch_shapes=[
                pltpu.VMEM(product_shape, jnp.float32),
                pltpu.VMEM((2, blocks_a_step, piece_rows, LANES), jnp.bfloat16),
                pltpu.SemaphoreType.DMA((2,)),
            ],
        ),
        out_shape=[jax.ShapeDtypeStruct(table.shape, table.dtype) for table in tables],
        input_output_aliases={3 + i: i for i in range(len(tables))},
        cost_estimate=pl.CostEstimate(
            flops=2 * row_total * depth * col_count,
            bytes_accessed=2 * row_total * col_count,
            transcendentals=0,
        ),
        compiler_params=params(),
    )(positions, left_t, right, *tables)


def optimizer_update(
    sources, slot_sources, slot_rows, slot_kinds, kinds_used, slot_masks, small_rates,
    master, moment_one, moment_two, capacity, block_range, most_blocks, earlier,
):
    piece_size = master.shape[1]
    chunks = piece_size // CHUNK
    rows = CHUNK // LANES
    last_block = pl.cdiv(capacity, 8) - 1
    steps = most_blocks * chunks

    def place(step, first, end):
        now = jnp.minimum(step, jnp.maximum((end - first) * chunks - 1, 0))
        return jnp.minimum(first + now // chunks, last_block), lax.rem(now, chunks)

    def kernel(range_ref, kinds_ref, sources_ref, rows_ref, *refs):
        source_refs, refs = refs[: len(sources)], refs[len(sources) :]
        masks_ref, small_ref, master_ref, one_ref, two_ref = refs[:5]
        refs = refs[5 + len(earlier) :]
        grad_out, master_out, one_out, two_out, low_out, scratch, buffer, sem = refs
        step = pl.program_id(0)
        count = jnp.maximum((range_ref[1] - range_ref[0]) * chunks, 1)
        first = place(step, range_ref[0], range_ref[1])[0] * 8
        slot = lax.rem(step, 2)

        def start(step, which):
            block, chunk = place(step, range_ref[0], range_ref[1])
            for s in range(8):
                for i, source_ref in enumerate(source_refs):

                    @pl.when(sources_ref[block * 8 + s] == i)
                    def _():
                        pltpu.make_async_copy(
                            source_ref.at[
                                rows_ref[block * 8 + s],
                                pl.ds(pl.multiple_of(chunk * rows, rows), rows),
                            ],
                            buffer.at[which, s],
                            sem.at[which],
                        ).start()

                @pl.when(sources_ref[block * 8 + s] >= len(sources))
                def _():
                    pltpu.make_async_copy(
                        source_refs[0].at[0, pl.ds(0, rows)], buffer.at[which, s], sem.at[which]
                    ).start()

        @pl.when(step == 0)
        def _():
            start(0, 0)

        @pl.when(step + 1 < count)
        def _():
            start(step + 1, 1 - slot)

        @pl.when(step < count)
        def _():
            pltpu.make_async_copy(buffer.at[slot], buffer.at[slot], sem.at[slot]).wait()
            for s in range(8):
                kind_now = kinds_ref[first + s]
                for kind in kinds_used:

                    @pl.when(kind_now == kind)
                    def _():
                        for tile in range(rows // TILE):
                            row_tile, column = divmod(tile, kind)
                            start_row = (row_tile * TILE * kind + column) * 8 + s
                            scratch[pl.ds(start_row, TILE, stride=8 * kind), :] = buffer[
                                slot, s, TILE * tile : TILE * tile + TILE, :
                            ].astype(jnp.float32)

            present = masks_ref[0] > 0.5
            is_small = masks_ref[1] > 0.5
            rate_rows = masks_ref[2]
            for j in range(rows):
                lanes = slice(LANES * j, LANES * j + LANES)
                grad = jnp.where(present, scratch[8 * j : 8 * j + 8, :], 0.0)
                rate = jnp.where(is_small, small_ref[:, lanes], rate_rows)
                master_now = master_ref[:, lanes]
                one_new = BETA_ONE * one_ref[:, lanes] + (1.0 - BETA_ONE) * grad
                two_new = BETA_TWO * two_ref[:, lanes] + (1.0 - BETA_TWO) * grad * grad
                first_hat = one_new / (1.0 - BETA_ONE**STEP)
                second_hat = two_new / (1.0 - BETA_TWO**STEP)
                master_new = master_now - rate * (
                    first_hat / (jnp.sqrt(second_hat) + ADAM_EPSILON) + WEIGHT_DECAY * master_now
                )
                grad_out[:, lanes] = grad
                master_out[:, lanes] = master_new
                one_out[:, lanes] = one_new
                two_out[:, lanes] = two_new
                low_out[:, lanes] = master_new.astype(jnp.bfloat16)

    state_spec = pl.BlockSpec((8, CHUNK), lambda t, ends, *tables: place(t, ends[0], ends[1]))
    anywhere = pl.BlockSpec(memory_space=pl.ANY)
    wide = jax.ShapeDtypeStruct((capacity, piece_size), jnp.float32)
    operands = [*sources, slot_masks, small_rates, master, moment_one, moment_two, *earlier]
    return pl.pallas_call(
        kernel,
        grid_spec=pltpu.PrefetchScalarGridSpec(
            num_scalar_prefetch=4,
            grid=(steps,),
            in_specs=[pl.BlockSpec(memory_space=pltpu.HBM) for source in sources]
            + [
                pl.BlockSpec((3, 8, LANES), lambda t, ends, *tables: (0, place(t, ends[0], ends[1])[0], 0)),
                pl.BlockSpec((1, CHUNK), lambda t, ends, *tables: (0, place(t, ends[0], ends[1])[1])),
                state_spec,
                state_spec,
                state_spec,
            ]
            + [anywhere for array in earlier],
            out_specs=[state_spec] * 5,
            scratch_shapes=[
                pltpu.VMEM((8 * rows, LANES), jnp.float32),
                pltpu.VMEM((2, 8, rows, LANES), jnp.bfloat16),
                pltpu.SemaphoreType.DMA((2,)),
            ],
        ),
        out_shape=[wide] * 4 + [jax.ShapeDtypeStruct((capacity, piece_size), jnp.bfloat16)],
        input_output_aliases={
            4 + len(operands) - len(earlier) + i: i for i in range(len(earlier))
        },
        cost_estimate=pl.CostEstimate(
            flops=20 * most_blocks * 8 * piece_size,
            bytes_accessed=16 * most_blocks * 8 * piece_size,
            transcendentals=2 * most_blocks * 8 * piece_size,
        ),
        compiler_params=params(),
    )(block_range, slot_kinds, slot_sources, slot_rows, *operands)


def weight_grad(left, right):
    return jnp.einsum("td,tc->dc", left, right, preferred_element_type=jnp.float32)


def back_product(grad_rows, weight):
    return jnp.dot(grad_rows, weight.T, preferred_element_type=jnp.float32)


def gather_rest(packed, first, trips, most, extra_step):
    devices = lax.axis_size("seq")
    rows = devices * extra_step
    room = reserve((most * rows,) + packed.shape[1:], packed.dtype)

    def more(trip, table):
        part = lax.dynamic_slice_in_dim(packed, first + trip * extra_step, extra_step)
        if devices != 8:
            part = lax.all_gather(part, "seq", axis=0, tiled=True)
            return lax.dynamic_update_slice_in_dim(table, part, trip * rows, axis=0)
        me = lax.axis_index("seq").astype(jnp.int32)
        chips = [part] + [moved_by(part, mask) for mask in (2, 4, 6)]
        for mask, chip in zip((0, 2, 4, 6), chips):
            for core, block in ((0, chip), (1, moved_by(chip, 1))):
                place = trip * rows + (me ^ (mask + core)) * extra_step
                table = lax.dynamic_update_slice_in_dim(table, block, place, axis=0)
        return table

    return lax.fori_loop(0, trips, more, room)


def reduce_rest(rest, trips, most, extra_step):
    devices = lax.axis_size("seq")
    rows = devices * extra_step
    room = reserve((most * extra_step,) + rest.shape[1:], rest.dtype)

    def more(trip, table):
        part = lax.dynamic_slice_in_dim(rest, trip * rows, rows)
        part = lax.psum_scatter(part, "seq", scatter_dimension=0, tiled=True)
        return lax.dynamic_update_slice_in_dim(table, part, trip * extra_step, axis=0)

    return lax.fori_loop(0, trips, more, room)


def on_device(inputs, cotangent, owners, master, moment_one, moment_two):
    head_parts = lax.axis_size("head")
    seq_parts = lax.axis_size("seq")
    local_heads = HEADS // head_parts
    capacity, piece_size = master.shape
    piece_count = owners.shape[0]
    row_count = inputs.shape[0]
    rim_width = KCONV - 1
    segments_list = shard_layout(local_heads, head_parts)
    columns = {name: c for name, r, c, rate in segments_list}
    counts = {name: r * c // piece_size for name, r, c, rate in segments_list[:8]}
    firsts = dict(zip(counts, np.cumsum([0] + list(counts.values())).tolist()))
    mixer_count = firsts["wgate"]
    big_count = piece_count - 1
    my_head = lax.axis_index("head").astype(jnp.int32)
    my_index = lax.axis_index("seq").astype(jnp.int32)
    my_head_row, my_index_row = my_head.reshape(1), my_index.reshape(1)

    onehot = (owners[:, None] == jnp.arange(seq_parts, dtype=jnp.int32)[None, :]).astype(jnp.int32)
    ranks = jnp.sum((jnp.cumsum(onehot, axis=0) - onehot) * onehot, axis=1)
    mixer_held = jnp.sum(onehot[:mixer_count], axis=0)
    mlp_held = jnp.sum(onehot[mixer_count:big_count], axis=0)
    padded = capacity + -capacity % 8
    small_rank = ranks[big_count]
    big_owners, big_ranks = owners[:big_count], ranks[:big_count]

    def rest_row(over, owner):
        return over // extra_step * (seq_parts * extra_step) + owner * extra_step + over % extra_step

    early = -(-capacity * FIRST_GATHER // (8 * CAPACITY_UNIT)) * 8
    late = capacity - early
    late_room = min(late, -(-capacity * SECOND_GATHER // CAPACITY_UNIT))
    extra_step = 2 if late % 2 == 0 else 1
    most_gather = -(-late // extra_step)
    trips_gather = jnp.maximum(-(-(jnp.max(mixer_held) - early) // extra_step), 0)
    early_row = big_owners * early + big_ranks
    mixer_fetch = jnp.where(
        big_ranks < early, early_row, TABLE + rest_row(big_ranks - early, big_owners)
    )
    neighbours = np.arange(seq_parts) ^ 1
    late_held = jnp.maximum(mixer_held + mlp_held - early, 0)
    late_spare = jnp.maximum(late_room - late_held[neighbours], 0)
    late_over = jnp.maximum(late_held - late_room, 0)
    trips_late = -(-jnp.max(jnp.maximum(late_over - late_spare, 0)) // extra_step)
    spare_there = jnp.sum(onehot[:big_count] * late_spare[None, :], axis=1)
    past = big_ranks - early - late_room
    rest_trip = (past - spare_there) // extra_step
    rest_start = late_room + spare_there + rest_trip * extra_step
    rest_start = jnp.minimum(rest_start, late - extra_step)
    mlp_fetch = jnp.where(
        big_ranks < early,
        TABLE + early_row,
        jnp.where(
            past < 0,
            big_owners * late_room + big_ranks - early,
            jnp.where(
                past < spare_there,
                (big_owners ^ 1) * late_room + late_room - spare_there + past,
                2 * TABLE
                + rest_trip * (seq_parts * extra_step)
                + big_owners * extra_step
                + big_ranks - early - rest_start,
            ),
        ),
    )
    first_room = -(-capacity * FIRST_REDUCE // CAPACITY_UNIT)
    second_room = -(-capacity * SECOND_REDUCE // CAPACITY_UNIT)
    most_reduce = -(-(capacity - second_room) // extra_step)
    second_held = mixer_held + jnp.maximum(mlp_held - first_room, 0)
    second_there = jnp.sum(onehot[:big_count] * second_held[None, :], axis=1)
    spill_plan, spill_taken = [], jnp.zeros_like(second_held)
    hosted = jnp.zeros_like(second_held)
    over_held = jnp.maximum(second_held - second_room, 0)
    for mask, most in (((1, 6), (2, 4), (4, 4), (6, 4)) if seq_parts == 8 else ((1, 4),)):
        most = min(most, second_room)
        partner = np.arange(seq_parts) ^ mask
        free = jnp.maximum(second_room - second_held - hosted, 0)[partner]
        take = jnp.minimum(jnp.minimum(over_held - spill_taken, most - hosted[partner]), free)
        take = jnp.maximum(take, 0)
        first_row = second_room - hosted[partner] - take
        spill_plan.append((mask, most, spill_taken, take, first_row))
        spill_taken = spill_taken + take
        hosted = hosted + take[partner]
    trips_reduce = -(-jnp.max(over_held - spill_taken) // extra_step)

    def of_owner(values):
        return jnp.sum(onehot[:big_count] * values[None, :], axis=1)

    second_over = big_ranks - second_room
    second_spot = jnp.where(
        second_over < 0,
        TABLE + big_owners * second_room + big_ranks,
        2 * TABLE + rest_row(second_over - of_owner(spill_taken), big_owners),
    )
    for mask, most, before, take, first_row in spill_plan:
        inside = second_over - of_owner(before)
        second_spot = jnp.where(
            (inside >= 0) & (inside < of_owner(take)),
            TABLE + (big_owners ^ mask) * second_room + of_owner(first_row) + inside,
            second_spot,
        )
    store = jnp.where(
        big_ranks >= second_there,
        big_owners * first_room + big_ranks - second_there,
        second_spot,
    )
    small_owner = owners[big_count]

    def spots(table, name):
        return table[firsts[name] : firsts[name] + counts[name]]

    my_mixer = mixer_held[my_index]
    my_mlp = mlp_held[my_index]
    my_count = my_mixer + my_mlp
    slot_ids = jnp.arange(padded, dtype=jnp.int32)
    mine = owners == my_index
    matches = (mine[None, :] & (ranks[None, :] == slot_ids[:, None])).astype(jnp.int32)
    kind_table = piece_kinds(segments_list, piece_count, piece_size)
    piece_rates, small_rates = rate_parts(segments_list, piece_count, piece_size)
    present = jnp.sum(matches, axis=1)
    slot_kinds = 1 + jnp.sum(matches * jnp.asarray(kind_table - 1)[None, :], axis=1)
    slot_rates = PAD_RATE + jnp.sum(
        matches.astype(jnp.float32) * jnp.asarray(piece_rates - np.float32(PAD_RATE))[None, :], axis=1
    )
    is_small = matches[:, big_count]
    kinds_used = sorted(set(kind_table.tolist()) | {1})
    my_held = second_held[my_index]
    in_first = slot_ids >= my_held
    my_over = slot_ids - second_room
    rest_source = 3 + len(spill_plan)
    slot_sources = jnp.where(my_over < 0, 2, rest_source)
    slot_rows = jnp.where(my_over < 0, slot_ids, my_over - spill_taken[my_index])
    for number, (mask, most, before, take, first_row) in enumerate(spill_plan):
        inside = my_over - before[my_index]
        here = (inside >= 0) & (inside < take[my_index])
        slot_sources = jnp.where(here, 3 + number, slot_sources)
        slot_rows = jnp.where(
            here, first_row[my_index] + inside - (second_room - most), slot_rows
        )
    slot_sources = jnp.where(in_first, 0, slot_sources)
    slot_rows = jnp.where(in_first, slot_ids - my_held, slot_rows)
    slot_sources = jnp.where(present > 0, jnp.where(is_small > 0, 1, slot_sources), 0)
    slot_rows = jnp.where(is_small > 0, 0, slot_rows)
    slot_rows = jnp.where(present > 0, slot_rows, 0)
    slot_masks = jnp.stack([present.astype(jnp.float32), is_small.astype(jnp.float32), slot_rates])
    slot_masks = jnp.broadcast_to(slot_masks[:, :, None], slot_masks.shape + (LANES,))
    all_blocks = padded // 8
    plain_blocks = second_room // 8
    from_first = jnp.clip((my_held + 7) // 8, plain_blocks, all_blocks).astype(jnp.int32)
    ranges = [
        jnp.stack([from_first, jnp.int32(all_blocks)]),
        jnp.array([0, plain_blocks], jnp.int32),
        jnp.stack([jnp.int32(plain_blocks), jnp.maximum(from_first, plain_blocks + 1)]),
    ]

    small_rows = -(-sum(r * c for name, r, c, rate in segments_list[8:]) // (TILE * LANES)) * TILE
    gain_width = D // head_parts
    norm_width = DV // head_parts
    gain_first = sum(r * c for name, r, c, rate in segments_list[8:14])
    my_small = lax.dynamic_slice(master, (small_rank, 0), (1, small_rows * LANES))
    my_small = my_small.astype(jnp.bfloat16)
    gains = my_small[:, gain_first : gain_first + 2 * gain_width + norm_width]
    gains = in_order(exchange([gains] * head_parts, "head"), my_head, 0)
    gains = jnp.concatenate(
        [
            gains[:, :gain_width].reshape(1, D),
            gains[:, gain_width : 2 * gain_width].reshape(1, D),
            gains[:, 2 * gain_width :].reshape(1, DV),
        ],
        axis=1,
    )
    rows_of_piece = piece_size // LANES
    small_width = small_rows * LANES
    small_part = jnp.concatenate([my_small, gains], axis=1).reshape(-1, LANES)
    small_table, small_base = gather_states(small_part)
    input_blocks = exchange([inputs] * head_parts, "head")
    early_part = pack_blocks(master, slot_kinds, kinds_used, 0, early)
    early_table = lax.all_gather(early_part, "seq", axis=0, tiled=True)
    late_part = pack_blocks(master, slot_kinds, kinds_used, early, late)
    late_send = late_part[:late_room]
    if late_room < late:
        guests = lax.ppermute(
            late_part[late_room:], "seq", [(i, i ^ 1) for i in range(seq_parts)]
        )
        late_send = lax.dynamic_update_slice_in_dim(
            late_part, guests, late_held[my_index], axis=0
        )[:late_room]
    back_blocks = exchange([cotangent] * head_parts, "head")
    rows_full = in_order(input_blocks, my_head, 1)
    back_full = in_order(back_blocks, my_head, 1)
    small_flat = lax.dynamic_index_in_dim(
        small_table, small_owner ^ small_base[0], axis=0, keepdims=False
    ).reshape(-1)
    by_name, small_used = unpack(small_flat, segments_list[8:])
    gains = small_flat[small_width:].astype(jnp.float32)[None, :]
    gain_one, gain_two, norm_row = gains[:, :D], gains[:, D : 2 * D], gains[:, 2 * D :]
    gain_one_mine = by_name["gainone"].astype(jnp.float32)
    gain_two_mine = by_name["gaintwo"].astype(jnp.float32)

    rows_wide = rows_full.astype(jnp.float32)
    scale_one = lax.rsqrt(jnp.mean(rows_wide * rows_wide, axis=-1, keepdims=True) + NORM_EPSILON)
    normed = (rows_wide * scale_one * gain_one).astype(jnp.bfloat16)
    normed_ext = stored(
        jnp.concatenate([shifted(normed[row_count - RIM :], "seq", 1), normed], axis=0)
    )

    decay_weight = jnp.pad(by_name["wab"], ((0, 0), (0, LANES - 2 * local_heads)))
    decay_proj = jnp.dot(normed, decay_weight, preferred_element_type=jnp.float32)
    taps = jnp.concatenate([by_name["cv"], by_name["ck"]], axis=1)
    taps = jnp.pad(taps.astype(jnp.float32), ((0, 8 - KCONV), (0, 0)))
    query_taps = jnp.pad(by_name["cq"].astype(jnp.float32), ((0, 8 - KCONV), (0, 0)))
    scalars = jnp.pad(
        jnp.concatenate([by_name["alog"], by_name["dtbias"]], axis=0).astype(jnp.float32),
        ((0, 6), (0, LANES - local_heads)),
    )

    mixer_rest = gather_rest(late_part, 0, trips_gather, most_gather, extra_step)
    beside = (
        mixer_rest, late_part, late_send, normed, normed_ext, scale_one, decay_proj, decay_weight, taps, query_taps, scalars,
        back_full, mixer_fetch, mlp_fetch, store, gain_two, norm_row,
        slot_sources, slot_rows, slot_masks, ranges, trips_late, trips_reduce,
    )
    early_table, beside = lax.optimization_barrier((early_table, beside))
    (
        mixer_rest, late_part, late_send, normed, normed_ext, scale_one, decay_proj, decay_weight, taps, query_taps, scalars,
        back_full, mixer_fetch, mlp_fetch, store, gain_two, norm_row,
        slot_sources, slot_rows, slot_masks, ranges, trips_late, trips_reduce,
    ) = beside
    late_table = lax.all_gather(late_send, "seq", axis=0, tiled=True)

    value_key_weights, value_key = assemble(
        [early_table, mixer_rest],
        [(spots(mixer_fetch, name), columns[name]) for name in ("wv", "wk")],
        512,
        normed_ext,
    )
    solve, fresh, wy_keys, handoff = mixer_local(
        local_heads, value_key, taps, decay_proj, scalars
    )
    query_gate_weights, query_gate = assemble(
        [early_table, mixer_rest],
        [(spots(mixer_fetch, name), columns[name]) for name in ("wq", "wg")],
        512,
        normed_ext,
    )
    reach, zero_out = mixer_reach(
        local_heads, query_gate, value_key, query_taps, taps, decay_proj, scalars, fresh, wy_keys
    )
    (out_weights,) = assemble(
        [early_table, mixer_rest], [(spots(mixer_fetch, "wo"), columns["wo"])], 256
    )
    entering_state, kept_states, beside = entering(
        local_heads,
        my_index_row,
        handoff,
        (query_gate_weights, query_gate, reach, zero_out, out_weights),
    )
    query_gate_weights, query_gate, reach, zero_out, out_weights = beside
    recurred, gated_low = mixer_out(
        local_heads, entering_state, reach, zero_out, query_gate, norm_row
    )
    mixed_parts = exchange(
        spread_products(my_head_row, head_parts, [((gated_low,), out_weights, False)]), "head"
    )
    mixed = total_of(mixed_parts)
    inputs_wide = inputs.astype(jnp.float32)
    residual = inputs_wide + mixed
    resid_low = residual.astype(jnp.bfloat16)

    resid_blocks = exchange([resid_low] * head_parts, "head")
    trips_now, late_table = lax.optimization_barrier((trips_late, late_table))
    late_rest = gather_rest(
        late_part, late_room + late_spare[my_index], trips_now, most_gather, extra_step
    )
    mlp_tables = [late_table, early_table, late_rest]
    (down_weights,) = assemble(
        mlp_tables, [(spots(mlp_fetch, "wdown"), columns["wdown"])], 352
    )
    (mlp_weights,) = assemble(
        mlp_tables,
        [(spots(mlp_fetch, name), columns[name]) for name in ("wgate", "wup")],
        512,
    )
    resid_blocks, down_weights, mlp_weights = lax.optimization_barrier(
        (resid_blocks, down_weights, mlp_weights)
    )
    resid_full = in_order(resid_blocks, my_head, 1).astype(jnp.float32)
    scale_two = lax.rsqrt(jnp.mean(resid_full * resid_full, axis=-1, keepdims=True) + NORM_EPSILON)
    hidden_in = (resid_full * scale_two * gain_two).astype(jnp.bfloat16)
    gate_up = jnp.dot(hidden_in, mlp_weights, preferred_element_type=jnp.float32)
    hidden_width = columns["wgate"]
    gate_mlp, up_mlp = gate_up[:, :hidden_width], gate_up[:, hidden_width:]
    logistic_output_multiplier = jax.nn.sigmoid(gate_mlp)
    silu_gate = gate_mlp * logistic_output_multiplier
    hidden = (silu_gate * up_mlp).astype(jnp.bfloat16)
    mlp_blocks = spread_products(my_head_row, head_parts, [((hidden,), down_weights, False)])
    d_hidden = back_product(back_full, down_weights)
    d_gate_mlp = (
        d_hidden
        * up_mlp
        * logistic_output_multiplier
        * (1.0 + gate_mlp * (1.0 - logistic_output_multiplier))
    ).astype(jnp.bfloat16)
    d_up_mlp = (d_hidden * silu_gate).astype(jnp.bfloat16)
    def store_grad(tables, name, left_t, right, right_block, blocks_a_step):
        return weight_grad_blocks(
            left_t, right, right_block, columns[name], spots(store, name), tables, blocks_a_step
        )

    grad_tables = [
        reserve((rows, rows_of_piece, LANES), jnp.bfloat16)
        for rows in (
            seq_parts * first_room,
            seq_parts * second_room,
            most_reduce * seq_parts * extra_step,
        )
    ]
    grad_tables = store_grad(grad_tables, "wdown", hidden.T, back_full, 0, 11)
    hidden_in_t = hidden_in.T
    grad_tables = store_grad(grad_tables, "wgate", hidden_in_t, d_gate_mlp, 0, 11)
    grad_tables = store_grad(grad_tables, "wup", hidden_in_t, d_up_mlp, 0, 11)
    grad_tables, d_gate_mlp, d_up_mlp = lax.optimization_barrier(
        (grad_tables, d_gate_mlp, d_up_mlp)
    )
    d_hidden_parts = exchange(
        spread_products(my_head_row, head_parts, [((d_gate_mlp, d_up_mlp), mlp_weights, True)]), "head"
    )
    first_reduced = lax.psum_scatter(grad_tables[0], "seq", scatter_dimension=0, tiled=True)
    grad_tables = grad_tables[1:]
    store = store - TABLE
    d_hidden_mine = total_of(d_hidden_parts)

    resid_mine = resid_low.astype(jnp.float32)
    d_hidden_low = d_hidden_mine.astype(jnp.bfloat16)
    dot_mine = jnp.sum(d_hidden_mine * gain_two_mine * resid_mine, axis=-1)
    d_hidden_blocks = exchange([d_hidden_low] * head_parts, "head")
    dot_two = sum_over(dot_mine.reshape(-1, LANES), "head").reshape(row_count, 1)
    grad_gaintwo = jnp.sum(d_hidden_mine * resid_mine * scale_two, axis=0)
    d_resid = (
        cotangent.astype(jnp.float32)
        + scale_two * d_hidden_mine * gain_two_mine
        - scale_two**3 / D * resid_mine * dot_two
    )
    d_hidden_full = in_order(d_hidden_blocks, my_head, 1).astype(jnp.float32)
    back_mix_full = (
        back_full.astype(jnp.float32)
        + scale_two * d_hidden_full * gain_two
        - scale_two**3 / D * resid_full * dot_two
    ).astype(jnp.bfloat16)

    d_gated = back_product(back_mix_full, out_weights)
    d_recurred, d_gate, norm_grad, d_entering = mixer_gate_back(
        local_heads, d_gated, recurred, query_gate, norm_row, reach
    )
    normed_t = normed.T
    grad_tables = store_grad(grad_tables, "wo", gated_low.T, back_mix_full, 0, 8)
    grad_tables = store_grad(grad_tables, "wg", normed_t, d_gate, 0, 8)
    d_leaving, (grad_tables, mlp_blocks) = leaving(
        local_heads, my_index_row, d_entering, kept_states, (grad_tables, mlp_blocks)
    )
    mlp_parts = exchange(mlp_blocks, "head")
    d_conv, d_tail, d_rim, d_taps, d_decay_wide, d_scalars = mixer_back(
        local_heads,
        query_gate,
        value_key,
        query_taps,
        taps,
        decay_proj,
        scalars,
        solve,
        fresh,
        wy_keys,
        entering_state,
        d_recurred,
        d_leaving,
    )
    d_rims = shifted(tuple(part[8 - rim_width :] for part in d_rim), "seq", -1)

    def with_rim(whole, tail, rim_grad):
        tail = tail + jnp.pad(rim_grad, ((8 - rim_width, 0), (0, 0)))
        return lax.dynamic_update_slice(whole, tail.astype(jnp.bfloat16), (row_count - 8, 0))

    d_query, d_value_key = (
        with_rim(*parts) for parts in zip(d_conv, d_tail, d_rims)
    )
    grad_tables = store_grad(grad_tables, "wv", normed_t, d_value_key, 0, 8)
    grad_tables = store_grad(grad_tables, "wk", normed_t, d_value_key, 2, 4)
    grad_tables = store_grad(grad_tables, "wq", normed_t, d_query, 0, 4)
    second_table, first_reduced, mlp_parts = lax.optimization_barrier(
        (grad_tables[0], first_reduced, mlp_parts)
    )
    block_out = (residual + total_of(mlp_parts)).astype(jnp.bfloat16)
    second_reduced = lax.psum_scatter(second_table, "seq", scatter_dimension=0, tiled=True)
    d_decay = d_decay_wide.astype(jnp.bfloat16)
    grad_wab = weight_grad(normed, d_decay)[:, : 2 * local_heads]
    d_normed_mine = total_of(
        exchange(
            spread_products(
                my_head_row,
                head_parts,
                [
                    ((d_value_key,), value_key_weights, True),
                    ((d_query, d_gate), query_gate_weights, True),
                    ((d_decay,), decay_weight, True),
                ],
            ),
            "head",
        )
    )
    dot_one = jnp.sum(d_normed_mine * gain_one_mine * inputs_wide, axis=-1)
    sums = sum_over(
        jnp.concatenate([dot_one.reshape(-1, LANES), norm_grad[0].reshape(-1, LANES)]), "head"
    )
    dot_one = sums[: row_count // LANES].reshape(row_count, 1)
    grad_wnorm = lax.dynamic_slice_in_dim(
        sums[row_count // LANES :].reshape(-1), my_head * norm_width, norm_width
    )
    grad_gainone = jnp.sum(d_normed_mine * inputs_wide * scale_one, axis=0)
    input_grad = (
        d_resid
        + scale_one * d_normed_mine * gain_one_mine
        - scale_one**3 / D * inputs_wide * dot_one
    )

    small_grads = [
        d_taps[0][:KCONV],
        d_taps[1][:KCONV, local_heads * DV :],
        d_taps[1][:KCONV, : local_heads * DV],
        grad_wab,
        d_scalars[0, :local_heads],
        d_scalars[1, :local_heads],
        grad_gainone,
        grad_gaintwo,
        grad_wnorm,
    ]
    small_block = jnp.concatenate(
        [grad_now.reshape(-1) for grad_now in small_grads]
        + [jnp.zeros((small_rows * LANES - small_used,), jnp.float32)]
    ).reshape(-1, LANES)
    mask = 1
    while mask < seq_parts:
        small_block = small_block + lax.ppermute(
            small_block, "seq", [(i, i ^ mask) for i in range(seq_parts)]
        )
        mask *= 2
    small_block = jnp.pad(
        small_block.astype(jnp.bfloat16), ((0, rows_of_piece - small_rows), (0, 0))
    )[None]

    def update(sources, block_range, most_blocks, states, earlier):
        return optimizer_update(
            sources,
            slot_sources,
            slot_rows,
            slot_kinds,
            kinds_used,
            slot_masks,
            jnp.asarray(small_rates)[None, :],
            *states,
            capacity,
            block_range,
            most_blocks,
            earlier,
        )

    states = [master, moment_one, moment_two]
    done = update([first_reduced, small_block], ranges[0], all_blocks - plain_blocks, states, [])
    done, second_reduced, input_grad, block_out = lax.optimization_barrier(
        (done, second_reduced, input_grad, block_out)
    )
    spilled = []
    for mask, most, before, take, first_row in spill_plan:
        spilled.append(moved_by(second_reduced[second_room - most :], mask))
    sources = [first_reduced, small_block, second_reduced]
    if plain_blocks:
        done = update(sources, ranges[1], plain_blocks, states, done)
    done, spilled, rest_grads, trips_now = lax.optimization_barrier(
        (done, spilled, grad_tables[1], trips_reduce)
    )
    rest_reduced = reduce_rest(rest_grads, trips_now, most_reduce, extra_step)
    grad_slots, master_new, moment_new, second_new, weights_low = update(
        sources + spilled + [rest_reduced],
        ranges[2],
        all_blocks - plain_blocks,
        states,
        done,
    )
    return (
        block_out,
        input_grad,
        grad_slots,
        master_new,
        moment_new,
        second_new,
        weights_low,
    )


def solution(mesh):
    return jax.shard_map(
        on_device,
        mesh=mesh,
        in_specs=(
            P("seq", "head"),
            P("seq", "head"),
            P(),
            P("seq", "head"),
            P("seq", "head"),
            P("seq", "head"),
        ),
        out_specs=(
            P("seq", "head"),
            P("seq", "head"),
            P("seq", "head"),
            P("seq", "head"),
            P("seq", "head"),
            P("seq", "head"),
            P("seq", "head"),
        ),
        check_vma=False,
    )
```

```python
import jax
import jax.numpy as jnp
import numpy as np
from jax import lax
from jax.experimental import pallas as pl
from jax.experimental.pallas import tpu as pltpu
from jax.sharding import PartitionSpec as P

D = 2048
HEADS = 16
DK = 128
DV = 256
FF = 5632
KCONV = 4
STEP = 5


EXACT_ARITHMETIC = lax.Precision.HIGHEST
NORM_EPSILON = 1e-06
UNIT_EPSILON = 1e-06
HEAD_EPSILON = 1e-05
ADAM_EPSILON = 1e-08
BETA_ONE = 0.5
BETA_TWO = 0.5
WEIGHT_DECAY = 0.1
PAD_RATE = 0.1


def shifted(block, axis, distance):
    devices = range(lax.axis_size(axis))
    route = [(i - distance, i) for i in devices if i - distance in devices]
    return lax.ppermute(block, axis, route)


def shard_layout(local_heads, head_parts):
    return [
        ("wq", D, local_heads * DK, 0.02),
        ("wk", D, local_heads * DK, 0.02),
        ("wv", D, local_heads * DV, 0.02),
        ("wg", D, local_heads * DV, 0.02),
        ("wo", local_heads * DV, D, 0.015),
        ("wgate", D, FF // head_parts, 0.02),
        ("wup", D, FF // head_parts, 0.02),
        ("wdown", FF // head_parts, D, 0.012),
        ("cq", KCONV, local_heads * DK, 0.4),
        ("ck", KCONV, local_heads * DK, 0.4),
        ("cv", KCONV, local_heads * DV, 0.4),
        ("wab", D, 2 * local_heads, 0.04),
        ("alog", 1, local_heads, 0.5),
        ("dtbias", 1, local_heads, 0.5),
        ("gainone", 1, D // head_parts, 0.1),
        ("gaintwo", 1, D // head_parts, 0.1),
        ("wnorm", 1, DV // head_parts, 0.1),
    ]


def piece_table(owners, seq_parts, capacity):
    piece_count = owners.shape[0]
    devices = jnp.arange(seq_parts, dtype=jnp.int32)
    onehot = (owners[:, None] == devices[None, :]).astype(jnp.int32)
    before = jnp.cumsum(onehot, axis=0) - onehot
    rank_within = jnp.sum(before * onehot, axis=1)
    slot_of_piece = owners * capacity + rank_within
    matches = slot_of_piece[None, :] == jnp.arange(seq_parts * capacity, dtype=jnp.int32)[:, None]
    present = jnp.any(matches, axis=1)
    piece_of_slot = jnp.sum(
        matches.astype(jnp.int32) * jnp.arange(piece_count, dtype=jnp.int32)[None, :], axis=1
    )
    return (slot_of_piece, piece_of_slot, present)


def unpack(flat_weights, segments_list):
    by_name = {}
    offset_now = 0
    for seg_name, row_count, col_count, seg_rate in segments_list:
        by_name[seg_name] = flat_weights[offset_now : offset_now + row_count * col_count].reshape(
            row_count, col_count
        )
        offset_now += row_count * col_count
    return (by_name, offset_now)


def rate_parts(segments_list, piece_count, piece_size):
    piece_rates = np.full(piece_count, PAD_RATE, np.float32)
    small_rates = np.full(piece_size, PAD_RATE, np.float32)
    offset_now = 0
    big_total = (piece_count - 1) * piece_size
    for seg_name, row_count, col_count, seg_rate in segments_list:
        seg_size = row_count * col_count
        if offset_now < big_total:
            piece_rates[offset_now // piece_size : (offset_now + seg_size) // piece_size] = seg_rate
        else:
            small_rates[offset_now - big_total : offset_now - big_total + seg_size] = seg_rate
        offset_now += seg_size
    return (piece_rates, small_rates)


HEADS_A_STEP = 1


def product(left, right, left_axis, right_axis, exact=False):
    def dot(a, b):
        return lax.dot_general(
            a,
            b,
            (((left_axis,), (right_axis,)), ((), ())),
            preferred_element_type=jnp.float32,
        )

    left_low, right_low = left.astype(jnp.bfloat16), right.astype(jnp.bfloat16)
    if not exact:
        return dot(left_low, right_low)
    left_rest = (left - left_low.astype(jnp.float32)).astype(jnp.bfloat16)
    right_rest = (right - right_low.astype(jnp.float32)).astype(jnp.bfloat16)
    return dot(left_low, right_low) + (dot(left_low, right_rest) + dot(left_rest, right_low))


def take_lane(wide, lane):
    lanes = lax.broadcasted_iota(jnp.int32, wide.shape, 1)
    return jnp.sum(jnp.where(lanes == lane, wide, 0.0), axis=1, keepdims=True)


def put_lane(column, lane):
    lanes = lax.broadcasted_iota(jnp.int32, (column.shape[0], 128), 1)
    return jnp.where(lanes == lane, column, 0.0)


def to_row(column, diagonal):
    return jnp.sum(jnp.where(diagonal, column, 0.0), axis=0, keepdims=True)


def convolved(extended, taps_ref, columns):
    row_count = extended.shape[0] - RIM
    first = RIM - (KCONV - 1)
    running = taps_ref[0:1, columns] * extended[first : first + row_count, columns]
    for tap in range(1, KCONV):
        running = running + taps_ref[tap : tap + 1, columns] * extended[
            first + tap : first + tap + row_count, columns
        ]
    return running


def decay_terms(head, local_heads, decay_ref, scalars_ref):
    row_count = decay_ref.shape[0]
    shape = (row_count, row_count)
    row_ids = lax.broadcasted_iota(jnp.int32, shape, 0)
    column_ids = lax.broadcasted_iota(jnp.int32, shape, 1)
    decay_in = take_lane(decay_ref[...], head) + take_lane(scalars_ref[1:2, :], head)
    rate = -jnp.exp(take_lane(scalars_ref[0:1, :], head))
    soft = jnp.maximum(decay_in, 0.0) + jnp.log1p(jnp.exp(-jnp.abs(decay_in)))
    logs = rate * soft
    beta = jax.nn.sigmoid(take_lane(decay_ref[...], head + local_heads))
    diagonal = row_ids == column_ids
    logs_row = to_row(logs, diagonal)
    upto = row_ids >= column_ids
    sums = jnp.sum(jnp.where(upto, logs_row, 0.0), axis=1, keepdims=True)
    sums_row = to_row(sums, diagonal)
    within = jnp.exp(jnp.where(upto, sums - sums_row, -1e30))
    return decay_in, rate, logs, beta, sums, within, row_ids, column_ids


def unit_rows(rows):
    scale = lax.rsqrt(jnp.sum(rows * rows, axis=-1, keepdims=True) + UNIT_EPSILON)
    return rows * scale, scale


def mixer_specs(local_heads, row_count):
    def spec(rows, width, first):
        width *= HEADS_A_STEP
        return pl.BlockSpec((rows, width), lambda h, first=first // width: (0, first + h))

    def query(rows):
        return spec(rows, DK, 0)

    def key(rows):
        return spec(rows, DK, local_heads * DV)

    def value(rows):
        return spec(rows, DV, 0)

    whole = pl.BlockSpec((row_count, 128), lambda h: (0, 0))
    scalars = pl.BlockSpec((8, 128), lambda h: (0, 0))
    return query, key, value, whole, scalars


def per_head(*shape):
    return pl.BlockSpec((HEADS_A_STEP,) + shape, lambda h: (h,) + (0,) * len(shape))


def head_columns(sub):
    return slice(DK * sub, DK * sub + DK), slice(DV * sub, DV * sub + DV)


def mixer_local(local_heads, value_key, taps, decay_proj, scalars):
    row_count = value_key.shape[0] - RIM
    query, key, value, whole, scalar_spec = mixer_specs(local_heads, row_count)

    def kernel(
        pv, pk, tv, tk, decay_ref, scalars_ref, solve_ref, fresh_ref, wy_ref, handoff_ref
    ):
        for sub in range(HEADS_A_STEP):
            head = pl.program_id(0) * HEADS_A_STEP + sub
            narrow, wide = head_columns(sub)
            key_rows = unit_rows(jax.nn.silu(convolved(pk, tk, narrow)))[0]
            values = jax.nn.silu(convolved(pv, tv, wide))
            decay_in, rate, logs, beta, sums, within, row_ids, column_ids = decay_terms(
                head, local_heads, decay_ref, scalars_ref
            )
            gram = product(key_rows, key_rows, 1, 1, True)
            system = jnp.where(row_ids > column_ids, beta * gram * within, 0.0)
            unit = jnp.where(row_ids == column_ids, 1.0, 0.0)
            solve = unit
            size = 1
            while size < row_count:
                lower = (row_ids // (2 * size) == column_ids // (2 * size)) & (
                    row_ids // size != column_ids // size
                )
                part = jnp.where(lower, system, 0.0)
                if size == 1:
                    solve = solve - part
                else:
                    solve = solve - product(solve, product(part, solve, 1, 0), 1, 0)
                size *= 2
            remainder = (unit - solve) - product(system, solve, 1, 0, True)
            solve = solve + product(solve, remainder, 1, 0)
            grown = jnp.exp(sums)
            fresh = product(solve, beta * values, 1, 0, True)
            wy_keys = product(solve, (beta * grown) * key_rows, 1, 0, True)
            last = sums[row_count - 1 : row_count, :]
            tail_keys = jnp.exp(last - sums) * key_rows
            eye = lax.broadcasted_iota(jnp.int32, (DK, DK), 0) == lax.broadcasted_iota(
                jnp.int32, (DK, DK), 1
            )
            solve_ref[sub] = solve
            fresh_ref[sub] = fresh
            wy_ref[sub] = wy_keys
            handoff_ref[sub, :, :DK] = (
                jnp.where(eye, jnp.exp(last), 0.0) - product(tail_keys, wy_keys, 0, 0)
            ).astype(jnp.bfloat16)
            handoff_ref[sub, :, DK:] = product(tail_keys, fresh, 0, 0).astype(jnp.bfloat16)

    def out(*shape, kind=jnp.float32):
        return jax.ShapeDtypeStruct((local_heads,) + shape, kind)

    return pl.pallas_call(
        kernel,
        grid=(local_heads // HEADS_A_STEP,),
        in_specs=[
            value(RIM + row_count), key(RIM + row_count), value(8), key(8), whole, scalar_spec,
        ],
        out_specs=[
            per_head(row_count, row_count),
            per_head(row_count, DV),
            per_head(row_count, DK),
            per_head(DK, DK + DV),
        ],
        out_shape=[
            out(row_count, row_count),
            out(row_count, DV),
            out(row_count, DK),
            out(DK, DK + DV, kind=jnp.bfloat16),
        ],
        compiler_params=params(),
    )(value_key, value_key, taps, taps, decay_proj, scalars)


def mixer_reach(local_heads, query_gate, value_key, query_taps, taps, decay_proj, scalars, fresh, wy_keys):
    row_count = value_key.shape[0] - RIM
    query, key, value, whole, scalar_spec = mixer_specs(local_heads, row_count)

    def kernel(pq, pk, tq, tk, decay_ref, scalars_ref, fresh_ref, wy_ref, reach_ref, zero_ref):
        for sub in range(HEADS_A_STEP):
            head = pl.program_id(0) * HEADS_A_STEP + sub
            narrow, wide = head_columns(sub)
            queries = unit_rows(jax.nn.silu(convolved(pq, tq, narrow)))[0] * DK ** (-0.5)
            key_rows = unit_rows(jax.nn.silu(convolved(pk, tk, narrow)))[0]
            decay_in, rate, logs, beta, sums, within, row_ids, column_ids = decay_terms(
                head, local_heads, decay_ref, scalars_ref
            )
            attention = product(queries, key_rows, 1, 1) * within
            reach_ref[sub] = jnp.exp(sums) * queries - product(attention, wy_ref[sub], 1, 0)
            zero_ref[sub] = product(attention, fresh_ref[sub], 1, 0)

    return pl.pallas_call(
        kernel,
        grid=(local_heads // HEADS_A_STEP,),
        in_specs=[
            query(RIM + row_count), key(RIM + row_count), query(8), key(8), whole, scalar_spec,
            per_head(row_count, DV),
            per_head(row_count, DK),
        ],
        out_specs=[per_head(row_count, DK), per_head(row_count, DV)],
        out_shape=[
            jax.ShapeDtypeStruct((local_heads, row_count, DK), jnp.float32),
            jax.ShapeDtypeStruct((local_heads, row_count, DV), jnp.float32),
        ],
        compiler_params=params(),
    )(query_gate, value_key, query_taps, taps, decay_proj, scalars, fresh, wy_keys)


def advance_state(block, state, back):
    moved = product(block[:, :DK].astype(jnp.float32), state, 0 if back else 1, 0)
    return moved, block[:, DK:].astype(jnp.float32)


def chain_all(local_heads, my_index, handoffs, inputs, back):
    devices = handoffs.shape[0]

    def kernel(index_ref, handoffs_ref, inputs_ref, state_ref):
        state_ref[...] = jnp.zeros_like(state_ref)

        def advance(step, carry):
            j = devices - 1 - step if back else step
            for h in range(local_heads):
                moved, added = advance_state(handoffs_ref[j, h], state_ref[h], back)
                if back:
                    added = inputs_ref[j, h].astype(jnp.float32)
                state_ref[h] = moved + added
            return carry

        count = devices - 1 - index_ref[0] if back else index_ref[0]
        lax.fori_loop(0, count, advance, 0)

    vmem = pl.BlockSpec(memory_space=pltpu.VMEM)
    return pl.pallas_call(
        kernel,
        in_specs=[pl.BlockSpec(memory_space=pltpu.SMEM), vmem, vmem],
        out_specs=vmem,
        out_shape=jax.ShapeDtypeStruct((local_heads, DK, DV), jnp.float32),
        compiler_params=params(),
    )(my_index, handoffs, inputs)


def join_cores(local_heads, my_index, mine, theirs, inputs):
    half = local_heads // 2

    def kernel(index_ref, mine_ref, theirs_ref, *refs):
        out_ref = refs[-1]
        core = lax.rem(index_ref[0], 2)
        for i in range(half):
            h = core * half + i
            own, other = mine_ref[h], theirs_ref[h]
            first = jnp.where(core == 0, own, other)
            second = jnp.where(core == 0, other, own)
            if inputs:
                own, other = refs[0][h], refs[1][h]
                early = jnp.where(core == 0, own, other).astype(jnp.float32)
                late = jnp.where(core == 0, other, own).astype(jnp.float32)
                out_ref[i] = (advance_state(first, late, True)[0] + early).astype(jnp.bfloat16)
                continue
            moved, added = advance_state(second, first.astype(jnp.float32), False)
            out_ref[i, :, :DK] = moved[:, :DK].astype(jnp.bfloat16)
            out_ref[i, :, DK:] = (moved[:, DK:] + added).astype(jnp.bfloat16)

    vmem = pl.BlockSpec(memory_space=pltpu.VMEM)
    return pl.pallas_call(
        kernel,
        in_specs=[pl.BlockSpec(memory_space=pltpu.SMEM)] + [vmem] * (2 + len(inputs)),
        out_specs=vmem,
        out_shape=jax.ShapeDtypeStruct((half, DK, DV if inputs else DK + DV), jnp.bfloat16),
        compiler_params=params(),
    )(my_index, mine, theirs, *inputs)


def chain_chips(local_heads, my_index, theirs, chips, their_input, chip_inputs):
    half = local_heads // 2
    masks = len(chips) // 2
    back = their_input is not None
    flat = [theirs, *chips] + ([their_input, *chip_inputs] if back else [])

    def kernel(index_ref, *refs):
        state_ref = refs[-1]
        state_ref[...] = jnp.zeros_like(state_ref)
        core, chip = lax.rem(index_ref[0], 2), index_ref[0] // 2
        offset = 1 + len(chips)

        def update(h, block, extra):
            moved, added = advance_state(block, state_ref[h], back)
            state_ref[h] = moved + (extra.astype(jnp.float32) if back else added)

        order = range(masks, 0, -1) if back else range(masks)
        for other in order:
            for mask in range(1, masks + 1):
                here = (other ^ chip) == mask

                @pl.when(here & ((other > chip) if back else (other < chip)))
                def _():
                    for h in range(local_heads):
                        mine = core == h // half
                        pair = [refs[1 + 2 * (mask - 1) + i][h % half] for i in range(2)]
                        extra = None
                        if back:
                            extra = [
                                refs[offset + 1 + 2 * (mask - 1) + i][h % half] for i in range(2)
                            ]
                            extra = jnp.where(mine, *extra)
                        update(h, jnp.where(mine, *pair), extra)

        @pl.when(core == (0 if back else 1))
        def _():
            for h in range(local_heads):
                update(h, refs[0][h], refs[offset][h] if back else None)

    vmem = pl.BlockSpec(memory_space=pltpu.VMEM)
    return pl.pallas_call(
        kernel,
        in_specs=[pl.BlockSpec(memory_space=pltpu.SMEM)] + [vmem] * len(flat),
        out_specs=vmem,
        out_shape=jax.ShapeDtypeStruct((local_heads, DK, DV), jnp.float32),
        compiler_params=params(),
    )(my_index, *flat)


def moved_by(array, mask):
    return lax.ppermute(array, "seq", [(i, i ^ mask) for i in range(lax.axis_size("seq"))])


def pass_chips(block, beside):
    arrived = [moved_by(block, mask) for mask in (2, 4, 6)]
    arrived, beside = lax.optimization_barrier((arrived, beside))
    return [array for part in arrived for array in (part, moved_by(part, 1))], beside


def entering(local_heads, my_index, handoff, beside):
    if lax.axis_size("seq") != 8:
        handoffs = lax.all_gather(handoff, "seq", axis=0, tiled=False)
        return chain_all(local_heads, my_index, handoffs, handoffs, False), handoffs, beside
    theirs = moved_by(handoff, 1)
    chips, beside = pass_chips(join_cores(local_heads, my_index, handoff, theirs, []), beside)
    state = chain_chips(local_heads, my_index, theirs, chips, None, [])
    return state, (handoff, theirs, chips), beside


def leaving(local_heads, my_index, d_entering, kept, beside):
    if lax.axis_size("seq") != 8:
        inputs = lax.all_gather(d_entering, "seq", axis=0, tiled=False)
        return chain_all(local_heads, my_index, kept, inputs, True), beside
    handoff, theirs, chips = kept
    their_input = moved_by(d_entering, 1)
    joined = join_cores(local_heads, my_index, handoff, theirs, [d_entering, their_input])
    inputs, beside = pass_chips(joined, beside)
    return chain_chips(local_heads, my_index, theirs, chips, their_input, inputs), beside


def mixer_out(local_heads, entering_state, reach, zero_out, query_gate, norm_gain):
    row_count = query_gate.shape[0] - RIM
    gate_first = local_heads * DK

    def kernel(state_ref, reach_ref, zero_ref, gate_ref, norm_ref, out_ref, gated_ref):
        for h in range(local_heads):
            columns = slice(DV * h, DV * h + DV)
            out = zero_ref[h] + product(reach_ref[h], state_ref[h], 1, 0)
            normed = out * lax.rsqrt(jnp.mean(out * out, axis=-1, keepdims=True) + HEAD_EPSILON)
            out_ref[:, columns] = out
            gate = gate_ref[RIM:, gate_first + DV * h : gate_first + DV * h + DV]
            gated_ref[:, columns] = (normed * norm_ref[...] * jax.nn.silu(gate)).astype(
                jnp.bfloat16
            )

    vmem = pl.BlockSpec(memory_space=pltpu.VMEM)
    width = local_heads * DV
    return pl.pallas_call(
        kernel,
        in_specs=[vmem] * 5,
        out_specs=[vmem, vmem],
        out_shape=[
            jax.ShapeDtypeStruct((row_count, width), jnp.float32),
            jax.ShapeDtypeStruct((row_count, width), jnp.bfloat16),
        ],
        compiler_params=params(),
    )(entering_state, reach, zero_out, query_gate, norm_gain)


def mixer_gate_back(local_heads, d_gated, recurred, query_gate, norm_gain, reach):
    row_count = query_gate.shape[0] - RIM
    gate_first = local_heads * DK // DV

    def kernel(d_gated_ref, out_ref, gate_ref, norm_ref, reach_ref, d_out_ref, d_gate_ref, d_norm_ref, d_state_ref):
        out, gate, norm_row, d_gated_now = (
            out_ref[...], gate_ref[RIM:, :], norm_ref[...], d_gated_ref[...]
        )
        scale = lax.rsqrt(jnp.mean(out * out, axis=-1, keepdims=True) + HEAD_EPSILON)
        normed = out * scale
        logistic = jax.nn.sigmoid(gate)
        silu = gate * logistic
        d_norm = jnp.sum(d_gated_now * normed * silu, axis=0, keepdims=True)

        @pl.when(pl.program_id(0) == 0)
        def _():
            d_norm_ref[...] = jnp.zeros_like(d_norm_ref)

        d_norm_ref[0:1, :] = d_norm_ref[0:1, :] + d_norm
        d_gate_ref[...] = (
            d_gated_now * normed * norm_row * logistic * (1.0 + gate * (1.0 - logistic))
        ).astype(jnp.bfloat16)
        d_normed = d_gated_now * norm_row * silu
        d_out = scale * d_normed - (scale * scale * scale) * out * jnp.mean(
            d_normed * out, axis=-1, keepdims=True
        )
        d_out_ref[...] = d_out
        d_state_ref[0] = product(reach_ref[0], d_out, 0, 0).astype(jnp.bfloat16)

    width = local_heads * DV
    block = pl.BlockSpec((row_count, DV), lambda h: (0, h))
    return pl.pallas_call(
        kernel,
        grid=(local_heads,),
        in_specs=[
            block,
            block,
            pl.BlockSpec((RIM + row_count, DV), lambda h: (0, gate_first + h)),
            pl.BlockSpec((1, DV), lambda h: (0, 0)),
            pl.BlockSpec((1, row_count, DK), lambda h: (h, 0, 0)),
        ],
        out_specs=[
            block,
            block,
            pl.BlockSpec((8, DV), lambda h: (0, 0)),
            pl.BlockSpec((1, DK, DV), lambda h: (h, 0, 0)),
        ],
        out_shape=[
            jax.ShapeDtypeStruct((row_count, width), jnp.float32),
            jax.ShapeDtypeStruct((row_count, width), jnp.bfloat16),
            jax.ShapeDtypeStruct((8, DV), jnp.float32),
            jax.ShapeDtypeStruct((local_heads, DK, DV), jnp.bfloat16),
        ],
        compiler_params=params(),
    )(d_gated, recurred, query_gate, norm_gain, reach)


def conv_back(
    d_pre, extended, taps_ref, padded, d_block_ref, d_tail_ref, d_rim_ref, d_taps_ref, columns
):
    row_count = d_pre.shape[0]
    first = RIM - (KCONV - 1)
    padded[0:8, :] = jnp.zeros((8, d_pre.shape[1]), jnp.float32)
    padded[8 : 8 + row_count, :] = d_pre
    padded[8 + row_count : 16 + row_count, :] = jnp.zeros((8, d_pre.shape[1]), jnp.float32)
    total = None
    d_taps_ref[:, columns] = jnp.zeros((8, d_pre.shape[1]), jnp.float32)
    for tap in range(KCONV):
        start = KCONV - 1 - tap
        term = taps_ref[tap : tap + 1, columns] * padded[start : start + row_count + 8, :]
        total = term if total is None else total + term
        d_taps_ref[tap : tap + 1, columns] = jnp.sum(
            d_pre * extended[first + tap : first + tap + row_count, columns], axis=0, keepdims=True
        )
    d_rim_ref[:, columns] = total[0:8, :]
    d_block_ref[:, columns] = total[8:, :].astype(jnp.bfloat16)
    d_tail_ref[:, columns] = total[row_count:, :]


def mixer_back(
    local_heads, query_gate, value_key, query_taps, taps, decay_proj, scalars,
    solve, fresh, wy_keys, entering_state, d_recurred, d_leaving,
):
    row_count = value_key.shape[0] - RIM
    query, key, value, whole, scalar_spec = mixer_specs(local_heads, row_count)

    def kernel(
        pq, pk, pv, tq, tk, tv, decay_ref, scalars_ref,
        solve_ref, fresh_ref, wy_ref, enter_ref, d_out_ref, d_leave_ref,
        dq_ref, dk_ref, dv_ref, tail_q, tail_k, tail_v, rim_q, rim_k, rim_v,
        taps_q, taps_k, taps_v, d_decay_ref, d_scalars_ref,
        pad_q, pad_k, pad_v,
    ):
        @pl.when(pl.program_id(0) == 0)
        def _():
            d_decay_ref[...] = jnp.zeros_like(d_decay_ref)
            d_scalars_ref[...] = jnp.zeros_like(d_scalars_ref)

        for sub in range(HEADS_A_STEP):
            head = pl.program_id(0) * HEADS_A_STEP + sub
            narrow, wide = head_columns(sub)
            pre_q = convolved(pq, tq, narrow)
            pre_k = convolved(pk, tk, narrow)
            pre_v = convolved(pv, tv, wide)
            conv_q, conv_k = jax.nn.silu(pre_q), jax.nn.silu(pre_k)
            unit_q, scale_q = unit_rows(conv_q)
            queries = unit_q * DK ** (-0.5)
            key_rows, scale_k = unit_rows(conv_k)
            values = jax.nn.silu(pre_v)
            decay_in, rate, logs, beta, sums, within, row_ids, column_ids = decay_terms(
                head, local_heads, decay_ref, scalars_ref
            )
            strict = row_ids > column_ids
            grown = jnp.exp(sums)
            last = sums[row_count - 1 : row_count, :]
            tail = jnp.exp(last - sums)
            tail_keys = tail * key_rows
            gram = product(key_rows, key_rows, 1, 1, True)
            scores = jnp.where(strict, gram * within, 0.0)
            attention = product(queries, key_rows, 1, 1) * within
            enter, d_out, d_leave = enter_ref[sub], d_out_ref[:, wide], d_leave_ref[sub]
            update = fresh_ref[sub] - product(wy_ref[sub], enter, 1, 0)
            d_update = product(attention, d_out, 0, 0) + product(tail_keys, d_leave, 1, 0)
            d_right = product(solve_ref[sub], d_update, 0, 0, True)
            d_attention = product(d_out, update, 1, 1) * within
            d_system = -product(d_right, update, 1, 1)
            out_state = product(d_out, enter, 1, 1)
            right_state = product(d_right, enter, 1, 1)
            leave_update = product(update, d_leave, 1, 1)
            remainder = values - grown * product(key_rows, enter, 1, 0)
            d_values = beta * d_right
            d_beta = jnp.sum(d_right * remainder, axis=1, keepdims=True) + jnp.sum(
                d_system * scores, axis=1, keepdims=True
            )
            pair = beta * (d_system * scores)
            d_gram = jnp.where(strict, beta * d_system * within, 0.0)
            d_queries = grown * out_state + product(d_attention, key_rows, 1, 0)
            d_keys = (
                product(d_attention, queries, 0, 0)
                + product(d_gram, key_rows, 1, 0)
                + product(d_gram, key_rows, 0, 0)
                + tail * leave_update
                - (beta * grown) * right_state
            )
            both = pair + d_attention * product(queries, key_rows, 1, 1)
            tail_rows = jnp.sum(tail_keys * leave_update, axis=1, keepdims=True)
            diagonal = row_ids == column_ids
            columns = jnp.sum(both, axis=0, keepdims=True)
            d_sums = (
                jnp.sum(both, axis=1, keepdims=True)
                - jnp.sum(jnp.where(diagonal, columns, 0.0), axis=1, keepdims=True)
                + jnp.sum(out_state * (grown * queries), axis=1, keepdims=True)
                - jnp.sum(right_state * ((beta * grown) * key_rows), axis=1, keepdims=True)
                - tail_rows
            )
            d_last = jnp.exp(last) * jnp.sum(
                jnp.sum(d_leave * enter, axis=1, keepdims=True), axis=0, keepdims=True
            ) + jnp.sum(tail_rows, axis=0, keepdims=True)
            d_logs = d_last + jnp.sum(
                jnp.where(row_ids <= column_ids, to_row(d_sums, diagonal), 0.0), axis=1, keepdims=True
            )
            d_decay_in = d_logs * rate * jax.nn.sigmoid(decay_in)
            d_beta_in = d_beta * beta * (1.0 - beta)
            d_decay_ref[...] = (
                d_decay_ref[...]
                + put_lane(d_decay_in, head)
                + put_lane(d_beta_in, head + local_heads)
            )
            d_rate = jnp.sum(d_logs * logs, axis=0, keepdims=True)
            d_bias = jnp.sum(d_decay_in, axis=0, keepdims=True)
            d_scalars_ref[0:1, :] = d_scalars_ref[0:1, :] + put_lane(d_rate, head)
            d_scalars_ref[1:2, :] = d_scalars_ref[1:2, :] + put_lane(d_bias, head)

            def unit_back(d_unit, unit, scale):
                return scale * (d_unit - unit * jnp.sum(unit * d_unit, axis=1, keepdims=True))

            def silu_back(d_act, pre):
                logistic = jax.nn.sigmoid(pre)
                return d_act * logistic * (1.0 + pre * (1.0 - logistic))

            d_pre_q = silu_back(unit_back(d_queries * DK ** (-0.5), unit_q, scale_q), pre_q)
            conv_back(d_pre_q, pq, tq, pad_q.at[sub], dq_ref, tail_q, rim_q, taps_q, narrow)
            d_pre_k = silu_back(unit_back(d_keys, key_rows, scale_k), pre_k)
            conv_back(d_pre_k, pk, tk, pad_k.at[sub], dk_ref, tail_k, rim_k, taps_k, narrow)
            conv_back(
                silu_back(d_values, pre_v), pv, tv, pad_v.at[sub],
                dv_ref, tail_v, rim_v, taps_v, wide,
            )

    def blocks(rows):
        return [
            pl.BlockSpec((rows, HEADS_A_STEP * width), lambda h: (0, h)) for width in (DK, DK, DV)
        ]

    def shapes(rows, kind):
        return [
            jax.ShapeDtypeStruct((rows, local_heads * width), kind) for width in (DK, DK, DV)
        ]

    outs = pl.pallas_call(
        kernel,
        grid=(local_heads // HEADS_A_STEP,),
        in_specs=[each(RIM + row_count) for each in (query, key, value)]
        + [each(8) for each in (query, key, value)]
        + [
            whole,
            scalar_spec,
            per_head(row_count, row_count),
            per_head(row_count, DV),
            per_head(row_count, DK),
            per_head(DK, DV),
            pl.BlockSpec((row_count, HEADS_A_STEP * DV), lambda h: (0, h)),
            per_head(DK, DV),
        ],
        out_specs=blocks(row_count) + blocks(8) * 3 + [whole, scalar_spec],
        out_shape=shapes(row_count, jnp.bfloat16)
        + shapes(8, jnp.float32) * 3
        + [
            jax.ShapeDtypeStruct((row_count, 128), jnp.float32),
            jax.ShapeDtypeStruct((8, 128), jnp.float32),
        ],
        scratch_shapes=[
            pltpu.VMEM((HEADS_A_STEP, row_count + 16, DK), jnp.float32),
            pltpu.VMEM((HEADS_A_STEP, row_count + 16, DK), jnp.float32),
            pltpu.VMEM((HEADS_A_STEP, row_count + 16, DV), jnp.float32),
        ],
        compiler_params=params(),
    )(
        query_gate, value_key, value_key, query_taps, taps, taps, decay_proj, scalars,
        solve, fresh, wy_keys, entering_state, d_recurred, d_leaving,
    )
    joined = [
        (outs[3 * i], jnp.concatenate([outs[3 * i + 2], outs[3 * i + 1]], axis=1))
        for i in range(4)
    ]
    return (*joined, outs[12], outs[13])


LANES = 128
CHUNK = 32768
TILE = 16
CAPACITY_UNIT = 44
FIRST_GATHER = 24
FIRST_REDUCE = 16
SECOND_REDUCE = 20
SECOND_GATHER = 16
RIM = 16
TABLE = 1 << 16
VMEM_LIMIT = 48 * 1024 * 1024


def params(**kwargs):
    return pltpu.CompilerParams(vmem_limit_bytes=VMEM_LIMIT, **kwargs)


def piece_kinds(segments_list, piece_count, piece_size):
    kinds = np.ones(piece_count, np.int32)
    offset_now = 0
    for seg_name, row_count, col_count, seg_rate in segments_list:
        if offset_now >= (piece_count - 1) * piece_size:
            break
        tiles = col_count // LANES
        if tiles in (2, 4, 8, 16):
            first = offset_now // piece_size
            kinds[first : first + row_count * col_count // piece_size] = tiles
        offset_now += row_count * col_count
    return kinds


def pack_blocks(master, slot_kinds, kinds_used, first_slot, slot_count):
    piece_size = master.shape[1]
    rows = piece_size // LANES
    first_block = first_slot // 8
    slot_blocks = pl.cdiv(slot_count, 8)

    def kernel(kinds_ref, master_ref, out_ref, scratch):
        first = (first_block + pl.program_id(0)) * 8
        for j in range(rows):
            scratch[8 * j : 8 * j + 8, :] = master_ref[:, LANES * j : LANES * j + LANES]
        for s in range(8):
            kind_now = kinds_ref[first + s]
            for kind in kinds_used:

                @pl.when(kind_now == kind)
                def _():
                    for tile in range(rows // TILE):
                        row_tile, column = divmod(tile, kind)
                        start = (row_tile * TILE * kind + column) * 8 + s
                        out_ref[s, TILE * tile : TILE * tile + TILE, :] = scratch[
                            pl.ds(start, TILE, stride=8 * kind), :
                        ].astype(jnp.bfloat16)

    return pl.pallas_call(
        kernel,
        grid_spec=pltpu.PrefetchScalarGridSpec(
            num_scalar_prefetch=1,
            grid=(slot_blocks,),
            in_specs=[pl.BlockSpec((8, piece_size), lambda i, kinds: (first_block + i, 0))],
            out_specs=pl.BlockSpec((8, rows, LANES), lambda i, kinds: (i, 0, 0)),
            scratch_shapes=[pltpu.VMEM((8 * rows, LANES), jnp.float32)],
        ),
        out_shape=jax.ShapeDtypeStruct((slot_count, piece_size // LANES, LANES), jnp.bfloat16),
        compiler_params=params(),
    )(slot_kinds, master)


def reserve(shape, kind):
    def kernel(out_ref):
        pass

    return pl.pallas_call(
        kernel,
        out_specs=pl.BlockSpec(memory_space=pl.ANY),
        out_shape=jax.ShapeDtypeStruct(shape, kind),
        compiler_params=params(),
    )()


def assemble(tables, matrices, step_rows, rows_in=None):
    piece_rows = tables[0].shape[1]
    plans = []
    first_block, first_column = 0, 0
    for positions, col_count in matrices:
        tiles = col_count // LANES
        blocks = step_rows * tiles // piece_rows
        plans.append((first_block, first_column, tiles, blocks))
        first_block += blocks
        first_column += col_count
    blocks_a_step, width = first_block, first_column
    steps = matrices[0][0].shape[0] // plans[0][3]
    order = jnp.concatenate(
        [
            positions.reshape(steps, plan[3])
            for (positions, col_count), plan in zip(matrices, plans)
        ],
        axis=1,
    ).reshape(-1)
    uneven = [plan for plan in plans if piece_rows * plan[3] != step_rows * plan[2] or plan[2] not in (2, 4, 8, 16)]
    multiply = rows_in is not None

    def kernel(order_ref, *refs):
        if multiply:
            rows_ref, refs = refs[0], refs[1:]
        table_refs, refs = refs[: len(tables)], refs[len(tables) :]
        out_ref, refs = refs[0], refs[1:]
        if multiply:
            product_ref, refs = refs[0], refs[1:]
        buffer, sem, scratch = refs
        g = pl.program_id(0)
        slot = lax.rem(g, 2)

        def start(step, which):
            def one(j, carry):
                position = order_ref[step * blocks_a_step + j]
                for number, table_ref in enumerate(table_refs):

                    @pl.when(position // TABLE == number)
                    def _():
                        pltpu.make_async_copy(
                            table_ref.at[lax.rem(position, TABLE)],
                            buffer.at[which, j],
                            sem.at[which],
                        ).start()

                return carry

            lax.fori_loop(0, blocks_a_step, one, 0)

        @pl.when(g == 0)
        def _():
            start(0, 0)

        @pl.when(g + 1 < steps)
        def _():
            start(g + 1, 1 - slot)

        pltpu.make_async_copy(buffer.at[slot], buffer.at[slot], sem.at[slot]).wait()
        for plan in plans:
            first, left, tiles, blocks = plan
            if plan in uneven:
                for j in range(blocks):
                    scratch[piece_rows * j : piece_rows * j + piece_rows, :] = buffer[
                        slot, first + j
                    ].astype(jnp.float32)
                for c in range(tiles):
                    out_ref[:, left + LANES * c : left + LANES * c + LANES] = scratch[
                        pl.ds(c, step_rows, stride=tiles), :
                    ].astype(jnp.bfloat16)
                continue
            for j in range(blocks):
                for tile in range(piece_rows // TILE):
                    row_tile, column = divmod(tile, tiles)
                    row = piece_rows // tiles * j + TILE * row_tile
                    column = left + LANES * column
                    out_ref[row : row + TILE, column : column + LANES] = buffer[
                        slot, first + j, TILE * tile : TILE * tile + TILE, :
                    ]
        if multiply:
            part = jnp.dot(rows_ref[...], out_ref[...], preferred_element_type=jnp.float32)

            @pl.when(g == 0)
            def _():
                product_ref[...] = part

            @pl.when(g > 0)
            def _():
                product_ref[...] = product_ref[...] + part

    anywhere = pl.BlockSpec(memory_space=pl.ANY)
    in_specs = [anywhere for table in tables]
    operands = list(tables)
    out_specs = [pl.BlockSpec((step_rows, width), lambda g, order: (g, 0))]
    out_shape = [jax.ShapeDtypeStruct((steps * step_rows, width), jnp.bfloat16)]
    if multiply:
        row_count = rows_in.shape[0]
        in_specs.insert(0, pl.BlockSpec((row_count, step_rows), lambda g, order: (0, g)))
        operands.insert(0, rows_in)
        out_specs.append(pl.BlockSpec((row_count, width), lambda g, order: (0, 0)))
        out_shape.append(jax.ShapeDtypeStruct((row_count, width), jnp.float32))
    scratch_rows = max([plan[3] * piece_rows for plan in uneven], default=8)
    return pl.pallas_call(
        kernel,
        grid_spec=pltpu.PrefetchScalarGridSpec(
            num_scalar_prefetch=1,
            grid=(steps,),
            in_specs=in_specs,
            out_specs=out_specs,
            scratch_shapes=[
                pltpu.VMEM((2, blocks_a_step, piece_rows, LANES), jnp.bfloat16),
                pltpu.SemaphoreType.DMA((2,)),
                pltpu.VMEM((scratch_rows, LANES), jnp.float32),
            ],
        ),
        out_shape=out_shape,
        cost_estimate=pl.CostEstimate(
            flops=2 * steps * step_rows * width * (rows_in.shape[0] if multiply else 0),
            bytes_accessed=4 * steps * step_rows * width,
            transcendentals=0,
        ),
        compiler_params=params(),
    )(order, *operands)


def spread_products(my_part, parts, pairs):
    row_count = pairs[0][0][0].shape[0]
    total = pairs[0][1].shape[0 if pairs[0][2] else 1]
    width = total // parts

    def kernel(part_ref, *refs):
        ins, outs = list(refs[:-parts]), refs[-parts:]
        for m in range(parts):
            first = pl.multiple_of((part_ref[0] ^ m) * width, width)
            result, place = None, 0
            for lefts, right, transposed in pairs:
                left_refs, right_ref = ins[place : place + len(lefts)], ins[place + len(lefts)]
                place += len(lefts) + 1
                depth = 0
                for left_ref in left_refs:
                    inner = slice(depth, depth + left_ref.shape[1])
                    depth += left_ref.shape[1]
                    if transposed:
                        block, axis = right_ref[pl.ds(first, width), inner], 1
                    else:
                        block, axis = right_ref[inner, pl.ds(first, width)], 0
                    part = lax.dot_general(
                        left_ref[...],
                        block,
                        (((1,), (axis,)), ((), ())),
                        preferred_element_type=jnp.float32,
                    )
                    result = part if result is None else result + part
            outs[m][...] = result.astype(jnp.bfloat16)

    vmem = pl.BlockSpec(memory_space=pltpu.VMEM)
    flat = [array for lefts, right, transposed in pairs for array in (*lefts, right)]
    return pl.pallas_call(
        kernel,
        in_specs=[pl.BlockSpec(memory_space=pltpu.SMEM)] + [vmem] * len(flat),
        out_specs=[vmem] * parts,
        out_shape=[jax.ShapeDtypeStruct((row_count, width), jnp.bfloat16)] * parts,
        cost_estimate=pl.CostEstimate(
            flops=2 * row_count * sum(pair[1].size for pair in pairs),
            bytes_accessed=2 * sum(pair[1].size for pair in pairs),
            transcendentals=0,
        ),
        compiler_params=params(),
    )(my_part, *flat)


def stored(array):
    def kernel(in_ref, out_ref):
        out_ref[...] = in_ref[...]

    return pl.pallas_call(
        kernel,
        out_shape=jax.ShapeDtypeStruct(array.shape, array.dtype),
        compiler_params=params(),
    )(array)


def exchange(blocks, axis):
    devices = lax.axis_size(axis)
    return [blocks[0]] + [
        lax.ppermute(blocks[m], axis, [(i, i ^ m) for i in range(devices)])
        for m in range(1, devices)
    ]


def total_of(blocks):
    total = blocks[0].astype(jnp.float32)
    for block in blocks[1:]:
        total = total + block.astype(jnp.float32)
    return total


def sum_over(block, axis):
    return total_of(exchange([block] * lax.axis_size(axis), axis))


def in_order(blocks, my_part, axis):
    stacked = jnp.stack(blocks)
    return jnp.concatenate(
        [
            lax.dynamic_index_in_dim(stacked, my_part ^ j, 0, keepdims=False)
            for j in range(len(blocks))
        ],
        axis=axis,
    )


def gather_states(block):
    devices = lax.axis_size("seq")
    if devices != 8:
        return lax.all_gather(block, "seq", axis=0, tiled=False), jnp.zeros((1,), jnp.int32)

    def moved(array, mask):
        return lax.ppermute(array, "seq", [(i, i ^ mask) for i in range(devices)])

    chips = [block] + [moved(block, mask) for mask in (2, 4, 6)]
    pairs = [(chip, moved(chip, 1)) for chip in chips]
    rows = jnp.stack([array for pair in pairs for array in pair])
    return rows, lax.axis_index("seq").astype(jnp.int32).reshape(1)


def weight_grad_blocks(left_t, rights, col_count, positions, tables, blocks_a_step):
    row_total, depth = left_t.shape
    tiles = col_count // LANES
    piece_rows = 512
    even = tiles in (2, 4, 8, 16)
    step_rows = blocks_a_step * piece_rows // tiles
    steps = row_total // step_rows

    total_steps = steps * len(rights)

    def multiply(left, right_ref, product, staged, slot):
        for c in range(0, tiles, 2):
            width = min(2, tiles - c)
            part = jnp.dot(
                left,
                right_ref[:, LANES * c : LANES * (c + width)],
                preferred_element_type=jnp.float32,
            )
            for w in range(width):
                column = part[:, LANES * w : LANES * w + LANES]
                if not even:
                    product[pl.ds(c + w, step_rows, stride=tiles), :] = column
                    continue
                for row_tile in range(step_rows // TILE):
                    block, row = divmod(TILE * (row_tile * tiles + c + w), piece_rows)
                    staged[slot, block, row : row + TILE, :] = column[
                        TILE * row_tile : TILE * row_tile + TILE
                    ].astype(jnp.bfloat16)
        if not even:
            for block in range(blocks_a_step):
                staged[slot, block] = product[
                    piece_rows * block : piece_rows * block + piece_rows, :
                ].astype(jnp.bfloat16)

    def kernel(positions_ref, left_ref, *refs):
        right_refs, refs = refs[: len(rights)], refs[len(rights) :]
        table_refs = refs[len(tables) : 2 * len(tables)]
        product, staged, sem = refs[2 * len(tables) :]
        g = pl.program_id(0)
        slot = lax.rem(g, 2)

        def settle(which):
            pltpu.make_async_copy(staged.at[which], staged.at[which], sem.at[which]).wait()

        @pl.when(g >= 2)
        def _():
            settle(slot)

        for number, right_ref in enumerate(right_refs):

            @pl.when(g // steps == number)
            def _():
                multiply(left_ref[...], right_ref, product, staged, slot)

        for block in range(blocks_a_step):
            position = positions_ref[g * blocks_a_step + block]

            for number, table_ref in enumerate(table_refs):

                @pl.when(position // TABLE == number)
                def _():
                    pltpu.make_async_copy(
                        staged.at[slot, block],
                        table_ref.at[lax.rem(position, TABLE)],
                        sem.at[slot],
                    ).start()

        @pl.when(g == total_steps - 1)
        def _():
            settle(slot)
            if total_steps > 1:
                settle(1 - slot)

    anywhere = pl.BlockSpec(memory_space=pl.ANY)
    in_specs = [
        pl.BlockSpec((step_rows, depth), lambda g, positions: (lax.rem(g, steps), 0)),
    ]
    for right, right_block in rights:
        in_specs.append(
            pl.BlockSpec((depth, col_count), lambda g, positions, k=right_block: (0, k))
        )
    in_specs += [anywhere for table in tables]
    product_shape = (8, LANES) if even else (step_rows * tiles, LANES)
    return pl.pallas_call(
        kernel,
        grid_spec=pltpu.PrefetchScalarGridSpec(
            num_scalar_prefetch=1,
            grid=(total_steps,),
            in_specs=in_specs,
            out_specs=[anywhere for table in tables],
            scratch_shapes=[
                pltpu.VMEM(product_shape, jnp.float32),
                pltpu.VMEM((2, blocks_a_step, piece_rows, LANES), jnp.bfloat16),
                pltpu.SemaphoreType.DMA((2,)),
            ],
        ),
        out_shape=[jax.ShapeDtypeStruct(table.shape, table.dtype) for table in tables],
        input_output_aliases={2 + len(rights) + i: i for i in range(len(tables))},
        cost_estimate=pl.CostEstimate(
            flops=2 * len(rights) * row_total * depth * col_count,
            bytes_accessed=2 * len(rights) * row_total * col_count,
            transcendentals=0,
        ),
        compiler_params=params(),
    )(positions, left_t, *[right for right, right_block in rights], *tables)


def optimizer_update(
    sources, slot_sources, slot_rows, slot_kinds, kinds_used, slot_masks, small_rates,
    master, moment_one, moment_two, capacity, block_range, most_blocks, earlier,
):
    piece_size = master.shape[1]
    chunks = piece_size // CHUNK
    rows = CHUNK // LANES
    last_block = pl.cdiv(capacity, 8) - 1
    steps = most_blocks * chunks

    def place(step, first, end):
        now = jnp.minimum(step, jnp.maximum((end - first) * chunks - 1, 0))
        return jnp.minimum(first + now // chunks, last_block), lax.rem(now, chunks)

    def kernel(range_ref, kinds_ref, sources_ref, rows_ref, *refs):
        source_refs, refs = refs[: len(sources)], refs[len(sources) :]
        masks_ref, small_ref, master_ref, one_ref, two_ref = refs[:5]
        refs = refs[5 + len(earlier) :]
        grad_out, master_out, one_out, two_out, low_out, scratch, buffer, sem = refs
        step = pl.program_id(0)
        count = jnp.maximum((range_ref[1] - range_ref[0]) * chunks, 1)
        first = place(step, range_ref[0], range_ref[1])[0] * 8
        slot = lax.rem(step, 2)

        def start(step, which):
            block, chunk = place(step, range_ref[0], range_ref[1])
            for s in range(8):
                for i, source_ref in enumerate(source_refs):

                    @pl.when(sources_ref[block * 8 + s] == i)
                    def _():
                        pltpu.make_async_copy(
                            source_ref.at[
                                rows_ref[block * 8 + s],
                                pl.ds(pl.multiple_of(chunk * rows, rows), rows),
                            ],
                            buffer.at[which, s],
                            sem.at[which],
                        ).start()

                @pl.when(sources_ref[block * 8 + s] >= len(sources))
                def _():
                    pltpu.make_async_copy(
                        source_refs[0].at[0, pl.ds(0, rows)], buffer.at[which, s], sem.at[which]
                    ).start()

        @pl.when(step == 0)
        def _():
            start(0, 0)

        @pl.when(step + 1 < count)
        def _():
            start(step + 1, 1 - slot)

        @pl.when(step < count)
        def _():
            pltpu.make_async_copy(buffer.at[slot], buffer.at[slot], sem.at[slot]).wait()
            for s in range(8):
                kind_now = kinds_ref[first + s]
                for kind in kinds_used:

                    @pl.when(kind_now == kind)
                    def _():
                        for tile in range(rows // TILE):
                            row_tile, column = divmod(tile, kind)
                            start_row = (row_tile * TILE * kind + column) * 8 + s
                            scratch[pl.ds(start_row, TILE, stride=8 * kind), :] = buffer[
                                slot, s, TILE * tile : TILE * tile + TILE, :
                            ].astype(jnp.float32)

            present = masks_ref[0] > 0.5
            is_small = masks_ref[1] > 0.5
            rate_rows = masks_ref[2]
            for j in range(rows):
                lanes = slice(LANES * j, LANES * j + LANES)
                grad = jnp.where(present, scratch[8 * j : 8 * j + 8, :], 0.0)
                rate = jnp.where(is_small, small_ref[:, lanes], rate_rows)
                master_now = master_ref[:, lanes]
                one_new = BETA_ONE * one_ref[:, lanes] + (1.0 - BETA_ONE) * grad
                two_new = BETA_TWO * two_ref[:, lanes] + (1.0 - BETA_TWO) * grad * grad
                first_hat = one_new / (1.0 - BETA_ONE**STEP)
                second_hat = two_new / (1.0 - BETA_TWO**STEP)
                master_new = master_now - rate * (
                    first_hat / (jnp.sqrt(second_hat) + ADAM_EPSILON) + WEIGHT_DECAY * master_now
                )
                grad_out[:, lanes] = grad
                master_out[:, lanes] = master_new
                one_out[:, lanes] = one_new
                two_out[:, lanes] = two_new
                low_out[:, lanes] = master_new.astype(jnp.bfloat16)

    state_spec = pl.BlockSpec((8, CHUNK), lambda t, ends, *tables: place(t, ends[0], ends[1]))
    anywhere = pl.BlockSpec(memory_space=pl.ANY)
    wide = jax.ShapeDtypeStruct((capacity, piece_size), jnp.float32)
    operands = [*sources, slot_masks, small_rates, master, moment_one, moment_two, *earlier]
    return pl.pallas_call(
        kernel,
        grid_spec=pltpu.PrefetchScalarGridSpec(
            num_scalar_prefetch=4,
            grid=(steps,),
            in_specs=[pl.BlockSpec(memory_space=pltpu.HBM) for source in sources]
            + [
                pl.BlockSpec((3, 8, LANES), lambda t, ends, *tables: (0, place(t, ends[0], ends[1])[0], 0)),
                pl.BlockSpec((1, CHUNK), lambda t, ends, *tables: (0, place(t, ends[0], ends[1])[1])),
                state_spec,
                state_spec,
                state_spec,
            ]
            + [anywhere for array in earlier],
            out_specs=[state_spec] * 5,
            scratch_shapes=[
                pltpu.VMEM((8 * rows, LANES), jnp.float32),
                pltpu.VMEM((2, 8, rows, LANES), jnp.bfloat16),
                pltpu.SemaphoreType.DMA((2,)),
            ],
        ),
        out_shape=[wide] * 4 + [jax.ShapeDtypeStruct((capacity, piece_size), jnp.bfloat16)],
        input_output_aliases={
            4 + len(operands) - len(earlier) + i: i for i in range(len(earlier))
        },
        cost_estimate=pl.CostEstimate(
            flops=20 * most_blocks * 8 * piece_size,
            bytes_accessed=16 * most_blocks * 8 * piece_size,
            transcendentals=2 * most_blocks * 8 * piece_size,
        ),
        compiler_params=params(),
    )(block_range, slot_kinds, slot_sources, slot_rows, *operands)


def weight_grad(left, right):
    return jnp.einsum("td,tc->dc", left, right, preferred_element_type=jnp.float32)


def back_product(grad_rows, weight):
    return jnp.dot(grad_rows, weight.T, preferred_element_type=jnp.float32)


def gather_rest(packed, first, trips, most, extra_step):
    devices = lax.axis_size("seq")
    rows = devices * extra_step
    room = reserve((most * rows,) + packed.shape[1:], packed.dtype)

    def more(trip, table):
        part = lax.dynamic_slice_in_dim(packed, first + trip * extra_step, extra_step)
        if devices != 8:
            part = lax.all_gather(part, "seq", axis=0, tiled=True)
            return lax.dynamic_update_slice_in_dim(table, part, trip * rows, axis=0)
        me = lax.axis_index("seq").astype(jnp.int32)
        chips = [part] + [moved_by(part, mask) for mask in (2, 4, 6)]
        for mask, chip in zip((0, 2, 4, 6), chips):
            for core, block in ((0, chip), (1, moved_by(chip, 1))):
                place = trip * rows + (me ^ (mask + core)) * extra_step
                table = lax.dynamic_update_slice_in_dim(table, block, place, axis=0)
        return table

    return lax.fori_loop(0, trips, more, room)


def reduce_rest(rest, trips, most, extra_step):
    devices = lax.axis_size("seq")
    rows = devices * extra_step
    room = reserve((most * extra_step,) + rest.shape[1:], rest.dtype)

    def more(trip, table):
        part = lax.dynamic_slice_in_dim(rest, trip * rows, rows)
        part = lax.psum_scatter(part, "seq", scatter_dimension=0, tiled=True)
        return lax.dynamic_update_slice_in_dim(table, part, trip * extra_step, axis=0)

    return lax.fori_loop(0, trips, more, room)


def on_device(inputs, cotangent, owners, master, moment_one, moment_two):
    head_parts = lax.axis_size("head")
    seq_parts = lax.axis_size("seq")
    local_heads = HEADS // head_parts
    capacity, piece_size = master.shape
    piece_count = owners.shape[0]
    row_count = inputs.shape[0]
    rim_width = KCONV - 1
    segments_list = shard_layout(local_heads, head_parts)
    columns = {name: c for name, r, c, rate in segments_list}
    counts = {name: r * c // piece_size for name, r, c, rate in segments_list[:8]}
    firsts = dict(zip(counts, np.cumsum([0] + list(counts.values())).tolist()))
    mixer_count = firsts["wgate"]
    big_count = piece_count - 1
    my_head = lax.axis_index("head").astype(jnp.int32)
    my_index = lax.axis_index("seq").astype(jnp.int32)
    my_head_row, my_index_row = my_head.reshape(1), my_index.reshape(1)

    onehot = (owners[:, None] == jnp.arange(seq_parts, dtype=jnp.int32)[None, :]).astype(jnp.int32)
    ranks = jnp.sum((jnp.cumsum(onehot, axis=0) - onehot) * onehot, axis=1)
    mixer_held = jnp.sum(onehot[:mixer_count], axis=0)
    mlp_held = jnp.sum(onehot[mixer_count:big_count], axis=0)
    padded = capacity + -capacity % 8
    small_rank = ranks[big_count]
    big_owners, big_ranks = owners[:big_count], ranks[:big_count]

    def rest_row(over, owner):
        return over // extra_step * (seq_parts * extra_step) + owner * extra_step + over % extra_step

    early = -(-capacity * FIRST_GATHER // (8 * CAPACITY_UNIT)) * 8
    late = capacity - early
    late_room = min(late, -(-capacity * SECOND_GATHER // CAPACITY_UNIT))
    extra_step = 2 if late % 2 == 0 else 1
    most_gather = -(-late // extra_step)
    trips_gather = jnp.maximum(-(-(jnp.max(mixer_held) - early) // extra_step), 0)
    early_row = big_owners * early + big_ranks
    mixer_fetch = jnp.where(
        big_ranks < early, early_row, TABLE + rest_row(big_ranks - early, big_owners)
    )
    neighbours = np.arange(seq_parts) ^ 1
    late_held = jnp.maximum(mixer_held + mlp_held - early, 0)
    late_spare = jnp.maximum(late_room - late_held[neighbours], 0)
    late_over = jnp.maximum(late_held - late_room, 0)
    trips_late = -(-jnp.max(jnp.maximum(late_over - late_spare, 0)) // extra_step)
    spare_there = jnp.sum(onehot[:big_count] * late_spare[None, :], axis=1)
    past = big_ranks - early - late_room
    rest_trip = (past - spare_there) // extra_step
    rest_start = late_room + spare_there + rest_trip * extra_step
    rest_start = jnp.minimum(rest_start, late - extra_step)
    mlp_fetch = jnp.where(
        big_ranks < early,
        TABLE + early_row,
        jnp.where(
            past < 0,
            big_owners * late_room + big_ranks - early,
            jnp.where(
                past < spare_there,
                (big_owners ^ 1) * late_room + late_room - spare_there + past,
                2 * TABLE
                + rest_trip * (seq_parts * extra_step)
                + big_owners * extra_step
                + big_ranks - early - rest_start,
            ),
        ),
    )
    first_room = -(-capacity * FIRST_REDUCE // CAPACITY_UNIT)
    second_room = -(-capacity * SECOND_REDUCE // CAPACITY_UNIT)
    most_reduce = -(-(capacity - second_room) // extra_step)
    second_held = mixer_held + jnp.maximum(mlp_held - first_room, 0)
    second_there = jnp.sum(onehot[:big_count] * second_held[None, :], axis=1)
    spill_plan, spill_taken = [], jnp.zeros_like(second_held)
    hosted = jnp.zeros_like(second_held)
    over_held = jnp.maximum(second_held - second_room, 0)
    for mask, most in (((1, 6), (2, 4), (4, 4), (6, 4)) if seq_parts == 8 else ((1, 4),)):
        most = min(most, second_room)
        partner = np.arange(seq_parts) ^ mask
        free = jnp.maximum(second_room - second_held - hosted, 0)[partner]
        take = jnp.minimum(jnp.minimum(over_held - spill_taken, most - hosted[partner]), free)
        take = jnp.maximum(take, 0)
        first_row = second_room - hosted[partner] - take
        spill_plan.append((mask, most, spill_taken, take, first_row))
        spill_taken = spill_taken + take
        hosted = hosted + take[partner]
    trips_reduce = -(-jnp.max(over_held - spill_taken) // extra_step)

    def of_owner(values):
        return jnp.sum(onehot[:big_count] * values[None, :], axis=1)

    second_over = big_ranks - second_room
    second_spot = jnp.where(
        second_over < 0,
        TABLE + big_owners * second_room + big_ranks,
        2 * TABLE + rest_row(second_over - of_owner(spill_taken), big_owners),
    )
    for mask, most, before, take, first_row in spill_plan:
        inside = second_over - of_owner(before)
        second_spot = jnp.where(
            (inside >= 0) & (inside < of_owner(take)),
            TABLE + (big_owners ^ mask) * second_room + of_owner(first_row) + inside,
            second_spot,
        )
    store = jnp.where(
        big_ranks >= second_there,
        big_owners * first_room + big_ranks - second_there,
        second_spot,
    )
    small_owner = owners[big_count]

    def spots(table, name):
        return table[firsts[name] : firsts[name] + counts[name]]

    my_mixer = mixer_held[my_index]
    my_mlp = mlp_held[my_index]
    my_count = my_mixer + my_mlp
    slot_ids = jnp.arange(padded, dtype=jnp.int32)
    mine = owners == my_index
    matches = (mine[None, :] & (ranks[None, :] == slot_ids[:, None])).astype(jnp.int32)
    kind_table = piece_kinds(segments_list, piece_count, piece_size)
    piece_rates, small_rates = rate_parts(segments_list, piece_count, piece_size)
    present = jnp.sum(matches, axis=1)
    slot_kinds = 1 + jnp.sum(matches * jnp.asarray(kind_table - 1)[None, :], axis=1)
    slot_rates = PAD_RATE + jnp.sum(
        matches.astype(jnp.float32) * jnp.asarray(piece_rates - np.float32(PAD_RATE))[None, :], axis=1
    )
    is_small = matches[:, big_count]
    kinds_used = sorted(set(kind_table.tolist()) | {1})
    my_held = second_held[my_index]
    in_first = slot_ids >= my_held
    my_over = slot_ids - second_room
    rest_source = 3 + len(spill_plan)
    slot_sources = jnp.where(my_over < 0, 2, rest_source)
    slot_rows = jnp.where(my_over < 0, slot_ids, my_over - spill_taken[my_index])
    for number, (mask, most, before, take, first_row) in enumerate(spill_plan):
        inside = my_over - before[my_index]
        here = (inside >= 0) & (inside < take[my_index])
        slot_sources = jnp.where(here, 3 + number, slot_sources)
        slot_rows = jnp.where(
            here, first_row[my_index] + inside - (second_room - most), slot_rows
        )
    slot_sources = jnp.where(in_first, 0, slot_sources)
    slot_rows = jnp.where(in_first, slot_ids - my_held, slot_rows)
    slot_sources = jnp.where(present > 0, jnp.where(is_small > 0, 1, slot_sources), 0)
    slot_rows = jnp.where(is_small > 0, 0, slot_rows)
    slot_rows = jnp.where(present > 0, slot_rows, 0)
    slot_masks = jnp.stack([present.astype(jnp.float32), is_small.astype(jnp.float32), slot_rates])
    slot_masks = jnp.broadcast_to(slot_masks[:, :, None], slot_masks.shape + (LANES,))
    all_blocks = padded // 8
    plain_blocks = second_room // 8
    from_first = jnp.clip((my_held + 7) // 8, plain_blocks, all_blocks).astype(jnp.int32)
    ranges = [
        jnp.stack([from_first, jnp.int32(all_blocks)]),
        jnp.array([0, plain_blocks], jnp.int32),
        jnp.stack([jnp.int32(plain_blocks), jnp.maximum(from_first, plain_blocks + 1)]),
    ]

    small_rows = -(-sum(r * c for name, r, c, rate in segments_list[8:]) // (TILE * LANES)) * TILE
    gain_width = D // head_parts
    norm_width = DV // head_parts
    gain_first = sum(r * c for name, r, c, rate in segments_list[8:14])
    my_small = lax.dynamic_slice(master, (small_rank, 0), (1, small_rows * LANES))
    my_small = my_small.astype(jnp.bfloat16)
    gains = my_small[:, gain_first : gain_first + 2 * gain_width + norm_width]
    gains = in_order(exchange([gains] * head_parts, "head"), my_head, 0)
    gains = jnp.concatenate(
        [
            gains[:, :gain_width].reshape(1, D),
            gains[:, gain_width : 2 * gain_width].reshape(1, D),
            gains[:, 2 * gain_width :].reshape(1, DV),
        ],
        axis=1,
    )
    rows_of_piece = piece_size // LANES
    small_width = small_rows * LANES
    small_part = jnp.concatenate([my_small, gains], axis=1).reshape(-1, LANES)
    small_table, small_base = gather_states(small_part)
    input_blocks = exchange([inputs] * head_parts, "head")
    early_part = pack_blocks(master, slot_kinds, kinds_used, 0, early)
    early_table = lax.all_gather(early_part, "seq", axis=0, tiled=True)
    late_part = pack_blocks(master, slot_kinds, kinds_used, early, late)
    late_send = late_part[:late_room]
    if late_room < late:
        guests = lax.ppermute(
            late_part[late_room:], "seq", [(i, i ^ 1) for i in range(seq_parts)]
        )
        late_send = lax.dynamic_update_slice_in_dim(
            late_part, guests, late_held[my_index], axis=0
        )[:late_room]
    back_blocks = exchange([cotangent] * head_parts, "head")
    rows_full = in_order(input_blocks, my_head, 1)
    back_full = in_order(back_blocks, my_head, 1)
    small_flat = lax.dynamic_index_in_dim(
        small_table, small_owner ^ small_base[0], axis=0, keepdims=False
    ).reshape(-1)
    by_name, small_used = unpack(small_flat, segments_list[8:])
    gains = small_flat[small_width:].astype(jnp.float32)[None, :]
    gain_one, gain_two, norm_row = gains[:, :D], gains[:, D : 2 * D], gains[:, 2 * D :]
    gain_one_mine = by_name["gainone"].astype(jnp.float32)
    gain_two_mine = by_name["gaintwo"].astype(jnp.float32)

    rows_wide = rows_full.astype(jnp.float32)
    scale_one = lax.rsqrt(jnp.mean(rows_wide * rows_wide, axis=-1, keepdims=True) + NORM_EPSILON)
    normed = (rows_wide * scale_one * gain_one).astype(jnp.bfloat16)
    normed_ext = stored(
        jnp.concatenate([shifted(normed[row_count - RIM :], "seq", 1), normed], axis=0)
    )

    decay_weight = jnp.pad(by_name["wab"], ((0, 0), (0, LANES - 2 * local_heads)))
    decay_proj = jnp.dot(normed, decay_weight, preferred_element_type=jnp.float32)
    taps = jnp.concatenate([by_name["cv"], by_name["ck"]], axis=1)
    taps = jnp.pad(taps.astype(jnp.float32), ((0, 8 - KCONV), (0, 0)))
    query_taps = jnp.pad(by_name["cq"].astype(jnp.float32), ((0, 8 - KCONV), (0, 0)))
    scalars = jnp.pad(
        jnp.concatenate([by_name["alog"], by_name["dtbias"]], axis=0).astype(jnp.float32),
        ((0, 6), (0, LANES - local_heads)),
    )

    mixer_rest = gather_rest(late_part, 0, trips_gather, most_gather, extra_step)
    beside = (
        mixer_rest, late_part, late_send, normed, normed_ext, scale_one, decay_proj, decay_weight, taps, query_taps, scalars,
        back_full, mixer_fetch, mlp_fetch, store, gain_two, norm_row,
        slot_sources, slot_rows, slot_masks, ranges, trips_late, trips_reduce,
    )
    early_table, beside = lax.optimization_barrier((early_table, beside))
    (
        mixer_rest, late_part, late_send, normed, normed_ext, scale_one, decay_proj, decay_weight, taps, query_taps, scalars,
        back_full, mixer_fetch, mlp_fetch, store, gain_two, norm_row,
        slot_sources, slot_rows, slot_masks, ranges, trips_late, trips_reduce,
    ) = beside
    late_table = lax.all_gather(late_send, "seq", axis=0, tiled=True)

    value_key_weights, value_key = assemble(
        [early_table, mixer_rest],
        [(spots(mixer_fetch, name), columns[name]) for name in ("wv", "wk")],
        512,
        normed_ext,
    )
    solve, fresh, wy_keys, handoff = mixer_local(
        local_heads, value_key, taps, decay_proj, scalars
    )
    query_gate_weights, query_gate = assemble(
        [early_table, mixer_rest],
        [(spots(mixer_fetch, name), columns[name]) for name in ("wq", "wg")],
        512,
        normed_ext,
    )
    reach, zero_out = mixer_reach(
        local_heads, query_gate, value_key, query_taps, taps, decay_proj, scalars, fresh, wy_keys
    )
    (out_weights,) = assemble(
        [early_table, mixer_rest], [(spots(mixer_fetch, "wo"), columns["wo"])], 256
    )
    entering_state, kept_states, beside = entering(
        local_heads,
        my_index_row,
        handoff,
        (query_gate_weights, query_gate, reach, zero_out, out_weights),
    )
    query_gate_weights, query_gate, reach, zero_out, out_weights = beside
    recurred, gated_low = mixer_out(
        local_heads, entering_state, reach, zero_out, query_gate, norm_row
    )
    mixed_parts = exchange(
        spread_products(my_head_row, head_parts, [((gated_low,), out_weights, False)]), "head"
    )
    mixed = total_of(mixed_parts)
    inputs_wide = inputs.astype(jnp.float32)
    residual = inputs_wide + mixed
    resid_low = residual.astype(jnp.bfloat16)

    resid_blocks = exchange([resid_low] * head_parts, "head")
    trips_now, late_table = lax.optimization_barrier((trips_late, late_table))
    late_rest = gather_rest(
        late_part, late_room + late_spare[my_index], trips_now, most_gather, extra_step
    )
    mlp_tables = [late_table, early_table, late_rest]
    (down_weights,) = assemble(
        mlp_tables, [(spots(mlp_fetch, "wdown"), columns["wdown"])], 352
    )
    (mlp_weights,) = assemble(
        mlp_tables,
        [(spots(mlp_fetch, name), columns[name]) for name in ("wgate", "wup")],
        512,
    )
    resid_blocks, down_weights, mlp_weights = lax.optimization_barrier(
        (resid_blocks, down_weights, mlp_weights)
    )
    resid_full = in_order(resid_blocks, my_head, 1).astype(jnp.float32)
    scale_two = lax.rsqrt(jnp.mean(resid_full * resid_full, axis=-1, keepdims=True) + NORM_EPSILON)
    hidden_in = (resid_full * scale_two * gain_two).astype(jnp.bfloat16)
    gate_up = jnp.dot(hidden_in, mlp_weights, preferred_element_type=jnp.float32)
    hidden_width = columns["wgate"]
    gate_mlp, up_mlp = gate_up[:, :hidden_width], gate_up[:, hidden_width:]
    logistic_output_multiplier = jax.nn.sigmoid(gate_mlp)
    silu_gate = gate_mlp * logistic_output_multiplier
    hidden = (silu_gate * up_mlp).astype(jnp.bfloat16)
    mlp_blocks = spread_products(my_head_row, head_parts, [((hidden,), down_weights, False)])
    d_hidden = back_product(back_full, down_weights)
    d_gate_mlp = (
        d_hidden
        * up_mlp
        * logistic_output_multiplier
        * (1.0 + gate_mlp * (1.0 - logistic_output_multiplier))
    ).astype(jnp.bfloat16)
    d_up_mlp = (d_hidden * silu_gate).astype(jnp.bfloat16)
    def store_grad(tables, names, left_t, rights, blocks_a_step):
        positions = jnp.concatenate([spots(store, name) for name in names])
        return weight_grad_blocks(
            left_t, rights, columns[names[0]], positions, tables, blocks_a_step
        )

    grad_tables = [
        reserve((rows, rows_of_piece, LANES), jnp.bfloat16)
        for rows in (
            seq_parts * first_room,
            seq_parts * second_room,
            most_reduce * seq_parts * extra_step,
        )
    ]
    grad_tables = store_grad(grad_tables, ["wdown"], hidden.T, [(back_full, 0)], 11)
    hidden_in_t = hidden_in.T
    grad_tables = store_grad(
        grad_tables, ["wgate", "wup"], hidden_in_t, [(d_gate_mlp, 0), (d_up_mlp, 0)], 11
    )
    grad_tables, d_gate_mlp, d_up_mlp = lax.optimization_barrier(
        (grad_tables, d_gate_mlp, d_up_mlp)
    )
    d_hidden_parts = exchange(
        spread_products(my_head_row, head_parts, [((d_gate_mlp, d_up_mlp), mlp_weights, True)]), "head"
    )
    first_reduced = lax.psum_scatter(grad_tables[0], "seq", scatter_dimension=0, tiled=True)
    grad_tables = grad_tables[1:]
    store = store - TABLE
    d_hidden_mine = total_of(d_hidden_parts)

    resid_mine = resid_low.astype(jnp.float32)
    d_hidden_low = d_hidden_mine.astype(jnp.bfloat16)
    dot_mine = jnp.sum(d_hidden_mine * gain_two_mine * resid_mine, axis=-1)
    d_hidden_blocks = exchange([d_hidden_low] * head_parts, "head")
    dot_two = sum_over(dot_mine.reshape(-1, LANES), "head").reshape(row_count, 1)
    grad_gaintwo = jnp.sum(d_hidden_mine * resid_mine * scale_two, axis=0)
    d_resid = (
        cotangent.astype(jnp.float32)
        + scale_two * d_hidden_mine * gain_two_mine
        - scale_two**3 / D * resid_mine * dot_two
    )
    d_hidden_full = in_order(d_hidden_blocks, my_head, 1).astype(jnp.float32)
    back_mix_full = (
        back_full.astype(jnp.float32)
        + scale_two * d_hidden_full * gain_two
        - scale_two**3 / D * resid_full * dot_two
    ).astype(jnp.bfloat16)

    d_gated = back_product(back_mix_full, out_weights)
    d_recurred, d_gate, norm_grad, d_entering = mixer_gate_back(
        local_heads, d_gated, recurred, query_gate, norm_row, reach
    )
    normed_t = normed.T
    grad_tables = store_grad(grad_tables, ["wo"], gated_low.T, [(back_mix_full, 0)], 8)
    grad_tables = store_grad(grad_tables, ["wg"], normed_t, [(d_gate, 0)], 8)
    d_leaving, (grad_tables, mlp_blocks) = leaving(
        local_heads, my_index_row, d_entering, kept_states, (grad_tables, mlp_blocks)
    )
    mlp_parts = exchange(mlp_blocks, "head")
    d_conv, d_tail, d_rim, d_taps, d_decay_wide, d_scalars = mixer_back(
        local_heads,
        query_gate,
        value_key,
        query_taps,
        taps,
        decay_proj,
        scalars,
        solve,
        fresh,
        wy_keys,
        entering_state,
        d_recurred,
        d_leaving,
    )
    d_rims = shifted(tuple(part[8 - rim_width :] for part in d_rim), "seq", -1)

    def with_rim(whole, tail, rim_grad):
        tail = tail + jnp.pad(rim_grad, ((8 - rim_width, 0), (0, 0)))
        return lax.dynamic_update_slice(whole, tail.astype(jnp.bfloat16), (row_count - 8, 0))

    d_query, d_value_key = (
        with_rim(*parts) for parts in zip(d_conv, d_tail, d_rims)
    )
    grad_tables = store_grad(grad_tables, ["wv"], normed_t, [(d_value_key, 0)], 8)
    grad_tables = store_grad(
        grad_tables, ["wk", "wq"], normed_t, [(d_value_key, 2), (d_query, 0)], 4
    )
    second_table, first_reduced, mlp_parts = lax.optimization_barrier(
        (grad_tables[0], first_reduced, mlp_parts)
    )
    block_out = (residual + total_of(mlp_parts)).astype(jnp.bfloat16)
    second_reduced = lax.psum_scatter(second_table, "seq", scatter_dimension=0, tiled=True)
    d_decay = d_decay_wide.astype(jnp.bfloat16)
    grad_wab = weight_grad(normed, d_decay)[:, : 2 * local_heads]
    d_normed_mine = total_of(
        exchange(
            spread_products(
                my_head_row,
                head_parts,
                [
                    ((d_value_key,), value_key_weights, True),
                    ((d_query, d_gate), query_gate_weights, True),
                    ((d_decay,), decay_weight, True),
                ],
            ),
            "head",
        )
    )
    dot_one = jnp.sum(d_normed_mine * gain_one_mine * inputs_wide, axis=-1)
    sums = sum_over(
        jnp.concatenate([dot_one.reshape(-1, LANES), norm_grad[0].reshape(-1, LANES)]), "head"
    )
    dot_one = sums[: row_count // LANES].reshape(row_count, 1)
    grad_wnorm = lax.dynamic_slice_in_dim(
        sums[row_count // LANES :].reshape(-1), my_head * norm_width, norm_width
    )
    grad_gainone = jnp.sum(d_normed_mine * inputs_wide * scale_one, axis=0)
    input_grad = (
        d_resid
        + scale_one * d_normed_mine * gain_one_mine
        - scale_one**3 / D * inputs_wide * dot_one
    )

    small_grads = [
        d_taps[0][:KCONV],
        d_taps[1][:KCONV, local_heads * DV :],
        d_taps[1][:KCONV, : local_heads * DV],
        grad_wab,
        d_scalars[0, :local_heads],
        d_scalars[1, :local_heads],
        grad_gainone,
        grad_gaintwo,
        grad_wnorm,
    ]
    small_block = jnp.concatenate(
        [grad_now.reshape(-1) for grad_now in small_grads]
        + [jnp.zeros((small_rows * LANES - small_used,), jnp.float32)]
    ).reshape(-1, LANES)
    mask = 1
    while mask < seq_parts:
        small_block = small_block + lax.ppermute(
            small_block, "seq", [(i, i ^ mask) for i in range(seq_parts)]
        )
        mask *= 2
    small_block = jnp.pad(
        small_block.astype(jnp.bfloat16), ((0, rows_of_piece - small_rows), (0, 0))
    )[None]

    def update(sources, block_range, most_blocks, states, earlier):
        return optimizer_update(
            sources,
            slot_sources,
            slot_rows,
            slot_kinds,
            kinds_used,
            slot_masks,
            jnp.asarray(small_rates)[None, :],
            *states,
            capacity,
            block_range,
            most_blocks,
            earlier,
        )

    states = [master, moment_one, moment_two]
    done = update([first_reduced, small_block], ranges[0], all_blocks - plain_blocks, states, [])
    done, second_reduced, input_grad, block_out = lax.optimization_barrier(
        (done, second_reduced, input_grad, block_out)
    )
    spilled = []
    for mask, most, before, take, first_row in spill_plan:
        spilled.append(moved_by(second_reduced[second_room - most :], mask))
    sources = [first_reduced, small_block, second_reduced]
    if plain_blocks:
        done = update(sources, ranges[1], plain_blocks, states, done)
    done, spilled, rest_grads, trips_now = lax.optimization_barrier(
        (done, spilled, grad_tables[1], trips_reduce)
    )
    rest_reduced = reduce_rest(rest_grads, trips_now, most_reduce, extra_step)
    grad_slots, master_new, moment_new, second_new, weights_low = update(
        sources + spilled + [rest_reduced],
        ranges[2],
        all_blocks - plain_blocks,
        states,
        done,
    )
    return (
        block_out,
        input_grad,
        grad_slots,
        master_new,
        moment_new,
        second_new,
        weights_low,
    )


def solution(mesh):
    return jax.shard_map(
        on_device,
        mesh=mesh,
        in_specs=(
            P("seq", "head"),
            P("seq", "head"),
            P(),
            P("seq", "head"),
            P("seq", "head"),
            P("seq", "head"),
        ),
        out_specs=(
            P("seq", "head"),
            P("seq", "head"),
            P("seq", "head"),
            P("seq", "head"),
            P("seq", "head"),
            P("seq", "head"),
            P("seq", "head"),
        ),
        check_vma=False,
    )
```
